32 devices in a mesh: dp: 8 (over y, x, core), seq: 4 (over z).
Axes of the slice: x: 2, y: 2, z: 4, core: 2. Of those that a mesh axis runs over, the one named last changes fastest.
Arguments:
- tokens: bfloat16 [32768, 768], P(('dp', 'seq')), may hold values from -6 to 6
- item_types: int32 [8, 64], P('dp'), may hold values from 0 to 3, as said below
- first_gain: float32 [768], replicated, may hold values from 0.5 to 1.5
- first_shift: float32 [768], replicated, may hold values from -4 to 4
- qkv_weight: bfloat16 [768, 2304], replicated, may hold values from -0.21875 to 0.21875
- query_bias: float32 [768], replicated, may hold values from -6 to 6
- value_bias: float32 [768], replicated, may hold values from -6 to 6
- attn_weight: bfloat16 [768, 768], replicated, may hold values from -1.75 to 1.75
- attn_bias: float32 [768], replicated, may hold values from -3 to 3
- second_gain: float32 [3, 768], replicated, may hold values from 0.5 to 1.5
- second_shift: float32 [3, 768], replicated, may hold values from -4 to 4
- expert_up: bfloat16 [3, 768, 3072], replicated, may hold values from -0.21875 to 0.21875
- up_bias: float32 [3, 3072], replicated, may hold values from -1.5 to 1.5
- expert_down: bfloat16 [3, 3072, 768], replicated, may hold values from -0.15625 to 0.15625
- down_bias: float32 [3, 768], replicated, may hold values from -1.5 to 1.5
- cotangent: bfloat16 [32768, 768], P(('dp', 'seq')), may hold values from -6 to 6
Outputs:
- mixed: bfloat16 [32768, 768], P(('dp', 'seq'))
- grad_tokens: float32 [32768, 768], P(('dp', 'seq'))
- grad_first_gain: float32 [768], P(('dp', 'seq'))
- grad_first_shift: float32 [768], P(('dp', 'seq'))
- grad_qkv_weight: float32 [768, 2304], P(None, ('dp', 'seq'))
- grad_query_bias: float32 [768], P(('dp', 'seq'))
- grad_value_bias: float32 [768], P(('dp', 'seq'))
- grad_attn_weight: float32 [768, 768], P(None, ('dp', 'seq'))
- grad_attn_bias: float32 [768], P(('dp', 'seq'))
- grad_second_gain: float32 [3, 768], P(None, ('dp', 'seq'))
- grad_second_shift: float32 [3, 768], P(None, ('dp', 'seq'))
- grad_expert_up: float32 [3, 768, 3072], P(None, ('dp', 'seq'))
- grad_up_bias: float32 [3, 3072], replicated
- grad_expert_down: float32 [3, 3072, 768], P(None, None, ('dp', 'seq'))
- grad_down_bias: float32 [3, 768], P(None, ('dp', 'seq'))
The draws below stay inside these ranges and needn't reach their ends.
Inputs may be any that keep to these rules, and one draw needn't show every extreme that they name: `item_types`: 0, 1, 2 are image, text and image-text items, 3 an empty slot; the slots of a packed sequence are filled from the first, its items take at most 4096 tokens and leave fewer than 261 unused.
All inputs are finite; a program needn't handle non-finite values.
Results may differ from the reference program's by a relative error of at most 0.0095.
The reference program's roundings to bfloat16 on the way count: a program that leaves them out, or rounds other values in their place, can miss the bound.
Values may be sent and summed in bfloat16 or wider, within the bound.
No kernel may reach another device: no remote copies, remote signals or barrier semaphores. Data moves between devices by JAX's collectives and lax.ppermute only.
A program may use at most 384 MiB of HBM per device.

```python
import jax
import jax.numpy as jnp
from jax import lax

D = 768
HEADS = 12
HD = 64
FF = 3072
EXPERTS = 3
QBLK = 512
IMG_LEN = 197
TXT_LEN = 64
SEQ_TOK = 4096
ITEMS = 64
GROUPS = 8
TOKENS = 32768


def draw_item_types(key, part):
    key = jax.random.fold_in(key, 7)
    picked = jax.random.randint(key, (GROUPS, ITEMS), 0, 3).astype(jnp.int32)
    lengths = jnp.where(picked == 0, IMG_LEN, jnp.where(picked == 1, TXT_LEN, IMG_LEN + TXT_LEN)).astype(jnp.int32)
    ends = jnp.cumsum(lengths, axis=1).astype(jnp.int32)
    return jnp.where(ends <= SEQ_TOK, picked, 3).astype(jnp.int32)


def block_levels(rng, extent, pieces, low, top_value):
    level, own = 1.0, jax.random.fold_in(rng, 6)
    for position, shards_of in pieces:
        heights = jnp.exp(jax.random.uniform(jax.random.fold_in(own, position), (shards_of,), jnp.float32, low / len(pieces), top_value / len(pieces)))
        level = level * jnp.repeat(heights, extent[position] // shards_of).reshape([-1 if axis == position else 1 for axis in range(len(extent))])
    return level


def gaussian(rng, shape, scale, bound, cuts=(), kind=jnp.bfloat16):
    factor_of = block_levels(rng, shape, cuts, -0.22, 0.18) if cuts else 1.0
    entries = jax.random.normal(rng, shape, jnp.float32) * scale * factor_of
    return jnp.minimum(jnp.maximum(entries, -bound), bound).astype(kind)


def setup_inputs(seed: int = 0) -> dict:
    key_of = jax.random.split(jax.random.key(seed), 17)
    tokens = gaussian(key_of[0], (TOKENS, D), 1.0, 6.0, ((0, 32),))
    item_types = draw_item_types(jax.random.fold_in(key_of[16], 71), 0)
    first_gain = jnp.clip(1.0 + 0.1 * jax.random.normal(key_of[2], (D,), jnp.float32), 0.5, 1.5)
    first_shift = gaussian(key_of[3], (D,), 0.3, 4.0, (), jnp.float32)
    qkv_weight = gaussian(key_of[4], (D, 3 * D), D ** -0.5, 0.21875)
    query_bias = gaussian(key_of[5], (D,), 0.5, 6.0, (), jnp.float32)
    value_bias = gaussian(key_of[6], (D,), 0.5, 6.0, (), jnp.float32)
    attn_weight = gaussian(key_of[7], (D, D), (D // 64) ** -0.5, 1.75)
    attn_bias = gaussian(key_of[8], (D,), 0.2, 3.0, (), jnp.float32)
    second_gain = jnp.clip(1.0 + 0.1 * jax.random.normal(key_of[9], (EXPERTS, D), jnp.float32), 0.5, 1.5)
    second_shift = gaussian(key_of[10], (EXPERTS, D), 0.3, 4.0, (), jnp.float32)
    expert_up = gaussian(key_of[11], (EXPERTS, D, FF), D ** -0.5, 0.21875)
    up_bias = gaussian(key_of[12], (EXPERTS, FF), 0.1, 1.5, (), jnp.float32)
    expert_down = gaussian(key_of[13], (EXPERTS, FF, D), (FF // 2) ** -0.5, 0.15625)
    down_bias = gaussian(key_of[14], (EXPERTS, D), 0.1, 1.5, (), jnp.float32)
    cotangent = gaussian(key_of[15], (TOKENS, D), 1.0, 6.0, ((0, 32),))
    return dict(tokens=tokens, item_types=item_types, first_gain=first_gain, first_shift=first_shift, qkv_weight=qkv_weight, query_bias=query_bias, value_bias=value_bias, attn_weight=attn_weight, attn_bias=attn_bias, second_gain=second_gain, second_shift=second_shift, expert_up=expert_up, up_bias=up_bias, expert_down=expert_down, down_bias=down_bias, cotangent=cotangent)


EPS = 1e-05
NEG = -1e+30
HIGH = lax.Precision.HIGHEST

@jax.custom_vjp
def low(v):
    return lax.optimization_barrier(v.astype(jnp.bfloat16)).astype(jnp.float32)

@jax.custom_vjp
def low_back(v):
    return v

def low_keep(v):
    return (low(v), None)

def low_pass(kept, grad):
    return (grad,)

def back_keep(v):
    return (v, None)

def back_low(kept, grad):
    return (low(grad),)
low.defvjp(low_keep, low_pass)
low_back.defvjp(back_keep, back_low)

def normalize(v):
    mean = lax.optimization_barrier(jnp.mean(v, axis=-1, keepdims=True))
    cent = v - mean
    var = lax.optimization_barrier(jnp.mean(cent * cent, axis=-1, keepdims=True))
    return cent * lax.rsqrt(var + EPS)

def layout(types_row, positions):
    lengths = jnp.where(types_row == 0, IMG_LEN, jnp.where(types_row == 1, TXT_LEN, jnp.where(types_row == 2, IMG_LEN + TXT_LEN, 0))).astype(jnp.int32)
    ends = jnp.cumsum(lengths).astype(jnp.int32)
    segment = lax.optimization_barrier(jnp.sum((positions[:, None] >= ends[None, :]).astype(jnp.int32), axis=1)).astype(jnp.int32)
    item_hot = (segment[:, None] == jnp.arange(ITEMS, dtype=jnp.int32)[None, :]).astype(jnp.float32)
    type_hot = (types_row[:, None] == jnp.arange(EXPERTS, dtype=jnp.int32)[None, :]).astype(jnp.float32)
    modal = jnp.dot(item_hot, type_hot, precision=HIGH)
    return (segment, modal)

def attention(qkv, segment):
    group = qkv.shape[0]
    blocks = group // QBLK
    query = qkv[:, 0]
    keys = qkv[:, 1]
    values = qkv[:, 2]

    def one_block(index):
        start = (index * QBLK).astype(jnp.int32)
        begin = jnp.clip(start - QBLK, 0, group - 3 * QBLK).astype(jnp.int32)
        rows = lax.dynamic_slice_in_dim(query, start, QBLK, 0)
        cols = lax.dynamic_slice_in_dim(keys, begin, 3 * QBLK, 0)
        vals = lax.dynamic_slice_in_dim(values, begin, 3 * QBLK, 0)
        seg_rows = lax.dynamic_slice_in_dim(segment, start, QBLK, 0)
        seg_cols = lax.dynamic_slice_in_dim(segment, begin, 3 * QBLK, 0)
        scores = low_back(jnp.einsum('qhd,khd->hqk', rows, cols, precision=HIGH))
        mask = (seg_rows[:, None] == seg_cols[None, :])[None]
        masked = jnp.where(mask, scores, NEG)
        top = lax.optimization_barrier(jnp.max(masked, axis=-1, keepdims=True))
        expo = jnp.exp(masked - top)
        prob = low(expo / lax.optimization_barrier(jnp.sum(expo, axis=-1, keepdims=True)))
        return jnp.einsum('hqk,khd->qhd', prob, vals, precision=HIGH)
    outs = lax.map(jax.checkpoint(one_block), jnp.arange(blocks, dtype=jnp.int32))
    return outs.reshape(group, HEADS * HD)

def forward(x, first_gain, first_shift, qkv_weight, query_bias, value_bias, attn_weight, attn_bias, second_gain, second_shift, expert_up, up_bias, expert_down, down_bias, segment, modal):
    width = x.shape[1]
    scale = HD ** (-0.5)
    hidden_one = low(normalize(x) * first_gain + first_shift)
    bias_full = jnp.concatenate([query_bias, jnp.zeros((width,), x.dtype), value_bias])
    scale_vec = jnp.concatenate([jnp.full((width,), scale, x.dtype), jnp.ones((2 * width,), x.dtype)])
    qkv = low(low_back((jnp.dot(hidden_one, qkv_weight, precision=HIGH) + bias_full) * scale_vec))
    attended = low(low_back(attention(qkv.reshape(-1, 3, HEADS, HD), segment)))
    middle = x + low_back(jnp.dot(attended, attn_weight, precision=HIGH) + attn_bias)
    gains = jnp.dot(modal, second_gain, precision=HIGH)
    shifts = jnp.dot(modal, second_shift, precision=HIGH)
    hidden_two = low(normalize(middle) * gains + shifts)
    branch = jnp.zeros_like(middle)
    for expert in range(EXPERTS):
        upper = low_back(jnp.dot(hidden_two, expert_up[expert], precision=HIGH) + up_bias[expert])
        active = low(jax.nn.gelu(upper, approximate=False))
        lower = jnp.dot(active, expert_down[expert], precision=HIGH) + down_bias[expert]
        branch = branch + modal[:, expert:expert + 1] * lower
    return middle + branch

def reference(tokens, item_types, first_gain, first_shift, qkv_weight, query_bias, value_bias, attn_weight, attn_bias, second_gain, second_shift, expert_up, up_bias, expert_down, down_bias, cotangent):
    params = (first_gain, first_shift, qkv_weight.astype(jnp.float32), query_bias, value_bias, attn_weight.astype(jnp.float32), attn_bias, second_gain, second_shift, expert_up.astype(jnp.float32), up_bias, expert_down.astype(jnp.float32), down_bias)
    inputs_all = tokens.astype(jnp.float32).reshape(GROUPS, SEQ_TOK, D)
    cots_all = cotangent.astype(jnp.float32).reshape(GROUPS, SEQ_TOK, D)
    positions = jnp.arange(SEQ_TOK, dtype=jnp.int32)

    def step(totals, inputs):
        x_group, cot_group, types_row = inputs
        segment, modal = layout(types_row, positions)

        def apply_layer(x_value, *weights):
            return forward(x_value, *weights, segment, modal)
        result, back = jax.vjp(apply_layer, x_group, *params)
        grads = back(cot_group)
        totals = tuple((total + grad for total, grad in zip(totals, grads[1:])))
        return (totals, (result, grads[0]))
    zeros = tuple((jnp.zeros_like(param) for param in params))
    totals, (results, grad_inputs) = lax.scan(step, zeros, (inputs_all, cots_all, item_types))
    g_first_gain, g_first_shift, g_qkv, g_query, g_value, g_attn, g_attn_bias, g_second_gain, g_second_shift, g_up, g_up_bias, g_down, g_down_bias = totals
    return (results.reshape(TOKENS, D).astype(jnp.bfloat16), grad_inputs.reshape(TOKENS, D), g_first_gain, g_first_shift, g_qkv, g_query, g_value, g_attn, g_attn_bias, g_second_gain, g_second_shift, g_up, g_up_bias, g_down, g_down_bias)
```

```python
from functools import partial

import jax
import jax.numpy as jnp
from jax import lax
from jax.experimental import pallas as pl
from jax.experimental.pallas import tpu as pltpu
from jax.sharding import PartitionSpec as P

HD = 64
EXPERTS = 3
IMG_LEN = 197
TXT_LEN = 64
LENS = (IMG_LEN, TXT_LEN, IMG_LEN + TXT_LEN)
SLOTS = (208, 64, 272)
TXT_PAIR = 128
PAD_ROWS = 384
HALO = 144
ROW = 128
BLK = 256

EPS = 1e-05
NEG = -1e30
VMEM = 60 << 20
F32 = jnp.float32
BF16 = jnp.bfloat16

N_IMG, N_TXT, N_BOTH, N_PAD = 0, 1, 2, 3
G_IMG, G_TXT, G_BOTH, G_PAD, G_END = 4, 5, 6, 7, 8
PAD_LEN, OWN_N = 9, 10
TABLE = 16
INFO = 256


def nn(a, b):
    return lax.dot_general(a, b, (((1,), (0,)), ((), ())), preferred_element_type=F32)


def nt(a, b):
    return lax.dot_general(a, b, (((1,), (1,)), ((), ())), preferred_element_type=F32)


def tn(a, b):
    return lax.dot_general(a, b, (((0,), (0,)), ((), ())), preferred_element_type=F32)


def up_to(value, unit):
    return ((value + unit - 1) // unit) * unit


def normalize(v):
    mean = jnp.mean(v, axis=-1, keepdims=True)
    cent = v - mean
    var = jnp.mean(cent * cent, axis=-1, keepdims=True)
    inverse = lax.rsqrt(var + EPS)
    return (cent * inverse, inverse)


def norm_back(grad, normed, inverse):
    inner = jnp.mean(grad * normed, axis=-1, keepdims=True)
    return inverse * (grad - jnp.mean(grad, axis=-1, keepdims=True) - normed * inner)


def capacity(tok):
    rows = tok + LENS[2] - 1
    best = 0
    for images in range(rows // LENS[0] + 1):
        for both in range((rows - images * LENS[0]) // LENS[2] + 1):
            left = rows - images * LENS[0] - both * LENS[2]
            for pad in (0, 1):
                spare = left - pad * (1 + LENS[2] // 2)
                if spare < 0:
                    continue
                texts = spare // LENS[1]
                for count in range(texts + 1):
                    total = (
                        up_to(images * SLOTS[0], ROW)
                        + up_to(count * SLOTS[1], ROW)
                        + up_to(both * SLOTS[2], ROW)
                        + pad * PAD_ROWS
                    )
                    best = max(best, total)
    return up_to(best, BLK)


def sort_kernel(
    tok, group, pos, types, x_left, x_own, x_right, d_left, d_own, d_right,
    x_out, d_out, info, x_win, d_win,
):
    items = types.shape[1]
    low = pos[0] * tok
    for win, parts in ((x_win, (x_left, x_own, x_right)), (d_win, (d_left, d_own, d_right))):
        win[pl.ds(0, HALO), :] = parts[0][...]
        win[pl.ds(HALO, tok), :] = parts[1][...]
        win[pl.ds(HALO + tok, HALO), :] = parts[2][...]
        rest = win.shape[0] - (2 * HALO + tok)
        win[pl.ds(2 * HALO + tok, rest), :] = jnp.zeros((rest, win.shape[1]), win.dtype)

    def length(kind):
        return jnp.where(
            kind == 0, LENS[0], jnp.where(kind == 1, LENS[1], jnp.where(kind == 2, LENS[2], 0))
        )

    def owned(start, size):
        middle = (start + start + size) // 2
        return (middle >= low) & (middle < low + tok) & (size > 0)

    def count(index, carry):
        start, images, texts, boths = carry
        kind = types[0, index]
        size = length(kind)
        mine = owned(start, size)
        return (
            start + size,
            images + jnp.where(mine & (kind == 0), 1, 0),
            texts + jnp.where(mine & (kind == 1), 1, 0),
            boths + jnp.where(mine & (kind == 2), 1, 0),
        )

    zero = jnp.int32(0)
    total, images, texts, boths = lax.fori_loop(0, items, count, (zero, zero, zero, zero))
    pad_len = group - total
    pad = owned(total, pad_len)
    g_txt = up_to(images * SLOTS[0], ROW)
    g_both = g_txt + up_to(texts * SLOTS[1], ROW)
    g_pad = g_both + up_to(boths * SLOTS[2], ROW)
    g_end = g_pad + jnp.where(pad, PAD_ROWS, 0)
    info[N_IMG] = images
    info[N_TXT] = texts
    info[N_BOTH] = boths
    info[N_PAD] = jnp.where(pad, 1, 0)
    info[G_IMG] = zero
    info[G_TXT] = g_txt
    info[G_BOTH] = g_both
    info[G_PAD] = g_pad
    info[G_END] = g_end
    info[PAD_LEN] = pad_len
    x_out[...] = jnp.zeros_like(x_out)
    d_out[...] = jnp.zeros_like(d_out)

    def copy_rows(source, target, size, slot):
        begin = pl.multiple_of((source // 16) * 16, 16)
        shift = source - begin
        rows = lax.broadcasted_iota(jnp.int32, (slot, slot + 16), 0)
        cols = lax.broadcasted_iota(jnp.int32, (slot, slot + 16), 1)
        chosen = ((cols == rows + shift) & (rows < size)).astype(F32).astype(BF16)
        for win, out in ((x_win, x_out), (d_win, d_out)):
            out[pl.ds(target, slot), :] = nn(chosen, win[pl.ds(begin, slot + 16), :]).astype(BF16)

    def place(index, carry):
        start, images, texts, boths, own = carry
        kind = types[0, index]
        size = length(kind)
        mine = owned(start, size)
        source = start - low + HALO
        target = jnp.where(
            kind == 0,
            images * SLOTS[0],
            jnp.where(kind == 1, g_txt + texts * SLOTS[1], g_both + boths * SLOTS[2]),
        )
        target = pl.multiple_of(target, 16)

        @pl.when(mine)
        def _():
            info[TABLE + 3 * own] = source
            info[TABLE + 3 * own + 1] = target
            info[TABLE + 3 * own + 2] = kind

        for which in range(EXPERTS):

            @pl.when(mine & (kind == which))
            def _(which=which):
                copy_rows(source, target, LENS[which], SLOTS[which])

        return (
            start + size,
            images + jnp.where(mine & (kind == 0), 1, 0),
            texts + jnp.where(mine & (kind == 1), 1, 0),
            boths + jnp.where(mine & (kind == 2), 1, 0),
            own + jnp.where(mine, 1, 0),
        )

    own = lax.fori_loop(0, items, place, (zero, zero, zero, zero, zero))[-1]
    pad_source = total - low + HALO

    @pl.when(pad)
    def _():
        copy_rows(pad_source, pl.multiple_of(g_pad, ROW), pad_len, SLOTS[2])
        info[TABLE + 3 * own] = pad_source
        info[TABLE + 3 * own + 1] = g_pad
        info[TABLE + 3 * own + 2] = 3

    info[OWN_N] = own + jnp.where(pad, 1, 0)


def sort_rows(seq, types, x_parts, d_parts, rows, tok, group):
    width = x_parts[1].shape[1]
    smem = pl.BlockSpec(memory_space=pltpu.SMEM)
    vmem = pl.BlockSpec(memory_space=pltpu.VMEM)
    spare = tok + HALO + 288
    return pl.pallas_call(
        partial(sort_kernel, tok, group),
        out_shape=[
            jax.ShapeDtypeStruct((rows, width), BF16),
            jax.ShapeDtypeStruct((rows, width), BF16),
            jax.ShapeDtypeStruct((INFO,), jnp.int32),
        ],
        in_specs=[smem, smem] + [vmem] * 6,
        out_specs=[vmem, vmem, smem],
        scratch_shapes=[pltpu.VMEM((spare, width), BF16)] * 2,
        compiler_params=pltpu.CompilerParams(vmem_limit_bytes=VMEM),
        name="sort_rows",
    )(seq, types, *x_parts, *d_parts)


def unsort_kernel(tok, info, mixed, grad, m_own, m_left, m_right, g_own, g_left, g_right, m_win, g_win):
    m_win[...] = jnp.zeros_like(m_win)
    g_win[...] = jnp.zeros_like(g_win)

    def place(index, carry):
        source = info[TABLE + 3 * index]
        target = pl.multiple_of(info[TABLE + 3 * index + 1], 16)
        kind = info[TABLE + 3 * index + 2]
        begin = pl.multiple_of((source // 16) * 16, 16)
        shift = source - begin
        for which in range(EXPERTS):
            slot = SLOTS[which]
            fits = (kind == which) if which < 2 else (kind >= 2)
            size = LENS[which] if which < 2 else jnp.where(kind == 2, LENS[2], info[PAD_LEN])

            @pl.when(fits)
            def _(slot=slot, size=size):
                rows = lax.broadcasted_iota(jnp.int32, (slot + 16, slot), 0)
                cols = lax.broadcasted_iota(jnp.int32, (slot + 16, slot), 1)
                chosen = ((rows == cols + shift) & (cols < size)).astype(F32).astype(BF16)
                at, to = pl.ds(target, slot), pl.ds(begin, slot + 16)
                m_win[to, :] += nn(chosen, mixed[at, :])
                value = grad[at, :]
                high = value.astype(BF16)
                rest = (value - high.astype(F32)).astype(BF16)
                g_win[to, :] += nn(chosen, high) + nn(chosen, rest)

        return carry

    lax.fori_loop(0, info[OWN_N], place, 0)
    for win, parts in ((m_win, (m_left, m_own, m_right)), (g_win, (g_left, g_own, g_right))):
        for part, begin, size in ((parts[0], 0, HALO), (parts[1], HALO, tok), (parts[2], HALO + tok, HALO)):
            part[...] = win[pl.ds(begin, size), :].astype(part.dtype)


def unsort_rows(info, mixed, grad, tok):
    width = mixed.shape[1]
    smem = pl.BlockSpec(memory_space=pltpu.SMEM)
    vmem = pl.BlockSpec(memory_space=pltpu.VMEM)
    spare = tok + HALO + 288
    shapes = [
        jax.ShapeDtypeStruct((size, width), kind)
        for kind in (BF16, F32)
        for size in (tok, HALO, HALO)
    ]
    return pl.pallas_call(
        partial(unsort_kernel, tok),
        out_shape=shapes,
        in_specs=[smem, vmem, vmem],
        out_specs=[vmem] * 6,
        scratch_shapes=[pltpu.VMEM((spare, width), F32)] * 2,
        compiler_params=pltpu.CompilerParams(vmem_limit_bytes=VMEM),
        name="unsort_rows",
    )(info, mixed, grad)


def qkv_kernel(info, x, gain, shift, weight, bias, h_out, qkv_out):
    used = pl.program_id(0) * BLK < info[G_END]
    width = x.shape[1]

    @pl.when(used)
    def _():
        normed, _ = normalize(x[...].astype(F32))
        hidden = (normed * gain[...] + shift[...]).astype(BF16)
        h_out[...] = hidden
        for part in range(3):
            cols = pl.ds(part * width, width)
            value = nn(hidden, weight[:, cols]) + bias[:, cols]
            if part == 0:
                value = value * (HD ** (-0.5))
            qkv_out[:, cols] = value.astype(BF16)

    @pl.when(jnp.logical_not(used))
    def _():
        h_out[...] = jnp.zeros_like(h_out)
        qkv_out[...] = jnp.zeros_like(qkv_out)


def full(shape):
    return pl.BlockSpec(shape, lambda *_: (0,) * len(shape))


def held(shape):
    return pl.BlockSpec(shape, lambda *_: (0,) * len(shape), pipeline_mode=pl.Buffered(1))


SMEM_SPEC = pl.BlockSpec(memory_space=pltpu.SMEM)


def project_qkv(info, x, gain, shift, weight, bias):
    rows, width = x.shape
    return pl.pallas_call(
        qkv_kernel,
        grid=(rows // BLK,),
        out_shape=[
            jax.ShapeDtypeStruct((rows, width), BF16),
            jax.ShapeDtypeStruct((rows, 3 * width), BF16),
        ],
        in_specs=[
            SMEM_SPEC,
            pl.BlockSpec((BLK, width), lambda i: (i, 0)),
            full((1, width)),
            full((1, width)),
            held((width, 3 * width)),
            full((1, 3 * width)),
        ],
        out_specs=[
            pl.BlockSpec((BLK, width), lambda i: (i, 0)),
            pl.BlockSpec((BLK, 3 * width), lambda i: (i, 0)),
        ],
        compiler_params=pltpu.CompilerParams(vmem_limit_bytes=VMEM),
        name="project_qkv",
    )(info, x, gain, shift, weight, bias)


def softmax_rows(scores, keep):
    masked = jnp.where(keep, scores, NEG)
    expo = jnp.exp(masked - jnp.max(masked, axis=-1, keepdims=True))
    return expo / jnp.sum(expo, axis=-1, keepdims=True)


def for_items(info, visit):
    def image(index, carry):
        slot = SLOTS[0]
        keep = lax.broadcasted_iota(jnp.int32, (slot, slot), 1) < LENS[0]
        visit(pl.multiple_of(index * slot, 16), slot, keep)
        return carry

    def text(index, carry):
        slot = TXT_PAIR
        rows = lax.broadcasted_iota(jnp.int32, (slot, slot), 0) // TXT_LEN
        cols = lax.broadcasted_iota(jnp.int32, (slot, slot), 1) // TXT_LEN
        visit(pl.multiple_of(info[G_TXT] + index * slot, ROW), slot, rows == cols)
        return carry

    def both(index, carry):
        slot = SLOTS[2]
        real = index < info[N_BOTH]
        start = jnp.where(real, info[G_BOTH] + index * slot, info[G_PAD])
        size = jnp.where(real, LENS[2], info[PAD_LEN])
        keep = lax.broadcasted_iota(jnp.int32, (slot, slot), 1) < size
        visit(pl.multiple_of(start, 16), slot, keep)
        return carry

    lax.fori_loop(0, info[N_IMG], image, 0)
    lax.fori_loop(0, (info[N_TXT] + 1) // 2, text, 0)
    lax.fori_loop(0, info[N_BOTH] + info[N_PAD], both, 0)


def attend_kernel(info, query, key, value, out):
    out[...] = jnp.zeros_like(out)

    def visit(start, slot, keep):
        at = pl.ds(start, slot)
        q, k, v = query[at, :], key[at, :], value[at, :]
        first = lax.broadcasted_iota(jnp.int32, (1, 2 * HD), 1) < HD
        results = []
        for mine in (first, jnp.logical_not(first)):
            prob = softmax_rows(nt(jnp.where(mine, q, 0), k), keep)
            results.append(nn(prob.astype(BF16), v))
        out[at, :] = jnp.where(first, results[0], results[1]).astype(BF16)

    for_items(info, visit)


def attend(info, qkv):
    rows = qkv.shape[0]
    width = qkv.shape[1] // 3
    pairs = width // (2 * HD)
    cols = 2 * HD
    return pl.pallas_call(
        attend_kernel,
        grid=(pairs,),
        out_shape=jax.ShapeDtypeStruct((rows, width), BF16),
        in_specs=[
            SMEM_SPEC,
            pl.BlockSpec((rows, cols), lambda p: (0, p)),
            pl.BlockSpec((rows, cols), lambda p: (0, pairs + p)),
            pl.BlockSpec((rows, cols), lambda p: (0, 2 * pairs + p)),
        ],
        out_specs=pl.BlockSpec((rows, cols), lambda p: (0, p)),
        compiler_params=pltpu.CompilerParams(vmem_limit_bytes=VMEM),
        name="attend",
    )(info, qkv, qkv, qkv)


def attend_back_kernel(info, query, key, value, grad, dq_out, dk_out, dv_out):
    for out in (dq_out, dk_out, dv_out):
        out[...] = jnp.zeros_like(out)

    def visit(start, slot, keep):
        at = pl.ds(start, slot)
        q, k, v, g = query[at, :], key[at, :], value[at, :], grad[at, :]
        first = lax.broadcasted_iota(jnp.int32, (1, 2 * HD), 1) < HD
        dqs, dks, dvs = [], [], []
        for mine in (first, jnp.logical_not(first)):
            prob = softmax_rows(nt(jnp.where(mine, q, 0), k), keep)
            grad_prob = nt(jnp.where(mine, g, 0), v)
            inner = jnp.sum(prob * grad_prob, axis=-1, keepdims=True)
            grad_score = (prob * (grad_prob - inner)).astype(BF16)
            dqs.append(nn(grad_score, k))
            dks.append(tn(grad_score, q))
            dvs.append(tn(prob.astype(BF16), g))
        scale = HD ** (-0.5)
        dq = jnp.where(first, dqs[0], dqs[1]).astype(BF16)
        dq_out[at, :] = (dq.astype(F32) * scale).astype(BF16)
        dk_out[at, :] = jnp.where(first, dks[0], dks[1]).astype(BF16)
        dv_out[at, :] = jnp.where(first, dvs[0], dvs[1]).astype(BF16)

    for_items(info, visit)


def attend_back(info, qkv, grad):
    rows = qkv.shape[0]
    width = qkv.shape[1] // 3
    pairs = width // (2 * HD)
    cols = 2 * HD
    spec = pl.BlockSpec((rows, cols), lambda p: (0, p))
    return pl.pallas_call(
        attend_back_kernel,
        grid=(pairs,),
        out_shape=[jax.ShapeDtypeStruct((rows, width), BF16)] * 3,
        in_specs=[
            SMEM_SPEC,
            spec,
            pl.BlockSpec((rows, cols), lambda p: (0, pairs + p)),
            pl.BlockSpec((rows, cols), lambda p: (0, 2 * pairs + p)),
            spec,
        ],
        out_specs=[spec] * 3,
        compiler_params=pltpu.CompilerParams(vmem_limit_bytes=VMEM),
        name="attend_back",
    )(info, qkv, qkv, qkv, grad)


def group_of(info, row):
    return (
        (row >= info[G_TXT]).astype(jnp.int32)
        + (row >= info[G_BOTH]).astype(jnp.int32)
        + (row >= info[G_PAD]).astype(jnp.int32)
    )


def middle_kernel(info, x, att, grad, weight, bias, gains, shifts, mid_out, h_out, ht_out, gt_out):
    row = pl.program_id(0) * ROW
    used = row < info[G_END]

    @pl.when(used)
    def _():
        middle = x[...].astype(F32) + (nn(att[...], weight[...]) + bias[...])
        mid_out[...] = middle
        normed, _ = normalize(middle)
        which = pl.ds(group_of(info, row), 1)
        hidden = (normed * gains[which, :] + shifts[which, :]).astype(BF16)
        h_out[...] = hidden
        ht_out[...] = hidden.T
        gt_out[...] = grad[...].T

    @pl.when(jnp.logical_not(used))
    def _():
        mid_out[...] = jnp.zeros_like(mid_out)
        h_out[...] = jnp.zeros_like(h_out)
        ht_out[...] = jnp.zeros_like(ht_out)
        gt_out[...] = jnp.zeros_like(gt_out)


def middle_norm(info, x, att, grad, weight, bias, gains, shifts):
    rows, width = x.shape
    spec = pl.BlockSpec((ROW, width), lambda i: (i, 0))
    turned = pl.BlockSpec((width, ROW), lambda i: (0, i))
    return pl.pallas_call(
        middle_kernel,
        grid=(rows // ROW,),
        out_shape=[
            jax.ShapeDtypeStruct((rows, width), F32),
            jax.ShapeDtypeStruct((rows, width), BF16),
            jax.ShapeDtypeStruct((width, rows), BF16),
            jax.ShapeDtypeStruct((width, rows), BF16),
        ],
        in_specs=[
            SMEM_SPEC,
            spec,
            spec,
            spec,
            held((width, width)),
            full((1, width)),
            full(gains.shape),
            full(shifts.shape),
        ],
        out_specs=[spec, spec, turned, turned],
        compiler_params=pltpu.CompilerParams(vmem_limit_bytes=VMEM),
        name="middle_norm",
    )(info, x, att, grad, weight, bias, gains, shifts)


def gelu_parts(up):
    size = jnp.abs(up) * (0.5**0.5)
    expo = jnp.exp(-size * size)
    t = 1.0 / (1.0 + 0.3275911 * size)
    poly = 1.061405429 * t - 1.453152027
    poly = poly * t + 1.421413741
    poly = poly * t - 0.284496736
    poly = poly * t + 0.254829592
    tail = 0.5 * (poly * t) * expo
    cdf = jnp.where(up >= 0, 1.0 - tail, tail)
    return (up * cdf, cdf + up * (expo * 0.3989422804014327))


def expert_kernel(
    expert, info, h, ht, g, gt, w_up, b_up, w_down, y_in, d_in,
    grad_out, bias_out, y_out, d_out, act, dup, y_acc, d_acc, w_acc, sems,
):
    step = pl.program_id(0)
    steps = pl.num_programs(0)
    start = info[G_IMG + expert]
    count = info[G_IMG + expert + 1] - start
    blocks = count // BLK
    odd = count % BLK > 0
    bias_out[...] = jnp.zeros_like(bias_out)

    def rows_of(local, size):
        at = pl.ds(pl.multiple_of(start + local, ROW), size)
        here = pl.ds(pl.multiple_of(local, ROW), size)
        up = nn(h[at, :], w_up[0]) + b_up[0]
        grad_act = nt(g[at, :], w_down[0])
        active, slope = gelu_parts(up)
        active = active.astype(BF16)
        grad_up = (slope * grad_act).astype(BF16)
        act[here, :] = active
        dup[here, :] = grad_up
        bias_out[...] += jnp.sum(grad_up.astype(F32), axis=0, keepdims=True)
        y_part = nn(active, w_down[0])
        d_part = nt(grad_up, w_up[0])

        @pl.when(step == 0)
        def _():
            y_acc[here, :] = y_part
            d_acc[here, :] = d_part

        @pl.when(step > 0)
        def _():
            y_acc[here, :] += y_part
            d_acc[here, :] += d_part

    def block(index, carry):
        rows_of(index * BLK, BLK)
        return carry

    lax.fori_loop(0, blocks, block, 0)

    @pl.when(odd)
    def _():
        rows_of(blocks * BLK, ROW)

    for slot, (turned, right) in enumerate(((ht, dup), (gt, act))):
        w_acc[...] = jnp.zeros_like(w_acc)

        def add(local, size, turned=turned, right=right):
            at = pl.ds(pl.multiple_of(start + local, ROW), size)
            here = pl.ds(pl.multiple_of(local, ROW), size)
            w_acc[...] += nn(turned[:, at], right[here, :])

        def add_block(index, carry, add=add):
            add(index * BLK, BLK)
            return carry

        lax.fori_loop(0, blocks, add_block, 0)

        @pl.when(odd)
        def _(add=add):
            add(blocks * BLK, ROW)

        grad_out[slot] = w_acc[...].astype(BF16)

    @pl.when(step == steps - 1)
    def _():
        def copies(index):
            here = pl.ds(pl.multiple_of(index * ROW, ROW), ROW)
            at = pl.ds(pl.multiple_of(start + index * ROW, ROW), ROW)
            return (
                pltpu.make_async_copy(y_acc.at[here, :], y_out.at[at, :], sems.at[0, index]),
                pltpu.make_async_copy(d_acc.at[here, :], d_out.at[at, :], sems.at[1, index]),
            )

        def send(index, carry):
            for copy in copies(index):
                copy.start()
            return carry

        def wait(index, carry):
            for copy in copies(index):
                copy.wait()
            return carry

        lax.fori_loop(0, count // ROW, send, 0)
        lax.fori_loop(0, count // ROW, wait, 0)


def run_expert(expert, info, h, ht, g, gt, expert_up, up_bias, expert_down, y_buf, d_buf):
    rows, width = h.shape
    hidden = expert_up.shape[2]
    tile = min(hidden, 768)
    any_spec = pl.BlockSpec(memory_space=pl.ANY)
    return pl.pallas_call(
        partial(expert_kernel, expert),
        grid=(hidden // tile,),
        out_shape=[
            jax.ShapeDtypeStruct((2, width, hidden), BF16),
            jax.ShapeDtypeStruct((1, hidden), F32),
            jax.ShapeDtypeStruct((rows, width), F32),
            jax.ShapeDtypeStruct((rows, width), F32),
        ],
        in_specs=[
            SMEM_SPEC,
            held((rows, width)),
            held((width, rows)),
            held((rows, width)),
            held((width, rows)),
            pl.BlockSpec((1, width, tile), lambda f: (expert, 0, f)),
            pl.BlockSpec((1, 1, tile), lambda f: (expert, 0, f)),
            pl.BlockSpec((1, tile, width), lambda f: (expert, f, 0)),
            any_spec,
            any_spec,
        ],
        out_specs=[
            pl.BlockSpec((2, width, tile), lambda f: (0, 0, f)),
            pl.BlockSpec((1, tile), lambda f: (0, f)),
            any_spec,
            any_spec,
        ],
        scratch_shapes=[
            pltpu.VMEM((rows, tile), BF16),
            pltpu.VMEM((rows, tile), BF16),
            pltpu.VMEM((rows, width), F32),
            pltpu.VMEM((rows, width), F32),
            pltpu.VMEM((width, tile), F32),
            pltpu.SemaphoreType.DMA((2, rows // ROW)),
        ],
        input_output_aliases={8: 2, 9: 3},
        compiler_params=pltpu.CompilerParams(vmem_limit_bytes=VMEM),
        name="expert",
    )(info, h, ht, g, gt, expert_up, up_bias, expert_down, y_buf, d_buf)


def after_kernel(
    info, mid, y, dh, g, gains, down_bias, weight,
    mixed_out, dx_out, proj_out, att_out, gain_sum, shift_sum, down_sum, bias_sum,
):
    row = pl.program_id(0) * ROW
    used = row < info[G_END]

    @pl.when(row == 0)
    def _():
        for out in (gain_sum, shift_sum, down_sum, bias_sum):
            out[...] = jnp.zeros_like(out)

    @pl.when(used)
    def _():
        which = pl.ds(group_of(info, row), 1)
        middle = mid[...]
        grad = g[...].astype(F32)
        grad_hidden = dh[...]
        mixed_out[...] = (middle + (y[...] + down_bias[which, :])).astype(BF16)
        normed, inverse = normalize(middle)
        gain_sum[which, :] += jnp.sum(grad_hidden * normed, axis=0, keepdims=True)
        shift_sum[which, :] += jnp.sum(grad_hidden, axis=0, keepdims=True)
        down_sum[which, :] += jnp.sum(grad, axis=0, keepdims=True)
        grad_middle = grad + norm_back(grad_hidden * gains[which, :], normed, inverse)
        dx_out[...] = grad_middle
        proj = grad_middle.astype(BF16)
        proj_out[...] = proj
        bias_sum[...] += jnp.sum(proj.astype(F32), axis=0, keepdims=True)
        att_out[...] = nt(proj, weight[...]).astype(BF16)

    @pl.when(jnp.logical_not(used))
    def _():
        for out in (mixed_out, dx_out, proj_out, att_out):
            out[...] = jnp.zeros_like(out)


def after_experts(info, mid, y, dh, g, gains, down_bias, weight):
    rows, width = mid.shape
    spec = pl.BlockSpec((ROW, width), lambda i: (i, 0))
    sums = full((4, width))
    return pl.pallas_call(
        after_kernel,
        grid=(rows // ROW,),
        out_shape=[
            jax.ShapeDtypeStruct((rows, width), BF16),
            jax.ShapeDtypeStruct((rows, width), F32),
            jax.ShapeDtypeStruct((rows, width), BF16),
            jax.ShapeDtypeStruct((rows, width), BF16),
            jax.ShapeDtypeStruct((4, width), F32),
            jax.ShapeDtypeStruct((4, width), F32),
            jax.ShapeDtypeStruct((4, width), F32),
            jax.ShapeDtypeStruct((1, width), F32),
        ],
        in_specs=[SMEM_SPEC, spec, spec, spec, spec, sums, sums, held((width, width))],
        out_specs=[spec, spec, spec, spec, sums, sums, sums, full((1, width))],
        compiler_params=pltpu.CompilerParams(vmem_limit_bytes=VMEM),
        name="after_experts",
    )(info, mid, y, dh, g, gains, down_bias, weight)


def last_kernel(
    info, x, dx, dq, dk, dv, gain, weight, out, gain_sum, shift_sum, query_sum, value_sum
):
    width = x.shape[1]
    used = pl.program_id(0) * BLK < info[G_END]

    @pl.when(pl.program_id(0) == 0)
    def _():
        for total in (gain_sum, shift_sum, query_sum, value_sum):
            total[...] = jnp.zeros_like(total)

    @pl.when(used)
    def _():
        hidden = nt(dq[...], weight[:, pl.ds(0, width)])
        hidden += nt(dk[...], weight[:, pl.ds(width, width)])
        hidden += nt(dv[...], weight[:, pl.ds(2 * width, width)])
        normed, inverse = normalize(x[...].astype(F32))
        gain_sum[...] += jnp.sum(hidden * normed, axis=0, keepdims=True)
        shift_sum[...] += jnp.sum(hidden, axis=0, keepdims=True)
        query_sum[...] += jnp.sum(dq[...].astype(F32), axis=0, keepdims=True)
        value_sum[...] += jnp.sum(dv[...].astype(F32), axis=0, keepdims=True)
        out[...] = dx[...] + norm_back(hidden * gain[...], normed, inverse)

    @pl.when(jnp.logical_not(used))
    def _():
        out[...] = jnp.zeros_like(out)


def last_norm(info, x, dx, dq, dk, dv, gain, weight):
    rows, width = x.shape
    spec = pl.BlockSpec((BLK, width), lambda i: (i, 0))
    one = full((1, width))
    return pl.pallas_call(
        last_kernel,
        grid=(rows // BLK,),
        out_shape=[jax.ShapeDtypeStruct((rows, width), F32)]
        + [jax.ShapeDtypeStruct((1, width), F32)] * 4,
        in_specs=[SMEM_SPEC, spec, spec, spec, spec, spec, one, held((width, 3 * width))],
        out_specs=[spec, one, one, one, one],
        compiler_params=pltpu.CompilerParams(vmem_limit_bytes=VMEM),
        name="last_norm",
    )(info, x, dx, dq, dk, dv, gain, weight)


def low_add(a, b):
    return (a.astype(F32) + b.astype(F32)).astype(BF16)


def swap(value, bit):
    ways = lax.axis_size("dp")
    return lax.ppermute(value, "dp", [(i, i ^ (1 << bit)) for i in range(ways)])


def halve(parts, axis, bit):
    mine = (lax.axis_index("dp") >> bit) & 1

    def pick(which):
        taken = [lax.dynamic_index_in_dim(part, which, axis, keepdims=False) for part in parts]
        total = taken[0]
        for more in taken[1:]:
            total = low_add(total, more)
        return total

    send, keep = pick(1 - mine), pick(mine)
    return [keep, swap(send, bit)]


def scatter_sum(value):
    dp, seq = lax.axis_size("dp"), lax.axis_size("seq")
    bits = dp.bit_length() - 1
    two, depth, cols = value.shape
    rows = depth // (dp * seq)
    shaped = value.reshape((2,) + (2,) * bits + (seq, rows, cols))
    parts = halve([shaped], bits, 0)
    results = []
    for lane in range(2):
        lane_parts = [part[lane] for part in parts]
        order = list(range(1, bits))
        if lane:
            order = order[::-1]
        left = list(range(bits - 1, 0, -1))
        for bit in order:
            axis = left.index(bit)
            left.remove(bit)
            lane_parts = halve(lane_parts, axis, bit)
        results.append(low_add(lane_parts[0], lane_parts[1]))
    half = jnp.stack(results)
    here = lax.axis_index("seq")
    total = lax.dynamic_index_in_dim(half, here, 1, keepdims=False).astype(F32)
    for hop in range(1, seq):
        block = lax.dynamic_index_in_dim(half, (here + hop) % seq, 1, keepdims=False)
        got = lax.ppermute(block, "seq", [(i, (i + hop) % seq) for i in range(seq)])
        total = total + got.astype(F32)
    return total


def exchange(value, rows):
    seq = lax.axis_size("seq")
    from_left = lax.ppermute(value[-rows:], "seq", [(i, i + 1) for i in range(seq - 1)])
    from_right = lax.ppermute(value[:rows], "seq", [(i + 1, i) for i in range(seq - 1)])
    return (from_left, from_right)


def per_device(
    tokens, item_types, first_gain, first_shift, qkv_weight, query_bias, value_bias, attn_weight,
    attn_bias, second_gain, second_shift, expert_up, up_bias, expert_down, down_bias, cotangent,
):
    tok, width = tokens.shape
    seq = lax.axis_size("seq")
    rows = capacity(tok)
    place = lax.axis_index("seq").astype(jnp.int32).reshape(1)
    x_left, x_right = exchange(tokens, HALO)
    d_left, d_right = exchange(cotangent, HALO)
    x, g, info = sort_rows(
        place, item_types, (x_left, tokens, x_right), (d_left, cotangent, d_right), rows, tok, tok * seq
    )
    bias_full = jnp.concatenate([query_bias, jnp.zeros((width,), F32), value_bias])[None]
    pad_row = jnp.zeros((1, width), F32)
    gains = jnp.concatenate([second_gain, pad_row])
    shifts = jnp.concatenate([second_shift, pad_row])
    downs = jnp.concatenate([down_bias, pad_row])

    h, qkv = project_qkv(info, x, first_gain[None], first_shift[None], qkv_weight, bias_full)
    att = attend(info, qkv)
    mid, h2, h2t, gt = middle_norm(info, x, att, g, attn_weight, attn_bias[None], gains, shifts)

    y = jnp.zeros((rows, width), F32)
    dh = jnp.zeros((rows, width), F32)
    expert_sums, up_biases = [], []
    for expert in range(EXPERTS):
        grads, bias, y, dh = run_expert(
            expert, info, h2, h2t, g, gt, expert_up, up_bias[:, None, :], expert_down, y, dh
        )
        up_biases.append(bias)
        expert_sums.append(scatter_sum(grads))

    mixed, dx, proj, datt, gain_sum, shift_sum, down_sum, attn_bias_sum = after_experts(
        info, mid, y, dh, g, gains, downs, attn_weight
    )
    half = width // 2
    d_attn = tn(proj, att).astype(BF16)
    attn_sum = scatter_sum(jnp.stack([d_attn[:, :half], d_attn[:, half:]]))
    dq, dk, dv = attend_back(info, qkv, datt)
    grad_x, fgain, fshift, qsum, vsum = last_norm(
        info, x, dx, dq, dk, dv, first_gain[None], qkv_weight
    )
    d_qkv = jnp.concatenate([tn(dq, h), tn(dk, h), tn(dv, h)]).astype(BF16)
    qkv_sum = scatter_sum(jnp.stack([d_qkv[:, :half], d_qkv[:, half:]]))

    m_own, m_left, m_right, g_own, g_left, g_right = unsort_rows(info, mixed, grad_x, tok)

    def merge(own, left, right):
        to_left = lax.ppermute(left, "seq", [(i + 1, i) for i in range(seq - 1)])
        to_right = lax.ppermute(right, "seq", [(i, i + 1) for i in range(seq - 1)])
        own = own.at[:HALO].add(to_right)
        return own.at[tok - HALO :].add(to_left)

    mixed_out = merge(m_own, m_left, m_right)
    grad_out = merge(g_own, g_left, g_right)

    small = jnp.concatenate(
        [fgain[0], fshift[0], qsum[0], vsum[0], attn_bias_sum[0]]
        + [gain_sum[:EXPERTS].reshape(-1), shift_sum[:EXPERTS].reshape(-1), down_sum[:EXPERTS].reshape(-1)]
        + [bias[0] for bias in up_biases]
    )
    small = lax.psum(small, ("dp", "seq"))
    devices = lax.axis_size("dp") * seq
    own = width // devices
    rank = lax.axis_index("dp") * seq + lax.axis_index("seq")
    vectors = small[: 14 * width].reshape(14, width)
    vectors = lax.dynamic_slice_in_dim(vectors, rank * own, own, 1)
    sum_up = jnp.stack([total[0] for total in expert_sums])
    sum_down = jnp.stack([total[1] for total in expert_sums]).swapaxes(1, 2)

    def joined(total):
        return jnp.concatenate([total[0], total[1]], axis=1).T

    return (
        mixed_out,
        grad_out,
        vectors[0],
        vectors[1],
        joined(qkv_sum),
        vectors[2],
        vectors[3],
        joined(attn_sum),
        vectors[4],
        vectors[5:8],
        vectors[8:11],
        sum_up,
        small[14 * width :].reshape(EXPERTS, -1),
        sum_down,
        vectors[11:14],
    )


def solution(mesh):
    split = P(("dp", "seq"))
    in_specs = (P(("dp", "seq"), None), P("dp", None)) + (P(),) * 13 + (P(("dp", "seq"), None),)
    out_specs = (
        P(("dp", "seq"), None),
        P(("dp", "seq"), None),
        split,
        split,
        P(None, ("dp", "seq")),
        split,
        split,
        P(None, ("dp", "seq")),
        split,
        P(None, ("dp", "seq")),
        P(None, ("dp", "seq")),
        P(None, ("dp", "seq"), None),
        P(),
        P(None, None, ("dp", "seq")),
        P(None, ("dp", "seq")),
    )
    return jax.shard_map(
        per_device, mesh=mesh, in_specs=in_specs, out_specs=out_specs, check_vma=False
    )
```

```python
from functools import partial

import jax
import jax.numpy as jnp
from jax import lax
from jax.experimental import pallas as pl
from jax.experimental.pallas import tpu as pltpu
from jax.sharding import PartitionSpec as P

HD = 64
EXPERTS = 3
IMG_LEN = 197
TXT_LEN = 64
LENS = (IMG_LEN, TXT_LEN, IMG_LEN + TXT_LEN)
SLOTS = (208, 64, 272)
TXT_PAIR = 128
PAD_ROWS = 384
HALO = 144
ROW = 128
BLK = 256

EPS = 1e-05
NEG = -1e30
VMEM = 60 << 20
F32 = jnp.float32
BF16 = jnp.bfloat16

N_IMG, N_TXT, N_BOTH, N_PAD = 0, 1, 2, 3
G_IMG, G_TXT, G_BOTH, G_PAD, G_END = 4, 5, 6, 7, 8
PAD_LEN, OWN_N, CORE = 9, 10, 11
TABLE = 16
INFO = 256


def nn(a, b):
    return lax.dot_general(a, b, (((1,), (0,)), ((), ())), preferred_element_type=F32)


def nt(a, b):
    return lax.dot_general(a, b, (((1,), (1,)), ((), ())), preferred_element_type=F32)


def tn(a, b):
    return lax.dot_general(a, b, (((0,), (0,)), ((), ())), preferred_element_type=F32)


def cost(microseconds):
    return pl.CostEstimate(flops=int(microseconds * 1e10), bytes_accessed=0, transcendentals=0)


SMEM_SPEC = pl.BlockSpec(memory_space=pltpu.SMEM)


def up_to(value, unit):
    return ((value + unit - 1) // unit) * unit


def normalize(v):
    mean = jnp.mean(v, axis=-1, keepdims=True)
    cent = v - mean
    var = jnp.mean(cent * cent, axis=-1, keepdims=True)
    inverse = lax.rsqrt(var + EPS)
    return (cent * inverse, inverse)


def norm_back(grad, normed, inverse):
    inner = jnp.mean(grad * normed, axis=-1, keepdims=True)
    return inverse * (grad - jnp.mean(grad, axis=-1, keepdims=True) - normed * inner)


def capacity(tok):
    rows = tok + LENS[2] - 1
    best = 0
    for images in range(rows // LENS[0] + 1):
        for both in range((rows - images * LENS[0]) // LENS[2] + 1):
            left = rows - images * LENS[0] - both * LENS[2]
            for pad in (0, 1):
                spare = left - pad * (1 + LENS[2] // 2)
                if spare < 0:
                    continue
                texts = spare // LENS[1]
                for count in range(texts + 1):
                    total = (
                        up_to(images * SLOTS[0], ROW)
                        + up_to(count * SLOTS[1], ROW)
                        + up_to(both * SLOTS[2], ROW)
                        + pad * PAD_ROWS
                    )
                    best = max(best, total)
    return up_to(best, BLK)


def fill_window(win, left, own, right):
    tok = own.shape[0]
    win[pl.ds(0, HALO), :] = left[...]
    win[pl.ds(HALO, tok), :] = own[...]
    win[pl.ds(HALO + tok, HALO), :] = right[...]
    rest = win.shape[0] - (2 * HALO + tok)
    win[pl.ds(2 * HALO + tok, rest), :] = jnp.zeros((rest, win.shape[1]), win.dtype)


def gather_rows(info, win, out):
    out[...] = jnp.zeros_like(out)

    def place(index, carry):
        source = info[TABLE + 3 * index]
        target = pl.multiple_of(info[TABLE + 3 * index + 1], 16)
        kind = info[TABLE + 3 * index + 2]
        begin = pl.multiple_of((source // 16) * 16, 16)
        shift = source - begin
        for which in range(EXPERTS):
            slot = SLOTS[which]
            fits = (kind == which) if which < 2 else (kind >= 2)
            size = LENS[which] if which < 2 else jnp.where(kind == 2, LENS[2], info[PAD_LEN])

            @pl.when(fits)
            def _(slot=slot, size=size):
                rows = lax.broadcasted_iota(jnp.int32, (slot, slot + 16), 0)
                cols = lax.broadcasted_iota(jnp.int32, (slot, slot + 16), 1)
                chosen = ((cols == rows + shift) & (rows < size)).astype(F32).astype(BF16)
                value = nn(chosen, win[pl.ds(begin, slot + 16), :])
                out[pl.ds(target, slot), :] = value.astype(BF16)

        return carry

    lax.fori_loop(0, info[OWN_N], place, 0)


def sort_kernel(tok, group, place_ref, types, left, own_rows, right, out, info, win):
    items = types.shape[1]
    low = place_ref[0] * tok
    info[CORE] = place_ref[1]
    fill_window(win, left, own_rows, right)

    def length(kind):
        return jnp.where(
            kind == 0, LENS[0], jnp.where(kind == 1, LENS[1], jnp.where(kind == 2, LENS[2], 0))
        )

    def owned(start, size):
        middle = (start + start + size) // 2
        return (middle >= low) & (middle < low + tok) & (size > 0)

    def count(index, carry):
        start, images, texts, boths = carry
        kind = types[0, index]
        size = length(kind)
        mine = owned(start, size)
        return (
            start + size,
            images + jnp.where(mine & (kind == 0), 1, 0),
            texts + jnp.where(mine & (kind == 1), 1, 0),
            boths + jnp.where(mine & (kind == 2), 1, 0),
        )

    zero = jnp.int32(0)
    total, images, texts, boths = lax.fori_loop(0, items, count, (zero, zero, zero, zero))
    pad_len = group - total
    pad = owned(total, pad_len)
    g_txt = up_to(images * SLOTS[0], ROW)
    g_both = g_txt + up_to(texts * SLOTS[1], ROW)
    g_pad = g_both + up_to(boths * SLOTS[2], ROW)
    info[N_IMG] = images
    info[N_TXT] = texts
    info[N_BOTH] = boths
    info[N_PAD] = jnp.where(pad, 1, 0)
    info[G_IMG] = zero
    info[G_TXT] = g_txt
    info[G_BOTH] = g_both
    info[G_PAD] = g_pad
    info[G_END] = g_pad + jnp.where(pad, PAD_ROWS, 0)
    info[PAD_LEN] = pad_len

    def note(own, source, target, kind):
        info[TABLE + 3 * own] = source
        info[TABLE + 3 * own + 1] = target
        info[TABLE + 3 * own + 2] = kind

    def place(index, carry):
        start, images, texts, boths, own = carry
        kind = types[0, index]
        size = length(kind)
        mine = owned(start, size)

        @pl.when(mine)
        def _():
            target = jnp.where(
                kind == 0,
                images * SLOTS[0],
                jnp.where(kind == 1, g_txt + texts * SLOTS[1], g_both + boths * SLOTS[2]),
            )
            note(own, start - low + HALO, target, kind)

        return (
            start + size,
            images + jnp.where(mine & (kind == 0), 1, 0),
            texts + jnp.where(mine & (kind == 1), 1, 0),
            boths + jnp.where(mine & (kind == 2), 1, 0),
            own + jnp.where(mine, 1, 0),
        )

    own = lax.fori_loop(0, items, place, (zero, zero, zero, zero, zero))[-1]

    @pl.when(pad)
    def _():
        note(own, total - low + HALO, g_pad, jnp.int32(EXPERTS))

    info[OWN_N] = own + jnp.where(pad, 1, 0)
    gather_rows(info, win, out)


def sort_rows(seq, types, parts, rows, group):
    tok, width = parts[1].shape
    vmem = pl.BlockSpec(memory_space=pltpu.VMEM)
    return pl.pallas_call(
        partial(sort_kernel, tok, group),
        out_shape=[
            jax.ShapeDtypeStruct((rows, width), BF16),
            jax.ShapeDtypeStruct((INFO,), jnp.int32),
        ],
        in_specs=[SMEM_SPEC, SMEM_SPEC] + [vmem] * 3,
        out_specs=[vmem, SMEM_SPEC],
        scratch_shapes=[pltpu.VMEM((tok + HALO + 288, width), BF16)],
        compiler_params=pltpu.CompilerParams(vmem_limit_bytes=VMEM),
        cost_estimate=cost(7),
        name="sort_rows",
    )(seq, types, *parts)


def sort_more_kernel(info, left, own_rows, right, out, win):
    fill_window(win, left, own_rows, right)
    gather_rows(info, win, out)


def sort_more(info, parts, rows):
    tok, width = parts[1].shape
    vmem = pl.BlockSpec(memory_space=pltpu.VMEM)
    return pl.pallas_call(
        sort_more_kernel,
        out_shape=jax.ShapeDtypeStruct((rows, width), BF16),
        in_specs=[SMEM_SPEC] + [vmem] * 3,
        out_specs=vmem,
        scratch_shapes=[pltpu.VMEM((tok + HALO + 288, width), BF16)],
        compiler_params=pltpu.CompilerParams(vmem_limit_bytes=VMEM),
        cost_estimate=cost(6),
        name="sort_more",
    )(info, *parts)


def unsort_kernel(tok, info, mixed, grad, m_own, m_left, m_right, g_own, g_left, g_right, m_win, g_win):
    m_win[...] = jnp.zeros_like(m_win)
    g_win[...] = jnp.zeros_like(g_win)

    def place(index, carry):
        source = info[TABLE + 3 * index]
        target = pl.multiple_of(info[TABLE + 3 * index + 1], 16)
        kind = info[TABLE + 3 * index + 2]
        begin = pl.multiple_of((source // 16) * 16, 16)
        shift = source - begin
        for which in range(EXPERTS):
            slot = SLOTS[which]
            fits = (kind == which) if which < 2 else (kind >= 2)
            size = LENS[which] if which < 2 else jnp.where(kind == 2, LENS[2], info[PAD_LEN])

            @pl.when(fits)
            def _(slot=slot, size=size):
                rows = lax.broadcasted_iota(jnp.int32, (slot + 16, slot), 0)
                cols = lax.broadcasted_iota(jnp.int32, (slot + 16, slot), 1)
                chosen = ((rows == cols + shift) & (cols < size)).astype(F32).astype(BF16)
                at, to = pl.ds(target, slot), pl.ds(begin, slot + 16)
                m_win[to, :] += nn(chosen, mixed[at, :])
                value = grad[at, :]
                high = value.astype(BF16)
                rest = (value - high.astype(F32)).astype(BF16)
                g_win[to, :] += nn(chosen, high) + nn(chosen, rest)

        return carry

    lax.fori_loop(0, info[OWN_N], place, 0)
    for win, parts in ((m_win, (m_left, m_own, m_right)), (g_win, (g_left, g_own, g_right))):
        for part, begin, size in ((parts[0], 0, HALO), (parts[1], HALO, tok), (parts[2], HALO + tok, HALO)):
            part[...] = win[pl.ds(begin, size), :].astype(part.dtype)


def unsort_rows(info, mixed, grad, tok):
    width = mixed.shape[1]
    smem = pl.BlockSpec(memory_space=pltpu.SMEM)
    vmem = pl.BlockSpec(memory_space=pltpu.VMEM)
    spare = tok + HALO + 288
    shapes = [
        jax.ShapeDtypeStruct((size, width), kind)
        for kind in (BF16, F32)
        for size in (tok, HALO, HALO)
    ]
    return pl.pallas_call(
        partial(unsort_kernel, tok),
        out_shape=shapes,
        in_specs=[smem, vmem, vmem],
        out_specs=[vmem] * 6,
        scratch_shapes=[pltpu.VMEM((spare, width), F32)] * 2,
        compiler_params=pltpu.CompilerParams(vmem_limit_bytes=VMEM),
        cost_estimate=cost(8),
        name="unsort_rows",
    )(info, mixed, grad)


def qkv_kernel(info, x, gain, shift, weight, query_bias, value_bias, h_out, qkv_out):
    used = pl.program_id(0) * BLK < info[G_END]
    width = x.shape[1]

    @pl.when(used)
    def _():
        normed, _ = normalize(x[...].astype(F32))
        hidden = (normed * gain[...] + shift[...]).astype(BF16)
        h_out[...] = hidden
        for part in range(3):
            cols = pl.ds(part * width, width)
            value = nn(hidden, weight[:, cols])
            if part == 0:
                value = (value + query_bias[...]) * (HD ** (-0.5))
            if part == 2:
                value = value + value_bias[...]
            qkv_out[:, cols] = value.astype(BF16)

    @pl.when(jnp.logical_not(used))
    def _():
        h_out[...] = jnp.zeros_like(h_out)
        qkv_out[...] = jnp.zeros_like(qkv_out)


def full(shape):
    return pl.BlockSpec(shape, lambda *_: (0,) * len(shape))


def held(shape):
    return pl.BlockSpec(shape, lambda *_: (0,) * len(shape), pipeline_mode=pl.Buffered(1))


def project_qkv(info, x, gain, shift, weight, query_bias, value_bias):
    rows, width = x.shape
    return pl.pallas_call(
        qkv_kernel,
        grid=(rows // BLK,),
        out_shape=[
            jax.ShapeDtypeStruct((rows, width), BF16),
            jax.ShapeDtypeStruct((rows, 3 * width), BF16),
        ],
        in_specs=[
            SMEM_SPEC,
            pl.BlockSpec((BLK, width), lambda i: (i, 0)),
            full(gain.shape),
            full(shift.shape),
            held((width, 3 * width)),
            full(query_bias.shape),
            full(value_bias.shape),
        ],
        out_specs=[
            pl.BlockSpec((BLK, width), lambda i: (i, 0)),
            pl.BlockSpec((BLK, 3 * width), lambda i: (i, 0)),
        ],
        compiler_params=pltpu.CompilerParams(vmem_limit_bytes=VMEM),
        cost_estimate=cost(11),
        name="project_qkv",
    )(info, x, gain, shift, weight, query_bias, value_bias)


PAIRS = 3


def softmax_cols(scores, bias):
    masked = scores + bias
    expo = jnp.exp(masked - jnp.max(masked, axis=0, keepdims=True))
    return expo * (1.0 / jnp.sum(expo, axis=0, keepdims=True))


def for_items(info, visit):
    def cut(slot, size):
        return jnp.where(lax.broadcasted_iota(jnp.int32, (slot, 1), 0) < size, 0.0, NEG)

    def image(index, carry):
        slot = SLOTS[0]
        visit(pl.multiple_of(index * slot, 16), slot, cut(slot, LENS[0]))
        return carry

    def text(index, carry):
        slot = TXT_PAIR
        rows = lax.broadcasted_iota(jnp.int32, (slot, slot), 0) // TXT_LEN
        cols = lax.broadcasted_iota(jnp.int32, (slot, slot), 1) // TXT_LEN
        start = pl.multiple_of(info[G_TXT] + index * slot, ROW)
        visit(start, slot, jnp.where(rows == cols, 0.0, NEG))
        return carry

    def both(index, carry):
        slot = SLOTS[2]
        real = index < info[N_BOTH]
        start = jnp.where(real, info[G_BOTH] + index * slot, info[G_PAD])
        size = jnp.where(real, LENS[2], info[PAD_LEN])
        visit(pl.multiple_of(start, 16), slot, cut(slot, size))
        return carry

    lax.fori_loop(0, info[N_IMG], image, 0)
    lax.fori_loop(0, (info[N_TXT] + 1) // 2, text, 0)
    lax.fori_loop(0, info[N_BOTH] + info[N_PAD], both, 0)


def first_head():
    return lax.broadcasted_iota(jnp.int32, (1, 2 * HD), 1) < HD


def attend_kernel(info, query, key, value, out):
    out[...] = jnp.zeros_like(out)

    def visit(start, slot, bias):
        at = pl.ds(start, slot)
        first = first_head()
        for pair in range(PAIRS):
            cols = pl.ds(pair * 2 * HD, 2 * HD)
            q, k, v = query[at, cols], key[at, cols], value[at, cols]
            results = []
            for mine in (first, jnp.logical_not(first)):
                prob = softmax_cols(nt(jnp.where(mine, k, 0), q), bias)
                results.append(tn(prob.astype(BF16), v))
            out[at, cols] = jnp.where(first, results[0], results[1]).astype(BF16)

    for_items(info, visit)


def attend(info, qkv):
    rows = qkv.shape[0]
    width = qkv.shape[1] // 3
    cols = 2 * HD * PAIRS
    steps = width // cols
    return pl.pallas_call(
        attend_kernel,
        grid=(steps,),
        out_shape=jax.ShapeDtypeStruct((rows, width), BF16),
        in_specs=[
            SMEM_SPEC,
            pl.BlockSpec((rows, cols), lambda p: (0, p)),
            pl.BlockSpec((rows, cols), lambda p: (0, steps + p)),
            pl.BlockSpec((rows, cols), lambda p: (0, 2 * steps + p)),
        ],
        out_specs=pl.BlockSpec((rows, cols), lambda p: (0, p)),
        compiler_params=pltpu.CompilerParams(vmem_limit_bytes=VMEM),
        cost_estimate=cost(25),
        name="attend",
    )(info, qkv, qkv, qkv)


def attend_back_kernel(info, query, key, value, grad, dq_out, dk_out, dv_out):
    for out in (dq_out, dk_out, dv_out):
        out[...] = jnp.zeros_like(out)

    def visit(start, slot, bias):
        at = pl.ds(start, slot)
        first = first_head()
        for pair in range(PAIRS):
            cols = pl.ds(pair * 2 * HD, 2 * HD)
            q, k, v, g = query[at, cols], key[at, cols], value[at, cols], grad[at, cols]
            dqs, dks, dvs = [], [], []
            for mine in (first, jnp.logical_not(first)):
                prob = softmax_cols(nt(jnp.where(mine, k, 0), q), bias)
                product = prob * nt(jnp.where(mine, v, 0), g)
                inner = jnp.sum(product, axis=0, keepdims=True)
                grad_score = (product - prob * inner).astype(BF16)
                dqs.append(tn(grad_score, k))
                dks.append(nn(grad_score, q))
                dvs.append(nn(prob.astype(BF16), g))
            scale = HD ** (-0.5)
            dq = jnp.where(first, dqs[0], dqs[1]).astype(BF16)
            dq_out[at, cols] = (dq.astype(F32) * scale).astype(BF16)
            dk_out[at, cols] = jnp.where(first, dks[0], dks[1]).astype(BF16)
            dv_out[at, cols] = jnp.where(first, dvs[0], dvs[1]).astype(BF16)

    for_items(info, visit)


def attend_back(info, qkv, grad):
    rows = qkv.shape[0]
    width = qkv.shape[1] // 3
    cols = 2 * HD * PAIRS
    steps = width // cols
    spec = pl.BlockSpec((rows, cols), lambda p: (0, p))
    return pl.pallas_call(
        attend_back_kernel,
        grid=(steps,),
        out_shape=[jax.ShapeDtypeStruct((rows, width), BF16)] * 3,
        in_specs=[
            SMEM_SPEC,
            spec,
            pl.BlockSpec((rows, cols), lambda p: (0, steps + p)),
            pl.BlockSpec((rows, cols), lambda p: (0, 2 * steps + p)),
            spec,
        ],
        out_specs=[spec] * 3,
        compiler_params=pltpu.CompilerParams(vmem_limit_bytes=VMEM),
        cost_estimate=cost(42),
        name="attend_back",
    )(info, qkv, qkv, qkv, grad)


def group_of(info, row):
    return (
        (row >= info[G_TXT]).astype(jnp.int32)
        + (row >= info[G_BOTH]).astype(jnp.int32)
        + (row >= info[G_PAD]).astype(jnp.int32)
    )


def middle_kernel(info, x, att, weight, bias, gains, shifts, mid_out, h_out):
    first = pl.program_id(0) * BLK

    @pl.when(first < info[G_END])
    def _():
        middle = x[...].astype(F32) + (nn(att[...], weight[...]) + bias[...])
        mid_out[...] = middle
        normed, _ = normalize(middle)
        for part in range(BLK // ROW):
            which = pl.ds(jnp.minimum(group_of(info, first + part * ROW), EXPERTS - 1), 1)
            at = pl.ds(part * ROW, ROW)
            here = normed[part * ROW : (part + 1) * ROW]
            h_out[at, :] = (here * gains[which, :] + shifts[which, :]).astype(BF16)


def middle_norm(info, x, att, weight, bias, gains, shifts):
    rows, width = x.shape
    spec = pl.BlockSpec((BLK, width), lambda i: (i, 0))
    return pl.pallas_call(
        middle_kernel,
        grid=(rows // BLK,),
        out_shape=[
            jax.ShapeDtypeStruct((rows, width), F32),
            jax.ShapeDtypeStruct((rows, width), BF16),
        ],
        in_specs=[
            SMEM_SPEC,
            spec,
            spec,
            held((width, width)),
            full(bias.shape),
            full(gains.shape),
            full(shifts.shape),
        ],
        out_specs=[spec, spec],
        compiler_params=pltpu.CompilerParams(vmem_limit_bytes=VMEM),
        cost_estimate=cost(10),
        name="middle_norm",
    )(info, x, att, weight, bias, gains, shifts)


def gelu_parts(up):
    size = jnp.abs(up) * (0.5**0.5)
    expo = jnp.exp(-size * size)
    t = 1.0 / (1.0 + 0.3275911 * size)
    poly = 1.061405429 * t - 1.453152027
    poly = poly * t + 1.421413741
    poly = poly * t - 0.284496736
    poly = poly * t + 0.254829592
    tail = 0.5 * (poly * t) * expo
    cdf = jnp.where(up >= 0, 1.0 - tail, tail)
    return (up * cdf, cdf + up * (expo * 0.3989422804014327))


def hidden_kernel(part, chunk, *refs):
    info, h, g, w_up, b_up, w_down = refs[:6]
    outs = refs[6:]
    if chunk:
        send_out, keep_out = outs[:2]
        outs = outs[2:]
    else:
        all_out = outs[0]
        outs = outs[1:]
    bias_out, act_hbm, dup_hbm, act, dup, up_acc, down_acc, sems = outs
    expert = pl.program_id(0)
    start = info[G_IMG + expert]
    count = info[G_IMG + expert + 1] - start
    blocks = count // BLK
    bias_out[...] = jnp.zeros_like(bias_out)
    up_acc[...] = jnp.zeros_like(up_acc)
    down_acc[...] = jnp.zeros_like(down_acc)

    def out_copies(index):
        at = pl.ds(pl.multiple_of(index * ROW, ROW), ROW)
        return (
            pltpu.make_async_copy(act.at[at, :], act_hbm.at[at, :], sems.at[0, index]),
            pltpu.make_async_copy(dup.at[at, :], dup_hbm.at[at, :], sems.at[1, index]),
        )

    def rows_of(local, size):
        row = start + local
        at = pl.ds(pl.multiple_of(row, ROW), size)
        left, grad = h[at, :], g[at, :]
        tile = w_up.shape[2]
        up = nn(left, w_up[0]) + b_up[pl.ds(expert, 1), pl.ds(part * tile, tile)]
        grad_act = nt(grad, w_down[0])
        active, slope = gelu_parts(up)
        active = active.astype(BF16)
        grad_up = (slope * grad_act).astype(BF16)
        act[at, :] = active
        dup[at, :] = grad_up
        bias_out[0] += jnp.sum(grad_up.astype(F32), axis=0, keepdims=True)
        up_acc[...] += tn(left, grad_up)
        down_acc[...] += tn(grad, active)
        for place in range(size // ROW):
            for copy in out_copies(row // ROW + place):
                copy.start()

    def block(index, carry):
        rows_of(index * BLK, BLK)
        return carry

    lax.fori_loop(0, blocks, block, 0)

    @pl.when(count % BLK > 0)
    def _():
        rows_of(blocks * BLK, ROW)

    for slot, acc in enumerate((up_acc, down_acc)):
        if chunk:
            mine = info[CORE]
            for pair in range(acc.shape[0] // (2 * chunk)):
                first = pair * 2 * chunk
                kept = pl.ds(pl.multiple_of(first + mine * chunk, 16), chunk)
                sent = pl.ds(pl.multiple_of(first + (1 - mine) * chunk, 16), chunk)
                keep_out[slot, 0, pair] = acc[kept, :].astype(BF16)
                send_out[slot, 0, pair] = acc[sent, :].astype(BF16)
        else:
            all_out[slot, 0] = acc[...].astype(BF16)

    @pl.when(expert == pl.num_programs(0) - 1)
    def _():
        def wait(index, carry):
            for copy in out_copies(index):
                copy.wait()
            return carry

        lax.fori_loop(0, info[G_PAD] // ROW, wait, 0)


def run_hidden(part, parts, info, h, g, w_up, b_up, w_down, chunk):
    rows, width = h.shape
    tile = w_up.shape[2] // parts
    any_spec = pl.BlockSpec(memory_space=pl.ANY)
    if chunk:
        pairs = width // (2 * chunk)
        weight_shapes = [jax.ShapeDtypeStruct((2, EXPERTS, pairs, chunk, tile), BF16)] * 2
        weight_specs = [pl.BlockSpec((2, 1, pairs, chunk, tile), lambda e: (0, e, 0, 0, 0))] * 2
    else:
        weight_shapes = [jax.ShapeDtypeStruct((2, EXPERTS, width, tile), BF16)]
        weight_specs = [pl.BlockSpec((2, 1, width, tile), lambda e: (0, e, 0, 0))]
    return pl.pallas_call(
        partial(hidden_kernel, part, chunk),
        grid=(EXPERTS,),
        out_shape=weight_shapes
        + [
            jax.ShapeDtypeStruct((EXPERTS, 1, tile), F32),
            jax.ShapeDtypeStruct((rows, tile), BF16),
            jax.ShapeDtypeStruct((rows, tile), BF16),
        ],
        in_specs=[
            SMEM_SPEC,
            held((rows, width)),
            held((rows, width)),
            pl.BlockSpec((1, width, tile), lambda e: (e, 0, part)),
            full(b_up.shape),
            pl.BlockSpec((1, tile, width), lambda e: (e, part, 0)),
        ],
        out_specs=weight_specs
        + [pl.BlockSpec((1, 1, tile), lambda e: (e, 0, 0)), any_spec, any_spec],
        scratch_shapes=[
            pltpu.VMEM((rows, tile), BF16),
            pltpu.VMEM((rows, tile), BF16),
            pltpu.VMEM((width, tile), F32),
            pltpu.VMEM((width, tile), F32),
            pltpu.SemaphoreType.DMA((2, rows // ROW)),
        ],
        compiler_params=pltpu.CompilerParams(vmem_limit_bytes=VMEM),
        cost_estimate=cost(22),
        name="hidden",
    )(info, h, g, w_up, b_up, w_down)


SUMS = 16


def finish_kernel(parts, *refs):
    info = refs[0]
    hbm = refs[1 : 3 + 2 * parts]
    w_up, w_down, gains, downs, w_attn = refs[3 + 2 * parts : 8 + 2 * parts]
    refs = refs[8 + 2 * parts :]
    sums_out, outs_hbm = refs[0], refs[1:5]
    held_in = refs[5 : 7 + 2 * parts]
    held_out = refs[7 + 2 * parts : 11 + 2 * parts]
    in_sems, out_sems = refs[11 + 2 * parts :]
    group = pl.program_id(0)
    start = info[G_IMG + group]
    count = info[G_IMG + group + 1] - start
    blocks = (count + BLK - 1) // BLK
    real = group < EXPERTS

    @pl.when(group == 0)
    def _():
        sums_out[...] = jnp.zeros_like(sums_out)

    def halves(index, visit):
        for half in range(BLK // ROW):
            local = index * BLK + half * ROW

            @pl.when(local < count)
            def _(half=half, local=local):
                visit(half, pl.ds(pl.multiple_of(start + local, ROW), ROW))

    def in_copies(slot, half, at):
        here = pl.ds(half * ROW, ROW)
        return [
            pltpu.make_async_copy(
                source.at[at, :], target.at[slot, here, :], in_sems.at[slot, half, which]
            )
            for which, (source, target) in enumerate(zip(hbm, held_in))
        ]

    def out_copies(slot, half, at):
        here = pl.ds(half * ROW, ROW)
        return [
            pltpu.make_async_copy(
                source.at[slot, here, :], target.at[at, :], out_sems.at[slot, half, which]
            )
            for which, (source, target) in enumerate(zip(held_out, outs_hbm))
        ]

    def fetch(index):
        def visit(half, at):
            copies = in_copies(index % 2, half, at)
            for copy in copies[:2]:
                copy.start()

            @pl.when(real)
            def _():
                for copy in copies[2:]:
                    copy.start()

        halves(index, visit)

    def arrived(index):
        def visit(half, at):
            copies = in_copies(index % 2, half, at)
            for copy in copies[:2]:
                copy.wait()

            @pl.when(real)
            def _():
                for copy in copies[2:]:
                    copy.wait()

        halves(index, visit)

    def send(index):
        def visit(half, at):
            for copy in out_copies(index % 2, half, at):
                copy.start()

        halves(index, visit)

    def sent(index):
        def visit(half, at):
            for copy in out_copies(index % 2, half, at):
                copy.wait()

        halves(index, visit)

    @pl.when(blocks > 0)
    def _():
        fetch(0)

    which = pl.ds(jnp.minimum(group, EXPERTS - 1), 1)
    one = real.astype(F32)

    def block(index, carry):
        slot = index % 2

        @pl.when(index + 1 < blocks)
        def _():
            fetch(index + 1)

        arrived(index)

        @pl.when(index >= 2)
        def _():
            sent(index - 2)

        mid, grad_in = held_in[0], held_in[1]
        acts, dups = held_in[2 : 2 + parts], held_in[2 + parts :]
        mixed, dx, proj_out, datt = held_out
        middle = mid[slot]
        grad = grad_in[slot].astype(F32)
        tile = acts[0].shape[2]
        lower = jnp.zeros_like(middle)
        grad_hidden = jnp.zeros_like(middle)
        for part in range(parts):
            cols = pl.ds(part * tile, tile)
            lower += nn(acts[part][slot], w_down[0, cols, :])
            grad_hidden += nt(dups[part][slot], w_up[0, :, cols])
        valid = index * BLK + lax.broadcasted_iota(jnp.int32, (BLK, 1), 0) < count
        lower = jnp.where(real, lower + downs[which, :], 0.0)
        grad_hidden = jnp.where(valid & real, grad_hidden, 0.0)
        grad = jnp.where(valid, grad, 0.0)
        middle = jnp.where(valid, middle, 0.0)
        mixed[slot] = (middle + lower).astype(BF16)
        normed, inverse = normalize(middle)
        grad_middle = grad + norm_back(grad_hidden * gains[which, :], normed, inverse)
        dx[slot] = grad_middle
        proj = grad_middle.astype(BF16)
        proj_out[slot] = proj
        datt[slot] = nt(proj, w_attn[...]).astype(BF16)
        send(index)
        sums_out[pl.ds(0, 1), :] += jnp.sum(proj.astype(F32), axis=0, keepdims=True)

        @pl.when(real)
        def _():
            for place, value in enumerate((grad_hidden * normed, grad_hidden, grad)):
                at = pl.ds(1 + place * EXPERTS + group, 1)
                sums_out[at, :] += jnp.sum(value, axis=0, keepdims=True)

        return carry

    lax.fori_loop(0, blocks, block, 0)

    @pl.when(blocks >= 2)
    def _():
        sent(blocks - 2)

    @pl.when(blocks >= 1)
    def _():
        sent(blocks - 1)


def finish_experts(info, mid, g, acts, dups, w_up, w_down, gains, downs, w_attn):
    rows, width = mid.shape
    parts = len(acts)
    tile = acts[0].shape[1]
    any_spec = pl.BlockSpec(memory_space=pl.ANY)
    kinds = (BF16, F32, BF16, BF16)
    expert = lambda e: (jnp.minimum(e, EXPERTS - 1), 0, 0)
    return pl.pallas_call(
        partial(finish_kernel, parts),
        grid=(EXPERTS + 1,),
        out_shape=[jax.ShapeDtypeStruct((SUMS, width), F32)]
        + [jax.ShapeDtypeStruct((rows, width), kind) for kind in kinds],
        in_specs=[SMEM_SPEC]
        + [any_spec] * (2 + 2 * parts)
        + [
            pl.BlockSpec((1,) + w_up.shape[1:], expert),
            pl.BlockSpec((1,) + w_down.shape[1:], expert),
            full(gains.shape),
            full(downs.shape),
            held((width, width)),
        ],
        out_specs=[full((SUMS, width))] + [any_spec] * 4,
        scratch_shapes=[pltpu.VMEM((2, BLK, width), F32), pltpu.VMEM((2, BLK, width), BF16)]
        + [pltpu.VMEM((2, BLK, tile), BF16)] * (2 * parts)
        + [pltpu.VMEM((2, BLK, width), kind) for kind in kinds]
        + [
            pltpu.SemaphoreType.DMA((2, BLK // ROW, 2 + 2 * parts)),
            pltpu.SemaphoreType.DMA((2, BLK // ROW, 4)),
        ],
        compiler_params=pltpu.CompilerParams(vmem_limit_bytes=VMEM),
        cost_estimate=cost(30),
        name="finish_experts",
    )(info, mid, g, *acts, *dups, w_up, w_down, gains, downs, w_attn)


def weights_kernel(dp, seq, info, dq, dk, dv, proj, h, att, send_out, keep_out, acc, attn_acc):
    index = pl.program_id(0)

    @pl.when(index == 0)
    def _():
        acc[...] = jnp.zeros_like(acc)
        attn_acc[...] = jnp.zeros_like(attn_acc)

    @pl.when(index * BLK < info[G_END])
    def _():
        row = index * BLK + lax.broadcasted_iota(jnp.int32, (BLK, 1), 0)
        real = row < info[G_END]
        hidden = h[...]
        width = hidden.shape[1]
        for part, grad in enumerate((dq, dk, dv)):
            acc[pl.ds(part * width, width), :] += tn(grad[...], hidden)
        attn_acc[...] += tn(
            jnp.where(real, proj[...], jnp.zeros_like(proj)),
            jnp.where(real, att[...], jnp.zeros_like(att)),
        )

    @pl.when(index == pl.num_programs(0) - 1)
    def _():
        width = attn_acc.shape[0]
        own = width // (dp * seq)
        half = width // 2
        for out, core in ((keep_out, info[CORE]), (send_out, 1 - info[CORE])):
            for pair in range(dp // 2):
                for place in range(seq):
                    device = (2 * pair + core) * seq + place
                    first = pl.ds(pl.multiple_of(device * 3 * own, 8), 3 * own)
                    second = pl.ds(pl.multiple_of(device * own, 8), own)
                    value = jnp.concatenate([acc[first, :], attn_acc[second, :]], axis=0)
                    value = value.astype(BF16)
                    at = pl.ds(place * 4 * own, 4 * own)
                    for lane in range(2):
                        out[lane, 0, pair, at, :] = value[:, lane * half : (lane + 1) * half]


def weights_kernel_plain(info, dq, dk, dv, proj, h, att, qkv_out, attn_out, acc, attn_acc):
    index = pl.program_id(0)

    @pl.when(index == 0)
    def _():
        acc[...] = jnp.zeros_like(acc)
        attn_acc[...] = jnp.zeros_like(attn_acc)

    @pl.when(index * BLK < info[G_END])
    def _():
        row = index * BLK + lax.broadcasted_iota(jnp.int32, (BLK, 1), 0)
        real = row < info[G_END]
        hidden = h[...]
        width = hidden.shape[1]
        for part, grad in enumerate((dq, dk, dv)):
            acc[pl.ds(part * width, width), :] += tn(grad[...], hidden)
        attn_acc[...] += tn(
            jnp.where(real, proj[...], jnp.zeros_like(proj)),
            jnp.where(real, att[...], jnp.zeros_like(att)),
        )

    @pl.when(index == pl.num_programs(0) - 1)
    def _():
        qkv_out[...] = acc[...].astype(BF16)
        attn_out[...] = attn_acc[...].astype(BF16)


def projection_grads(info, dq, dk, dv, proj, h, att, dp, seq):
    rows, width = h.shape
    spec = pl.BlockSpec((BLK, width), lambda i: (i, 0))
    own = width // (dp * seq)
    direct = own % 8 == 0
    if direct:
        shapes = [(2, 1, dp // 2, seq * 4 * own, width // 2)] * 2
        body = partial(weights_kernel, dp, seq)
    else:
        shapes = [(3 * width, width), (width, width)]
        body = weights_kernel_plain
    results = pl.pallas_call(
        body,
        grid=(rows // BLK,),
        out_shape=[jax.ShapeDtypeStruct(shape, BF16) for shape in shapes],
        in_specs=[SMEM_SPEC] + [spec] * 6,
        out_specs=[full(shape) for shape in shapes],
        scratch_shapes=[pltpu.VMEM((3 * width, width), F32), pltpu.VMEM((width, width), F32)],
        compiler_params=pltpu.CompilerParams(vmem_limit_bytes=VMEM),
        cost_estimate=cost(15),
        name="projection_grads",
    )(info, dq, dk, dv, proj, h, att)
    if direct:
        return results[1], results[0]
    d_qkv = results[0].reshape(dp * seq, -1, width)
    d_attn = results[1].reshape(dp * seq, -1, width)
    d_all = jnp.concatenate([d_qkv, d_attn], axis=1).reshape(1, -1, width)
    half = width // 2
    return core_split(jnp.stack([d_all[..., :half], d_all[..., half:]]))


VECTORS = 24


def last_kernel(parts, *refs):
    (info, x, dx, dq, dk, dv, gain, weight, row_sums) = refs[:9]
    biases = refs[9 : 9 + parts]
    out, packed = refs[9 + parts :]
    width = x.shape[1]
    step = pl.program_id(0)

    @pl.when(step == 0)
    def _():
        packed[...] = jnp.zeros_like(packed)
        packed[pl.ds(4, 10), pl.ds(0, width)] = row_sums[pl.ds(0, 10), :]
        for part, bias in enumerate(biases):
            tile = bias.shape[2]
            for expert in range(EXPERTS):
                packed[pl.ds(14 + part * EXPERTS + expert, 1), pl.ds(0, tile)] = bias[expert]

    @pl.when(step * BLK < info[G_END])
    def _():
        hidden = nt(dq[...], weight[:, pl.ds(0, width)])
        hidden += nt(dk[...], weight[:, pl.ds(width, width)])
        hidden += nt(dv[...], weight[:, pl.ds(2 * width, width)])
        normed, inverse = normalize(x[...].astype(F32))
        totals = (hidden * normed, hidden, dq[...].astype(F32), dv[...].astype(F32))
        for place, value in enumerate(totals):
            packed[pl.ds(place, 1), pl.ds(0, width)] += jnp.sum(value, axis=0, keepdims=True)
        out[...] = dx[...] + norm_back(hidden * gain[...], normed, inverse)


def last_norm(info, x, dx, dq, dk, dv, gain, weight, row_sums, biases):
    rows, width = x.shape
    spec = pl.BlockSpec((BLK, width), lambda i: (i, 0))
    cols = max(width, biases[0].shape[2])
    packed = (VECTORS, cols)
    return pl.pallas_call(
        partial(last_kernel, len(biases)),
        grid=(rows // BLK,),
        out_shape=[jax.ShapeDtypeStruct((rows, width), F32), jax.ShapeDtypeStruct(packed, F32)],
        in_specs=[SMEM_SPEC, spec, spec, spec, spec, spec, full(gain.shape), held((width, 3 * width))]
        + [full(row_sums.shape)]
        + [full(bias.shape) for bias in biases],
        out_specs=[spec, full(packed)],
        compiler_params=pltpu.CompilerParams(vmem_limit_bytes=VMEM),
        cost_estimate=cost(14),
        name="last_norm",
    )(info, x, dx, dq, dk, dv, gain, weight, row_sums, *biases)


def swap(value, bit):
    ways = lax.axis_size("dp")
    return lax.ppermute(value, "dp", [(i, i ^ (1 << bit)) for i in range(ways)])


def half_of(parts, axis, bit, mine):
    own = (lax.axis_index("dp") >> bit) & 1
    which = own if mine else 1 - own
    return [lax.dynamic_index_in_dim(part, which, axis, keepdims=False) for part in parts]


DEPTH = 4


def combine_kernel(blocks, arrays, seq, *refs):
    place, sources = refs[0], refs[1 : 1 + arrays]
    in_buf, out_buf, own_buf, send_buf, total, in_sems, out_sems = refs[-7:]
    outs = refs[1 + arrays : -7]
    ends = outs[len(outs) - seq :]
    here = place[0]

    def fetch(index):
        return [
            pltpu.make_async_copy(
                sources[which].at[number(place)],
                in_buf.at[index % DEPTH, part],
                in_sems.at[index % DEPTH, part],
            )
            for part, (which, number) in enumerate(blocks[index][0])
        ]

    def send(index):
        _, target, at = blocks[index]
        slot = index % 2
        if target != "ends":
            return [pltpu.make_async_copy(out_buf.at[slot], outs[target].at[at], out_sems.at[slot, 0])]
        copies = [pltpu.make_async_copy(own_buf.at[slot], ends[0].at[at], out_sems.at[slot, 0])]
        for hop in range(seq - 1):
            copies.append(
                pltpu.make_async_copy(
                    send_buf.at[slot, hop], ends[1 + hop].at[at], out_sems.at[slot, 1 + hop]
                )
            )
        return copies

    for index in range(min(DEPTH - 1, len(blocks))):
        for copy in fetch(index):
            copy.start()
    for index, (parts, target, _) in enumerate(blocks):
        if index + DEPTH - 1 < len(blocks):
            for copy in fetch(index + DEPTH - 1):
                copy.start()
        for copy in fetch(index):
            copy.wait()
        if index >= 2:
            for copy in send(index - 2):
                copy.wait()
        value = in_buf[index % DEPTH, 0].astype(F32)
        for part in range(1, len(parts)):
            value = value + in_buf[index % DEPTH, part].astype(F32)
        slot = index % 2
        if target != "ends":
            out_buf[slot] = value.astype(BF16)
        else:
            total[...] = value
            rows = total.shape[0] // seq
            for hop in range(seq):
                first = pl.multiple_of(lax.rem(here + hop, seq) * rows, 8)
                block = total[pl.ds(first, rows), :]
                if hop == 0:
                    own_buf[slot] = block
                else:
                    send_buf[slot, hop - 1] = block.astype(BF16)
        for copy in send(index):
            copy.start()
    for index in range(max(0, len(blocks) - 2), len(blocks)):
        for copy in send(index):
            copy.wait()


class Sum:

    def __init__(self, kept, sent):
        self.bits = lax.axis_size("dp").bit_length() - 1
        self.seq = lax.axis_size("seq")
        self.many, self.pairs, self.chunk, self.cols = kept.shape[1:]
        every = list(range(self.bits - 1, 0, -1))
        got = swap(sent, 0)
        self.lanes = [
            [(self.flat(value), lane * self.many * self.pairs, every) for value in (kept, got)]
            for lane in range(2)
        ]
        self.left = [list(every), list(every)]
        self.own = None

    def flat(self, value):
        return value.reshape(-1, self.chunk, self.cols)

    def more(self):
        return bool(self.left[0])

    def direct(self):
        return (self.chunk // self.seq) % 8 == 0

    def sources(self, lane, other, free, one, value):
        results = []
        for array, base, bits in self.lanes[lane]:

            def number(place, base=base, bits=bits):
                at = one
                for bit in bits:
                    if bit in free:
                        at = at * 2 + ((value >> (len(free) - 1 - free.index(bit))) & 1)
                    elif bit == other:
                        at = at * 2 + (1 - place[1 + bit])
                    else:
                        at = at * 2 + place[1 + bit]
                return base + at

            results.append((array, number))
        return results


def advance(place, steps, closing=None):
    arrays, blocks, payloads, turns = [], [], {}, []
    model = steps[0] if steps else closing

    def add(parts, target, at):
        known = []
        for array, number in parts:
            found = [i for i, other in enumerate(arrays) if other is array]
            if not found:
                arrays.append(array)
            known.append((found[0] if found else len(arrays) - 1, number))
        blocks.append((known, target, at))

    for total in steps:
        for lane in range(2):
            left = total.left[lane]
            bit = min(left) if lane == 0 else max(left)
            left.remove(bit)
            free = list(left)
            count = payloads.get(bit, 0)
            turns.append((total, lane, bit, free, count))
            for one in range(total.many):
                for value in range(2 ** len(free)):
                    add(total.sources(lane, bit, free, one, value), bit, count)
                    count += 1
            payloads[bit] = count
    order = sorted(payloads)
    seq, chunk, cols = model.seq, model.chunk, model.cols
    shapes = [jax.ShapeDtypeStruct((payloads[bit], chunk, cols), BF16) for bit in order]
    rows = chunk // seq
    split = closing is not None and closing.direct()
    if closing is not None:
        target = "ends" if split else len(order)
        for lane in range(2):
            for one in range(closing.many):
                add(closing.sources(lane, None, [], one, 0), target, lane * closing.many + one)
        count = 2 * closing.many
        if split:
            shapes.append(jax.ShapeDtypeStruct((count, rows, cols), F32))
            shapes += [jax.ShapeDtypeStruct((count, rows, cols), BF16)] * (seq - 1)
        else:
            shapes.append(jax.ShapeDtypeStruct((count, chunk, cols), BF16))
    blocks = [
        (parts, order.index(target) if target in order else target, at)
        for parts, target, at in blocks
    ]
    most = max(len(parts) for parts, _, _ in blocks)
    end_rows = rows if split else 8
    any_spec = pl.BlockSpec(memory_space=pl.ANY)
    results = pl.pallas_call(
        partial(combine_kernel, blocks, len(arrays), seq),
        in_specs=[SMEM_SPEC] + [any_spec] * len(arrays),
        out_specs=[any_spec] * len(shapes),
        out_shape=shapes,
        scratch_shapes=[
            pltpu.VMEM((DEPTH, most, chunk, cols), BF16),
            pltpu.VMEM((2, chunk, cols), BF16),
            pltpu.VMEM((2, end_rows, cols), F32),
            pltpu.VMEM((2, seq - 1, end_rows, cols), BF16),
            pltpu.VMEM((chunk, cols), F32),
            pltpu.SemaphoreType.DMA((DEPTH, most)),
            pltpu.SemaphoreType.DMA((2, seq)),
        ],
        compiler_params=pltpu.CompilerParams(vmem_limit_bytes=VMEM),
        cost_estimate=cost(4),
        name="combine",
    )(place, *arrays)

    def go():
        got = {bit: swap(value, bit) for bit, value in zip(order, results)}
        for total, lane, bit, free, first in turns:
            total.lanes[lane].append((got[bit], first, free))
        if closing is not None:
            parts = results[len(order) :]
            if not split:
                half = parts[0].reshape(2 * closing.many, seq, rows, cols)
                here = lax.axis_index("seq")
                parts = [
                    lax.dynamic_index_in_dim(half, (here + hop) % seq, 1, keepdims=False)
                    for hop in range(seq)
                ]
            closing.own = parts[0].astype(F32)
            closing.got = [
                lax.ppermute(send, "seq", [(i, (i + hop + 1) % seq) for i in range(seq)])
                for hop, send in enumerate(parts[1:])
            ]

    return list(results), go


def finish_sum(total):
    value = total.own
    for got in total.got:
        value = value + got.astype(F32)
    return value.reshape(2, total.many, -1, total.cols)


def sum_everywhere(value):
    for bit in range(lax.axis_size("dp").bit_length() - 1):
        value = value + swap(value, bit)
    seq = lax.axis_size("seq")
    for bit in range(seq.bit_length() - 1):
        value = value + lax.ppermute(value, "seq", [(i, i ^ (1 << bit)) for i in range(seq)])
    return value


def after(info, *values):
    return lax.optimization_barrier((info,) + values)[0] if values else info


def arrived(sums):
    return [got for total in sums if total.own is not None for got in total.got]


def exchange(value, rows):
    seq = lax.axis_size("seq")
    from_left = lax.ppermute(value[-rows:], "seq", [(i, i + 1) for i in range(seq - 1)])
    from_right = lax.ppermute(value[:rows], "seq", [(i + 1, i) for i in range(seq - 1)])
    return (from_left, from_right)


def core_split(value):
    pairs = lax.axis_size("dp") // 2
    two, many, depth, cols = value.shape
    shaped = value.reshape(two, many, pairs, 2, depth // (2 * pairs), cols)
    kept = half_of([shaped], 3, 0, True)[0]
    sent = half_of([shaped], 3, 0, False)[0]
    return (kept, sent)


PARTS = 3


def per_device(
    tokens, item_types, first_gain, first_shift, qkv_weight, query_bias, value_bias, attn_weight,
    attn_bias, second_gain, second_shift, expert_up, up_bias, expert_down, down_bias, cotangent,
):
    tok, width = tokens.shape
    dp, seq = lax.axis_size("dp"), lax.axis_size("seq")
    rows = capacity(tok)
    chunk = width // dp
    chunk = chunk if chunk % 16 == 0 else 0
    bits = [(lax.axis_index("dp") >> bit) & 1 for bit in range(dp.bit_length() - 1)]
    place = jnp.stack([lax.axis_index("seq")] + bits).astype(jnp.int32)
    x_left, x_right = exchange(tokens, HALO)
    x, info = sort_rows(place, item_types, (x_left, tokens, x_right), rows, tok * seq)
    d_left, d_right = exchange(after(cotangent, info), HALO)

    h, qkv = project_qkv(info, x, first_gain, first_shift, qkv_weight, query_bias, value_bias)
    att = attend(info, qkv)
    g = sort_more(info, (d_left, cotangent, d_right), rows)
    mid, h2 = middle_norm(info, x, att, attn_weight, attn_bias, second_gain, second_shift)

    def window(sums, *more):
        steps = [total for total in sums if total.more()]
        closing = [total for total in sums if not total.more() and total.own is None]
        if not steps and not closing:
            return after(info, *more)
        ready, go = advance(place, steps, closing[0] if closing else None)
        go()
        return after(info, *ready, *more)

    sums, up_biases, acts, dups = [], [], [], []
    gate = info
    for part in range(PARTS):
        results = run_hidden(part, PARTS, gate, h2, g, expert_up, up_bias, expert_down, chunk)
        bias, act, dup = results[-3:]
        up_biases.append(bias)
        acts.append(act)
        dups.append(dup)
        if chunk:
            sent, kept = results[0], results[1]
        else:
            kept, sent = core_split(results[0])
        gate = window(sums)
        sums.append(Sum(kept, sent))
    row_sums, mixed, dx, proj, datt = finish_experts(
        gate, mid, g, acts, dups, expert_up, expert_down, second_gain, down_bias, attn_weight
    )
    gate = window(sums)
    dq, dk, dv = attend_back(gate, qkv, datt)
    gate = window(sums, *arrived(sums[:1]))
    kept, sent = projection_grads(gate, dq, dk, dv, proj, h, att, dp, seq)
    last = Sum(kept, sent)
    gate = window(sums)
    grad_x, packed = last_norm(
        gate, x, dx, dq, dk, dv, first_gain, qkv_weight, row_sums, up_biases
    )
    gate = window([last], *arrived(sums[:2]))
    m_own, m_left, m_right, g_own, g_left, g_right = unsort_rows(gate, mixed, grad_x, tok)
    while any(total.own is None for total in sums):
        window(sums)
    while last.own is None:
        window([last])
    expert_sums = [finish_sum(total) for total in sums]
    last_sums = finish_sum(last)

    def merge(own, left, right):
        to_left = lax.ppermute(left, "seq", [(i + 1, i) for i in range(seq - 1)])
        to_right = lax.ppermute(right, "seq", [(i, i + 1) for i in range(seq - 1)])
        own = own.at[:HALO].add(to_right)
        return own.at[tok - HALO :].add(to_left)

    mixed_out = merge(m_own, m_left, m_right)
    grad_out = merge(g_own, g_left, g_right)

    packed = sum_everywhere(packed)
    own = width // (dp * seq)
    rank = lax.axis_index("dp") * seq + lax.axis_index("seq")
    vectors = lax.dynamic_slice(packed, (0, rank * own), (14, own))
    tile = up_biases[0].shape[2]
    up_total = packed[14 : 14 + PARTS * EXPERTS, :tile].reshape(PARTS, EXPERTS, tile)
    sum_up = jnp.concatenate([total[0] for total in expert_sums], axis=-1)
    sum_down = jnp.concatenate([total[1] for total in expert_sums], axis=-1).swapaxes(1, 2)
    last_sums = jnp.concatenate([last_sums[0, 0], last_sums[1, 0]], axis=1).T

    return (
        mixed_out,
        grad_out,
        vectors[0],
        vectors[1],
        last_sums[:, : 3 * own],
        vectors[2],
        vectors[3],
        last_sums[:, 3 * own :],
        vectors[4],
        vectors[5:8],
        vectors[8:11],
        sum_up,
        up_total.swapaxes(0, 1).reshape(EXPERTS, -1),
        sum_down,
        vectors[11:14],
    )


def solution(mesh):
    split = P(("dp", "seq"))
    in_specs = (P(("dp", "seq"), None), P("dp", None)) + (P(),) * 13 + (P(("dp", "seq"), None),)
    out_specs = (
        P(("dp", "seq"), None),
        P(("dp", "seq"), None),
        split,
        split,
        P(None, ("dp", "seq")),
        split,
        split,
        P(None, ("dp", "seq")),
        split,
        P(None, ("dp", "seq")),
        P(None, ("dp", "seq")),
        P(None, ("dp", "seq"), None),
        P(),
        P(None, None, ("dp", "seq")),
        P(None, ("dp", "seq")),
    )
    return jax.shard_map(
        per_device, mesh=mesh, in_specs=in_specs, out_specs=out_specs, check_vma=False
    )
```

```python
from functools import partial

import jax
import jax.numpy as jnp
from jax import lax
from jax.experimental import pallas as pl
from jax.experimental.pallas import tpu as pltpu
from jax.sharding import PartitionSpec as P

HD = 64
EXPERTS = 3
IMG_LEN = 197
TXT_LEN = 64
LENS = (IMG_LEN, TXT_LEN, IMG_LEN + TXT_LEN)
SLOTS = (208, 64, 272)
TXT_PAIR = 128
PAD_ROWS = 384
HALO = 144
ROW = 128
BLK = 256

EPS = 1e-05
NEG = -1e30
VMEM = 60 << 20
F32 = jnp.float32
BF16 = jnp.bfloat16

N_IMG, N_TXT, N_BOTH, N_PAD = 0, 1, 2, 3
G_IMG, G_TXT, G_BOTH, G_PAD, G_END = 4, 5, 6, 7, 8
PAD_LEN, OWN_N, CORE = 9, 10, 11
TABLE = 16
INFO = 256


def nn(a, b):
    return lax.dot_general(a, b, (((1,), (0,)), ((), ())), preferred_element_type=F32)


def nt(a, b):
    return lax.dot_general(a, b, (((1,), (1,)), ((), ())), preferred_element_type=F32)


def tn(a, b):
    return lax.dot_general(a, b, (((0,), (0,)), ((), ())), preferred_element_type=F32)


def cost(microseconds):
    return pl.CostEstimate(flops=int(microseconds * 1e10), bytes_accessed=0, transcendentals=0)


SMEM_SPEC = pl.BlockSpec(memory_space=pltpu.SMEM)


def up_to(value, unit):
    return ((value + unit - 1) // unit) * unit


def normalize(v):
    mean = jnp.mean(v, axis=-1, keepdims=True)
    cent = v - mean
    var = jnp.mean(cent * cent, axis=-1, keepdims=True)
    inverse = lax.rsqrt(var + EPS)
    return (cent * inverse, inverse)


def norm_back(grad, normed, inverse):
    inner = jnp.mean(grad * normed, axis=-1, keepdims=True)
    return inverse * (grad - jnp.mean(grad, axis=-1, keepdims=True) - normed * inner)


def capacity(tok):
    rows = tok + LENS[2] - 1
    best = 0
    for images in range(rows // LENS[0] + 1):
        for both in range((rows - images * LENS[0]) // LENS[2] + 1):
            left = rows - images * LENS[0] - both * LENS[2]
            for pad in (0, 1):
                spare = left - pad * (1 + LENS[2] // 2)
                if spare < 0:
                    continue
                texts = spare // LENS[1]
                for count in range(texts + 1):
                    total = (
                        up_to(images * SLOTS[0], ROW)
                        + up_to(count * SLOTS[1], ROW)
                        + up_to(both * SLOTS[2], ROW)
                        + pad * PAD_ROWS
                    )
                    best = max(best, total)
    return up_to(best, BLK)


def gather_rows(info, wins, outs):
    for out in outs:
        out[...] = jnp.zeros_like(out)

    def place(index, carry):
        source = info[TABLE + 3 * index]
        target = pl.multiple_of(info[TABLE + 3 * index + 1], 16)
        kind = info[TABLE + 3 * index + 2]
        begin = pl.multiple_of((source // 16) * 16, 16)
        shift = source - begin
        for which in range(EXPERTS):
            slot = SLOTS[which]
            fits = (kind == which) if which < 2 else (kind >= 2)
            size = LENS[which] if which < 2 else jnp.where(kind == 2, LENS[2], info[PAD_LEN])

            @pl.when(fits)
            def _(slot=slot, size=size):
                rows = lax.broadcasted_iota(jnp.int32, (slot, slot + 16), 0)
                cols = lax.broadcasted_iota(jnp.int32, (slot, slot + 16), 1)
                chosen = ((cols == rows + shift) & (rows < size)).astype(F32).astype(BF16)
                for win, out in zip(wins, outs):
                    value = nn(chosen, win[pl.ds(begin, slot + 16), :])
                    out[pl.ds(target, slot), :] = value.astype(BF16)

        return carry

    lax.fori_loop(0, info[OWN_N], place, 0)


def sort_kernel(
    tok, group, place_ref, types, left, x_own, d_own, right, x_out, d_out, info, x_win, d_win
):
    items = types.shape[1]
    low = place_ref[0] * tok
    info[CORE] = place_ref[1]
    width = x_own.shape[1]
    for win, own_rows, at in ((x_win, x_own, 0), (d_win, d_own, width)):
        win[pl.ds(0, HALO), :] = left[:, pl.ds(at, width)]
        win[pl.ds(HALO, tok), :] = own_rows[...]
        win[pl.ds(HALO + tok, HALO), :] = right[:, pl.ds(at, width)]
        rest = win.shape[0] - (2 * HALO + tok)
        win[pl.ds(2 * HALO + tok, rest), :] = jnp.zeros((rest, width), BF16)

    def length(kind):
        return jnp.where(
            kind == 0, LENS[0], jnp.where(kind == 1, LENS[1], jnp.where(kind == 2, LENS[2], 0))
        )

    def owned(start, size):
        middle = (start + start + size) // 2
        return (middle >= low) & (middle < low + tok) & (size > 0)

    def count(index, carry):
        start, images, texts, boths = carry
        kind = types[0, index]
        size = length(kind)
        mine = owned(start, size)
        return (
            start + size,
            images + jnp.where(mine & (kind == 0), 1, 0),
            texts + jnp.where(mine & (kind == 1), 1, 0),
            boths + jnp.where(mine & (kind == 2), 1, 0),
        )

    zero = jnp.int32(0)
    total, images, texts, boths = lax.fori_loop(0, items, count, (zero, zero, zero, zero))
    pad_len = group - total
    pad = owned(total, pad_len)
    g_txt = up_to(images * SLOTS[0], ROW)
    g_both = g_txt + up_to(texts * SLOTS[1], ROW)
    g_pad = g_both + up_to(boths * SLOTS[2], ROW)
    info[N_IMG] = images
    info[N_TXT] = texts
    info[N_BOTH] = boths
    info[N_PAD] = jnp.where(pad, 1, 0)
    info[G_IMG] = zero
    info[G_TXT] = g_txt
    info[G_BOTH] = g_both
    info[G_PAD] = g_pad
    info[G_END] = g_pad + jnp.where(pad, PAD_ROWS, 0)
    info[PAD_LEN] = pad_len

    def note(own, source, target, kind):
        info[TABLE + 3 * own] = source
        info[TABLE + 3 * own + 1] = target
        info[TABLE + 3 * own + 2] = kind

    def place(index, carry):
        start, images, texts, boths, own = carry
        kind = types[0, index]
        size = length(kind)
        mine = owned(start, size)

        @pl.when(mine)
        def _():
            target = jnp.where(
                kind == 0,
                images * SLOTS[0],
                jnp.where(kind == 1, g_txt + texts * SLOTS[1], g_both + boths * SLOTS[2]),
            )
            note(own, start - low + HALO, target, kind)

        return (
            start + size,
            images + jnp.where(mine & (kind == 0), 1, 0),
            texts + jnp.where(mine & (kind == 1), 1, 0),
            boths + jnp.where(mine & (kind == 2), 1, 0),
            own + jnp.where(mine, 1, 0),
        )

    own = lax.fori_loop(0, items, place, (zero, zero, zero, zero, zero))[-1]

    @pl.when(pad)
    def _():
        note(own, total - low + HALO, g_pad, jnp.int32(EXPERTS))

    info[OWN_N] = own + jnp.where(pad, 1, 0)
    gather_rows(info, (x_win, d_win), (x_out, d_out))


def sort_rows(place, types, left, x, d, right, rows, group):
    tok, width = x.shape
    vmem = pl.BlockSpec(memory_space=pltpu.VMEM)
    return pl.pallas_call(
        partial(sort_kernel, tok, group),
        out_shape=[
            jax.ShapeDtypeStruct((rows, width), BF16),
            jax.ShapeDtypeStruct((rows, width), BF16),
            jax.ShapeDtypeStruct((INFO,), jnp.int32),
        ],
        in_specs=[SMEM_SPEC, SMEM_SPEC] + [vmem] * 4,
        out_specs=[vmem, vmem, SMEM_SPEC],
        scratch_shapes=[pltpu.VMEM((tok + HALO + 288, width), BF16)] * 2,
        compiler_params=pltpu.CompilerParams(vmem_limit_bytes=VMEM),
        cost_estimate=cost(11),
        name="sort_rows",
    )(place, types, left, x, d, right)


def unsort_kernel(info, mixed, grad, m_own, g_own, left, right, m_win, g_win):
    tok, width = m_own.shape
    m_win[...] = jnp.zeros_like(m_win)
    g_win[...] = jnp.zeros_like(g_win)

    def place(index, carry):
        source = info[TABLE + 3 * index]
        target = pl.multiple_of(info[TABLE + 3 * index + 1], 16)
        kind = info[TABLE + 3 * index + 2]
        begin = pl.multiple_of((source // 16) * 16, 16)
        shift = source - begin
        for which in range(EXPERTS):
            slot = SLOTS[which]
            fits = (kind == which) if which < 2 else (kind >= 2)
            size = LENS[which] if which < 2 else jnp.where(kind == 2, LENS[2], info[PAD_LEN])

            @pl.when(fits)
            def _(slot=slot, size=size):
                into = lax.broadcasted_iota(jnp.int32, (slot + 16, slot), 0)
                cols = lax.broadcasted_iota(jnp.int32, (slot + 16, slot), 1)
                chosen = ((into == cols + shift) & (cols < size)).astype(F32).astype(BF16)
                at, to = pl.ds(target, slot), pl.ds(begin, slot + 16)
                m_win[to, :] += nn(chosen, mixed[at, :])
                value = grad[at, :]
                high = value.astype(BF16)
                rest = (value - high.astype(F32)).astype(BF16)
                g_win[to, :] += nn(chosen, high) + nn(chosen, rest)

        return carry

    lax.fori_loop(0, info[OWN_N], place, 0)
    m_own[...] = m_win[pl.ds(HALO, tok), :].astype(m_own.dtype)
    g_own[...] = g_win[pl.ds(HALO, tok), :]
    for out, begin in ((left, 0), (right, HALO + tok)):
        out[:, pl.ds(0, width)] = g_win[pl.ds(begin, HALO), :].astype(BF16)
        out[:, pl.ds(width, width)] = m_win[pl.ds(begin, HALO), :].astype(BF16)


def unsort_rows(info, mixed, grad, tok):
    width = grad.shape[1]
    vmem = pl.BlockSpec(memory_space=pltpu.VMEM)
    return pl.pallas_call(
        unsort_kernel,
        out_shape=[
            jax.ShapeDtypeStruct((tok, width), BF16),
            jax.ShapeDtypeStruct((tok, width), F32),
            jax.ShapeDtypeStruct((HALO, 2 * width), BF16),
            jax.ShapeDtypeStruct((HALO, 2 * width), BF16),
        ],
        in_specs=[SMEM_SPEC, vmem, vmem],
        out_specs=[vmem] * 4,
        scratch_shapes=[pltpu.VMEM((tok + HALO + 288, width), F32)] * 2,
        compiler_params=pltpu.CompilerParams(vmem_limit_bytes=VMEM),
        cost_estimate=cost(10),
        name="unsort_rows",
    )(info, mixed, grad)


def qkv_kernel(info, x, gain, shift, weight, query_bias, value_bias, h_out, qkv_out):
    used = pl.program_id(0) * BLK < info[G_END]
    width = x.shape[1]

    @pl.when(used)
    def _():
        normed, _ = normalize(x[...].astype(F32))
        hidden = (normed * gain[...] + shift[...]).astype(BF16)
        h_out[...] = hidden
        for part in range(3):
            cols = pl.ds(part * width, width)
            value = nn(hidden, weight[:, cols])
            if part == 0:
                value = (value + query_bias[...]) * (HD ** (-0.5))
            if part == 2:
                value = value + value_bias[...]
            qkv_out[:, cols] = value.astype(BF16)

    @pl.when(jnp.logical_not(used))
    def _():
        h_out[...] = jnp.zeros_like(h_out)
        qkv_out[...] = jnp.zeros_like(qkv_out)


def full(shape):
    return pl.BlockSpec(shape, lambda *_: (0,) * len(shape))


def held(shape):
    return pl.BlockSpec(shape, lambda *_: (0,) * len(shape), pipeline_mode=pl.Buffered(1))


def project_qkv(info, x, gain, shift, weight, query_bias, value_bias):
    rows, width = x.shape
    return pl.pallas_call(
        qkv_kernel,
        grid=(rows // BLK,),
        out_shape=[
            jax.ShapeDtypeStruct((rows, width), BF16),
            jax.ShapeDtypeStruct((rows, 3 * width), BF16),
        ],
        in_specs=[
            SMEM_SPEC,
            pl.BlockSpec((BLK, width), lambda i: (i, 0)),
            full(gain.shape),
            full(shift.shape),
            held((width, 3 * width)),
            full(query_bias.shape),
            full(value_bias.shape),
        ],
        out_specs=[
            pl.BlockSpec((BLK, width), lambda i: (i, 0)),
            pl.BlockSpec((BLK, 3 * width), lambda i: (i, 0)),
        ],
        compiler_params=pltpu.CompilerParams(vmem_limit_bytes=VMEM),
        cost_estimate=cost(11),
        name="project_qkv",
    )(info, x, gain, shift, weight, query_bias, value_bias)


PAIRS = 3


def softmax_cols(scores, bias):
    masked = scores + bias
    expo = jnp.exp(masked - jnp.max(masked, axis=0, keepdims=True))
    return expo * (1.0 / jnp.sum(expo, axis=0, keepdims=True))


def for_items(info, visit):
    def cut(slot, size):
        return jnp.where(lax.broadcasted_iota(jnp.int32, (slot, 1), 0) < size, 0.0, NEG)

    def image(index, carry):
        slot = SLOTS[0]
        visit(pl.multiple_of(index * slot, 16), slot, cut(slot, LENS[0]))
        return carry

    def text(index, carry):
        slot = TXT_PAIR
        rows = lax.broadcasted_iota(jnp.int32, (slot, slot), 0) // TXT_LEN
        cols = lax.broadcasted_iota(jnp.int32, (slot, slot), 1) // TXT_LEN
        start = pl.multiple_of(info[G_TXT] + index * slot, ROW)
        visit(start, slot, jnp.where(rows == cols, 0.0, NEG))
        return carry

    def both(index, carry):
        slot = SLOTS[2]
        real = index < info[N_BOTH]
        start = jnp.where(real, info[G_BOTH] + index * slot, info[G_PAD])
        size = jnp.where(real, LENS[2], info[PAD_LEN])
        visit(pl.multiple_of(start, 16), slot, cut(slot, size))
        return carry

    lax.fori_loop(0, info[N_IMG], image, 0)
    lax.fori_loop(0, (info[N_TXT] + 1) // 2, text, 0)
    lax.fori_loop(0, info[N_BOTH] + info[N_PAD], both, 0)


def first_head():
    return lax.broadcasted_iota(jnp.int32, (1, 2 * HD), 1) < HD


def attend_kernel(info, query, key, value, out):
    out[...] = jnp.zeros_like(out)

    def visit(start, slot, bias):
        at = pl.ds(start, slot)
        first = first_head()
        for pair in range(PAIRS):
            cols = pl.ds(pair * 2 * HD, 2 * HD)
            q, k, v = query[at, cols], key[at, cols], value[at, cols]
            results = []
            for mine in (first, jnp.logical_not(first)):
                prob = softmax_cols(nt(jnp.where(mine, k, 0), q), bias)
                results.append(tn(prob.astype(BF16), v))
            out[at, cols] = jnp.where(first, results[0], results[1]).astype(BF16)

    for_items(info, visit)


def attend(info, qkv):
    rows = qkv.shape[0]
    width = qkv.shape[1] // 3
    cols = 2 * HD * PAIRS
    steps = width // cols
    return pl.pallas_call(
        attend_kernel,
        grid=(steps,),
        out_shape=jax.ShapeDtypeStruct((rows, width), BF16),
        in_specs=[
            SMEM_SPEC,
            pl.BlockSpec((rows, cols), lambda p: (0, p)),
            pl.BlockSpec((rows, cols), lambda p: (0, steps + p)),
            pl.BlockSpec((rows, cols), lambda p: (0, 2 * steps + p)),
        ],
        out_specs=pl.BlockSpec((rows, cols), lambda p: (0, p)),
        compiler_params=pltpu.CompilerParams(vmem_limit_bytes=VMEM),
        cost_estimate=cost(25),
        name="attend",
    )(info, qkv, qkv, qkv)


def attend_back_kernel(info, query, key, value, grad, dq_out, dk_out, dv_out):
    for out in (dq_out, dk_out, dv_out):
        out[...] = jnp.zeros_like(out)

    def visit(start, slot, bias):
        at = pl.ds(start, slot)
        first = first_head()
        for pair in range(PAIRS):
            cols = pl.ds(pair * 2 * HD, 2 * HD)
            q, k, v, g = query[at, cols], key[at, cols], value[at, cols], grad[at, cols]
            dqs, dks, dvs = [], [], []
            for mine in (first, jnp.logical_not(first)):
                prob = softmax_cols(nt(jnp.where(mine, k, 0), q), bias)
                product = prob * nt(jnp.where(mine, v, 0), g)
                inner = jnp.sum(product, axis=0, keepdims=True)
                grad_score = (product - prob * inner).astype(BF16)
                dqs.append(tn(grad_score, k))
                dks.append(nn(grad_score, q))
                dvs.append(nn(prob.astype(BF16), g))
            scale = HD ** (-0.5)
            dq = jnp.where(first, dqs[0], dqs[1]).astype(BF16)
            dq_out[at, cols] = (dq.astype(F32) * scale).astype(BF16)
            dk_out[at, cols] = jnp.where(first, dks[0], dks[1]).astype(BF16)
            dv_out[at, cols] = jnp.where(first, dvs[0], dvs[1]).astype(BF16)

    for_items(info, visit)


def attend_back(info, qkv, grad):
    rows = qkv.shape[0]
    width = qkv.shape[1] // 3
    cols = 2 * HD * PAIRS
    steps = width // cols
    spec = pl.BlockSpec((rows, cols), lambda p: (0, p))
    return pl.pallas_call(
        attend_back_kernel,
        grid=(steps,),
        out_shape=[jax.ShapeDtypeStruct((rows, width), BF16)] * 3,
        in_specs=[
            SMEM_SPEC,
            spec,
            pl.BlockSpec((rows, cols), lambda p: (0, steps + p)),
            pl.BlockSpec((rows, cols), lambda p: (0, 2 * steps + p)),
            spec,
        ],
        out_specs=[spec] * 3,
        compiler_params=pltpu.CompilerParams(vmem_limit_bytes=VMEM),
        cost_estimate=cost(42),
        name="attend_back",
    )(info, qkv, qkv, qkv, grad)


def group_of(info, row):
    return (
        (row >= info[G_TXT]).astype(jnp.int32)
        + (row >= info[G_BOTH]).astype(jnp.int32)
        + (row >= info[G_PAD]).astype(jnp.int32)
    )


def middle_kernel(info, x, att, weight, bias, gains, shifts, mid_out, h_out):
    first = pl.program_id(0) * BLK

    @pl.when(first < info[G_END])
    def _():
        middle = x[...].astype(F32) + (nn(att[...], weight[...]) + bias[...])
        mid_out[...] = middle
        normed, _ = normalize(middle)
        for part in range(BLK // ROW):
            which = pl.ds(jnp.minimum(group_of(info, first + part * ROW), EXPERTS - 1), 1)
            at = pl.ds(part * ROW, ROW)
            here = normed[part * ROW : (part + 1) * ROW]
            h_out[at, :] = (here * gains[which, :] + shifts[which, :]).astype(BF16)


def middle_norm(info, x, att, weight, bias, gains, shifts):
    rows, width = x.shape
    spec = pl.BlockSpec((BLK, width), lambda i: (i, 0))
    return pl.pallas_call(
        middle_kernel,
        grid=(rows // BLK,),
        out_shape=[
            jax.ShapeDtypeStruct((rows, width), F32),
            jax.ShapeDtypeStruct((rows, width), BF16),
        ],
        in_specs=[
            SMEM_SPEC,
            spec,
            spec,
            held((width, width)),
            full(bias.shape),
            full(gains.shape),
            full(shifts.shape),
        ],
        out_specs=[spec, spec],
        compiler_params=pltpu.CompilerParams(vmem_limit_bytes=VMEM),
        cost_estimate=cost(10),
        name="middle_norm",
    )(info, x, att, weight, bias, gains, shifts)


def gelu_parts(up):
    size = jnp.abs(up) * (0.5**0.5)
    expo = jnp.exp(-size * size)
    t = 1.0 / (1.0 + 0.3275911 * size)
    poly = 1.061405429 * t - 1.453152027
    poly = poly * t + 1.421413741
    poly = poly * t - 0.284496736
    poly = poly * t + 0.254829592
    tail = 0.5 * (poly * t) * expo
    cdf = jnp.where(up >= 0, 1.0 - tail, tail)
    return (up * cdf, cdf + up * (expo * 0.3989422804014327))


def hidden_kernel(part, chunk, *refs):
    info, h, g, w_up, b_up, w_down = refs[:6]
    outs = refs[6:]
    if chunk:
        send_out, keep_out = outs[:2]
        outs = outs[2:]
    else:
        all_out = outs[0]
        outs = outs[1:]
    bias_out, act_hbm, dup_hbm, act, dup, up_acc, down_acc, sems = outs
    expert = pl.program_id(0)
    start = info[G_IMG + expert]
    count = info[G_IMG + expert + 1] - start
    blocks = count // BLK
    bias_out[...] = jnp.zeros_like(bias_out)
    up_acc[...] = jnp.zeros_like(up_acc)
    down_acc[...] = jnp.zeros_like(down_acc)

    def out_copies(index):
        at = pl.ds(pl.multiple_of(index * ROW, ROW), ROW)
        return (
            pltpu.make_async_copy(act.at[at, :], act_hbm.at[at, :], sems.at[0, index]),
            pltpu.make_async_copy(dup.at[at, :], dup_hbm.at[at, :], sems.at[1, index]),
        )

    def rows_of(local, size):
        row = start + local
        at = pl.ds(pl.multiple_of(row, ROW), size)
        left, grad = h[at, :], g[at, :]
        tile = w_up.shape[2]
        up = nn(left, w_up[0]) + b_up[pl.ds(expert, 1), pl.ds(part * tile, tile)]
        grad_act = nt(grad, w_down[0])
        active, slope = gelu_parts(up)
        active = active.astype(BF16)
        grad_up = (slope * grad_act).astype(BF16)
        act[at, :] = active
        dup[at, :] = grad_up
        bias_out[0] += jnp.sum(grad_up.astype(F32), axis=0, keepdims=True)
        up_acc[...] += tn(left, grad_up)
        down_acc[...] += tn(grad, active)
        for place in range(size // ROW):
            for copy in out_copies(row // ROW + place):
                copy.start()

    def block(index, carry):
        rows_of(index * BLK, BLK)
        return carry

    lax.fori_loop(0, blocks, block, 0)

    @pl.when(count % BLK > 0)
    def _():
        rows_of(blocks * BLK, ROW)

    for slot, acc in enumerate((up_acc, down_acc)):
        if chunk:
            mine = info[CORE]
            for pair in range(acc.shape[0] // (2 * chunk)):
                first = pair * 2 * chunk
                kept = pl.ds(pl.multiple_of(first + mine * chunk, 16), chunk)
                sent = pl.ds(pl.multiple_of(first + (1 - mine) * chunk, 16), chunk)
                keep_out[slot, 0, pair] = acc[kept, :].astype(BF16)
                send_out[slot, 0, pair] = acc[sent, :].astype(BF16)
        else:
            all_out[slot, 0] = acc[...].astype(BF16)

    @pl.when(expert == pl.num_programs(0) - 1)
    def _():
        def wait(index, carry):
            for copy in out_copies(index):
                copy.wait()
            return carry

        lax.fori_loop(0, info[G_PAD] // ROW, wait, 0)


def run_hidden(part, parts, info, h, g, w_up, b_up, w_down, chunk):
    rows, width = h.shape
    tile = w_up.shape[2] // parts
    any_spec = pl.BlockSpec(memory_space=pl.ANY)
    if chunk:
        pairs = width // (2 * chunk)
        weight_shapes = [jax.ShapeDtypeStruct((2, EXPERTS, pairs, chunk, tile), BF16)] * 2
        weight_specs = [pl.BlockSpec((2, 1, pairs, chunk, tile), lambda e: (0, e, 0, 0, 0))] * 2
    else:
        weight_shapes = [jax.ShapeDtypeStruct((2, EXPERTS, width, tile), BF16)]
        weight_specs = [pl.BlockSpec((2, 1, width, tile), lambda e: (0, e, 0, 0))]
    return pl.pallas_call(
        partial(hidden_kernel, part, chunk),
        grid=(EXPERTS,),
        out_shape=weight_shapes
        + [
            jax.ShapeDtypeStruct((EXPERTS, 1, tile), F32),
            jax.ShapeDtypeStruct((rows, tile), BF16),
            jax.ShapeDtypeStruct((rows, tile), BF16),
        ],
        in_specs=[
            SMEM_SPEC,
            held((rows, width)),
            held((rows, width)),
            pl.BlockSpec((1, width, tile), lambda e: (e, 0, part)),
            full(b_up.shape),
            pl.BlockSpec((1, tile, width), lambda e: (e, part, 0)),
        ],
        out_specs=weight_specs
        + [pl.BlockSpec((1, 1, tile), lambda e: (e, 0, 0)), any_spec, any_spec],
        scratch_shapes=[
            pltpu.VMEM((rows, tile), BF16),
            pltpu.VMEM((rows, tile), BF16),
            pltpu.VMEM((width, tile), F32),
            pltpu.VMEM((width, tile), F32),
            pltpu.SemaphoreType.DMA((2, rows // ROW)),
        ],
        compiler_params=pltpu.CompilerParams(vmem_limit_bytes=VMEM),
        cost_estimate=cost(22),
        name="hidden",
    )(info, h, g, w_up, b_up, w_down)


SUMS = 16


def finish_kernel(parts, *refs):
    info = refs[0]
    hbm = refs[1 : 3 + 2 * parts]
    up_hbm, down_hbm, gains, downs, w_attn = refs[3 + 2 * parts : 8 + 2 * parts]
    refs = refs[8 + 2 * parts :]
    sums_out, outs_hbm = refs[0], refs[1:5]
    rows_in, acts, dups = refs[5:7], refs[7 : 7 + parts], refs[7 + parts : 7 + 2 * parts]
    refs = refs[7 + 2 * parts :]
    held_out, (w_up, w_down, lower_s, hidden_s) = refs[:4], refs[4:8]
    row_sems, act_sems, out_sems, weight_sems = refs[8:]
    width = lower_s.shape[2]

    groups = range(EXPERTS + 1)
    counts = [info[G_IMG + group + 1] - info[G_IMG + group] for group in groups]
    firsts = [jnp.int32(0)]
    for group in groups:
        firsts.append(firsts[-1] + (counts[group] + BLK - 1) // BLK)
    total = firsts[-1]

    def block_of(index):
        group = sum([(index >= firsts[k]).astype(jnp.int32) for k in groups[1:]])
        first, start, count = firsts[0], info[G_IMG], counts[0]
        for k in groups[1:]:
            first = jnp.where(group == k, firsts[k], first)
            start = jnp.where(group == k, info[G_IMG + k], start)
            count = jnp.where(group == k, counts[k], count)
        local = (index - first) * BLK
        return group, start + local, count - local, index == first

    def halves(index, visit):
        group, row, left, _ = block_of(index)
        for half in range(BLK // ROW):

            @pl.when(half * ROW < left)
            def _(half=half):
                visit(half, pl.ds(pl.multiple_of(row + half * ROW, ROW), ROW), group < EXPERTS)

    def in_copies(index, half, at):
        here = pl.ds(half * ROW, ROW)
        rows = [
            pltpu.make_async_copy(
                source.at[at, :], target.at[index % 4, here, :], row_sems.at[index % 4, half, which]
            )
            for which, (source, target) in enumerate(zip(hbm[:2], rows_in))
        ]
        hidden = [
            pltpu.make_async_copy(
                source.at[at, :], target.at[index % 3, here, :], act_sems.at[index % 3, half, which]
            )
            for which, (source, target) in enumerate(zip(hbm[2:], acts + dups))
        ]
        return rows, hidden

    def fetch(index, action):
        def visit(half, at, real):
            rows, hidden = in_copies(index, half, at)
            for copy in rows:
                action(copy)

            @pl.when(real)
            def _():
                for copy in hidden:
                    action(copy)

        halves(index, visit)

    def send(index, action):
        def visit(half, at, real):
            here = pl.ds(half * ROW, ROW)
            for which, (source, target) in enumerate(zip(held_out, outs_hbm)):
                action(
                    pltpu.make_async_copy(
                        source.at[index % 2, here, :],
                        target.at[at, :],
                        out_sems.at[index % 2, half, which],
                    )
                )

        halves(index, visit)

    def start(copy):
        copy.start()

    def wait(copy):
        copy.wait()

    def weights(group, action):
        for which, (source, target) in enumerate(((up_hbm, w_up), (down_hbm, w_down))):
            action(
                pltpu.make_async_copy(
                    source.at[group], target.at[group], weight_sems.at[group, which]
                )
            )

    sums_out[...] = jnp.zeros_like(sums_out)

    @pl.when(total > 0)
    def _():
        fetch(0, start)

    weights(0, start)

    @pl.when(total > 1)
    def _():
        fetch(1, start)

    for expert in range(1, EXPERTS):
        weights(expert, start)

    tile = acts[0].shape[2]

    def block(index, waited):
        group, _, _, _ = block_of(index)
        mine = jnp.minimum(group, EXPERTS - 1)

        @pl.when(index + 2 < total)
        def _():
            fetch(index + 2, start)

        for expert in range(EXPERTS):

            @pl.when((waited <= expert) & (expert <= mine))
            def _(expert=expert):
                weights(expert, wait)

        @pl.when(index < total)
        def _():
            fetch(index, wait)

        @pl.when(index >= 3)
        def _():
            send(index - 3, wait)

        slot, old = index % 2, (index + 1) % 2
        behind = jnp.maximum(index - 1, 0)
        group, _, left, _ = block_of(behind)
        left = jnp.where(index > 0, left, 0)
        real = group < EXPERTS
        which = pl.ds(jnp.minimum(group, EXPERTS - 1), 1)
        mixed, dx, proj_out, datt = held_out
        sub = BLK // 4

        def row_part(turn):
            at = pl.ds(turn * sub, sub)
            valid = turn * sub + lax.broadcasted_iota(jnp.int32, (sub, 1), 0) < left
            middle = jnp.where(valid, rows_in[0][behind % 4, at, :], 0.0)
            grad = jnp.where(valid, rows_in[1][behind % 4, at, :].astype(F32), 0.0)
            lower = jnp.where(real, lower_s[old, at, :] + downs[which, :], 0.0)
            grad_hidden = jnp.where(valid & real, hidden_s[old, at, :], 0.0)
            mixed[old, at, :] = (middle + lower).astype(BF16)
            normed, inverse = normalize(middle)
            grad_middle = grad + norm_back(grad_hidden * gains[which, :], normed, inverse)
            dx[old, at, :] = grad_middle
            proj = grad_middle.astype(BF16)
            proj_out[old, at, :] = proj
            dsel = jnp.where(real, grad, 0.0)
            values = (proj.astype(F32), grad_hidden * normed, grad_hidden, dsel)
            return [jnp.sum(value, axis=0, keepdims=True) for value in values]

        taken = index % 3

        def compute(multiply):
            lower_new = jnp.zeros((BLK, width), F32)
            hidden_new = jnp.zeros((BLK, width), F32)
            sums, turn = [0.0] * 4, 0
            for part in range(parts):
                cols = pl.ds(part * tile, tile)
                if multiply:
                    lower_new += nn(acts[part][taken], w_down[mine, cols, :])
                if turn < 4:
                    sums = [x + y for x, y in zip(sums, row_part(turn))]
                    turn += 1
                if multiply:
                    hidden_new += nt(dups[part][taken], w_up[mine, :, cols])
                if turn < 4:
                    sums = [x + y for x, y in zip(sums, row_part(turn))]
                    turn += 1
            while turn < 4:
                sums = [x + y for x, y in zip(sums, row_part(turn))]
                turn += 1
            if multiply:
                lower_s[slot] = lower_new
                hidden_s[slot] = hidden_new
            datt[old] = nt(proj_out[old], w_attn[...]).astype(BF16)
            sums_out[pl.ds(0, 1), :] += sums[0]
            for place, value in enumerate(sums[1:]):
                at = pl.ds(1 + place * EXPERTS + jnp.minimum(group, EXPERTS - 1), 1)
                sums_out[at, :] += value

        @pl.when(index < total)
        def _():
            compute(True)

        @pl.when(index == total)
        def _():
            compute(False)
        @pl.when(index > 0)
        def _():
            send(index - 1, start)

        return jnp.maximum(waited, mine + 1)

    waited = lax.fori_loop(0, jnp.where(total > 0, total + 1, 0), block, jnp.int32(0))
    for expert in range(EXPERTS):

        @pl.when(waited <= expert)
        def _(expert=expert):
            weights(expert, wait)

    for back in (2, 1):

        @pl.when(total >= back)
        def _(back=back):
            send(total - back, wait)


def finish_experts(info, mid, g, acts, dups, w_up, w_down, gains, downs, w_attn):
    rows, width = mid.shape
    parts = len(acts)
    tile = acts[0].shape[1]
    any_spec = pl.BlockSpec(memory_space=pl.ANY)
    vmem = pl.BlockSpec(memory_space=pltpu.VMEM)
    kinds = (BF16, F32, BF16, BF16)
    return pl.pallas_call(
        partial(finish_kernel, parts),
        out_shape=[jax.ShapeDtypeStruct((SUMS, width), F32)]
        + [jax.ShapeDtypeStruct((rows, width), kind) for kind in kinds],
        in_specs=[SMEM_SPEC] + [any_spec] * (4 + 2 * parts) + [vmem] * 3,
        out_specs=[vmem] + [any_spec] * 4,
        scratch_shapes=[pltpu.VMEM((4, BLK, width), F32), pltpu.VMEM((4, BLK, width), BF16)]
        + [pltpu.VMEM((3, BLK, tile), BF16)] * (2 * parts)
        + [pltpu.VMEM((2, BLK, width), kind) for kind in kinds]
        + [pltpu.VMEM(w_up.shape, BF16), pltpu.VMEM(w_down.shape, BF16)]
        + [pltpu.VMEM((2, BLK, width), F32)] * 2
        + [
            pltpu.SemaphoreType.DMA((4, BLK // ROW, 2)),
            pltpu.SemaphoreType.DMA((3, BLK // ROW, 2 * parts)),
            pltpu.SemaphoreType.DMA((2, BLK // ROW, 4)),
            pltpu.SemaphoreType.DMA((EXPERTS, 2)),
        ],
        compiler_params=pltpu.CompilerParams(vmem_limit_bytes=VMEM),
        cost_estimate=cost(30),
        name="finish_experts",
    )(info, mid, g, *acts, *dups, w_up, w_down, gains, downs, w_attn)


def weights_kernel(dp, seq, info, dq, dk, dv, proj, h, att, send_out, keep_out, acc, attn_acc):
    index = pl.program_id(0)

    @pl.when(index == 0)
    def _():
        acc[...] = jnp.zeros_like(acc)
        attn_acc[...] = jnp.zeros_like(attn_acc)

    @pl.when(index * BLK < info[G_END])
    def _():
        row = index * BLK + lax.broadcasted_iota(jnp.int32, (BLK, 1), 0)
        real = row < info[G_END]
        hidden = h[...]
        width = hidden.shape[1]
        for part, grad in enumerate((dq, dk, dv)):
            acc[pl.ds(part * width, width), :] += tn(grad[...], hidden)
        attn_acc[...] += tn(
            jnp.where(real, proj[...], jnp.zeros_like(proj)),
            jnp.where(real, att[...], jnp.zeros_like(att)),
        )

    @pl.when(index == pl.num_programs(0) - 1)
    def _():
        width = attn_acc.shape[0]
        own = width // (dp * seq)
        half = width // 2
        for out, core in ((keep_out, info[CORE]), (send_out, 1 - info[CORE])):
            for pair in range(dp // 2):
                for place in range(seq):
                    device = (2 * pair + core) * seq + place
                    first = pl.ds(pl.multiple_of(device * 3 * own, 8), 3 * own)
                    second = pl.ds(pl.multiple_of(device * own, 8), own)
                    value = jnp.concatenate([acc[first, :], attn_acc[second, :]], axis=0)
                    value = value.astype(BF16)
                    at = pl.ds(place * 4 * own, 4 * own)
                    for lane in range(2):
                        out[lane, 0, pair, at, :] = value[:, lane * half : (lane + 1) * half]


def weights_kernel_plain(info, dq, dk, dv, proj, h, att, qkv_out, attn_out, acc, attn_acc):
    index = pl.program_id(0)

    @pl.when(index == 0)
    def _():
        acc[...] = jnp.zeros_like(acc)
        attn_acc[...] = jnp.zeros_like(attn_acc)

    @pl.when(index * BLK < info[G_END])
    def _():
        row = index * BLK + lax.broadcasted_iota(jnp.int32, (BLK, 1), 0)
        real = row < info[G_END]
        hidden = h[...]
        width = hidden.shape[1]
        for part, grad in enumerate((dq, dk, dv)):
            acc[pl.ds(part * width, width), :] += tn(grad[...], hidden)
        attn_acc[...] += tn(
            jnp.where(real, proj[...], jnp.zeros_like(proj)),
            jnp.where(real, att[...], jnp.zeros_like(att)),
        )

    @pl.when(index == pl.num_programs(0) - 1)
    def _():
        qkv_out[...] = acc[...].astype(BF16)
        attn_out[...] = attn_acc[...].astype(BF16)


def projection_grads(info, dq, dk, dv, proj, h, att, dp, seq):
    rows, width = h.shape
    spec = pl.BlockSpec((BLK, width), lambda i: (i, 0))
    own = width // (dp * seq)
    direct = own % 8 == 0
    if direct:
        shapes = [(2, 1, dp // 2, seq * 4 * own, width // 2)] * 2
        body = partial(weights_kernel, dp, seq)
    else:
        shapes = [(3 * width, width), (width, width)]
        body = weights_kernel_plain
    results = pl.pallas_call(
        body,
        grid=(rows // BLK,),
        out_shape=[jax.ShapeDtypeStruct(shape, BF16) for shape in shapes],
        in_specs=[SMEM_SPEC] + [spec] * 6,
        out_specs=[full(shape) for shape in shapes],
        scratch_shapes=[pltpu.VMEM((3 * width, width), F32), pltpu.VMEM((width, width), F32)],
        compiler_params=pltpu.CompilerParams(vmem_limit_bytes=VMEM),
        cost_estimate=cost(15),
        name="projection_grads",
    )(info, dq, dk, dv, proj, h, att)
    if direct:
        return results[1], results[0]
    d_qkv = results[0].reshape(dp * seq, -1, width)
    d_attn = results[1].reshape(dp * seq, -1, width)
    d_all = jnp.concatenate([d_qkv, d_attn], axis=1).reshape(1, -1, width)
    half = width // 2
    return core_split(jnp.stack([d_all[..., :half], d_all[..., half:]]))


VECTORS = 24


def last_kernel(parts, *refs):
    (info, x, dx, dq, dk, dv, gain, weight, row_sums) = refs[:9]
    biases = refs[9 : 9 + parts]
    out, packed = refs[9 + parts :]
    width = x.shape[1]
    step = pl.program_id(0)

    @pl.when(step == 0)
    def _():
        packed[...] = jnp.zeros_like(packed)
        packed[pl.ds(4, 10), pl.ds(0, width)] = row_sums[pl.ds(0, 10), :]
        for part, bias in enumerate(biases):
            tile = bias.shape[2]
            for expert in range(EXPERTS):
                packed[pl.ds(14 + part * EXPERTS + expert, 1), pl.ds(0, tile)] = bias[expert]

    @pl.when(step * BLK < info[G_END])
    def _():
        hidden = nt(dq[...], weight[:, pl.ds(0, width)])
        hidden += nt(dk[...], weight[:, pl.ds(width, width)])
        hidden += nt(dv[...], weight[:, pl.ds(2 * width, width)])
        normed, inverse = normalize(x[...].astype(F32))
        totals = (hidden * normed, hidden, dq[...].astype(F32), dv[...].astype(F32))
        for place, value in enumerate(totals):
            packed[pl.ds(place, 1), pl.ds(0, width)] += jnp.sum(value, axis=0, keepdims=True)
        out[...] = dx[...] + norm_back(hidden * gain[...], normed, inverse)


def last_norm(info, x, dx, dq, dk, dv, gain, weight, row_sums, biases):
    rows, width = x.shape
    spec = pl.BlockSpec((BLK, width), lambda i: (i, 0))
    cols = max(width, biases[0].shape[2])
    packed = (VECTORS, cols)
    return pl.pallas_call(
        partial(last_kernel, len(biases)),
        grid=(rows // BLK,),
        out_shape=[jax.ShapeDtypeStruct((rows, width), F32), jax.ShapeDtypeStruct(packed, F32)],
        in_specs=[SMEM_SPEC, spec, spec, spec, spec, spec, full(gain.shape), held((width, 3 * width))]
        + [full(row_sums.shape)]
        + [full(bias.shape) for bias in biases],
        out_specs=[spec, full(packed)],
        compiler_params=pltpu.CompilerParams(vmem_limit_bytes=VMEM),
        cost_estimate=cost(14),
        name="last_norm",
    )(info, x, dx, dq, dk, dv, gain, weight, row_sums, *biases)


def swap(value, bit):
    ways = lax.axis_size("dp")
    return lax.ppermute(value, "dp", [(i, i ^ (1 << bit)) for i in range(ways)])


def half_of(parts, axis, bit, mine):
    own = (lax.axis_index("dp") >> bit) & 1
    which = own if mine else 1 - own
    return [lax.dynamic_index_in_dim(part, which, axis, keepdims=False) for part in parts]


DEPTH = 4


def combine_kernel(blocks, arrays, seq, ways, *refs):
    place, sources = refs[0], refs[1 : 1 + arrays]
    in_buf, out_buf, own_buf, send_buf, total, in_sems, out_sems = refs[-7:]
    outs = refs[1 + arrays : -7]
    ends = outs[len(outs) - ways :]
    here = lax.rem(place[0], ways)

    def fetch(index):
        return [
            pltpu.make_async_copy(
                sources[which].at[where(place)],
                in_buf.at[index % DEPTH, part],
                in_sems.at[index % DEPTH, part],
            )
            for part, (which, where) in enumerate(blocks[index][0])
        ]

    def send(index):
        _, target, at = blocks[index]
        slot = index % 2
        if target != "ends":
            return [pltpu.make_async_copy(out_buf.at[slot], outs[target].at[at], out_sems.at[slot, 0])]
        copies = [pltpu.make_async_copy(own_buf.at[slot], ends[0].at[at], out_sems.at[slot, 0])]
        for hop in range(ways - 1):
            copies.append(
                pltpu.make_async_copy(
                    send_buf.at[slot, hop], ends[1 + hop].at[at], out_sems.at[slot, 1 + hop]
                )
            )
        return copies

    for index in range(min(DEPTH - 1, len(blocks))):
        for copy in fetch(index):
            copy.start()
    for index, (parts, target, _) in enumerate(blocks):
        if index + DEPTH - 1 < len(blocks):
            for copy in fetch(index + DEPTH - 1):
                copy.start()
        for copy in fetch(index):
            copy.wait()
        if index >= 2:
            for copy in send(index - 2):
                copy.wait()
        value = in_buf[index % DEPTH, 0].astype(F32)
        for part in range(1, len(parts)):
            value = value + in_buf[index % DEPTH, part].astype(F32)
        slot = index % 2
        if target != "ends":
            out_buf[slot] = value.astype(BF16)
        else:
            total[...] = value
            rows = total.shape[1] // seq
            for hop in range(ways):
                for turn in range(seq // ways):
                    at = lax.rem(here + hop, ways) + turn * ways
                    block = total[:, pl.ds(pl.multiple_of(at * rows, 8), rows), :]
                    to = pl.ds(turn * rows, rows)
                    if hop == 0:
                        own_buf[slot, :, to, :] = block
                    else:
                        send_buf[slot, hop - 1, :, to, :] = block.astype(BF16)
        for copy in send(index):
            copy.start()
    for index in range(max(0, len(blocks) - 2), len(blocks)):
        for copy in send(index):
            copy.wait()


class Flight:

    def __init__(self):
        self.cells = []

    def start(self, value):
        cell = [value]
        self.cells.append(cell)
        return cell

    def land(self, *outputs, later=()):
        now = [cell for cell in self.cells if not any(cell is other for other in later)]
        outputs, arrays = lax.optimization_barrier((outputs, [cell[0] for cell in now]))
        for cell, array in zip(now, arrays):
            cell[0] = array
        self.cells = [cell for cell in self.cells if any(cell is other for other in later)]
        return outputs


class Sum:

    def __init__(self, flight, kept, sent):
        self.flight = flight
        self.bits = lax.axis_size("dp").bit_length() - 1
        self.seq = lax.axis_size("seq")
        self.many, self.pairs, self.chunk, self.cols = kept.shape[1:]
        every = list(range(self.bits - 1, 0, -1))
        shape = (2, self.many) + (2,) * len(every) + (self.chunk, self.cols)
        cells = [[kept.reshape(shape)], flight.start(swap(sent, 0).reshape(shape))]
        self.lanes = [[(cell, lane, every, True) for cell in cells] for lane in range(2)]
        self.left = [list(every), list(every)]
        self.ways = self.seq
        self.own = None
        self.seq_left = None

    def more(self):
        return bool(self.left[0])

    def direct(self):
        return (self.chunk // self.seq) % 8 == 0

    def sources(self, lane, other, free, value):
        results = []
        for cell, first, bits, whole in self.lanes[lane]:

            def where(place, first=first, bits=bits, whole=whole):
                chosen = []
                for bit in bits:
                    if bit in free:
                        chosen.append((value >> (len(free) - 1 - free.index(bit))) & 1)
                    elif bit == other:
                        chosen.append(1 - place[1 + bit])
                    else:
                        chosen.append(place[1 + bit])
                if whole:
                    return (first, slice(None)) + tuple(chosen)
                group = 0
                for one in chosen:
                    group = group * 2 + one
                return (first + group,)

            results.append((cell[0], where))
        return results


def advance(place, steps, closing=None):
    arrays, blocks, payloads, turns = [], [], {}, []
    model = steps[0] if steps else closing

    def add(parts, target, at):
        known = []
        for array, where in parts:
            found = [i for i, other in enumerate(arrays) if other is array]
            if not found:
                arrays.append(array)
            known.append((found[0] if found else len(arrays) - 1, where))
        blocks.append((known, target, at))

    for total in steps:
        for lane in range(2):
            left = total.left[lane]
            bit = min(left) if lane == 0 else max(left)
            left.remove(bit)
            free = list(left)
            count = payloads.get(bit, 0)
            turns.append((total, lane, bit, free, count))
            for value in range(2 ** len(free)):
                add(total.sources(lane, bit, free, value), bit, count)
                count += 1
            payloads[bit] = count
    order = sorted(payloads)
    seq, many, chunk, cols = model.seq, model.many, model.chunk, model.cols
    shapes = [jax.ShapeDtypeStruct((payloads[bit], many, chunk, cols), BF16) for bit in order]
    split = closing is not None and closing.direct()
    ways = closing.ways if split else 2
    rows = chunk // (ways if split else seq)
    if closing is not None:
        target = "ends" if split else len(order)
        for lane in range(2):
            add(closing.sources(lane, None, [], 0), target, lane)
        if split:
            shapes.append(jax.ShapeDtypeStruct((2, many, rows, cols), F32))
            shapes += [jax.ShapeDtypeStruct((2, many, rows, cols), BF16)] * (ways - 1)
        else:
            shapes.append(jax.ShapeDtypeStruct((2, many, chunk, cols), BF16))
    blocks = [
        (parts, order.index(target) if target in order else target, at)
        for parts, target, at in blocks
    ]
    most = max(len(parts) for parts, _, _ in blocks)
    end_rows = rows if split else 8
    any_spec = pl.BlockSpec(memory_space=pl.ANY)
    results = pl.pallas_call(
        partial(combine_kernel, blocks, len(arrays), seq, ways),
        in_specs=[SMEM_SPEC] + [any_spec] * len(arrays),
        out_specs=[any_spec] * len(shapes),
        out_shape=shapes,
        scratch_shapes=[
            pltpu.VMEM((DEPTH, most, many, chunk, cols), BF16),
            pltpu.VMEM((2, many, chunk, cols), BF16),
            pltpu.VMEM((2, many, end_rows, cols), F32),
            pltpu.VMEM((2, ways - 1, many, end_rows, cols), BF16),
            pltpu.VMEM((many, chunk, cols), F32),
            pltpu.SemaphoreType.DMA((DEPTH, most)),
            pltpu.SemaphoreType.DMA((2, ways)),
        ],
        compiler_params=pltpu.CompilerParams(vmem_limit_bytes=VMEM),
        cost_estimate=cost(4),
        name="combine",
    )(place, *arrays)

    def go(results):
        got = {bit: model.flight.start(swap(value, bit)) for bit, value in zip(order, results)}
        for total, lane, bit, free, first in turns:
            total.lanes[lane].append((got[bit], first, free, False))
        if closing is not None:
            parts = results[len(order) :]
            if not split:
                half = parts[0].reshape(2, many, seq, chunk // seq, cols)
                here = lax.axis_index("seq")
                parts = [
                    lax.dynamic_index_in_dim(half, (here + hop) % seq, 2, keepdims=False)
                    for hop in range(seq)
                ]
            closing.own = parts[0].astype(F32)
            if split and ways < seq:
                pairs = [(i, i ^ 1) for i in range(seq)]
                closing.got = [closing.flight.start(lax.ppermute(parts[1], "seq", pairs))]
                closing.seq_left = list(range(1, seq.bit_length() - 1))
                return
            closing.got = []
            for hop, send in enumerate(parts[1:]):
                pairs = [(i, (i + hop + 1) % seq) for i in range(seq)]
                closing.got.append(closing.flight.start(lax.ppermute(send, "seq", pairs)))

    return list(results), go


def advance_seq(total):
    bit = total.seq_left.pop(0)
    two, many, rows, cols = total.own.shape
    value = (total.own + total.got[0][0].astype(F32)).reshape(two, many, 2, rows // 2, cols)
    mine = (lax.axis_index("seq") >> bit) & 1
    send = lax.dynamic_index_in_dim(value, 1 - mine, 2, keepdims=False).astype(BF16)
    total.own = lax.dynamic_index_in_dim(value, mine, 2, keepdims=False)
    pairs = [(i, i ^ (1 << bit)) for i in range(total.seq)]

    def go(send):
        total.got = [total.flight.start(lax.ppermute(send, "seq", pairs))]

    return send, go


def finish_sum(total):
    value = total.own
    for got in total.got:
        value = value + got[0].astype(F32)
    return value.reshape(2, total.many, -1, total.cols)


def vector_hops():
    seq = lax.axis_size("seq")
    hops = []
    for bit in range(seq.bit_length() - 1):
        pairs = [(i, i ^ (1 << bit)) for i in range(seq)]
        hops.append(partial(lax.ppermute, axis_name="seq", perm=pairs))
    return hops + [partial(swap, bit=bit) for bit in range(lax.axis_size("dp").bit_length() - 1)]


def exchange(x, d, rows):
    seq = lax.axis_size("seq")
    first = jnp.concatenate([x[:rows], d[:rows]], axis=1)
    last = jnp.concatenate([x[-rows:], d[-rows:]], axis=1)
    from_left = lax.ppermute(last, "seq", [(i, i + 1) for i in range(seq - 1)])
    from_right = lax.ppermute(first, "seq", [(i + 1, i) for i in range(seq - 1)])
    return (from_left, from_right)


def core_split(value):
    pairs = lax.axis_size("dp") // 2
    two, many, depth, cols = value.shape
    shaped = value.reshape(two, many, pairs, 2, depth // (2 * pairs), cols)
    kept = half_of([shaped], 3, 0, True)[0]
    sent = half_of([shaped], 3, 0, False)[0]
    return (kept, sent)


PARTS = 3


def per_device(
    tokens, item_types, first_gain, first_shift, qkv_weight, query_bias, value_bias, attn_weight,
    attn_bias, second_gain, second_shift, expert_up, up_bias, expert_down, down_bias, cotangent,
):
    tok, width = tokens.shape
    dp, seq = lax.axis_size("dp"), lax.axis_size("seq")
    rows = capacity(tok)
    chunk = width // dp
    chunk = chunk if chunk % 16 == 0 else 0
    bits = [(lax.axis_index("dp") >> bit) & 1 for bit in range(dp.bit_length() - 1)]
    place = jnp.stack([lax.axis_index("seq")] + bits).astype(jnp.int32)
    left, right = exchange(tokens, cotangent, HALO)
    x, g, info = sort_rows(place, item_types, left, tokens, cotangent, right, rows, tok * seq)

    h, qkv = project_qkv(info, x, first_gain, first_shift, qkv_weight, query_bias, value_bias)
    att = attend(info, qkv)
    mid, h2 = middle_norm(info, x, att, attn_weight, attn_bias, second_gain, second_shift)

    flight = Flight()

    def window(sums):
        late = [total for total in sums if total.seq_left]
        steps = [total for total in sums if total.more()]
        closing = [total for total in sums if not total.more() and total.own is None]
        sends, actions = [], []
        if steps or closing:
            ready, go = advance(place, steps, closing[0] if closing else None)
            sends.append(ready)
            actions.append(go)
        for total in late:
            ready, go = advance_seq(total)
            sends.append(ready)
            actions.append(go)
        gate, sends = lax.optimization_barrier((info, sends))
        for go, ready in zip(actions, sends):
            go(ready)
        return gate

    sums, up_biases, acts, dups = [], [], [], []
    gate = info
    for part in range(PARTS):
        results = run_hidden(part, PARTS, gate, h2, g, expert_up, up_bias, expert_down, chunk)
        results = flight.land(*results)
        bias, act, dup = results[-3:]
        up_biases.append(bias)
        acts.append(act)
        dups.append(dup)
        if chunk:
            sent, kept = results[0], results[1]
        else:
            kept, sent = core_split(results[0])
        new = Sum(flight, kept, sent)
        new.ways = 2
        gate = window(sums)
        sums.append(new)
    results = finish_experts(
        gate, mid, g, acts, dups, expert_up, expert_down, second_gain, down_bias, attn_weight
    )
    row_sums, mixed, dx, proj, datt = flight.land(*results)
    gate = window(sums)
    dq, dk, dv = flight.land(*attend_back(gate, qkv, datt))
    gate = window(sums)
    kept, sent = flight.land(*projection_grads(gate, dq, dk, dv, proj, h, att, dp, seq))
    last = Sum(flight, kept, sent)
    gate = window(sums)
    results = last_norm(gate, x, dx, dq, dk, dv, first_gain, qkv_weight, row_sums, up_biases)
    grad_x, packed = flight.land(*results)

    hops = vector_hops()

    def hop(packed, moved=None):
        packed = packed if moved is None else packed + moved[0]
        return packed, flight.start(hops.pop(0)(packed))

    packed, moved = hop(packed)
    while any(total.own is None or total.seq_left for total in sums):
        window(sums)
    gate = window([last])
    m_own, g_own, left, right = flight.land(*unsort_rows(gate, mixed, grad_x, tok))
    expert_sums = [finish_sum(total) for total in sums]
    packed, moved = hop(packed, moved)
    from_right = flight.start(lax.ppermute(left, "seq", [(i + 1, i) for i in range(seq - 1)]))
    from_left = flight.start(lax.ppermute(right, "seq", [(i, i + 1) for i in range(seq - 1)]))
    while last.own is None:
        window([last])
        if last.own is None:
            expert_sums = flight.land(*expert_sums)

    def merge(own, at):
        cols = slice(at, at + width)
        own = own.at[:HALO].add(from_left[0][:, cols].astype(own.dtype))
        return own.at[tok - HALO :].add(from_right[0][:, cols].astype(own.dtype))

    mixed_out, grad_out = merge(m_own, width), merge(g_own, 0)
    while hops:
        packed, moved = hop(packed, moved)
    packed = packed + moved[0]
    last_sums = finish_sum(last)

    own = width // (dp * seq)
    rank = lax.axis_index("dp") * seq + lax.axis_index("seq")
    vectors = lax.dynamic_slice(packed, (0, rank * own), (14, own))
    tile = up_biases[0].shape[2]
    up_total = packed[14 : 14 + PARTS * EXPERTS, :tile].reshape(PARTS, EXPERTS, tile)
    sum_up = jnp.concatenate([total[0] for total in expert_sums], axis=-1)
    sum_down = jnp.concatenate([total[1] for total in expert_sums], axis=-1).swapaxes(1, 2)
    last_sums = jnp.concatenate([last_sums[0, 0], last_sums[1, 0]], axis=1).T

    return (
        mixed_out,
        grad_out,
        vectors[0],
        vectors[1],
        last_sums[:, : 3 * own],
        vectors[2],
        vectors[3],
        last_sums[:, 3 * own :],
        vectors[4],
        vectors[5:8],
        vectors[8:11],
        sum_up,
        up_total.swapaxes(0, 1).reshape(EXPERTS, -1),
        sum_down,
        vectors[11:14],
    )


def solution(mesh):
    split = P(("dp", "seq"))
    in_specs = (P(("dp", "seq"), None), P("dp", None)) + (P(),) * 13 + (P(("dp", "seq"), None),)
    out_specs = (
        P(("dp", "seq"), None),
        P(("dp", "seq"), None),
        split,
        split,
        P(None, ("dp", "seq")),
        split,
        split,
        P(None, ("dp", "seq")),
        split,
        P(None, ("dp", "seq")),
        P(None, ("dp", "seq")),
        P(None, ("dp", "seq"), None),
        P(),
        P(None, None, ("dp", "seq")),
        P(None, ("dp", "seq")),
    )
    return jax.shard_map(
        per_device, mesh=mesh, in_specs=in_specs, out_specs=out_specs, check_vma=False
    )
```

```python
from functools import partial

import jax
import jax.numpy as jnp
from jax import lax
from jax.experimental import pallas as pl
from jax.experimental.pallas import tpu as pltpu
from jax.sharding import PartitionSpec as P

HD = 64
EXPERTS = 3
IMG_LEN = 197
TXT_LEN = 64
LENS = (IMG_LEN, TXT_LEN, IMG_LEN + TXT_LEN)
SLOTS = (208, 64, 272)
TXT_PAIR = 128
PAD_ROWS = 384
HALO = 144
ROW = 128
BLK = 256

EPS = 1e-05
NEG = -1e30
VMEM = 60 << 20
F32 = jnp.float32
BF16 = jnp.bfloat16

N_IMG, N_TXT, N_BOTH, N_PAD = 0, 1, 2, 3
G_IMG, G_TXT, G_BOTH, G_PAD, G_END = 4, 5, 6, 7, 8
PAD_LEN, OWN_N, CORE = 9, 10, 11
TABLE = 16
INFO = 256


def nn(a, b):
    return lax.dot_general(a, b, (((1,), (0,)), ((), ())), preferred_element_type=F32)


def nt(a, b):
    return lax.dot_general(a, b, (((1,), (1,)), ((), ())), preferred_element_type=F32)


def tn(a, b):
    return lax.dot_general(a, b, (((0,), (0,)), ((), ())), preferred_element_type=F32)


def cost(microseconds):
    return pl.CostEstimate(flops=int(microseconds * 1e10), bytes_accessed=0, transcendentals=0)


SMEM_SPEC = pl.BlockSpec(memory_space=pltpu.SMEM)


def up_to(value, unit):
    return ((value + unit - 1) // unit) * unit


def normalize(v):
    mean = jnp.mean(v, axis=-1, keepdims=True)
    cent = v - mean
    var = jnp.mean(cent * cent, axis=-1, keepdims=True)
    inverse = lax.rsqrt(var + EPS)
    return (cent * inverse, inverse)


def norm_back(grad, normed, inverse):
    inner = jnp.mean(grad * normed, axis=-1, keepdims=True)
    return inverse * (grad - jnp.mean(grad, axis=-1, keepdims=True) - normed * inner)


def capacity(tok):
    rows = tok + LENS[2] - 1
    best = 0
    for images in range(rows // LENS[0] + 1):
        for both in range((rows - images * LENS[0]) // LENS[2] + 1):
            left = rows - images * LENS[0] - both * LENS[2]
            for pad in (0, 1):
                spare = left - pad * (1 + LENS[2] // 2)
                if spare < 0:
                    continue
                texts = spare // LENS[1]
                for count in range(texts + 1):
                    total = (
                        up_to(images * SLOTS[0], ROW)
                        + up_to(count * SLOTS[1], ROW)
                        + up_to(both * SLOTS[2], ROW)
                        + pad * PAD_ROWS
                    )
                    best = max(best, total)
    return up_to(best, BLK)


def gather_rows(info, wins, outs):
    for out in outs:
        out[...] = jnp.zeros_like(out)

    def place(index, carry):
        source = info[TABLE + 3 * index]
        target = pl.multiple_of(info[TABLE + 3 * index + 1], 16)
        kind = info[TABLE + 3 * index + 2]
        begin = pl.multiple_of((source // 16) * 16, 16)
        shift = source - begin
        for which in range(EXPERTS):
            slot = SLOTS[which]
            fits = (kind == which) if which < 2 else (kind >= 2)
            size = LENS[which] if which < 2 else jnp.where(kind == 2, LENS[2], info[PAD_LEN])

            @pl.when(fits)
            def _(slot=slot, size=size):
                rows = lax.broadcasted_iota(jnp.int32, (slot, slot + 16), 0)
                cols = lax.broadcasted_iota(jnp.int32, (slot, slot + 16), 1)
                chosen = ((cols == rows + shift) & (rows < size)).astype(F32).astype(BF16)
                for win, out in zip(wins, outs):
                    value = nn(chosen, win[pl.ds(begin, slot + 16), :])
                    out[pl.ds(target, slot), :] = value.astype(BF16)

        return carry

    lax.fori_loop(0, info[OWN_N], place, 0)


def sort_kernel(tok, group, place_ref, types, x_own, d_own, x_out, d_out, info, x_win, d_win):
    items = types.shape[1]
    low = place_ref[0] * tok
    info[CORE] = place_ref[1]
    width = x_own.shape[1]
    for win, own_rows in ((x_win, x_own), (d_win, d_own)):
        rest = win.shape[0] - (HALO + tok)
        win[pl.ds(0, HALO), :] = jnp.zeros((HALO, width), BF16)
        win[pl.ds(HALO, tok), :] = own_rows[...]
        win[pl.ds(HALO + tok, rest), :] = jnp.zeros((rest, width), BF16)

    def length(kind):
        return jnp.where(
            kind == 0, LENS[0], jnp.where(kind == 1, LENS[1], jnp.where(kind == 2, LENS[2], 0))
        )

    def owned(start, size):
        middle = (start + start + size) // 2
        return (middle >= low) & (middle < low + tok) & (size > 0)

    def count(index, carry):
        start, images, texts, boths = carry
        kind = types[0, index]
        size = length(kind)
        mine = owned(start, size)
        return (
            start + size,
            images + jnp.where(mine & (kind == 0), 1, 0),
            texts + jnp.where(mine & (kind == 1), 1, 0),
            boths + jnp.where(mine & (kind == 2), 1, 0),
        )

    zero = jnp.int32(0)
    total, images, texts, boths = lax.fori_loop(0, items, count, (zero, zero, zero, zero))
    pad_len = group - total
    pad = owned(total, pad_len)
    g_txt = up_to(images * SLOTS[0], ROW)
    g_both = g_txt + up_to(texts * SLOTS[1], ROW)
    g_pad = g_both + up_to(boths * SLOTS[2], ROW)
    info[N_IMG] = images
    info[N_TXT] = texts
    info[N_BOTH] = boths
    info[N_PAD] = jnp.where(pad, 1, 0)
    info[G_IMG] = zero
    info[G_TXT] = g_txt
    info[G_BOTH] = g_both
    info[G_PAD] = g_pad
    info[G_END] = g_pad + jnp.where(pad, PAD_ROWS, 0)
    info[PAD_LEN] = pad_len

    def note(own, source, target, kind):
        info[TABLE + 3 * own] = source
        info[TABLE + 3 * own + 1] = target
        info[TABLE + 3 * own + 2] = kind

    def place(index, carry):
        start, images, texts, boths, own = carry
        kind = types[0, index]
        size = length(kind)
        mine = owned(start, size)

        @pl.when(mine)
        def _():
            target = jnp.where(
                kind == 0,
                images * SLOTS[0],
                jnp.where(kind == 1, g_txt + texts * SLOTS[1], g_both + boths * SLOTS[2]),
            )
            note(own, start - low + HALO, target, kind)

        return (
            start + size,
            images + jnp.where(mine & (kind == 0), 1, 0),
            texts + jnp.where(mine & (kind == 1), 1, 0),
            boths + jnp.where(mine & (kind == 2), 1, 0),
            own + jnp.where(mine, 1, 0),
        )

    own = lax.fori_loop(0, items, place, (zero, zero, zero, zero, zero))[-1]

    @pl.when(pad)
    def _():
        note(own, total - low + HALO, g_pad, jnp.int32(EXPERTS))

    info[OWN_N] = own + jnp.where(pad, 1, 0)
    gather_rows(info, (x_win, d_win), (x_out, d_out))


def sort_rows(place, types, x, d, rows, group):
    tok, width = x.shape
    vmem = pl.BlockSpec(memory_space=pltpu.VMEM)
    return pl.pallas_call(
        partial(sort_kernel, tok, group),
        out_shape=[
            jax.ShapeDtypeStruct((rows, width), BF16),
            jax.ShapeDtypeStruct((rows, width), BF16),
            jax.ShapeDtypeStruct((INFO,), jnp.int32),
        ],
        in_specs=[SMEM_SPEC, SMEM_SPEC] + [vmem] * 2,
        out_specs=[vmem, vmem, SMEM_SPEC],
        scratch_shapes=[pltpu.VMEM((tok + HALO + 288, width), BF16)] * 2,
        compiler_params=pltpu.CompilerParams(vmem_limit_bytes=VMEM),
        cost_estimate=cost(11),
        name="sort_rows",
    )(place, types, x, d)


def patch_kernel(tok, info, left, right, x_in, d_in, x_out, d_out, held, sems):
    width = x_in.shape[1]
    count = info[OWN_N]

    def over_end(index, end):
        source = info[TABLE + 3 * index]
        kind = info[TABLE + 3 * index + 2]
        size = jnp.where(kind == 0, LENS[0], jnp.where(kind == 1, LENS[1], LENS[2]))
        size = jnp.where(kind == EXPERTS, info[PAD_LEN], size)
        over = (source + size > HALO + tok) if end else (source < HALO)
        return over & (count > 0), source, size, kind

    def for_slots(end, visit):
        index = jnp.maximum(count - 1, 0) if end else 0
        over, source, size, kind = over_end(index, end)
        target = pl.multiple_of(info[TABLE + 3 * index + 1], 16)
        for which in range(EXPERTS):
            slot = SLOTS[which]
            fits = (kind == which) if which < 2 else (kind >= 2)

            @pl.when(over & fits)
            def _(slot=slot):
                visit(end, slot, pl.ds(target, slot), source, size)

    def copies(end, slot, at, inward):
        here = pl.ds(0, slot)
        pairs = []
        for one, out in enumerate((x_out, d_out)):
            near, far = held.at[end, one, here, :], out.at[at, :]
            source, to = (far, near) if inward else (near, far)
            pairs.append(pltpu.make_async_copy(source, to, sems.at[end, one]))
        return pairs

    def fetch(end, slot, at, source, size):
        for copy in copies(end, slot, at, True):
            copy.start()

    def add(end, slot, at, source, size):
        rows = lax.broadcasted_iota(jnp.int32, (slot, HALO), 0)
        cols = lax.broadcasted_iota(jnp.int32, (slot, HALO), 1)
        shift = source - HALO - tok if end else source
        chosen = ((cols == rows + shift) & (rows < size)).astype(F32).astype(BF16)
        added = nn(chosen, (right if end else left)[...])
        for copy in copies(end, slot, at, True):
            copy.wait()
        for one in range(2):
            value = held[end, one, pl.ds(0, slot), :].astype(F32)
            value = value + added[:, one * width : (one + 1) * width]
            held[end, one, pl.ds(0, slot), :] = value.astype(BF16)
        for copy in copies(end, slot, at, False):
            copy.start()

    def finish(end, slot, at, source, size):
        for copy in copies(end, slot, at, False):
            copy.wait()

    for visit in (fetch, add, finish):
        for end in range(2):
            for_slots(end, visit)


def patch_rows(info, left, right, x, d, tok):
    width = x.shape[1]
    vmem = pl.BlockSpec(memory_space=pltpu.VMEM)
    any_spec = pl.BlockSpec(memory_space=pl.ANY)
    shape = jax.ShapeDtypeStruct(x.shape, BF16)
    return pl.pallas_call(
        partial(patch_kernel, tok),
        out_shape=[shape, shape],
        in_specs=[SMEM_SPEC, vmem, vmem, any_spec, any_spec],
        out_specs=[any_spec, any_spec],
        scratch_shapes=[
            pltpu.VMEM((2, 2, SLOTS[2], width), BF16),
            pltpu.SemaphoreType.DMA((2, 2)),
        ],
        input_output_aliases={3: 0, 4: 1},
        compiler_params=pltpu.CompilerParams(vmem_limit_bytes=VMEM),
        cost_estimate=cost(4),
        name="patch_rows",
    )(info, left, right, x, d)


def unsort_kernel(info, mixed, grad, m_own, g_own, left, right, m_win, g_win):
    tok, width = m_own.shape
    m_win[...] = jnp.zeros_like(m_win)
    g_win[...] = jnp.zeros_like(g_win)

    def place(index, carry):
        source = info[TABLE + 3 * index]
        target = pl.multiple_of(info[TABLE + 3 * index + 1], 16)
        kind = info[TABLE + 3 * index + 2]
        begin = pl.multiple_of((source // 16) * 16, 16)
        shift = source - begin
        for which in range(EXPERTS):
            slot = SLOTS[which]
            fits = (kind == which) if which < 2 else (kind >= 2)
            size = LENS[which] if which < 2 else jnp.where(kind == 2, LENS[2], info[PAD_LEN])

            @pl.when(fits)
            def _(slot=slot, size=size):
                into = lax.broadcasted_iota(jnp.int32, (slot + 16, slot), 0)
                cols = lax.broadcasted_iota(jnp.int32, (slot + 16, slot), 1)
                chosen = ((into == cols + shift) & (cols < size)).astype(F32).astype(BF16)
                at, to = pl.ds(target, slot), pl.ds(begin, slot + 16)
                m_win[to, :] += nn(chosen, mixed[at, :])
                value = grad[at, :]
                high = value.astype(BF16)
                rest = (value - high.astype(F32)).astype(BF16)
                g_win[to, :] += nn(chosen, high) + nn(chosen, rest)

        return carry

    lax.fori_loop(0, info[OWN_N], place, 0)
    m_own[...] = m_win[pl.ds(HALO, tok), :].astype(m_own.dtype)
    g_own[...] = g_win[pl.ds(HALO, tok), :]
    for out, begin in ((left, 0), (right, HALO + tok)):
        out[:, pl.ds(0, width)] = g_win[pl.ds(begin, HALO), :].astype(BF16)
        out[:, pl.ds(width, width)] = m_win[pl.ds(begin, HALO), :].astype(BF16)


def unsort_rows(info, mixed, grad, tok):
    width = grad.shape[1]
    vmem = pl.BlockSpec(memory_space=pltpu.VMEM)
    return pl.pallas_call(
        unsort_kernel,
        out_shape=[
            jax.ShapeDtypeStruct((tok, width), BF16),
            jax.ShapeDtypeStruct((tok, width), F32),
            jax.ShapeDtypeStruct((HALO, 2 * width), BF16),
            jax.ShapeDtypeStruct((HALO, 2 * width), BF16),
        ],
        in_specs=[SMEM_SPEC, vmem, vmem],
        out_specs=[vmem] * 4,
        scratch_shapes=[pltpu.VMEM((tok + HALO + 288, width), F32)] * 2,
        compiler_params=pltpu.CompilerParams(vmem_limit_bytes=VMEM),
        cost_estimate=cost(10),
        name="unsort_rows",
    )(info, mixed, grad)


def qkv_kernel(info, x, gain, shift, weight, query_bias, value_bias, h_out, qkv_out):
    used = pl.program_id(0) * BLK < info[G_END]
    width = x.shape[1]

    @pl.when(used)
    def _():
        normed, _ = normalize(x[...].astype(F32))
        hidden = (normed * gain[...] + shift[...]).astype(BF16)
        h_out[...] = hidden
        for part in range(3):
            cols = pl.ds(part * width, width)
            value = nn(hidden, weight[:, cols])
            if part == 0:
                value = (value + query_bias[...]) * (HD ** (-0.5))
            if part == 2:
                value = value + value_bias[...]
            qkv_out[:, cols] = value.astype(BF16)

    @pl.when(jnp.logical_not(used))
    def _():
        h_out[...] = jnp.zeros_like(h_out)
        qkv_out[...] = jnp.zeros_like(qkv_out)


def full(shape):
    return pl.BlockSpec(shape, lambda *_: (0,) * len(shape))


def held(shape):
    return pl.BlockSpec(shape, lambda *_: (0,) * len(shape), pipeline_mode=pl.Buffered(1))


def project_qkv(info, x, gain, shift, weight, query_bias, value_bias):
    rows, width = x.shape
    return pl.pallas_call(
        qkv_kernel,
        grid=(rows // BLK,),
        out_shape=[
            jax.ShapeDtypeStruct((rows, width), BF16),
            jax.ShapeDtypeStruct((rows, 3 * width), BF16),
        ],
        in_specs=[
            SMEM_SPEC,
            pl.BlockSpec((BLK, width), lambda i: (i, 0)),
            full(gain.shape),
            full(shift.shape),
            held((width, 3 * width)),
            full(query_bias.shape),
            full(value_bias.shape),
        ],
        out_specs=[
            pl.BlockSpec((BLK, width), lambda i: (i, 0)),
            pl.BlockSpec((BLK, 3 * width), lambda i: (i, 0)),
        ],
        compiler_params=pltpu.CompilerParams(vmem_limit_bytes=VMEM),
        cost_estimate=cost(11),
        name="project_qkv",
    )(info, x, gain, shift, weight, query_bias, value_bias)


PAIRS, BACK_PAIRS = 6, 3


def softmax_cols(scores, bias):
    masked = scores + bias
    expo = jnp.exp(masked - jnp.max(masked, axis=0, keepdims=True))
    return expo * (1.0 / jnp.sum(expo, axis=0, keepdims=True))


def for_items(info, visit):
    def cut(slot, size):
        return jnp.where(lax.broadcasted_iota(jnp.int32, (slot, 1), 0) < size, 0.0, NEG)

    def image(index, carry):
        slot = SLOTS[0]
        visit(pl.multiple_of(index * slot, 16), slot, cut(slot, LENS[0]))
        return carry

    def text(index, carry):
        slot = TXT_PAIR
        rows = lax.broadcasted_iota(jnp.int32, (slot, slot), 0) // TXT_LEN
        cols = lax.broadcasted_iota(jnp.int32, (slot, slot), 1) // TXT_LEN
        start = pl.multiple_of(info[G_TXT] + index * slot, ROW)
        visit(start, slot, jnp.where(rows == cols, 0.0, NEG))
        return carry

    def both(index, carry):
        slot = SLOTS[2]
        real = index < info[N_BOTH]
        start = jnp.where(real, info[G_BOTH] + index * slot, info[G_PAD])
        size = jnp.where(real, LENS[2], info[PAD_LEN])
        visit(pl.multiple_of(start, 16), slot, cut(slot, size))
        return carry

    lax.fori_loop(0, info[N_IMG], image, 0)
    lax.fori_loop(0, (info[N_TXT] + 1) // 2, text, 0)
    lax.fori_loop(0, info[N_BOTH] + info[N_PAD], both, 0)


def first_head():
    return lax.broadcasted_iota(jnp.int32, (1, 2 * HD), 1) < HD


def attend_kernel(info, query, key, value, out):
    out[...] = jnp.zeros_like(out)

    def visit(start, slot, bias):
        at = pl.ds(start, slot)
        first = first_head()
        for pair in range(PAIRS):
            cols = pl.ds(pair * 2 * HD, 2 * HD)
            q, k, v = query[at, cols], key[at, cols], value[at, cols]
            results = []
            for mine in (first, jnp.logical_not(first)):
                prob = softmax_cols(nt(jnp.where(mine, k, 0), q), bias)
                results.append(tn(prob.astype(BF16), v))
            out[at, cols] = jnp.where(first, results[0], results[1]).astype(BF16)

    for_items(info, visit)


def attend(info, qkv):
    rows = qkv.shape[0]
    width = qkv.shape[1] // 3
    cols = 2 * HD * PAIRS
    steps = width // cols
    return pl.pallas_call(
        attend_kernel,
        grid=(steps,),
        out_shape=jax.ShapeDtypeStruct((rows, width), BF16),
        in_specs=[
            SMEM_SPEC,
            pl.BlockSpec((rows, cols), lambda p: (0, p)),
            pl.BlockSpec((rows, cols), lambda p: (0, steps + p)),
            pl.BlockSpec((rows, cols), lambda p: (0, 2 * steps + p)),
        ],
        out_specs=pl.BlockSpec((rows, cols), lambda p: (0, p)),
        compiler_params=pltpu.CompilerParams(vmem_limit_bytes=VMEM),
        cost_estimate=cost(25),
        name="attend",
    )(info, qkv, qkv, qkv)


def attend_back_kernel(info, query, key, value, grad, dq_out, dk_out, dv_out):
    for out in (dq_out, dk_out, dv_out):
        out[...] = jnp.zeros_like(out)

    def visit(start, slot, bias):
        at = pl.ds(start, slot)
        first = first_head()
        for pair in range(BACK_PAIRS):
            cols = pl.ds(pair * 2 * HD, 2 * HD)
            q, k, v, g = query[at, cols], key[at, cols], value[at, cols], grad[at, cols]
            dqs, dks, dvs = [], [], []
            for mine in (first, jnp.logical_not(first)):
                prob = softmax_cols(nt(jnp.where(mine, k, 0), q), bias)
                product = prob * nt(jnp.where(mine, v, 0), g)
                inner = jnp.sum(product, axis=0, keepdims=True)
                grad_score = (product - prob * inner).astype(BF16)
                dqs.append(tn(grad_score, k))
                dks.append(nn(grad_score, q))
                dvs.append(nn(prob.astype(BF16), g))
            scale = HD ** (-0.5)
            dq = jnp.where(first, dqs[0], dqs[1]).astype(BF16)
            dq_out[at, cols] = (dq.astype(F32) * scale).astype(BF16)
            dk_out[at, cols] = jnp.where(first, dks[0], dks[1]).astype(BF16)
            dv_out[at, cols] = jnp.where(first, dvs[0], dvs[1]).astype(BF16)

    for_items(info, visit)


def attend_back(info, qkv, grad):
    rows = qkv.shape[0]
    width = qkv.shape[1] // 3
    cols = 2 * HD * BACK_PAIRS
    steps = width // cols
    spec = pl.BlockSpec((rows, cols), lambda p: (0, p))
    return pl.pallas_call(
        attend_back_kernel,
        grid=(steps,),
        out_shape=[jax.ShapeDtypeStruct((rows, width), BF16)] * 3,
        in_specs=[
            SMEM_SPEC,
            spec,
            pl.BlockSpec((rows, cols), lambda p: (0, steps + p)),
            pl.BlockSpec((rows, cols), lambda p: (0, 2 * steps + p)),
            spec,
        ],
        out_specs=[spec] * 3,
        compiler_params=pltpu.CompilerParams(vmem_limit_bytes=VMEM),
        cost_estimate=cost(42),
        name="attend_back",
    )(info, qkv, qkv, qkv, grad)


def group_of(info, row):
    return (
        (row >= info[G_TXT]).astype(jnp.int32)
        + (row >= info[G_BOTH]).astype(jnp.int32)
        + (row >= info[G_PAD]).astype(jnp.int32)
    )


def middle_kernel(info, x, att, weight, bias, gains, shifts, mid_out, h_out):
    first = pl.program_id(0) * BLK

    @pl.when(first < info[G_END])
    def _():
        middle = x[...].astype(F32) + (nn(att[...], weight[...]) + bias[...])
        mid_out[...] = middle
        normed, _ = normalize(middle)
        for part in range(BLK // ROW):
            which = pl.ds(jnp.minimum(group_of(info, first + part * ROW), EXPERTS - 1), 1)
            at = pl.ds(part * ROW, ROW)
            here = normed[part * ROW : (part + 1) * ROW]
            h_out[at, :] = (here * gains[which, :] + shifts[which, :]).astype(BF16)


def middle_norm(info, x, att, weight, bias, gains, shifts):
    rows, width = x.shape
    spec = pl.BlockSpec((BLK, width), lambda i: (i, 0))
    return pl.pallas_call(
        middle_kernel,
        grid=(rows // BLK,),
        out_shape=[
            jax.ShapeDtypeStruct((rows, width), F32),
            jax.ShapeDtypeStruct((rows, width), BF16),
        ],
        in_specs=[
            SMEM_SPEC,
            spec,
            spec,
            held((width, width)),
            full(bias.shape),
            full(gains.shape),
            full(shifts.shape),
        ],
        out_specs=[spec, spec],
        compiler_params=pltpu.CompilerParams(vmem_limit_bytes=VMEM),
        cost_estimate=cost(10),
        name="middle_norm",
    )(info, x, att, weight, bias, gains, shifts)


def gelu_parts(up):
    size = jnp.abs(up) * (0.5**0.5)
    expo = jnp.exp(-size * size)
    t = 1.0 / (1.0 + 0.3275911 * size)
    poly = 1.061405429 * t - 1.453152027
    poly = poly * t + 1.421413741
    poly = poly * t - 0.284496736
    poly = poly * t + 0.254829592
    tail = 0.5 * (poly * t) * expo
    cdf = jnp.where(up >= 0, 1.0 - tail, tail)
    return (up * cdf, cdf + up * (expo * 0.3989422804014327))


KROWS = 512
COLS = 1


def hidden_kernel(part, chunk, *refs):
    info, h_hbm, g_hbm, up_hbm, b_up, down_hbm = refs[:6]
    refs = refs[6:]
    weight_outs, refs = (refs[:2], refs[2:]) if chunk else (refs[:1], refs[1:])
    bias_out, act_hbm, dup_hbm, left, right, w_up, w_down, acc, stage = refs[:9]
    row_sems, weight_sems, hidden_sems, stage_sems = refs[9:]
    tile = w_up.shape[2]
    cols_at = pl.ds(part * tile, tile)
    bias_out[...] = jnp.zeros_like(bias_out)

    def rows_copies(index):
        at = pl.ds(pl.multiple_of(index * ROW, ROW), ROW)
        return [
            pltpu.make_async_copy(source.at[at, :], left.at[which, at, :], row_sems.at[which, index])
            for which, source in enumerate((h_hbm, g_hbm))
        ]

    def weight_copies(expert):
        return [
            pltpu.make_async_copy(
                up_hbm.at[expert, :, cols_at], w_up.at[expert], weight_sems.at[0, expert]
            ),
            pltpu.make_async_copy(
                down_hbm.at[expert, cols_at, :], w_down.at[expert], weight_sems.at[1, expert]
            ),
        ]

    def hidden_copies(index):
        at = pl.ds(pl.multiple_of(index * ROW, ROW), ROW)
        return [
            pltpu.make_async_copy(right.at[which, at, :], target.at[at, :], hidden_sems.at[which, index])
            for which, target in enumerate((dup_hbm, act_hbm))
        ]

    def stage_copies(slot, expert):
        return [
            pltpu.make_async_copy(
                stage.at[slot, which], out.at[slot, expert], stage_sems.at[slot, which]
            )
            for which, out in enumerate(weight_outs)
        ]

    def each(low, high, visit):
        def body(index, carry):
            visit(index)
            return carry

        lax.fori_loop(low, high, body, 0)

    def start_all(copies):
        for copy in copies:
            copy.start()

    def wait_all(copies):
        for copy in copies:
            copy.wait()

    def prefetch(expert):
        start_all(weight_copies(expert))
        low, high = info[G_IMG + expert] // ROW, info[G_IMG + expert + 1] // ROW
        each(low, high, lambda index: start_all(rows_copies(index)))

    each(0, EXPERTS, prefetch)

    def rows_of(expert, row, size):
        for place in range(size // ROW):
            wait_all(rows_copies(row // ROW + place))
        at = pl.ds(pl.multiple_of(row, ROW), size)
        hidden, grad = left[0, at, :], left[1, at, :]
        wide = tile // COLS
        for turn in range(COLS):
            cols = pl.ds(turn * wide, wide)
            bias = b_up[pl.ds(expert, 1), pl.ds(part * tile + turn * wide, wide)]
            up = nn(hidden, w_up[expert, :, cols]) + bias
            grad_act = nt(grad, w_down[expert, cols, :])
            active, slope = gelu_parts(up)
            grad_up = (slope * grad_act).astype(BF16)
            right[0, at, cols] = grad_up
            right[1, at, cols] = active.astype(BF16)
            bias_out[expert, :, cols] += jnp.sum(grad_up.astype(F32), axis=0, keepdims=True)
        for place in range(size // ROW):
            start_all(hidden_copies(row // ROW + place))

    def put(slot, value):
        if not chunk:
            stage[slot, 0] = value.astype(BF16)
            return
        for pair in range(value.shape[0] // (2 * chunk)):
            for core in range(2):
                first = (2 * pair + core) * chunk
                which = (info[CORE] + core) % 2
                stage[slot, which, pair] = value[first : first + chunk].astype(BF16)

    def one_expert(expert):
        wait_all(weight_copies(expert))
        start = info[G_IMG + expert]
        count = info[G_IMG + expert + 1] - start
        blocks = count // BLK
        each(0, blocks, lambda index: rows_of(expert, start + index * BLK, BLK))

        @pl.when(count % BLK > 0)
        def _():
            rows_of(expert, start + blocks * BLK, ROW)

        def one_side(slot):
            @pl.when(expert > 0)
            def _():
                wait_all(stage_copies(slot, expert - 1))

            def product(local, size):
                at = pl.ds(pl.multiple_of(start + local, ROW), size)
                return tn(left[slot, at, :], right[slot, at, :])

            before = (count - 1) // KROWS

            @pl.when(count == 0)
            def _():
                stage[slot] = jnp.zeros(stage.shape[1:], BF16)

            @pl.when(count > KROWS)
            def _():
                acc[...] = product(0, KROWS)

                def more(index):
                    acc[...] += product(index * KROWS, KROWS)

                each(1, before, more)

            for rest in range(ROW, KROWS + ROW, ROW):
                at_end = (count > 0) & (count - before * KROWS == rest)

                @pl.when(at_end & (before == 0))
                def _(rest=rest):
                    put(slot, product(0, rest))

                @pl.when(at_end & (before > 0))
                def _(rest=rest):
                    put(slot, acc[...] + product(before * KROWS, rest))

            start_all(stage_copies(slot, expert))

        each(0, 2, one_side)

    each(0, EXPERTS, one_expert)
    for slot in range(2):
        wait_all(stage_copies(slot, EXPERTS - 1))
    each(0, info[G_PAD] // ROW, lambda index: wait_all(hidden_copies(index)))


def run_hidden(part, parts, info, h, g, w_up, b_up, w_down, chunk):
    rows, width = h.shape
    tile = w_up.shape[2] // parts
    any_spec = pl.BlockSpec(memory_space=pl.ANY)
    vmem = pl.BlockSpec(memory_space=pltpu.VMEM)
    block = (width // (2 * chunk), chunk, tile) if chunk else (width, tile)
    sides = 2 if chunk else 1
    return pl.pallas_call(
        partial(hidden_kernel, part, chunk),
        out_shape=[jax.ShapeDtypeStruct((2, EXPERTS) + block, BF16)] * sides
        + [
            jax.ShapeDtypeStruct((EXPERTS, 1, tile), F32),
            jax.ShapeDtypeStruct((rows, tile), BF16),
            jax.ShapeDtypeStruct((rows, tile), BF16),
        ],
        in_specs=[SMEM_SPEC, any_spec, any_spec, any_spec, vmem, any_spec],
        out_specs=[any_spec] * sides + [vmem, any_spec, any_spec],
        scratch_shapes=[
            pltpu.VMEM((2, rows, width), BF16),
            pltpu.VMEM((2, rows, tile), BF16),
            pltpu.VMEM((EXPERTS, width, tile), BF16),
            pltpu.VMEM((EXPERTS, tile, width), BF16),
            pltpu.VMEM((width, tile), F32),
            pltpu.VMEM((2, sides) + block, BF16),
            pltpu.SemaphoreType.DMA((2, rows // ROW)),
            pltpu.SemaphoreType.DMA((2, EXPERTS)),
            pltpu.SemaphoreType.DMA((2, rows // ROW)),
            pltpu.SemaphoreType.DMA((2, sides)),
        ],
        compiler_params=pltpu.CompilerParams(vmem_limit_bytes=VMEM),
        cost_estimate=cost(18),
        name="hidden",
    )(info, h, g, w_up, b_up, w_down)


SUMS = 16


def finish_kernel(parts, *refs):
    info = refs[0]
    hbm = refs[1 : 3 + 2 * parts]
    up_hbm, down_hbm, gains, downs, w_attn = refs[3 + 2 * parts : 8 + 2 * parts]
    refs = refs[8 + 2 * parts :]
    sums_out, outs_hbm = refs[0], refs[1:5]
    rows_in, acts, dups = refs[5:7], refs[7 : 7 + parts], refs[7 + parts : 7 + 2 * parts]
    refs = refs[7 + 2 * parts :]
    held_out, (w_up, w_down, lower_s, hidden_s) = refs[:4], refs[4:8]
    row_sems, act_sems, out_sems, weight_sems = refs[8:]
    width = lower_s.shape[2]

    groups = range(EXPERTS + 1)
    counts = [info[G_IMG + group + 1] - info[G_IMG + group] for group in groups]
    firsts = [jnp.int32(0)]
    for group in groups:
        firsts.append(firsts[-1] + (counts[group] + BLK - 1) // BLK)
    total = firsts[-1]

    def block_of(index):
        group = sum([(index >= firsts[k]).astype(jnp.int32) for k in groups[1:]])
        first, start, count = firsts[0], info[G_IMG], counts[0]
        for k in groups[1:]:
            first = jnp.where(group == k, firsts[k], first)
            start = jnp.where(group == k, info[G_IMG + k], start)
            count = jnp.where(group == k, counts[k], count)
        local = (index - first) * BLK
        return group, start + local, count - local, index == first

    def halves(index, visit):
        group, row, left, _ = block_of(index)
        for half in range(BLK // ROW):

            @pl.when(half * ROW < left)
            def _(half=half):
                visit(half, pl.ds(pl.multiple_of(row + half * ROW, ROW), ROW), group < EXPERTS)

    def in_copies(index, half, at):
        here = pl.ds(half * ROW, ROW)
        rows = [
            pltpu.make_async_copy(
                source.at[at, :], target.at[index % 4, here, :], row_sems.at[index % 4, half, which]
            )
            for which, (source, target) in enumerate(zip(hbm[:2], rows_in))
        ]
        hidden = [
            pltpu.make_async_copy(
                source.at[at, :], target.at[index % 3, here, :], act_sems.at[index % 3, half, which]
            )
            for which, (source, target) in enumerate(zip(hbm[2:], acts + dups))
        ]
        return rows, hidden

    def fetch(index, action):
        def visit(half, at, real):
            rows, hidden = in_copies(index, half, at)
            for copy in rows:
                action(copy)

            @pl.when(real)
            def _():
                for copy in hidden:
                    action(copy)

        halves(index, visit)

    def send(index, action):
        def visit(half, at, real):
            here = pl.ds(half * ROW, ROW)
            for which, (source, target) in enumerate(zip(held_out, outs_hbm)):
                action(
                    pltpu.make_async_copy(
                        source.at[index % 2, here, :],
                        target.at[at, :],
                        out_sems.at[index % 2, half, which],
                    )
                )

        halves(index, visit)

    def start(copy):
        copy.start()

    def wait(copy):
        copy.wait()

    def weights(group, action):
        for which, (source, target) in enumerate(((up_hbm, w_up), (down_hbm, w_down))):
            action(
                pltpu.make_async_copy(
                    source.at[group], target.at[group], weight_sems.at[group, which]
                )
            )

    sums_out[...] = jnp.zeros_like(sums_out)

    @pl.when(total > 0)
    def _():
        fetch(0, start)

    weights(0, start)

    @pl.when(total > 1)
    def _():
        fetch(1, start)

    for expert in range(1, EXPERTS):
        weights(expert, start)

    tile = acts[0].shape[2]

    def block(index, waited):
        group, _, _, _ = block_of(index)
        mine = jnp.minimum(group, EXPERTS - 1)

        @pl.when(index + 2 < total)
        def _():
            fetch(index + 2, start)

        for expert in range(EXPERTS):

            @pl.when((waited <= expert) & (expert <= mine))
            def _(expert=expert):
                weights(expert, wait)

        @pl.when(index < total)
        def _():
            fetch(index, wait)

        @pl.when(index >= 3)
        def _():
            send(index - 3, wait)

        slot, old = index % 2, (index + 1) % 2
        behind = jnp.maximum(index - 1, 0)
        group, _, left, _ = block_of(behind)
        left = jnp.where(index > 0, left, 0)
        real = group < EXPERTS
        which = pl.ds(jnp.minimum(group, EXPERTS - 1), 1)
        mixed, dx, proj_out, datt = held_out
        sub = BLK // 4

        def row_part(turn):
            at = pl.ds(turn * sub, sub)
            valid = turn * sub + lax.broadcasted_iota(jnp.int32, (sub, 1), 0) < left
            middle = jnp.where(valid, rows_in[0][behind % 4, at, :], 0.0)
            grad = jnp.where(valid, rows_in[1][behind % 4, at, :].astype(F32), 0.0)
            lower = jnp.where(real, lower_s[old, at, :] + downs[which, :], 0.0)
            grad_hidden = jnp.where(valid & real, hidden_s[old, at, :], 0.0)
            mixed[old, at, :] = (middle + lower).astype(BF16)
            normed, inverse = normalize(middle)
            grad_middle = grad + norm_back(grad_hidden * gains[which, :], normed, inverse)
            dx[old, at, :] = grad_middle
            proj = grad_middle.astype(BF16)
            proj_out[old, at, :] = proj
            dsel = jnp.where(real, grad, 0.0)
            values = (proj.astype(F32), grad_hidden * normed, grad_hidden, dsel)
            return [jnp.sum(value, axis=0, keepdims=True) for value in values]

        taken = index % 3

        def compute(multiply):
            lower_new = jnp.zeros((BLK, width), F32)
            hidden_new = jnp.zeros((BLK, width), F32)
            sums, turn = [0.0] * 4, 0
            for part in range(parts):
                cols = pl.ds(part * tile, tile)
                if multiply:
                    lower_new += nn(acts[part][taken], w_down[mine, cols, :])
                if turn < 4:
                    sums = [x + y for x, y in zip(sums, row_part(turn))]
                    turn += 1
                if multiply:
                    hidden_new += nt(dups[part][taken], w_up[mine, :, cols])
                if turn < 4:
                    sums = [x + y for x, y in zip(sums, row_part(turn))]
                    turn += 1
            while turn < 4:
                sums = [x + y for x, y in zip(sums, row_part(turn))]
                turn += 1
            if multiply:
                lower_s[slot] = lower_new
                hidden_s[slot] = hidden_new
            datt[old] = nt(proj_out[old], w_attn[...]).astype(BF16)
            sums_out[pl.ds(0, 1), :] += sums[0]
            for place, value in enumerate(sums[1:]):
                at = pl.ds(1 + place * EXPERTS + jnp.minimum(group, EXPERTS - 1), 1)
                sums_out[at, :] += value

        @pl.when(index < total)
        def _():
            compute(True)

        @pl.when(index == total)
        def _():
            compute(False)
        @pl.when(index > 0)
        def _():
            send(index - 1, start)

        return jnp.maximum(waited, mine + 1)

    waited = lax.fori_loop(0, jnp.where(total > 0, total + 1, 0), block, jnp.int32(0))
    for expert in range(EXPERTS):

        @pl.when(waited <= expert)
        def _(expert=expert):
            weights(expert, wait)

    for back in (2, 1):

        @pl.when(total >= back)
        def _(back=back):
            send(total - back, wait)


def finish_experts(info, mid, g, acts, dups, w_up, w_down, gains, downs, w_attn):
    rows, width = mid.shape
    parts = len(acts)
    tile = acts[0].shape[1]
    any_spec = pl.BlockSpec(memory_space=pl.ANY)
    vmem = pl.BlockSpec(memory_space=pltpu.VMEM)
    kinds = (BF16, F32, BF16, BF16)
    return pl.pallas_call(
        partial(finish_kernel, parts),
        out_shape=[jax.ShapeDtypeStruct((SUMS, width), F32)]
        + [jax.ShapeDtypeStruct((rows, width), kind) for kind in kinds],
        in_specs=[SMEM_SPEC] + [any_spec] * (4 + 2 * parts) + [vmem] * 3,
        out_specs=[vmem] + [any_spec] * 4,
        scratch_shapes=[pltpu.VMEM((4, BLK, width), F32), pltpu.VMEM((4, BLK, width), BF16)]
        + [pltpu.VMEM((3, BLK, tile), BF16)] * (2 * parts)
        + [pltpu.VMEM((2, BLK, width), kind) for kind in kinds]
        + [pltpu.VMEM(w_up.shape, BF16), pltpu.VMEM(w_down.shape, BF16)]
        + [pltpu.VMEM((2, BLK, width), F32)] * 2
        + [
            pltpu.SemaphoreType.DMA((4, BLK // ROW, 2)),
            pltpu.SemaphoreType.DMA((3, BLK // ROW, 2 * parts)),
            pltpu.SemaphoreType.DMA((2, BLK // ROW, 4)),
            pltpu.SemaphoreType.DMA((EXPERTS, 2)),
        ],
        compiler_params=pltpu.CompilerParams(vmem_limit_bytes=VMEM),
        cost_estimate=cost(30),
        name="finish_experts",
    )(info, mid, g, *acts, *dups, w_up, w_down, gains, downs, w_attn)


def weights_kernel(dp, seq, info, dq, dk, dv, proj, h, att, send_out, keep_out, acc, attn_acc):
    index = pl.program_id(0)

    @pl.when(index == 0)
    def _():
        acc[...] = jnp.zeros_like(acc)
        attn_acc[...] = jnp.zeros_like(attn_acc)

    @pl.when(index * BLK < info[G_END])
    def _():
        row = index * BLK + lax.broadcasted_iota(jnp.int32, (BLK, 1), 0)
        real = row < info[G_END]
        hidden = h[...]
        width = hidden.shape[1]
        for part, grad in enumerate((dq, dk, dv)):
            acc[pl.ds(part * width, width), :] += tn(grad[...], hidden)
        attn_acc[...] += tn(
            jnp.where(real, proj[...], jnp.zeros_like(proj)),
            jnp.where(real, att[...], jnp.zeros_like(att)),
        )

    @pl.when(index == pl.num_programs(0) - 1)
    def _():
        width = attn_acc.shape[0]
        own = width // (dp * seq)
        half = width // 2
        for out, core in ((keep_out, info[CORE]), (send_out, 1 - info[CORE])):
            for pair in range(dp // 2):
                for place in range(seq):
                    device = (2 * pair + core) * seq + place
                    first = pl.ds(pl.multiple_of(device * 3 * own, 8), 3 * own)
                    second = pl.ds(pl.multiple_of(device * own, 8), own)
                    value = jnp.concatenate([acc[first, :], attn_acc[second, :]], axis=0)
                    value = value.astype(BF16)
                    at = pl.ds(place * 4 * own, 4 * own)
                    for lane in range(2):
                        out[lane, 0, pair, at, :] = value[:, lane * half : (lane + 1) * half]


def weights_kernel_plain(info, dq, dk, dv, proj, h, att, qkv_out, attn_out, acc, attn_acc):
    index = pl.program_id(0)

    @pl.when(index == 0)
    def _():
        acc[...] = jnp.zeros_like(acc)
        attn_acc[...] = jnp.zeros_like(attn_acc)

    @pl.when(index * BLK < info[G_END])
    def _():
        row = index * BLK + lax.broadcasted_iota(jnp.int32, (BLK, 1), 0)
        real = row < info[G_END]
        hidden = h[...]
        width = hidden.shape[1]
        for part, grad in enumerate((dq, dk, dv)):
            acc[pl.ds(part * width, width), :] += tn(grad[...], hidden)
        attn_acc[...] += tn(
            jnp.where(real, proj[...], jnp.zeros_like(proj)),
            jnp.where(real, att[...], jnp.zeros_like(att)),
        )

    @pl.when(index == pl.num_programs(0) - 1)
    def _():
        qkv_out[...] = acc[...].astype(BF16)
        attn_out[...] = attn_acc[...].astype(BF16)


def projection_grads(info, dq, dk, dv, proj, h, att, dp, seq):
    rows, width = h.shape
    spec = pl.BlockSpec((BLK, width), lambda i: (i, 0))
    own = width // (dp * seq)
    direct = own % 8 == 0
    if direct:
        shapes = [(2, 1, dp // 2, seq * 4 * own, width // 2)] * 2
        body = partial(weights_kernel, dp, seq)
    else:
        shapes = [(3 * width, width), (width, width)]
        body = weights_kernel_plain
    results = pl.pallas_call(
        body,
        grid=(rows // BLK,),
        out_shape=[jax.ShapeDtypeStruct(shape, BF16) for shape in shapes],
        in_specs=[SMEM_SPEC] + [spec] * 6,
        out_specs=[full(shape) for shape in shapes],
        scratch_shapes=[pltpu.VMEM((3 * width, width), F32), pltpu.VMEM((width, width), F32)],
        compiler_params=pltpu.CompilerParams(vmem_limit_bytes=VMEM),
        cost_estimate=cost(15),
        name="projection_grads",
    )(info, dq, dk, dv, proj, h, att)
    if direct:
        return results[1], results[0]
    d_qkv = results[0].reshape(dp * seq, -1, width)
    d_attn = results[1].reshape(dp * seq, -1, width)
    d_all = jnp.concatenate([d_qkv, d_attn], axis=1).reshape(1, -1, width)
    half = width // 2
    return core_split(jnp.stack([d_all[..., :half], d_all[..., half:]]))


VECTORS = 24


def last_kernel(parts, *refs):
    (info, x, dx, dq, dk, dv, gain, weight, row_sums) = refs[:9]
    biases = refs[9 : 9 + parts]
    out, packed = refs[9 + parts :]
    width = x.shape[1]
    step = pl.program_id(0)

    @pl.when(step == 0)
    def _():
        packed[...] = jnp.zeros_like(packed)
        packed[pl.ds(4, 10), pl.ds(0, width)] = row_sums[pl.ds(0, 10), :]
        for part, bias in enumerate(biases):
            tile = bias.shape[2]
            for expert in range(EXPERTS):
                packed[pl.ds(14 + part * EXPERTS + expert, 1), pl.ds(0, tile)] = bias[expert]

    @pl.when(step * BLK < info[G_END])
    def _():
        hidden = nt(dq[...], weight[:, pl.ds(0, width)])
        hidden += nt(dk[...], weight[:, pl.ds(width, width)])
        hidden += nt(dv[...], weight[:, pl.ds(2 * width, width)])
        normed, inverse = normalize(x[...].astype(F32))
        totals = (hidden * normed, hidden, dq[...].astype(F32), dv[...].astype(F32))
        for place, value in enumerate(totals):
            packed[pl.ds(place, 1), pl.ds(0, width)] += jnp.sum(value, axis=0, keepdims=True)
        out[...] = dx[...] + norm_back(hidden * gain[...], normed, inverse)


def last_norm(info, x, dx, dq, dk, dv, gain, weight, row_sums, biases):
    rows, width = x.shape
    spec = pl.BlockSpec((BLK, width), lambda i: (i, 0))
    cols = max(width, biases[0].shape[2])
    packed = (VECTORS, cols)
    return pl.pallas_call(
        partial(last_kernel, len(biases)),
        grid=(rows // BLK,),
        out_shape=[jax.ShapeDtypeStruct((rows, width), F32), jax.ShapeDtypeStruct(packed, F32)],
        in_specs=[SMEM_SPEC, spec, spec, spec, spec, spec, full(gain.shape), held((width, 3 * width))]
        + [full(row_sums.shape)]
        + [full(bias.shape) for bias in biases],
        out_specs=[spec, full(packed)],
        compiler_params=pltpu.CompilerParams(vmem_limit_bytes=VMEM),
        cost_estimate=cost(14),
        name="last_norm",
    )(info, x, dx, dq, dk, dv, gain, weight, row_sums, *biases)


def swap(value, bit):
    ways = lax.axis_size("dp")
    return lax.ppermute(value, "dp", [(i, i ^ (1 << bit)) for i in range(ways)])


def half_of(parts, axis, bit, mine):
    own = (lax.axis_index("dp") >> bit) & 1
    which = own if mine else 1 - own
    return [lax.dynamic_index_in_dim(part, which, axis, keepdims=False) for part in parts]


DEPTH = 4


def combine_kernel(blocks, arrays, shapes, seq, ways, *refs):
    place, sources = refs[0], refs[1 : 1 + arrays]
    outs = refs[1 + arrays : 1 + arrays + shapes]
    in_buf, out_buf, own_buf, send_buf, total, kept_buf, in_sems, out_sems = refs[1 + arrays + shapes :]
    here = lax.rem(place[0], ways)

    def fetch(index):
        parts, kind, _, _ = blocks[index]
        copies = []
        for part, (which, where) in enumerate(parts):
            source = sources[which].at[where(place)]
            buf = in_buf.at[index % DEPTH, part]
            if isinstance(kind, tuple):
                rows = source.shape[1]
                buf = kept_buf.at[index % DEPTH] if part == 0 else buf
                buf = buf.at[:, pl.ds(0, rows), :]
            copies.append(pltpu.make_async_copy(source, buf, in_sems.at[index % DEPTH, part]))
        return copies

    def send(index):
        _, kind, targets, at = blocks[index]
        slot = index % 2
        if kind == "add":
            held = [out_buf.at[slot]]
        else:
            held = [own_buf.at[slot]] + [send_buf.at[slot, hop] for hop in range(len(targets) - 1)]
        copies = []
        for which, (source, target) in enumerate(zip(held, targets)):
            target = outs[target].at[at]
            if kind != "add":
                source = source.at[:, pl.ds(0, target.shape[1]), :]
            copies.append(pltpu.make_async_copy(source, target, out_sems.at[slot, which]))
        return copies

    for index in range(min(DEPTH - 1, len(blocks))):
        for copy in fetch(index):
            copy.start()
    for index, (parts, kind, targets, _) in enumerate(blocks):
        if index + DEPTH - 1 < len(blocks):
            for copy in fetch(index + DEPTH - 1):
                copy.start()
        for copy in fetch(index):
            copy.wait()
        if index >= 2:
            for copy in send(index - 2):
                copy.wait()
        slot, source = index % 2, index % DEPTH
        if isinstance(kind, tuple):
            rows = outs[targets[0]].shape[2]
            mine = (place[0] >> kind[1]) & 1
            for which, chosen in enumerate((mine, 1 - mine)):
                at = pl.ds(pl.multiple_of(chosen * rows, 8), rows)
                total[:, pl.ds(0, 2 * rows), :] = in_buf[source, 1, :, pl.ds(0, 2 * rows), :].astype(F32)
                value = kept_buf[source, :, at, :] + total[:, at, :]
                if which == 0:
                    own_buf[slot, :, pl.ds(0, rows), :] = value
                else:
                    send_buf[slot, 0, :, pl.ds(0, rows), :] = value.astype(BF16)
        else:
            value = in_buf[source, 0].astype(F32)
            for part in range(1, len(parts)):
                value = value + in_buf[source, part].astype(F32)
            if kind == "add":
                out_buf[slot] = value.astype(BF16)
            else:
                total[...] = value
                rows = total.shape[1] // seq
                for hop in range(ways):
                    for turn in range(seq // ways):
                        at = lax.rem(here + hop, ways) + turn * ways
                        block = total[:, pl.ds(pl.multiple_of(at * rows, 8), rows), :]
                        to = pl.ds(turn * rows, rows)
                        if hop == 0:
                            own_buf[slot, :, to, :] = block
                        else:
                            send_buf[slot, hop - 1, :, to, :] = block.astype(BF16)
        for copy in send(index):
            copy.start()
    for index in range(max(0, len(blocks) - 2), len(blocks)):
        for copy in send(index):
            copy.wait()


class Flight:

    def __init__(self):
        self.cells = []

    def start(self, value):
        cell = [value]
        self.cells.append(cell)
        return cell

    def land(self, *outputs, later=()):
        now = [cell for cell in self.cells if not any(cell is other for other in later)]
        outputs, arrays = lax.optimization_barrier((outputs, [cell[0] for cell in now]))
        for cell, array in zip(now, arrays):
            cell[0] = array
        self.cells = [cell for cell in self.cells if any(cell is other for other in later)]
        return outputs


class Sum:

    def __init__(self, flight, kept, sent):
        self.flight = flight
        self.bits = lax.axis_size("dp").bit_length() - 1
        self.seq = lax.axis_size("seq")
        self.many, self.pairs, self.chunk, self.cols = kept.shape[1:]
        every = list(range(self.bits - 1, 0, -1))
        shape = (2, self.many) + (2,) * len(every) + (self.chunk, self.cols)
        cells = [[kept.reshape(shape)], flight.start(swap(sent, 0).reshape(shape))]
        self.lanes = [[(cell, lane, every, True) for cell in cells] for lane in range(2)]
        self.left = [list(every), list(every)]
        self.ways = self.seq
        self.own = None
        self.seq_left = None

    def more(self):
        return bool(self.left[0])

    def direct(self):
        return (self.chunk // self.seq) % 8 == 0

    def sources(self, lane, other, free, value):
        results = []
        for cell, first, bits, whole in self.lanes[lane]:

            def where(place, first=first, bits=bits, whole=whole):
                chosen = []
                for bit in bits:
                    if bit in free:
                        chosen.append((value >> (len(free) - 1 - free.index(bit))) & 1)
                    elif bit == other:
                        chosen.append(1 - place[1 + bit])
                    else:
                        chosen.append(place[1 + bit])
                if whole:
                    return (first, slice(None)) + tuple(chosen)
                group = 0
                for one in chosen:
                    group = group * 2 + one
                return (first + group,)

            results.append((cell[0], where))
        return results


def advance(place, steps, closing=None, halving=None):
    arrays, blocks, payloads, turns = [], [], {}, []
    model = steps[0] if steps else closing or halving

    def add(parts, kind, targets, at):
        known = []
        for array, where in parts:
            found = [i for i, other in enumerate(arrays) if other is array]
            if not found:
                arrays.append(array)
            known.append((found[0] if found else len(arrays) - 1, where))
        blocks.append((known, kind, targets, at))

    for total in steps:
        for lane in range(2):
            left = total.left[lane]
            bit = min(left) if lane == 0 else max(left)
            left.remove(bit)
            free = list(left)
            count = payloads.get(bit, 0)
            turns.append((total, lane, bit, free, count))
            for value in range(2 ** len(free)):
                add(total.sources(lane, bit, free, value), "add", bit, count)
                count += 1
            payloads[bit] = count
    order = sorted(payloads)
    blocks = [(parts, kind, [order.index(bit)], at) for parts, kind, bit, at in blocks]
    seq, many, chunk, cols = model.seq, model.many, model.chunk, model.cols
    shapes = [jax.ShapeDtypeStruct((payloads[bit], many, chunk, cols), BF16) for bit in order]
    split = closing is not None and closing.direct()
    ways = closing.ways if split else 2
    rows = chunk // ways
    first_end = len(shapes)
    if closing is not None:
        if split:
            shapes.append(jax.ShapeDtypeStruct((2, many, rows, cols), F32))
            shapes += [jax.ShapeDtypeStruct((2, many, rows, cols), BF16)] * (ways - 1)
        else:
            shapes.append(jax.ShapeDtypeStruct((2, many, chunk, cols), BF16))
        targets = list(range(first_end, len(shapes)))
        for lane in range(2):
            add(closing.sources(lane, None, [], 0), "ends" if split else "add", targets, lane)
    first_half = len(shapes)
    if halving is not None:
        seq_bit = halving.seq_left.pop(0)
        half = halving.own.shape[2] // 2
        shapes.append(jax.ShapeDtypeStruct((2, many, half, cols), F32))
        shapes.append(jax.ShapeDtypeStruct((2, many, half, cols), BF16))
        for lane in range(2):
            parts = [(array, lambda place, lane=lane: (lane,)) for array in (halving.own, halving.got[0][0])]
            add(parts, ("half", seq_bit), [first_half, first_half + 1], lane)
    most = max(len(parts) for parts, _, _, _ in blocks)
    end_rows = rows if split else chunk // 2 if halving is not None else 8
    kept_rows = halving.own.shape[2] if halving is not None else 8
    any_spec = pl.BlockSpec(memory_space=pl.ANY)
    results = pl.pallas_call(
        partial(combine_kernel, blocks, len(arrays), len(shapes), seq, ways),
        in_specs=[SMEM_SPEC] + [any_spec] * len(arrays),
        out_specs=[any_spec] * len(shapes),
        out_shape=shapes,
        scratch_shapes=[
            pltpu.VMEM((DEPTH, most, many, chunk, cols), BF16),
            pltpu.VMEM((2, many, chunk, cols), BF16),
            pltpu.VMEM((2, many, end_rows, cols), F32),
            pltpu.VMEM((2, ways - 1, many, end_rows, cols), BF16),
            pltpu.VMEM((many, chunk, cols), F32),
            pltpu.VMEM((DEPTH, many, kept_rows, cols), F32),
            pltpu.SemaphoreType.DMA((DEPTH, most)),
            pltpu.SemaphoreType.DMA((2, ways)),
        ],
        compiler_params=pltpu.CompilerParams(vmem_limit_bytes=VMEM),
        cost_estimate=cost(4),
        name="combine",
    )(place, *arrays)

    def go(results):
        got = {bit: model.flight.start(swap(value, bit)) for bit, value in zip(order, results)}
        for total, lane, bit, free, first in turns:
            total.lanes[lane].append((got[bit], first, free, False))
        if halving is not None:
            halving.own = results[first_half]
            pairs = [(i, i ^ (1 << seq_bit)) for i in range(seq)]
            sent = lax.ppermute(results[first_half + 1], "seq", pairs)
            halving.got = [halving.flight.start(sent)]
        if closing is None:
            return
        parts = results[first_end:first_half]
        if not split:
            half = parts[0].reshape(2, many, seq, chunk // seq, cols)
            here = lax.axis_index("seq")
            parts = [
                lax.dynamic_index_in_dim(half, (here + hop) % seq, 2, keepdims=False)
                for hop in range(seq)
            ]
        closing.own = parts[0].astype(F32)
        closing.seq_left = []
        if split and ways < seq:
            pairs = [(i, i ^ 1) for i in range(seq)]
            closing.got = [closing.flight.start(lax.ppermute(parts[1], "seq", pairs))]
            closing.seq_left = list(range(1, seq.bit_length() - 1))
            return
        closing.got = []
        for hop, send in enumerate(parts[1:]):
            pairs = [(i, (i + hop + 1) % seq) for i in range(seq)]
            closing.got.append(closing.flight.start(lax.ppermute(send, "seq", pairs)))

    return list(results), go


def finish_sum(total):
    value = total.own
    for got in total.got:
        value = value + got[0].astype(F32)
    return value.reshape(2, total.many, -1, total.cols)


def vector_hops():
    seq = lax.axis_size("seq")
    hops = []
    for bit in range(seq.bit_length() - 1):
        pairs = [(i, i ^ (1 << bit)) for i in range(seq)]
        hops.append(partial(lax.ppermute, axis_name="seq", perm=pairs))
    return hops + [partial(swap, bit=bit) for bit in range(lax.axis_size("dp").bit_length() - 1)]


def exchange(x, d, rows):
    seq = lax.axis_size("seq")
    first = jnp.concatenate([x[:rows], d[:rows]], axis=1)
    last = jnp.concatenate([x[-rows:], d[-rows:]], axis=1)
    from_left = lax.ppermute(last, "seq", [(i, i + 1) for i in range(seq - 1)])
    from_right = lax.ppermute(first, "seq", [(i + 1, i) for i in range(seq - 1)])
    return (from_left, from_right)


def core_split(value):
    pairs = lax.axis_size("dp") // 2
    two, many, depth, cols = value.shape
    shaped = value.reshape(two, many, pairs, 2, depth // (2 * pairs), cols)
    kept = half_of([shaped], 3, 0, True)[0]
    sent = half_of([shaped], 3, 0, False)[0]
    return (kept, sent)


PARTS = 3


def per_device(
    tokens, item_types, first_gain, first_shift, qkv_weight, query_bias, value_bias, attn_weight,
    attn_bias, second_gain, second_shift, expert_up, up_bias, expert_down, down_bias, cotangent,
):
    tok, width = tokens.shape
    dp, seq = lax.axis_size("dp"), lax.axis_size("seq")
    rows = capacity(tok)
    chunk = width // dp
    chunk = chunk if chunk % 16 == 0 else 0
    bits = [(lax.axis_index("dp") >> bit) & 1 for bit in range(dp.bit_length() - 1)]
    place = jnp.stack([lax.axis_index("seq")] + bits).astype(jnp.int32)
    left, right = exchange(tokens, cotangent, HALO)
    x, g, info = sort_rows(place, item_types, tokens, cotangent, rows, tok * seq)
    x, g, left, right = lax.optimization_barrier((x, g, left, right))
    x, g = patch_rows(info, left, right, x, g, tok)

    h, qkv = project_qkv(info, x, first_gain, first_shift, qkv_weight, query_bias, value_bias)
    att = attend(info, qkv)
    mid, h2 = middle_norm(info, x, att, attn_weight, attn_bias, second_gain, second_shift)

    flight = Flight()

    def window(sums, behind=None):
        late = [total for total in sums if total.seq_left]
        steps = [total for total in sums if total.more()]
        closing = [total for total in sums if not total.more() and total.own is None]
        if not (late or steps or closing):
            return info
        turn = place if behind is None else lax.optimization_barrier((place, behind))[0]
        ready, go = advance(
            turn, steps, closing[0] if closing else None, late[0] if late else None
        )
        gate, ready = lax.optimization_barrier((info, ready))
        go(ready)
        return gate

    sums, up_biases, acts, dups = [], [], [], []
    gate = info
    for part in range(PARTS):
        results = run_hidden(part, PARTS, gate, h2, g, expert_up, up_bias, expert_down, chunk)
        results = flight.land(*results)
        bias, act, dup = results[-3:]
        up_biases.append(bias)
        acts.append(act)
        dups.append(dup)
        if chunk:
            kept, sent = results[:2]
        else:
            kept, sent = core_split(results[0])
        new = Sum(flight, kept, sent)
        new.ways = 2
        gate = window(sums)
        sums.append(new)
    results = finish_experts(
        gate, mid, g, acts, dups, expert_up, expert_down, second_gain, down_bias, attn_weight
    )
    row_sums, mixed, dx, proj, datt = flight.land(*results)
    gate = window(sums)
    dq, dk, dv = flight.land(*attend_back(gate, qkv, datt))
    gate = window(sums)
    kept, sent = flight.land(*projection_grads(gate, dq, dk, dv, proj, h, att, dp, seq))
    last = Sum(flight, kept, sent)
    gate = window(sums)
    results = last_norm(gate, x, dx, dq, dk, dv, first_gain, qkv_weight, row_sums, up_biases)
    grad_x, packed = flight.land(*results)

    hops = vector_hops()

    def hop(packed, moved=None):
        packed = packed if moved is None else packed + moved[0]
        return packed, flight.start(hops.pop(0)(packed))

    packed, moved = hop(packed)
    gate = window([last])
    while any(total.own is None or total.seq_left for total in sums):
        gate = window(sums, gate)
    m_own, g_own, left, right = flight.land(*unsort_rows(gate, mixed, grad_x, tok))
    expert_sums = [finish_sum(total) for total in sums]
    packed, moved = hop(packed, moved)
    later = []
    while last.own is None:
        window([last])
        if not later:
            left, right, moved[0] = lax.optimization_barrier((left, right, moved[0]))
            packed, moved = hop(packed, moved)
            later.append(moved)
            to_left = lax.ppermute(left, "seq", [(i + 1, i) for i in range(seq - 1)])
            to_right = lax.ppermute(right, "seq", [(i, i + 1) for i in range(seq - 1)])
            from_right, from_left = flight.start(to_left), flight.start(to_right)
            later += [from_right, from_left]
        if last.own is None:
            expert_sums = flight.land(*expert_sums, later=later)

    def merge(own, at):
        cols = slice(at, at + width)
        own = own.at[:HALO].add(from_left[0][:, cols].astype(own.dtype))
        return own.at[tok - HALO :].add(from_right[0][:, cols].astype(own.dtype))

    mixed_out, grad_out = flight.land(merge(m_own, width), merge(g_own, 0), later=[moved])
    while hops:
        packed, moved = hop(packed, moved)
    packed = packed + moved[0]
    last_sums = finish_sum(last)

    own = width // (dp * seq)
    rank = lax.axis_index("dp") * seq + lax.axis_index("seq")
    vectors = lax.dynamic_slice(packed, (0, rank * own), (14, own))
    tile = up_biases[0].shape[2]
    up_total = packed[14 : 14 + PARTS * EXPERTS, :tile].reshape(PARTS, EXPERTS, tile)
    sum_up = jnp.concatenate([total[0] for total in expert_sums], axis=-1)
    sum_down = jnp.concatenate([total[1] for total in expert_sums], axis=-1).swapaxes(1, 2)
    last_sums = jnp.concatenate([last_sums[0, 0], last_sums[1, 0]], axis=1).T

    return (
        mixed_out,
        grad_out,
        vectors[0],
        vectors[1],
        last_sums[:, : 3 * own],
        vectors[2],
        vectors[3],
        last_sums[:, 3 * own :],
        vectors[4],
        vectors[5:8],
        vectors[8:11],
        sum_up,
        up_total.swapaxes(0, 1).reshape(EXPERTS, -1),
        sum_down,
        vectors[11:14],
    )


def solution(mesh):
    split = P(("dp", "seq"))
    in_specs = (P(("dp", "seq"), None), P("dp", None)) + (P(),) * 13 + (P(("dp", "seq"), None),)
    out_specs = (
        P(("dp", "seq"), None),
        P(("dp", "seq"), None),
        split,
        split,
        P(None, ("dp", "seq")),
        split,
        split,
        P(None, ("dp", "seq")),
        split,
        P(None, ("dp", "seq")),
        P(None, ("dp", "seq")),
        P(None, ("dp", "seq"), None),
        P(),
        P(None, None, ("dp", "seq")),
        P(None, ("dp", "seq")),
    )
    return jax.shard_map(
        per_device, mesh=mesh, in_specs=in_specs, out_specs=out_specs, check_vma=False
    )
```

```python
from functools import partial

import jax
import jax.numpy as jnp
from jax import lax
from jax.experimental import pallas as pl
from jax.experimental.pallas import tpu as pltpu
from jax.sharding import PartitionSpec as P

HD = 64
EXPERTS = 3
IMG_LEN = 197
TXT_LEN = 64
LENS = (IMG_LEN, TXT_LEN, IMG_LEN + TXT_LEN)
SLOTS = (208, 64, 272)
TXT_PAIR = 128
PAD_ROWS = 384
HALO = 144
ROW = 128
BLK = 256

EPS = 1e-05
NEG = -1e30
VMEM = 60 << 20
F32 = jnp.float32
BF16 = jnp.bfloat16

N_IMG, N_TXT, N_BOTH, N_PAD = 0, 1, 2, 3
G_IMG, G_TXT, G_BOTH, G_PAD, G_END = 4, 5, 6, 7, 8
PAD_LEN, OWN_N, CORE = 9, 10, 11
TABLE = 16
INFO = 256


def nn(a, b):
    return lax.dot_general(a, b, (((1,), (0,)), ((), ())), preferred_element_type=F32)


def nt(a, b):
    return lax.dot_general(a, b, (((1,), (1,)), ((), ())), preferred_element_type=F32)


def tn(a, b):
    return lax.dot_general(a, b, (((0,), (0,)), ((), ())), preferred_element_type=F32)


def cost(microseconds):
    return pl.CostEstimate(flops=int(microseconds * 1e10), bytes_accessed=0, transcendentals=0)


SMEM_SPEC = pl.BlockSpec(memory_space=pltpu.SMEM)


def up_to(value, unit):
    return ((value + unit - 1) // unit) * unit


def normalize(v):
    mean = jnp.mean(v, axis=-1, keepdims=True)
    cent = v - mean
    var = jnp.mean(cent * cent, axis=-1, keepdims=True)
    inverse = lax.rsqrt(var + EPS)
    return (cent * inverse, inverse)


def norm_back(grad, normed, inverse):
    inner = jnp.mean(grad * normed, axis=-1, keepdims=True)
    return inverse * (grad - jnp.mean(grad, axis=-1, keepdims=True) - normed * inner)


def capacity(tok):
    rows = tok + LENS[2] - 1
    best = 0
    for images in range(rows // LENS[0] + 1):
        for both in range((rows - images * LENS[0]) // LENS[2] + 1):
            left = rows - images * LENS[0] - both * LENS[2]
            for pad in (0, 1):
                spare = left - pad * (1 + LENS[2] // 2)
                if spare < 0:
                    continue
                texts = spare // LENS[1]
                for count in range(texts + 1):
                    total = (
                        up_to(images * SLOTS[0], ROW)
                        + up_to(count * SLOTS[1], ROW)
                        + up_to(both * SLOTS[2], ROW)
                        + pad * PAD_ROWS
                    )
                    best = max(best, total)
    return up_to(best, BLK)


def gather_rows(info, wins, outs):
    for out in outs:
        out[...] = jnp.zeros_like(out)

    def place(index, carry):
        source = info[TABLE + 3 * index]
        target = pl.multiple_of(info[TABLE + 3 * index + 1], 16)
        kind = info[TABLE + 3 * index + 2]
        begin = pl.multiple_of((source // 16) * 16, 16)
        shift = source - begin
        for which in range(EXPERTS):
            slot = SLOTS[which]
            fits = (kind == which) if which < 2 else (kind >= 2)
            size = LENS[which] if which < 2 else jnp.where(kind == 2, LENS[2], info[PAD_LEN])

            @pl.when(fits)
            def _(slot=slot, size=size):
                rows = lax.broadcasted_iota(jnp.int32, (slot, slot + 16), 0)
                cols = lax.broadcasted_iota(jnp.int32, (slot, slot + 16), 1)
                chosen = ((cols == rows + shift) & (rows < size)).astype(F32).astype(BF16)
                for win, out in zip(wins, outs):
                    value = nn(chosen, win[pl.ds(begin, slot + 16), :])
                    out[pl.ds(target, slot), :] = value.astype(BF16)

        return carry

    lax.fori_loop(0, info[OWN_N], place, 0)


def sort_kernel(tok, group, place_ref, types, x_own, d_own, x_out, d_out, info, x_win, d_win):
    items = types.shape[1]
    low = place_ref[0] * tok
    info[CORE] = place_ref[1]
    width = x_own.shape[1]
    for win, own_rows in ((x_win, x_own), (d_win, d_own)):
        rest = win.shape[0] - (HALO + tok)
        win[pl.ds(0, HALO), :] = jnp.zeros((HALO, width), BF16)
        win[pl.ds(HALO, tok), :] = own_rows[...]
        win[pl.ds(HALO + tok, rest), :] = jnp.zeros((rest, width), BF16)

    def length(kind):
        return jnp.where(
            kind == 0, LENS[0], jnp.where(kind == 1, LENS[1], jnp.where(kind == 2, LENS[2], 0))
        )

    def owned(start, size):
        middle = (start + start + size) // 2
        return (middle >= low) & (middle < low + tok) & (size > 0)

    def count(index, carry):
        start, images, texts, boths = carry
        kind = types[0, index]
        size = length(kind)
        mine = owned(start, size)
        return (
            start + size,
            images + jnp.where(mine & (kind == 0), 1, 0),
            texts + jnp.where(mine & (kind == 1), 1, 0),
            boths + jnp.where(mine & (kind == 2), 1, 0),
        )

    zero = jnp.int32(0)
    total, images, texts, boths = lax.fori_loop(0, items, count, (zero, zero, zero, zero))
    pad_len = group - total
    pad = owned(total, pad_len)
    g_txt = up_to(images * SLOTS[0], ROW)
    g_both = g_txt + up_to(texts * SLOTS[1], ROW)
    g_pad = g_both + up_to(boths * SLOTS[2], ROW)
    info[N_IMG] = images
    info[N_TXT] = texts
    info[N_BOTH] = boths
    info[N_PAD] = jnp.where(pad, 1, 0)
    info[G_IMG] = zero
    info[G_TXT] = g_txt
    info[G_BOTH] = g_both
    info[G_PAD] = g_pad
    info[G_END] = g_pad + jnp.where(pad, PAD_ROWS, 0)
    info[PAD_LEN] = pad_len

    def note(own, source, target, kind):
        info[TABLE + 3 * own] = source
        info[TABLE + 3 * own + 1] = target
        info[TABLE + 3 * own + 2] = kind

    def place(index, carry):
        start, images, texts, boths, own = carry
        kind = types[0, index]
        size = length(kind)
        mine = owned(start, size)

        @pl.when(mine)
        def _():
            target = jnp.where(
                kind == 0,
                images * SLOTS[0],
                jnp.where(kind == 1, g_txt + texts * SLOTS[1], g_both + boths * SLOTS[2]),
            )
            note(own, start - low + HALO, target, kind)

        return (
            start + size,
            images + jnp.where(mine & (kind == 0), 1, 0),
            texts + jnp.where(mine & (kind == 1), 1, 0),
            boths + jnp.where(mine & (kind == 2), 1, 0),
            own + jnp.where(mine, 1, 0),
        )

    own = lax.fori_loop(0, items, place, (zero, zero, zero, zero, zero))[-1]

    @pl.when(pad)
    def _():
        note(own, total - low + HALO, g_pad, jnp.int32(EXPERTS))

    info[OWN_N] = own + jnp.where(pad, 1, 0)
    gather_rows(info, (x_win, d_win), (x_out, d_out))


def sort_rows(place, types, x, d, rows, group):
    tok, width = x.shape
    vmem = pl.BlockSpec(memory_space=pltpu.VMEM)
    return pl.pallas_call(
        partial(sort_kernel, tok, group),
        out_shape=[
            jax.ShapeDtypeStruct((rows, width), BF16),
            jax.ShapeDtypeStruct((rows, width), BF16),
            jax.ShapeDtypeStruct((INFO,), jnp.int32),
        ],
        in_specs=[SMEM_SPEC, SMEM_SPEC] + [vmem] * 2,
        out_specs=[vmem, vmem, SMEM_SPEC],
        scratch_shapes=[pltpu.VMEM((tok + HALO + 288, width), BF16)] * 2,
        compiler_params=pltpu.CompilerParams(vmem_limit_bytes=VMEM),
        cost_estimate=cost(11),
        name="sort_rows",
    )(place, types, x, d)


def patch_ends(tok, info, left, right, arrived, visits):
    count = info[OWN_N]

    def for_slots(end, visit):
        index = jnp.maximum(count - 1, 0) if end else 0
        source = info[TABLE + 3 * index]
        target = pl.multiple_of(info[TABLE + 3 * index + 1], 16)
        kind = info[TABLE + 3 * index + 2]
        size = jnp.where(kind == 0, LENS[0], jnp.where(kind == 1, LENS[1], LENS[2]))
        size = jnp.where(kind == EXPERTS, info[PAD_LEN], size)
        over = (source + size > HALO + tok) if end else (source < HALO)
        for which in range(EXPERTS):
            slot = SLOTS[which]
            fits = (kind == which) if which < 2 else (kind >= 2)

            @pl.when(over & (count > 0) & fits)
            def _(slot=slot):
                def rows():
                    into = lax.broadcasted_iota(jnp.int32, (slot, HALO), 0)
                    cols = lax.broadcasted_iota(jnp.int32, (slot, HALO), 1)
                    shift = source - HALO - tok if end else source
                    chosen = ((cols == into + shift) & (into < size)).astype(F32).astype(BF16)
                    return nn(chosen, (right if end else left)[...])

                visit(end, slot, pl.ds(target, slot), rows)

    for number, visit in enumerate(visits):
        if number == arrived[0]:
            arrived[1]()
        for end in range(2):
            for_slots(end, visit)


def forward_kernel(
    tok, info, left, right, x_in, d_in, gain, shift, qkv_weight, query_bias, value_bias,
    attn_weight, attn_bias, gains, shifts,
    x_out, d_out, h_out, qkv_out, att_out, mid_out, h2_out,
    x_v, qkv_v, att_v, w_qkv, w_attn, d_v, h_v, mid_v, h2_v,
    load_sems, patch_sems, h_sems, qkv_sems, att_sems, mid_sems, h2_sems,
):
    width = x_v.shape[1]
    blocks = (info[G_END] + BLK - 1) // BLK
    load_x = pltpu.make_async_copy(x_in, x_v, load_sems.at[0])
    load_qkv = pltpu.make_async_copy(qkv_weight, w_qkv, load_sems.at[1])
    load_attn = pltpu.make_async_copy(attn_weight, w_attn, load_sems.at[2])
    load_x.start()
    load_qkv.start()

    def each(low, high, visit):
        def body(index, carry):
            visit(index)
            return carry

        lax.fori_loop(low, high, body, 0)

    def d_copy(end, slot, at, inward):
        near, far = d_v.at[end, pl.ds(0, slot), :], d_out.at[at, :]
        source, target = (far, near) if inward else (near, far)
        return pltpu.make_async_copy(source, target, patch_sems.at[end, 0])

    def x_copy(end, at):
        return pltpu.make_async_copy(x_v.at[at, :], x_out.at[at, :], patch_sems.at[end, 1])

    def fetch(end, slot, at, rows):
        d_copy(end, slot, at, True).start()

    def add(end, slot, at, rows):
        added = rows()
        x_v[at, :] = (x_v[at, :].astype(F32) + added[:, :width]).astype(BF16)
        x_copy(end, at).start()
        d_copy(end, slot, at, True).wait()
        here = pl.ds(0, slot)
        d_v[end, here, :] = (d_v[end, here, :].astype(F32) + added[:, width:]).astype(BF16)
        d_copy(end, slot, at, False).start()

    patch_ends(tok, info, left, right, (1, load_x.wait), (fetch, add))
    load_attn.start()
    load_qkv.wait()

    def h_copy(index):
        at = pl.ds(pl.multiple_of(index * BLK, BLK), BLK)
        return pltpu.make_async_copy(h_v.at[index % 2], h_out.at[at, :], h_sems.at[index % 2])

    def qkv_copy(index):
        at = pl.ds(pl.multiple_of(index * BLK, BLK), BLK)
        return pltpu.make_async_copy(qkv_v.at[at, :], qkv_out.at[at, :], qkv_sems.at[index])

    def project(index):
        at = pl.ds(pl.multiple_of(index * BLK, BLK), BLK)
        normed, _ = normalize(x_v[at, :].astype(F32))
        hidden = (normed * gain[...] + shift[...]).astype(BF16)

        @pl.when(index >= 2)
        def _():
            h_copy(index - 2).wait()

        h_v[index % 2] = hidden
        h_copy(index).start()
        for part in range(3):
            cols = pl.ds(part * width, width)
            value = nn(hidden, w_qkv[:, cols])
            if part == 0:
                value = (value + query_bias[...]) * (HD ** (-0.5))
            if part == 2:
                value = value + value_bias[...]
            qkv_v[at, cols] = value.astype(BF16)
        qkv_copy(index).start()

    each(0, blocks, project)

    att_v[...] = jnp.zeros_like(att_v)

    masks = head_masks(HEADS)
    wide = HEADS * HD

    def visit(start, slot, bias):
        at = pl.ds(start, slot)
        for group in range(width // wide):
            cols = [pl.ds(part * width + group * wide, wide) for part in range(3)]
            q, k, v = [qkv_v[at, one] for one in cols]
            scores = nt(stacked(k, masks), q)
            probs = []
            for head in range(HEADS):
                prob = softmax_cols(scores[head * slot : (head + 1) * slot], bias)
                probs.append(prob.astype(BF16))
            att_v[at, cols[0]] = tn(jnp.concatenate(probs), stacked(v, masks)).astype(BF16)

    for_items(info, visit)
    load_attn.wait()

    def block_copies(index):
        at = pl.ds(pl.multiple_of(index * BLK, BLK), BLK)
        slot = index % 2
        return (
            pltpu.make_async_copy(mid_v.at[slot], mid_out.at[at, :], mid_sems.at[slot]),
            pltpu.make_async_copy(h2_v.at[slot], h2_out.at[at, :], h2_sems.at[slot]),
        )

    def att_copy(index):
        at = pl.ds(pl.multiple_of(index * BLK, BLK), BLK)
        return pltpu.make_async_copy(att_v.at[at, :], att_out.at[at, :], att_sems.at[index])

    each(0, blocks, lambda index: att_copy(index).start())

    def middle(index):
        slot = index % 2
        row = index * BLK

        @pl.when(index >= 2)
        def _():
            for copy in block_copies(index - 2):
                copy.wait()

        at = pl.ds(pl.multiple_of(row, BLK), BLK)
        value = x_v[at, :].astype(F32) + (nn(att_v[at, :], w_attn[...]) + attn_bias[...])
        mid_v[slot] = value
        normed, _ = normalize(value)
        for part in range(BLK // ROW):
            which = pl.ds(jnp.minimum(group_of(info, row + part * ROW), EXPERTS - 1), 1)
            here = normed[part * ROW : (part + 1) * ROW]
            here = (here * gains[which, :] + shifts[which, :]).astype(BF16)
            h2_v[slot, pl.ds(part * ROW, ROW), :] = here
        for copy in block_copies(index):
            copy.start()

    each(0, blocks, middle)

    def wait_rows(end, slot, at, rows):
        x_copy(end, at).wait()
        d_copy(end, slot, at, False).wait()

    patch_ends(tok, info, left, right, (-1, None), (wait_rows,))
    each(0, blocks, lambda index: qkv_copy(index).wait())
    each(0, blocks, lambda index: att_copy(index).wait())
    for back in (2, 1):

        @pl.when(blocks >= back)
        def _(back=back):
            h_copy(blocks - back).wait()
            for copy in block_copies(blocks - back):
                copy.wait()


def forward_rows(
    info, left, right, x, d, gain, shift, qkv_weight, query_bias, value_bias, attn_weight,
    attn_bias, gains, shifts, tok,
):
    rows, width = x.shape
    vmem = pl.BlockSpec(memory_space=pltpu.VMEM)
    any_spec = pl.BlockSpec(memory_space=pl.ANY)
    low = lambda cols: jax.ShapeDtypeStruct((rows, cols), BF16)
    blocks = rows // BLK
    return pl.pallas_call(
        partial(forward_kernel, tok),
        out_shape=[
            low(width),
            low(width),
            low(width),
            low(3 * width),
            low(width),
            jax.ShapeDtypeStruct((rows, width), F32),
            low(width),
        ],
        in_specs=[SMEM_SPEC, vmem, vmem, any_spec, any_spec, vmem, vmem, any_spec, vmem, vmem]
        + [any_spec, vmem, vmem, vmem],
        out_specs=[any_spec] * 7,
        scratch_shapes=[
            pltpu.VMEM((rows, width), BF16),
            pltpu.VMEM((rows, 3 * width), BF16),
            pltpu.VMEM((rows, width), BF16),
            pltpu.VMEM(qkv_weight.shape, BF16),
            pltpu.VMEM(attn_weight.shape, BF16),
            pltpu.VMEM((2, SLOTS[2], width), BF16),
            pltpu.VMEM((2, BLK, width), BF16),
            pltpu.VMEM((2, BLK, width), F32),
            pltpu.VMEM((2, BLK, width), BF16),
            pltpu.SemaphoreType.DMA((3,)),
            pltpu.SemaphoreType.DMA((2, 2)),
            pltpu.SemaphoreType.DMA((2,)),
            pltpu.SemaphoreType.DMA((blocks,)),
            pltpu.SemaphoreType.DMA((blocks,)),
            pltpu.SemaphoreType.DMA((2,)),
            pltpu.SemaphoreType.DMA((2,)),
        ],
        input_output_aliases={3: 0, 4: 1},
        compiler_params=pltpu.CompilerParams(vmem_limit_bytes=VMEM),
        cost_estimate=cost(45),
        name="forward_rows",
    )(
        info, left, right, x, d, gain, shift, qkv_weight, query_bias, value_bias, attn_weight,
        attn_bias, gains, shifts,
    )


def unsort_kernel(info, rows, own_rows, left, right, win):
    tok = own_rows.shape[0]
    win[...] = jnp.zeros_like(win)

    def place(index, carry):
        source = info[TABLE + 3 * index]
        target = pl.multiple_of(info[TABLE + 3 * index + 1], 16)
        kind = info[TABLE + 3 * index + 2]
        begin = pl.multiple_of((source // 16) * 16, 16)
        shift = source - begin
        for which in range(EXPERTS):
            slot = SLOTS[which]
            fits = (kind == which) if which < 2 else (kind >= 2)
            size = LENS[which] if which < 2 else jnp.where(kind == 2, LENS[2], info[PAD_LEN])

            @pl.when(fits)
            def _(slot=slot, size=size):
                into = lax.broadcasted_iota(jnp.int32, (slot + 16, slot), 0)
                cols = lax.broadcasted_iota(jnp.int32, (slot + 16, slot), 1)
                chosen = ((into == cols + shift) & (cols < size)).astype(F32).astype(BF16)
                value = rows[pl.ds(target, slot), :]
                to = pl.ds(begin, slot + 16)
                high = value.astype(BF16)
                if rows.dtype == BF16:
                    win[to, :] += nn(chosen, high)
                else:
                    rest = (value - high.astype(F32)).astype(BF16)
                    win[to, :] += nn(chosen, high) + nn(chosen, rest)

        return carry

    lax.fori_loop(0, info[OWN_N], place, 0)
    for part, begin in ((left, 0), (own_rows, HALO), (right, HALO + tok)):
        part[...] = win[pl.ds(begin, part.shape[0]), :].astype(part.dtype)


def unsort_rows(info, rows, tok):
    width = rows.shape[1]
    vmem = pl.BlockSpec(memory_space=pltpu.VMEM)
    return pl.pallas_call(
        unsort_kernel,
        out_shape=[
            jax.ShapeDtypeStruct((tok, width), rows.dtype),
            jax.ShapeDtypeStruct((HALO, width), BF16),
            jax.ShapeDtypeStruct((HALO, width), BF16),
        ],
        in_specs=[SMEM_SPEC, vmem],
        out_specs=[vmem] * 3,
        scratch_shapes=[pltpu.VMEM((tok + HALO + 288, width), F32)],
        compiler_params=pltpu.CompilerParams(vmem_limit_bytes=VMEM),
        cost_estimate=cost(0.1),
        name="unsort_rows",
    )(info, rows)


def full(shape):
    return pl.BlockSpec(shape, lambda *_: (0,) * len(shape))


def held(shape):
    return pl.BlockSpec(shape, lambda *_: (0,) * len(shape), pipeline_mode=pl.Buffered(1))


HEADS, BACK_HEADS = 2, 4


def softmax_cols(scores, bias):
    masked = scores + bias
    expo = jnp.exp(masked - jnp.max(masked, axis=0, keepdims=True))
    return expo * (1.0 / jnp.sum(expo, axis=0, keepdims=True))


def for_items(info, visit):
    def cut(slot, size):
        return jnp.where(lax.broadcasted_iota(jnp.int32, (slot, 1), 0) < size, 0.0, NEG)

    def image(index, carry):
        slot = SLOTS[0]
        visit(pl.multiple_of(index * slot, 16), slot, cut(slot, LENS[0]))
        return carry

    def text(index, carry):
        slot = TXT_PAIR
        rows = lax.broadcasted_iota(jnp.int32, (slot, slot), 0) // TXT_LEN
        cols = lax.broadcasted_iota(jnp.int32, (slot, slot), 1) // TXT_LEN
        start = pl.multiple_of(info[G_TXT] + index * slot, ROW)
        visit(start, slot, jnp.where(rows == cols, 0.0, NEG))
        return carry

    def both(index, carry):
        slot = SLOTS[2]
        real = index < info[N_BOTH]
        start = jnp.where(real, info[G_BOTH] + index * slot, info[G_PAD])
        size = jnp.where(real, LENS[2], info[PAD_LEN])
        visit(pl.multiple_of(start, 16), slot, cut(slot, size))
        return carry

    lax.fori_loop(0, info[N_IMG], image, 0)
    lax.fori_loop(0, (info[N_TXT] + 1) // 2, text, 0)
    lax.fori_loop(0, info[N_BOTH] + info[N_PAD], both, 0)


def head_masks(heads):
    lanes = lax.broadcasted_iota(jnp.int32, (1, heads * HD), 1) // HD
    return [lanes == head for head in range(heads)]


def stacked(value, masks):
    return jnp.concatenate([jnp.where(mask, value, 0) for mask in masks], axis=0)


def own_columns(value, masks):
    rows = value.shape[0] // len(masks)
    result = value[:rows]
    for head in range(1, len(masks)):
        result = jnp.where(masks[head], value[head * rows : (head + 1) * rows], result)
    return result


def attend_back_kernel(info, query, key, value, grad, dq_out, dk_out, dv_out):
    for out in (dq_out, dk_out, dv_out):
        out[...] = jnp.zeros_like(out)
    masks = head_masks(BACK_HEADS)
    wide = BACK_HEADS * HD

    def visit(start, slot, bias):
        at = pl.ds(start, slot)
        for group in range(query.shape[1] // wide):
            cols = pl.ds(group * wide, wide)
            q, k, v, g = query[at, cols], key[at, cols], value[at, cols], grad[at, cols]
            keys = stacked(k, masks)
            scores = nt(keys, q)
            grad_probs = nt(stacked(v, masks), g)
            probs, grad_scores = [], []
            for head in range(BACK_HEADS):
                mine = slice(head * slot, (head + 1) * slot)
                prob = softmax_cols(scores[mine], bias)
                product = prob * grad_probs[mine]
                inner = jnp.sum(product, axis=0, keepdims=True)
                probs.append(prob.astype(BF16))
                grad_scores.append((product - prob * inner).astype(BF16))
            probs, grad_scores = jnp.concatenate(probs), jnp.concatenate(grad_scores)
            dq = tn(grad_scores, keys).astype(BF16)
            dq_out[at, cols] = (dq.astype(F32) * HD ** (-0.5)).astype(BF16)
            dk_out[at, cols] = own_columns(nn(grad_scores, q), masks).astype(BF16)
            dv_out[at, cols] = own_columns(nn(probs, g), masks).astype(BF16)

    for_items(info, visit)


def attend_back(info, qkv, grad):
    rows = qkv.shape[0]
    width = qkv.shape[1] // 3
    spec = pl.BlockSpec((rows, width), lambda p: (0, 0))
    return pl.pallas_call(
        attend_back_kernel,
        grid=(1,),
        out_shape=[jax.ShapeDtypeStruct((rows, width), BF16)] * 3,
        in_specs=[
            SMEM_SPEC,
            spec,
            pl.BlockSpec((rows, width), lambda p: (0, 1)),
            pl.BlockSpec((rows, width), lambda p: (0, 2)),
            spec,
        ],
        out_specs=[spec] * 3,
        compiler_params=pltpu.CompilerParams(vmem_limit_bytes=VMEM),
        cost_estimate=cost(30),
        name="attend_back",
    )(info, qkv, qkv, qkv, grad)


def group_of(info, row):
    return (
        (row >= info[G_TXT]).astype(jnp.int32)
        + (row >= info[G_BOTH]).astype(jnp.int32)
        + (row >= info[G_PAD]).astype(jnp.int32)
    )


def gelu_parts(up):
    size = jnp.abs(up) * (0.5**0.5)
    expo = jnp.exp(-size * size)
    t = 1.0 / (1.0 + 0.3275911 * size)
    poly = 1.061405429 * t - 1.453152027
    poly = poly * t + 1.421413741
    poly = poly * t - 0.284496736
    poly = poly * t + 0.254829592
    tail = 0.5 * (poly * t) * expo
    cdf = jnp.where(up >= 0, 1.0 - tail, tail)
    return (up * cdf, cdf + up * (expo * 0.3989422804014327))


KROWS = 512
COLS = 1


def hidden_kernel(part, chunk, *refs):
    info, h_hbm, g_hbm, up_hbm, b_up, down_hbm = refs[:6]
    refs = refs[6:]
    weight_outs, refs = (refs[:2], refs[2:]) if chunk else (refs[:1], refs[1:])
    bias_out, act_hbm, dup_hbm, left, right, w_up, w_down, acc, stage = refs[:9]
    row_sems, weight_sems, hidden_sems, stage_sems = refs[9:]
    tile = w_up.shape[2]
    cols_at = pl.ds(part * tile, tile)
    bias_out[...] = jnp.zeros_like(bias_out)

    def rows_copies(index):
        at = pl.ds(pl.multiple_of(index * ROW, ROW), ROW)
        return [
            pltpu.make_async_copy(source.at[at, :], left.at[which, at, :], row_sems.at[which, index])
            for which, source in enumerate((h_hbm, g_hbm))
        ]

    def weight_copies(expert):
        return [
            pltpu.make_async_copy(
                up_hbm.at[expert, :, cols_at], w_up.at[expert], weight_sems.at[0, expert]
            ),
            pltpu.make_async_copy(
                down_hbm.at[expert, cols_at, :], w_down.at[expert], weight_sems.at[1, expert]
            ),
        ]

    def hidden_copies(index):
        at = pl.ds(pl.multiple_of(index * ROW, ROW), ROW)
        return [
            pltpu.make_async_copy(right.at[which, at, :], target.at[at, :], hidden_sems.at[which, index])
            for which, target in enumerate((dup_hbm, act_hbm))
        ]

    def stage_copies(slot, expert):
        return [
            pltpu.make_async_copy(
                stage.at[slot, which], out.at[slot, expert], stage_sems.at[slot, which]
            )
            for which, out in enumerate(weight_outs)
        ]

    def each(low, high, visit):
        def body(index, carry):
            visit(index)
            return carry

        lax.fori_loop(low, high, body, 0)

    def start_all(copies):
        for copy in copies:
            copy.start()

    def wait_all(copies):
        for copy in copies:
            copy.wait()

    def prefetch(expert):
        start_all(weight_copies(expert))
        low, high = info[G_IMG + expert] // ROW, info[G_IMG + expert + 1] // ROW
        each(low, high, lambda index: start_all(rows_copies(index)))

    each(0, EXPERTS, prefetch)

    def rows_of(expert, row, size):
        for place in range(size // ROW):
            wait_all(rows_copies(row // ROW + place))
        at = pl.ds(pl.multiple_of(row, ROW), size)
        hidden, grad = left[0, at, :], left[1, at, :]
        wide = tile // COLS
        for turn in range(COLS):
            cols = pl.ds(turn * wide, wide)
            bias = b_up[pl.ds(expert, 1), pl.ds(part * tile + turn * wide, wide)]
            up = nn(hidden, w_up[expert, :, cols]) + bias
            grad_act = nt(grad, w_down[expert, cols, :])
            active, slope = gelu_parts(up)
            grad_up = (slope * grad_act).astype(BF16)
            right[0, at, cols] = grad_up
            right[1, at, cols] = active.astype(BF16)
            bias_out[expert, :, cols] += jnp.sum(grad_up.astype(F32), axis=0, keepdims=True)
        for place in range(size // ROW):
            start_all(hidden_copies(row // ROW + place))

    def put(slot, value):
        if not chunk:
            stage[slot, 0] = value.astype(BF16)
            return
        for pair in range(value.shape[0] // (2 * chunk)):
            for core in range(2):
                first = (2 * pair + core) * chunk
                which = (info[CORE] + core) % 2
                stage[slot, which, pair] = value[first : first + chunk].astype(BF16)

    def one_expert(expert):
        wait_all(weight_copies(expert))
        start = info[G_IMG + expert]
        count = info[G_IMG + expert + 1] - start
        blocks = count // BLK
        each(0, blocks, lambda index: rows_of(expert, start + index * BLK, BLK))

        @pl.when(count % BLK > 0)
        def _():
            rows_of(expert, start + blocks * BLK, ROW)

        def one_side(slot):
            @pl.when(expert > 0)
            def _():
                wait_all(stage_copies(slot, expert - 1))

            def product(local, size):
                at = pl.ds(pl.multiple_of(start + local, ROW), size)
                return tn(left[slot, at, :], right[slot, at, :])

            before = (count - 1) // KROWS

            @pl.when(count == 0)
            def _():
                stage[slot] = jnp.zeros(stage.shape[1:], BF16)

            @pl.when(count > KROWS)
            def _():
                acc[...] = product(0, KROWS)

                def more(index):
                    acc[...] += product(index * KROWS, KROWS)

                each(1, before, more)

            for rest in range(ROW, KROWS + ROW, ROW):
                at_end = (count > 0) & (count - before * KROWS == rest)

                @pl.when(at_end & (before == 0))
                def _(rest=rest):
                    put(slot, product(0, rest))

                @pl.when(at_end & (before > 0))
                def _(rest=rest):
                    put(slot, acc[...] + product(before * KROWS, rest))

            start_all(stage_copies(slot, expert))

        each(0, 2, one_side)

    each(0, EXPERTS, one_expert)
    for slot in range(2):
        wait_all(stage_copies(slot, EXPERTS - 1))
    each(0, info[G_PAD] // ROW, lambda index: wait_all(hidden_copies(index)))


def run_hidden(part, parts, info, h, g, w_up, b_up, w_down, chunk):
    rows, width = h.shape
    tile = w_up.shape[2] // parts
    any_spec = pl.BlockSpec(memory_space=pl.ANY)
    vmem = pl.BlockSpec(memory_space=pltpu.VMEM)
    block = (width // (2 * chunk), chunk, tile) if chunk else (width, tile)
    sides = 2 if chunk else 1
    return pl.pallas_call(
        partial(hidden_kernel, part, chunk),
        out_shape=[jax.ShapeDtypeStruct((2, EXPERTS) + block, BF16)] * sides
        + [
            jax.ShapeDtypeStruct((EXPERTS, 1, tile), F32),
            jax.ShapeDtypeStruct((rows, tile), BF16),
            jax.ShapeDtypeStruct((rows, tile), BF16),
        ],
        in_specs=[SMEM_SPEC, any_spec, any_spec, any_spec, vmem, any_spec],
        out_specs=[any_spec] * sides + [vmem, any_spec, any_spec],
        scratch_shapes=[
            pltpu.VMEM((2, rows, width), BF16),
            pltpu.VMEM((2, rows, tile), BF16),
            pltpu.VMEM((EXPERTS, width, tile), BF16),
            pltpu.VMEM((EXPERTS, tile, width), BF16),
            pltpu.VMEM((width, tile), F32),
            pltpu.VMEM((2, sides) + block, BF16),
            pltpu.SemaphoreType.DMA((2, rows // ROW)),
            pltpu.SemaphoreType.DMA((2, EXPERTS)),
            pltpu.SemaphoreType.DMA((2, rows // ROW)),
            pltpu.SemaphoreType.DMA((2, sides)),
        ],
        compiler_params=pltpu.CompilerParams(vmem_limit_bytes=VMEM),
        cost_estimate=cost(18),
        name="hidden",
    )(info, h, g, w_up, b_up, w_down)


SUMS = 16


def finish_kernel(parts, *refs):
    info = refs[0]
    hbm = refs[1 : 3 + 2 * parts]
    up_hbm, down_hbm, gains, downs, w_attn = refs[3 + 2 * parts : 8 + 2 * parts]
    refs = refs[8 + 2 * parts :]
    sums_out, outs_hbm = refs[0], refs[1:5]
    rows_in, acts, dups = refs[5:7], refs[7 : 7 + parts], refs[7 + parts : 7 + 2 * parts]
    refs = refs[7 + 2 * parts :]
    held_out, (w_up, w_down, lower_s, hidden_s) = refs[:4], refs[4:8]
    row_sems, act_sems, out_sems, weight_sems = refs[8:]
    width = lower_s.shape[2]

    groups = range(EXPERTS + 1)
    counts = [info[G_IMG + group + 1] - info[G_IMG + group] for group in groups]
    firsts = [jnp.int32(0)]
    for group in groups:
        firsts.append(firsts[-1] + (counts[group] + BLK - 1) // BLK)
    total = firsts[-1]

    def block_of(index):
        group = sum([(index >= firsts[k]).astype(jnp.int32) for k in groups[1:]])
        first, start, count = firsts[0], info[G_IMG], counts[0]
        for k in groups[1:]:
            first = jnp.where(group == k, firsts[k], first)
            start = jnp.where(group == k, info[G_IMG + k], start)
            count = jnp.where(group == k, counts[k], count)
        local = (index - first) * BLK
        return group, start + local, count - local, index == first

    def halves(index, visit):
        group, row, left, _ = block_of(index)
        for half in range(BLK // ROW):

            @pl.when(half * ROW < left)
            def _(half=half):
                visit(half, pl.ds(pl.multiple_of(row + half * ROW, ROW), ROW), group < EXPERTS)

    def in_copies(index, half, at):
        here = pl.ds(half * ROW, ROW)
        rows = [
            pltpu.make_async_copy(
                source.at[at, :], target.at[index % 4, here, :], row_sems.at[index % 4, half, which]
            )
            for which, (source, target) in enumerate(zip(hbm[:2], rows_in))
        ]
        hidden = [
            pltpu.make_async_copy(
                source.at[at, :], target.at[index % 3, here, :], act_sems.at[index % 3, half, which]
            )
            for which, (source, target) in enumerate(zip(hbm[2:], acts + dups))
        ]
        return rows, hidden

    def fetch(index, action):
        def visit(half, at, real):
            rows, hidden = in_copies(index, half, at)
            for copy in rows:
                action(copy)

            @pl.when(real)
            def _():
                for copy in hidden:
                    action(copy)

        halves(index, visit)

    def send(index, action):
        def visit(half, at, real):
            here = pl.ds(half * ROW, ROW)
            for which, (source, target) in enumerate(zip(held_out, outs_hbm)):
                action(
                    pltpu.make_async_copy(
                        source.at[index % 2, here, :],
                        target.at[at, :],
                        out_sems.at[index % 2, half, which],
                    )
                )

        halves(index, visit)

    def start(copy):
        copy.start()

    def wait(copy):
        copy.wait()

    def weights(group, action):
        for which, (source, target) in enumerate(((up_hbm, w_up), (down_hbm, w_down))):
            action(
                pltpu.make_async_copy(
                    source.at[group], target.at[group], weight_sems.at[group, which]
                )
            )

    sums_out[...] = jnp.zeros_like(sums_out)

    @pl.when(total > 0)
    def _():
        fetch(0, start)

    weights(0, start)

    @pl.when(total > 1)
    def _():
        fetch(1, start)

    for expert in range(1, EXPERTS):
        weights(expert, start)

    tile = acts[0].shape[2]

    def block(index, waited):
        group, _, _, _ = block_of(index)
        mine = jnp.minimum(group, EXPERTS - 1)

        @pl.when(index + 2 < total)
        def _():
            fetch(index + 2, start)

        for expert in range(EXPERTS):

            @pl.when((waited <= expert) & (expert <= mine))
            def _(expert=expert):
                weights(expert, wait)

        @pl.when(index < total)
        def _():
            fetch(index, wait)

        @pl.when(index >= 3)
        def _():
            send(index - 3, wait)

        slot, old = index % 2, (index + 1) % 2
        behind = jnp.maximum(index - 1, 0)
        group, _, left, _ = block_of(behind)
        left = jnp.where(index > 0, left, 0)
        real = group < EXPERTS
        which = pl.ds(jnp.minimum(group, EXPERTS - 1), 1)
        mixed, dx, proj_out, datt = held_out
        sub = BLK // 4

        def row_part(turn):
            at = pl.ds(turn * sub, sub)
            valid = turn * sub + lax.broadcasted_iota(jnp.int32, (sub, 1), 0) < left
            middle = jnp.where(valid, rows_in[0][behind % 4, at, :], 0.0)
            grad = jnp.where(valid, rows_in[1][behind % 4, at, :].astype(F32), 0.0)
            lower = jnp.where(real, lower_s[old, at, :] + downs[which, :], 0.0)
            grad_hidden = jnp.where(valid & real, hidden_s[old, at, :], 0.0)
            mixed[old, at, :] = (middle + lower).astype(BF16)
            normed, inverse = normalize(middle)
            grad_middle = grad + norm_back(grad_hidden * gains[which, :], normed, inverse)
            dx[old, at, :] = grad_middle
            proj = grad_middle.astype(BF16)
            proj_out[old, at, :] = proj
            dsel = jnp.where(real, grad, 0.0)
            values = (proj.astype(F32), grad_hidden * normed, grad_hidden, dsel)
            return [jnp.sum(value, axis=0, keepdims=True) for value in values]

        taken = index % 3

        def compute(multiply):
            lower_new = jnp.zeros((BLK, width), F32)
            hidden_new = jnp.zeros((BLK, width), F32)
            sums, turn = [0.0] * 4, 0
            for part in range(parts):
                cols = pl.ds(part * tile, tile)
                if multiply:
                    lower_new += nn(acts[part][taken], w_down[mine, cols, :])
                if turn < 4:
                    sums = [x + y for x, y in zip(sums, row_part(turn))]
                    turn += 1
                if multiply:
                    hidden_new += nt(dups[part][taken], w_up[mine, :, cols])
                if turn < 4:
                    sums = [x + y for x, y in zip(sums, row_part(turn))]
                    turn += 1
            while turn < 4:
                sums = [x + y for x, y in zip(sums, row_part(turn))]
                turn += 1
            if multiply:
                lower_s[slot] = lower_new
                hidden_s[slot] = hidden_new
            datt[old] = nt(proj_out[old], w_attn[...]).astype(BF16)
            sums_out[pl.ds(0, 1), :] += sums[0]
            for place, value in enumerate(sums[1:]):
                at = pl.ds(1 + place * EXPERTS + jnp.minimum(group, EXPERTS - 1), 1)
                sums_out[at, :] += value

        @pl.when(index < total)
        def _():
            compute(True)

        @pl.when(index == total)
        def _():
            compute(False)
        @pl.when(index > 0)
        def _():
            send(index - 1, start)

        return jnp.maximum(waited, mine + 1)

    waited = lax.fori_loop(0, jnp.where(total > 0, total + 1, 0), block, jnp.int32(0))
    for expert in range(EXPERTS):

        @pl.when(waited <= expert)
        def _(expert=expert):
            weights(expert, wait)

    for back in (2, 1):

        @pl.when(total >= back)
        def _(back=back):
            send(total - back, wait)


def finish_experts(info, mid, g, acts, dups, w_up, w_down, gains, downs, w_attn):
    rows, width = mid.shape
    parts = len(acts)
    tile = acts[0].shape[1]
    any_spec = pl.BlockSpec(memory_space=pl.ANY)
    vmem = pl.BlockSpec(memory_space=pltpu.VMEM)
    kinds = (BF16, F32, BF16, BF16)
    return pl.pallas_call(
        partial(finish_kernel, parts),
        out_shape=[jax.ShapeDtypeStruct((SUMS, width), F32)]
        + [jax.ShapeDtypeStruct((rows, width), kind) for kind in kinds],
        in_specs=[SMEM_SPEC] + [any_spec] * (4 + 2 * parts) + [vmem] * 3,
        out_specs=[vmem] + [any_spec] * 4,
        scratch_shapes=[pltpu.VMEM((4, BLK, width), F32), pltpu.VMEM((4, BLK, width), BF16)]
        + [pltpu.VMEM((3, BLK, tile), BF16)] * (2 * parts)
        + [pltpu.VMEM((2, BLK, width), kind) for kind in kinds]
        + [pltpu.VMEM(w_up.shape, BF16), pltpu.VMEM(w_down.shape, BF16)]
        + [pltpu.VMEM((2, BLK, width), F32)] * 2
        + [
            pltpu.SemaphoreType.DMA((4, BLK // ROW, 2)),
            pltpu.SemaphoreType.DMA((3, BLK // ROW, 2 * parts)),
            pltpu.SemaphoreType.DMA((2, BLK // ROW, 4)),
            pltpu.SemaphoreType.DMA((EXPERTS, 2)),
        ],
        compiler_params=pltpu.CompilerParams(vmem_limit_bytes=VMEM),
        cost_estimate=cost(30),
        name="finish_experts",
    )(info, mid, g, *acts, *dups, w_up, w_down, gains, downs, w_attn)


def weights_kernel(dp, seq, info, dq, dk, dv, proj, h, att, send_out, keep_out, acc, attn_acc):
    index = pl.program_id(0)

    @pl.when(index == 0)
    def _():
        acc[...] = jnp.zeros_like(acc)
        attn_acc[...] = jnp.zeros_like(attn_acc)

    @pl.when(index * BLK < info[G_END])
    def _():
        row = index * BLK + lax.broadcasted_iota(jnp.int32, (BLK, 1), 0)
        real = row < info[G_END]
        hidden = h[...]
        width = hidden.shape[1]
        for part, grad in enumerate((dq, dk, dv)):
            acc[pl.ds(part * width, width), :] += tn(grad[...], hidden)
        attn_acc[...] += tn(
            jnp.where(real, proj[...], jnp.zeros_like(proj)),
            jnp.where(real, att[...], jnp.zeros_like(att)),
        )

    @pl.when(index == pl.num_programs(0) - 1)
    def _():
        width = attn_acc.shape[0]
        own = width // (dp * seq)
        half = width // 2
        for out, core in ((keep_out, info[CORE]), (send_out, 1 - info[CORE])):
            for pair in range(dp // 2):
                for place in range(seq):
                    device = (2 * pair + core) * seq + place
                    first = pl.ds(pl.multiple_of(device * 3 * own, 8), 3 * own)
                    second = pl.ds(pl.multiple_of(device * own, 8), own)
                    value = jnp.concatenate([acc[first, :], attn_acc[second, :]], axis=0)
                    value = value.astype(BF16)
                    at = pl.ds(place * 4 * own, 4 * own)
                    for lane in range(2):
                        out[lane, 0, pair, at, :] = value[:, lane * half : (lane + 1) * half]


def weights_kernel_plain(info, dq, dk, dv, proj, h, att, qkv_out, attn_out, acc, attn_acc):
    index = pl.program_id(0)

    @pl.when(index == 0)
    def _():
        acc[...] = jnp.zeros_like(acc)
        attn_acc[...] = jnp.zeros_like(attn_acc)

    @pl.when(index * BLK < info[G_END])
    def _():
        row = index * BLK + lax.broadcasted_iota(jnp.int32, (BLK, 1), 0)
        real = row < info[G_END]
        hidden = h[...]
        width = hidden.shape[1]
        for part, grad in enumerate((dq, dk, dv)):
            acc[pl.ds(part * width, width), :] += tn(grad[...], hidden)
        attn_acc[...] += tn(
            jnp.where(real, proj[...], jnp.zeros_like(proj)),
            jnp.where(real, att[...], jnp.zeros_like(att)),
        )

    @pl.when(index == pl.num_programs(0) - 1)
    def _():
        qkv_out[...] = acc[...].astype(BF16)
        attn_out[...] = attn_acc[...].astype(BF16)


def projection_grads(info, dq, dk, dv, proj, h, att, dp, seq):
    rows, width = h.shape
    spec = pl.BlockSpec((BLK, width), lambda i: (i, 0))
    own = width // (dp * seq)
    direct = own % 8 == 0
    if direct:
        shapes = [(2, 1, dp // 2, seq * 4 * own, width // 2)] * 2
        body = partial(weights_kernel, dp, seq)
    else:
        shapes = [(3 * width, width), (width, width)]
        body = weights_kernel_plain
    results = pl.pallas_call(
        body,
        grid=(rows // BLK,),
        out_shape=[jax.ShapeDtypeStruct(shape, BF16) for shape in shapes],
        in_specs=[SMEM_SPEC] + [spec] * 6,
        out_specs=[full(shape) for shape in shapes],
        scratch_shapes=[pltpu.VMEM((3 * width, width), F32), pltpu.VMEM((width, width), F32)],
        compiler_params=pltpu.CompilerParams(vmem_limit_bytes=VMEM),
        cost_estimate=cost(15),
        name="projection_grads",
    )(info, dq, dk, dv, proj, h, att)
    if direct:
        return results[1], results[0]
    d_qkv = results[0].reshape(dp * seq, -1, width)
    d_attn = results[1].reshape(dp * seq, -1, width)
    d_all = jnp.concatenate([d_qkv, d_attn], axis=1).reshape(1, -1, width)
    half = width // 2
    return core_split(jnp.stack([d_all[..., :half], d_all[..., half:]]))


VECTORS = 24


def last_kernel(parts, *refs):
    (info, x, dx, dq, dk, dv, gain, weight, row_sums) = refs[:9]
    biases = refs[9 : 9 + parts]
    out, packed = refs[9 + parts :]
    width = x.shape[1]
    step = pl.program_id(0)

    @pl.when(step == 0)
    def _():
        packed[...] = jnp.zeros_like(packed)
        packed[pl.ds(4, 10), pl.ds(0, width)] = row_sums[pl.ds(0, 10), :]
        for part, bias in enumerate(biases):
            tile = bias.shape[2]
            for expert in range(EXPERTS):
                packed[pl.ds(14 + part * EXPERTS + expert, 1), pl.ds(0, tile)] = bias[expert]

    @pl.when(step * BLK < info[G_END])
    def _():
        hidden = nt(dq[...], weight[:, pl.ds(0, width)])
        hidden += nt(dk[...], weight[:, pl.ds(width, width)])
        hidden += nt(dv[...], weight[:, pl.ds(2 * width, width)])
        normed, inverse = normalize(x[...].astype(F32))
        totals = (hidden * normed, hidden, dq[...].astype(F32), dv[...].astype(F32))
        for place, value in enumerate(totals):
            packed[pl.ds(place, 1), pl.ds(0, width)] += jnp.sum(value, axis=0, keepdims=True)
        out[...] = dx[...] + norm_back(hidden * gain[...], normed, inverse)


def last_norm(info, x, dx, dq, dk, dv, gain, weight, row_sums, biases):
    rows, width = x.shape
    spec = pl.BlockSpec((BLK, width), lambda i: (i, 0))
    cols = max(width, biases[0].shape[2])
    packed = (VECTORS, cols)
    return pl.pallas_call(
        partial(last_kernel, len(biases)),
        grid=(rows // BLK,),
        out_shape=[jax.ShapeDtypeStruct((rows, width), F32), jax.ShapeDtypeStruct(packed, F32)],
        in_specs=[SMEM_SPEC, spec, spec, spec, spec, spec, full(gain.shape), held((width, 3 * width))]
        + [full(row_sums.shape)]
        + [full(bias.shape) for bias in biases],
        out_specs=[spec, full(packed)],
        compiler_params=pltpu.CompilerParams(vmem_limit_bytes=VMEM),
        cost_estimate=cost(14),
        name="last_norm",
    )(info, x, dx, dq, dk, dv, gain, weight, row_sums, *biases)


def swap(value, bit):
    ways = lax.axis_size("dp")
    return lax.ppermute(value, "dp", [(i, i ^ (1 << bit)) for i in range(ways)])


def half_of(parts, axis, bit, mine):
    own = (lax.axis_index("dp") >> bit) & 1
    which = own if mine else 1 - own
    return [lax.dynamic_index_in_dim(part, which, axis, keepdims=False) for part in parts]


DEPTH = 4


def combine_kernel(blocks, arrays, shapes, seq, ways, *refs):
    place, sources = refs[0], refs[1 : 1 + arrays]
    outs = refs[1 + arrays : 1 + arrays + shapes]
    in_buf, out_buf, own_buf, send_buf, total, kept_buf, in_sems, out_sems = refs[1 + arrays + shapes :]
    here = lax.rem(place[0], ways)

    def fetch(index):
        parts, kind, _, _ = blocks[index]
        copies = []
        for part, (which, where) in enumerate(parts):
            source = sources[which].at[where(place)]
            buf = in_buf.at[index % DEPTH, part]
            if isinstance(kind, tuple):
                rows = source.shape[1]
                buf = kept_buf.at[index % DEPTH] if part == 0 else buf
                buf = buf.at[:, pl.ds(0, rows), :]
            copies.append(pltpu.make_async_copy(source, buf, in_sems.at[index % DEPTH, part]))
        return copies

    def send(index):
        _, kind, targets, at = blocks[index]
        slot = index % 2
        if kind == "add":
            held = [out_buf.at[slot]]
        else:
            held = [own_buf.at[slot]] + [send_buf.at[slot, hop] for hop in range(len(targets) - 1)]
        copies = []
        for which, (source, target) in enumerate(zip(held, targets)):
            target = outs[target].at[at]
            if kind != "add":
                source = source.at[:, pl.ds(0, target.shape[1]), :]
            copies.append(pltpu.make_async_copy(source, target, out_sems.at[slot, which]))
        return copies

    for index in range(min(DEPTH - 1, len(blocks))):
        for copy in fetch(index):
            copy.start()
    for index, (parts, kind, targets, _) in enumerate(blocks):
        if index + DEPTH - 1 < len(blocks):
            for copy in fetch(index + DEPTH - 1):
                copy.start()
        for copy in fetch(index):
            copy.wait()
        if index >= 2:
            for copy in send(index - 2):
                copy.wait()
        slot, source = index % 2, index % DEPTH
        if isinstance(kind, tuple):
            rows = outs[targets[0]].shape[2]
            mine = (place[0] >> kind[1]) & 1
            for which, chosen in enumerate((mine, 1 - mine)):
                at = pl.ds(pl.multiple_of(chosen * rows, 8), rows)
                total[:, pl.ds(0, 2 * rows), :] = in_buf[source, 1, :, pl.ds(0, 2 * rows), :].astype(F32)
                value = kept_buf[source, :, at, :] + total[:, at, :]
                if which == 0:
                    own_buf[slot, :, pl.ds(0, rows), :] = value
                else:
                    send_buf[slot, 0, :, pl.ds(0, rows), :] = value.astype(BF16)
        else:
            value = in_buf[source, 0].astype(F32)
            for part in range(1, len(parts)):
                value = value + in_buf[source, part].astype(F32)
            if kind == "add":
                out_buf[slot] = value.astype(BF16)
            else:
                total[...] = value
                rows = total.shape[1] // seq
                for hop in range(ways):
                    for turn in range(seq // ways):
                        at = lax.rem(here + hop, ways) + turn * ways
                        block = total[:, pl.ds(pl.multiple_of(at * rows, 8), rows), :]
                        to = pl.ds(turn * rows, rows)
                        if hop == 0:
                            own_buf[slot, :, to, :] = block
                        else:
                            send_buf[slot, hop - 1, :, to, :] = block.astype(BF16)
        for copy in send(index):
            copy.start()
    for index in range(max(0, len(blocks) - 2), len(blocks)):
        for copy in send(index):
            copy.wait()


class Flight:

    def __init__(self):
        self.cells = []

    def start(self, value):
        cell = [value]
        self.cells.append(cell)
        return cell

    def land(self, *outputs, later=()):
        now = [cell for cell in self.cells if not any(cell is other for other in later)]
        outputs, arrays = lax.optimization_barrier((outputs, [cell[0] for cell in now]))
        for cell, array in zip(now, arrays):
            cell[0] = array
        self.cells = [cell for cell in self.cells if any(cell is other for other in later)]
        return outputs


class Sum:

    def __init__(self, flight, kept, sent):
        self.flight = flight
        self.bits = lax.axis_size("dp").bit_length() - 1
        self.seq = lax.axis_size("seq")
        self.many, self.pairs, self.chunk, self.cols = kept.shape[1:]
        every = list(range(self.bits - 1, 0, -1))
        shape = (2, self.many) + (2,) * len(every) + (self.chunk, self.cols)
        cells = [[kept.reshape(shape)], flight.start(swap(sent, 0).reshape(shape))]
        self.lanes = [[(cell, lane, every, True) for cell in cells] for lane in range(2)]
        self.left = [list(every), list(every)]
        self.ways = self.seq
        self.own = None
        self.seq_left = None

    def more(self):
        return bool(self.left[0])

    def direct(self):
        return (self.chunk // self.seq) % 8 == 0

    def sources(self, lane, other, free, value):
        results = []
        for cell, first, bits, whole in self.lanes[lane]:

            def where(place, first=first, bits=bits, whole=whole):
                chosen = []
                for bit in bits:
                    if bit in free:
                        chosen.append((value >> (len(free) - 1 - free.index(bit))) & 1)
                    elif bit == other:
                        chosen.append(1 - place[1 + bit])
                    else:
                        chosen.append(place[1 + bit])
                if whole:
                    return (first, slice(None)) + tuple(chosen)
                group = 0
                for one in chosen:
                    group = group * 2 + one
                return (first + group,)

            results.append((cell[0], where))
        return results


def advance(place, steps, closing=None, halving=None):
    arrays, blocks, payloads, turns = [], [], {}, []
    model = steps[0] if steps else closing or halving

    def add(parts, kind, targets, at):
        known = []
        for array, where in parts:
            found = [i for i, other in enumerate(arrays) if other is array]
            if not found:
                arrays.append(array)
            known.append((found[0] if found else len(arrays) - 1, where))
        blocks.append((known, kind, targets, at))

    for total in steps:
        for lane in range(2):
            left = total.left[lane]
            bit = min(left) if lane == 0 else max(left)
            left.remove(bit)
            free = list(left)
            count = payloads.get(bit, 0)
            turns.append((total, lane, bit, free, count))
            for value in range(2 ** len(free)):
                add(total.sources(lane, bit, free, value), "add", bit, count)
                count += 1
            payloads[bit] = count
    order = sorted(payloads)
    blocks = [(parts, kind, [order.index(bit)], at) for parts, kind, bit, at in blocks]
    seq, many, chunk, cols = model.seq, model.many, model.chunk, model.cols
    shapes = [jax.ShapeDtypeStruct((payloads[bit], many, chunk, cols), BF16) for bit in order]
    split = closing is not None and closing.direct()
    ways = closing.ways if split else 2
    rows = chunk // ways
    first_end = len(shapes)
    if closing is not None:
        if split:
            shapes.append(jax.ShapeDtypeStruct((2, many, rows, cols), F32))
            shapes += [jax.ShapeDtypeStruct((2, many, rows, cols), BF16)] * (ways - 1)
        else:
            shapes.append(jax.ShapeDtypeStruct((2, many, chunk, cols), BF16))
        targets = list(range(first_end, len(shapes)))
        for lane in range(2):
            add(closing.sources(lane, None, [], 0), "ends" if split else "add", targets, lane)
    first_half = len(shapes)
    if halving is not None:
        seq_bit = halving.seq_left.pop(0)
        half = halving.own.shape[2] // 2
        shapes.append(jax.ShapeDtypeStruct((2, many, half, cols), F32))
        shapes.append(jax.ShapeDtypeStruct((2, many, half, cols), BF16))
        for lane in range(2):
            parts = [(array, lambda place, lane=lane: (lane,)) for array in (halving.own, halving.got[0][0])]
            add(parts, ("half", seq_bit), [first_half, first_half + 1], lane)
    most = max(len(parts) for parts, _, _, _ in blocks)
    end_rows = rows if split else chunk // 2 if halving is not None else 8
    kept_rows = halving.own.shape[2] if halving is not None else 8
    any_spec = pl.BlockSpec(memory_space=pl.ANY)
    results = pl.pallas_call(
        partial(combine_kernel, blocks, len(arrays), len(shapes), seq, ways),
        in_specs=[SMEM_SPEC] + [any_spec] * len(arrays),
        out_specs=[any_spec] * len(shapes),
        out_shape=shapes,
        scratch_shapes=[
            pltpu.VMEM((DEPTH, most, many, chunk, cols), BF16),
            pltpu.VMEM((2, many, chunk, cols), BF16),
            pltpu.VMEM((2, many, end_rows, cols), F32),
            pltpu.VMEM((2, ways - 1, many, end_rows, cols), BF16),
            pltpu.VMEM((many, chunk, cols), F32),
            pltpu.VMEM((DEPTH, many, kept_rows, cols), F32),
            pltpu.SemaphoreType.DMA((DEPTH, most)),
            pltpu.SemaphoreType.DMA((2, ways)),
        ],
        compiler_params=pltpu.CompilerParams(vmem_limit_bytes=VMEM),
        cost_estimate=cost(4),
        name="combine",
    )(place, *arrays)

    def go(results):
        got = {bit: model.flight.start(swap(value, bit)) for bit, value in zip(order, results)}
        for total, lane, bit, free, first in turns:
            total.lanes[lane].append((got[bit], first, free, False))
        if halving is not None:
            halving.own = results[first_half]
            pairs = [(i, i ^ (1 << seq_bit)) for i in range(seq)]
            sent = lax.ppermute(results[first_half + 1], "seq", pairs)
            halving.got = [halving.flight.start(sent)]
        if closing is None:
            return
        parts = results[first_end:first_half]
        if not split:
            half = parts[0].reshape(2, many, seq, chunk // seq, cols)
            here = lax.axis_index("seq")
            parts = [
                lax.dynamic_index_in_dim(half, (here + hop) % seq, 2, keepdims=False)
                for hop in range(seq)
            ]
        closing.own = parts[0].astype(F32)
        closing.seq_left = []
        if split and ways < seq:
            pairs = [(i, i ^ 1) for i in range(seq)]
            closing.got = [closing.flight.start(lax.ppermute(parts[1], "seq", pairs))]
            closing.seq_left = list(range(1, seq.bit_length() - 1))
            return
        closing.got = []
        for hop, send in enumerate(parts[1:]):
            pairs = [(i, (i + hop + 1) % seq) for i in range(seq)]
            closing.got.append(closing.flight.start(lax.ppermute(send, "seq", pairs)))

    return list(results), go


def finish_sum(total):
    value = total.own
    for got in total.got:
        value = value + got[0].astype(F32)
    return value.reshape(2, total.many, -1, total.cols)


def vector_hops():
    seq = lax.axis_size("seq")
    hops = []
    for bit in range(seq.bit_length() - 1):
        pairs = [(i, i ^ (1 << bit)) for i in range(seq)]
        hops.append(partial(lax.ppermute, axis_name="seq", perm=pairs))
    return hops + [partial(swap, bit=bit) for bit in range(lax.axis_size("dp").bit_length() - 1)]


def exchange(x, d, rows):
    seq = lax.axis_size("seq")
    first = jnp.concatenate([x[:rows], d[:rows]], axis=1)
    last = jnp.concatenate([x[-rows:], d[-rows:]], axis=1)
    from_left = lax.ppermute(last, "seq", [(i, i + 1) for i in range(seq - 1)])
    from_right = lax.ppermute(first, "seq", [(i + 1, i) for i in range(seq - 1)])
    return (from_left, from_right)


def core_split(value):
    pairs = lax.axis_size("dp") // 2
    two, many, depth, cols = value.shape
    shaped = value.reshape(two, many, pairs, 2, depth // (2 * pairs), cols)
    kept = half_of([shaped], 3, 0, True)[0]
    sent = half_of([shaped], 3, 0, False)[0]
    return (kept, sent)


PARTS = 3


def per_device(
    tokens, item_types, first_gain, first_shift, qkv_weight, query_bias, value_bias, attn_weight,
    attn_bias, second_gain, second_shift, expert_up, up_bias, expert_down, down_bias, cotangent,
):
    tok, width = tokens.shape
    dp, seq = lax.axis_size("dp"), lax.axis_size("seq")
    rows = capacity(tok)
    chunk = width // dp
    chunk = chunk if chunk % 16 == 0 else 0
    bits = [(lax.axis_index("dp") >> bit) & 1 for bit in range(dp.bit_length() - 1)]
    place = jnp.stack([lax.axis_index("seq")] + bits).astype(jnp.int32)
    left, right = exchange(tokens, cotangent, HALO)
    x, g, info = sort_rows(place, item_types, tokens, cotangent, rows, tok * seq)
    x, g, left, right = lax.optimization_barrier((x, g, left, right))
    x, g, h, qkv, att, mid, h2 = forward_rows(
        info, left, right, x, g, first_gain, first_shift, qkv_weight, query_bias, value_bias,
        attn_weight, attn_bias, second_gain, second_shift, tok,
    )

    flight = Flight()

    def window(sums, behind=None):
        late = [total for total in sums if total.seq_left]
        steps = [total for total in sums if total.more()]
        closing = [total for total in sums if not total.more() and total.own is None]
        if not (late or steps or closing):
            return info
        turn = place if behind is None else lax.optimization_barrier((place, behind))[0]
        ready, go = advance(
            turn, steps, closing[0] if closing else None, late[0] if late else None
        )
        gate, ready = lax.optimization_barrier((info, ready))
        go(ready)
        return gate

    sums, up_biases, acts, dups = [], [], [], []
    gate = info
    for part in range(PARTS):
        results = run_hidden(part, PARTS, gate, h2, g, expert_up, up_bias, expert_down, chunk)
        results = flight.land(*results)
        bias, act, dup = results[-3:]
        up_biases.append(bias)
        acts.append(act)
        dups.append(dup)
        if chunk:
            kept, sent = results[:2]
        else:
            kept, sent = core_split(results[0])
        new = Sum(flight, kept, sent)
        new.ways = 2
        gate = window(sums)
        sums.append(new)
    results = finish_experts(
        gate, mid, g, acts, dups, expert_up, expert_down, second_gain, down_bias, attn_weight
    )
    row_sums, mixed, dx, proj, datt = flight.land(*results)
    gate = window(sums)
    results = attend_back(gate, qkv, datt)
    m_rows = unsort_rows(lax.optimization_barrier((gate, results[0]))[0], mixed, tok)
    dq, dk, dv, m_own, m_left, m_right = flight.land(*results, *m_rows)
    gate = window(sums)
    kept, sent = flight.land(*projection_grads(gate, dq, dk, dv, proj, h, att, dp, seq))
    last = Sum(flight, kept, sent)
    gate = window(sums)

    def send_rows(left, right):
        to_left = lax.ppermute(left, "seq", [(i + 1, i) for i in range(seq - 1)])
        to_right = lax.ppermute(right, "seq", [(i, i + 1) for i in range(seq - 1)])
        return flight.start(to_left), flight.start(to_right)

    def merge(own, got):
        own = own.at[:HALO].add(got[1][0].astype(own.dtype))
        return own.at[tok - HALO :].add(got[0][0].astype(own.dtype))

    gate, m_left, m_right = lax.optimization_barrier((gate, m_left, m_right))
    m_got = send_rows(m_left, m_right)
    results = last_norm(gate, x, dx, dq, dk, dv, first_gain, qkv_weight, row_sums, up_biases)
    grad_x, packed = flight.land(*results)

    hops = vector_hops()

    def hop(packed, moved=None):
        packed = packed if moved is None else packed + moved[0]
        return packed, flight.start(hops.pop(0)(packed))

    packed, moved = hop(packed)
    gate = window([last])
    while any(total.own is None or total.seq_left for total in sums):
        gate = window(sums, gate)
    results = flight.land(merge(m_own, m_got), *unsort_rows(gate, grad_x, tok))
    mixed_out, g_own, left, right = results
    expert_sums = [finish_sum(total) for total in sums]
    packed, moved = hop(packed, moved)
    later = []
    while last.own is None:
        window([last])
        if not later:
            left, right, moved[0] = lax.optimization_barrier((left, right, moved[0]))
            packed, moved = hop(packed, moved)
            later.append(moved)
            g_got = send_rows(left, right)
            later += list(g_got)
        if last.own is None:
            expert_sums = flight.land(*expert_sums, later=later)

    (grad_out,) = flight.land(merge(g_own, g_got), later=[moved])
    while hops:
        packed, moved = hop(packed, moved)
    packed = packed + moved[0]
    last_sums = finish_sum(last)

    own = width // (dp * seq)
    rank = lax.axis_index("dp") * seq + lax.axis_index("seq")
    vectors = lax.dynamic_slice(packed, (0, rank * own), (14, own))
    tile = up_biases[0].shape[2]
    up_total = packed[14 : 14 + PARTS * EXPERTS, :tile].reshape(PARTS, EXPERTS, tile)
    sum_up = jnp.concatenate([total[0] for total in expert_sums], axis=-1)
    sum_down = jnp.concatenate([total[1] for total in expert_sums], axis=-1).swapaxes(1, 2)
    last_sums = jnp.concatenate([last_sums[0, 0], last_sums[1, 0]], axis=1).T

    return (
        mixed_out,
        grad_out,
        vectors[0],
        vectors[1],
        last_sums[:, : 3 * own],
        vectors[2],
        vectors[3],
        last_sums[:, 3 * own :],
        vectors[4],
        vectors[5:8],
        vectors[8:11],
        sum_up,
        up_total.swapaxes(0, 1).reshape(EXPERTS, -1),
        sum_down,
        vectors[11:14],
    )


def solution(mesh):
    split = P(("dp", "seq"))
    in_specs = (P(("dp", "seq"), None), P("dp", None)) + (P(),) * 13 + (P(("dp", "seq"), None),)
    out_specs = (
        P(("dp", "seq"), None),
        P(("dp", "seq"), None),
        split,
        split,
        P(None, ("dp", "seq")),
        split,
        split,
        P(None, ("dp", "seq")),
        split,
        P(None, ("dp", "seq")),
        P(None, ("dp", "seq")),
        P(None, ("dp", "seq"), None),
        P(),
        P(None, None, ("dp", "seq")),
        P(None, ("dp", "seq")),
    )
    return jax.shard_map(
        per_device, mesh=mesh, in_specs=in_specs, out_specs=out_specs, check_vma=False
    )
```

```python
from functools import partial

import jax
import jax.numpy as jnp
from jax import lax
from jax.experimental import pallas as pl
from jax.experimental.pallas import tpu as pltpu
from jax.sharding import PartitionSpec as P

HD = 64
EXPERTS = 3
IMG_LEN = 197
TXT_LEN = 64
LENS = (IMG_LEN, TXT_LEN, IMG_LEN + TXT_LEN)
SLOTS = (208, 64, 272)
TXT_PAIR = 128
PAD_ROWS = 384
HALO = 144
ROW = 128
BLK = 256

EPS = 1e-05
NEG = -1e30
VMEM = 60 << 20
F32 = jnp.float32
BF16 = jnp.bfloat16

N_IMG, N_TXT, N_BOTH, N_PAD = 0, 1, 2, 3
G_IMG, G_TXT, G_BOTH, G_PAD, G_END = 4, 5, 6, 7, 8
PAD_LEN, OWN_N, CORE = 9, 10, 11
TABLE = 16
INFO = 256


def nn(a, b):
    return lax.dot_general(a, b, (((1,), (0,)), ((), ())), preferred_element_type=F32)


def nt(a, b):
    return lax.dot_general(a, b, (((1,), (1,)), ((), ())), preferred_element_type=F32)


def tn(a, b):
    return lax.dot_general(a, b, (((0,), (0,)), ((), ())), preferred_element_type=F32)


def cost(microseconds):
    return pl.CostEstimate(flops=int(microseconds * 1e10), bytes_accessed=0, transcendentals=0)


SMEM_SPEC = pl.BlockSpec(memory_space=pltpu.SMEM)


def up_to(value, unit):
    return ((value + unit - 1) // unit) * unit


def normalize(v):
    mean = jnp.mean(v, axis=-1, keepdims=True)
    cent = v - mean
    var = jnp.mean(cent * cent, axis=-1, keepdims=True)
    inverse = lax.rsqrt(var + EPS)
    return (cent * inverse, inverse)


def norm_back(grad, normed, inverse):
    inner = jnp.mean(grad * normed, axis=-1, keepdims=True)
    return inverse * (grad - jnp.mean(grad, axis=-1, keepdims=True) - normed * inner)


def capacity(tok):
    rows = tok + LENS[2] - 1
    best = 0
    for images in range(rows // LENS[0] + 1):
        for both in range((rows - images * LENS[0]) // LENS[2] + 1):
            left = rows - images * LENS[0] - both * LENS[2]
            for pad in (0, 1):
                spare = left - pad * (1 + LENS[2] // 2)
                if spare < 0:
                    continue
                texts = spare // LENS[1]
                for count in range(texts + 1):
                    total = (
                        up_to(images * SLOTS[0], ROW)
                        + up_to(count * SLOTS[1], ROW)
                        + up_to(both * SLOTS[2], ROW)
                        + pad * PAD_ROWS
                    )
                    best = max(best, total)
    return up_to(best, BLK)


def gather_rows(info, wins, outs):
    for out in outs:
        out[...] = jnp.zeros_like(out)

    def place(index, carry):
        source = info[TABLE + 3 * index]
        target = pl.multiple_of(info[TABLE + 3 * index + 1], 16)
        kind = info[TABLE + 3 * index + 2]
        begin = pl.multiple_of((source // 16) * 16, 16)
        shift = source - begin
        for which in range(EXPERTS):
            slot = SLOTS[which]
            fits = (kind == which) if which < 2 else (kind >= 2)
            size = LENS[which] if which < 2 else jnp.where(kind == 2, LENS[2], info[PAD_LEN])

            @pl.when(fits)
            def _(slot=slot, size=size):
                rows = lax.broadcasted_iota(jnp.int32, (slot, slot + 16), 0)
                cols = lax.broadcasted_iota(jnp.int32, (slot, slot + 16), 1)
                chosen = ((cols == rows + shift) & (rows < size)).astype(F32).astype(BF16)
                for win, out in zip(wins, outs):
                    value = nn(chosen, win[pl.ds(begin, slot + 16), :])
                    out[pl.ds(target, slot), :] = value.astype(BF16)

        return carry

    lax.fori_loop(0, info[OWN_N], place, 0)


def sort_kernel(tok, group, place_ref, types, x_own, d_own, x_out, d_out, info, x_win, d_win):
    items = types.shape[1]
    low = place_ref[0] * tok
    info[CORE] = place_ref[1]
    width = x_own.shape[1]
    for win, own_rows in ((x_win, x_own), (d_win, d_own)):
        rest = win.shape[0] - (HALO + tok)
        win[pl.ds(0, HALO), :] = jnp.zeros((HALO, width), BF16)
        win[pl.ds(HALO, tok), :] = own_rows[...]
        win[pl.ds(HALO + tok, rest), :] = jnp.zeros((rest, width), BF16)

    def length(kind):
        return jnp.where(
            kind == 0, LENS[0], jnp.where(kind == 1, LENS[1], jnp.where(kind == 2, LENS[2], 0))
        )

    def owned(start, size):
        middle = (start + start + size) // 2
        return (middle >= low) & (middle < low + tok) & (size > 0)

    def count(index, carry):
        start, images, texts, boths = carry
        kind = types[0, index]
        size = length(kind)
        mine = owned(start, size)
        return (
            start + size,
            images + jnp.where(mine & (kind == 0), 1, 0),
            texts + jnp.where(mine & (kind == 1), 1, 0),
            boths + jnp.where(mine & (kind == 2), 1, 0),
        )

    zero = jnp.int32(0)
    total, images, texts, boths = lax.fori_loop(0, items, count, (zero, zero, zero, zero))
    pad_len = group - total
    pad = owned(total, pad_len)
    g_txt = up_to(images * SLOTS[0], ROW)
    g_both = g_txt + up_to(texts * SLOTS[1], ROW)
    g_pad = g_both + up_to(boths * SLOTS[2], ROW)
    info[N_IMG] = images
    info[N_TXT] = texts
    info[N_BOTH] = boths
    info[N_PAD] = jnp.where(pad, 1, 0)
    info[G_IMG] = zero
    info[G_TXT] = g_txt
    info[G_BOTH] = g_both
    info[G_PAD] = g_pad
    info[G_END] = g_pad + jnp.where(pad, PAD_ROWS, 0)
    info[PAD_LEN] = pad_len

    def note(own, source, target, kind):
        info[TABLE + 3 * own] = source
        info[TABLE + 3 * own + 1] = target
        info[TABLE + 3 * own + 2] = kind

    def place(index, carry):
        start, images, texts, boths, own = carry
        kind = types[0, index]
        size = length(kind)
        mine = owned(start, size)

        @pl.when(mine)
        def _():
            target = jnp.where(
                kind == 0,
                images * SLOTS[0],
                jnp.where(kind == 1, g_txt + texts * SLOTS[1], g_both + boths * SLOTS[2]),
            )
            note(own, start - low + HALO, target, kind)

        return (
            start + size,
            images + jnp.where(mine & (kind == 0), 1, 0),
            texts + jnp.where(mine & (kind == 1), 1, 0),
            boths + jnp.where(mine & (kind == 2), 1, 0),
            own + jnp.where(mine, 1, 0),
        )

    own = lax.fori_loop(0, items, place, (zero, zero, zero, zero, zero))[-1]

    @pl.when(pad)
    def _():
        note(own, total - low + HALO, g_pad, jnp.int32(EXPERTS))

    info[OWN_N] = own + jnp.where(pad, 1, 0)
    gather_rows(info, (x_win, d_win), (x_out, d_out))


def sort_rows(place, types, x, d, rows, group):
    tok, width = x.shape
    vmem = pl.BlockSpec(memory_space=pltpu.VMEM)
    return pl.pallas_call(
        partial(sort_kernel, tok, group),
        out_shape=[
            jax.ShapeDtypeStruct((rows, width), BF16),
            jax.ShapeDtypeStruct((rows, width), BF16),
            jax.ShapeDtypeStruct((INFO,), jnp.int32),
        ],
        in_specs=[SMEM_SPEC, SMEM_SPEC] + [vmem] * 2,
        out_specs=[vmem, vmem, SMEM_SPEC],
        scratch_shapes=[pltpu.VMEM((tok + HALO + 288, width), BF16)] * 2,
        compiler_params=pltpu.CompilerParams(vmem_limit_bytes=VMEM),
        cost_estimate=cost(11),
        name="sort_rows",
    )(place, types, x, d)


def patch_ends(tok, info, left, right, arrived, visits):
    count = info[OWN_N]

    def for_slots(end, visit):
        index = jnp.maximum(count - 1, 0) if end else 0
        source = info[TABLE + 3 * index]
        target = pl.multiple_of(info[TABLE + 3 * index + 1], 16)
        kind = info[TABLE + 3 * index + 2]
        size = jnp.where(kind == 0, LENS[0], jnp.where(kind == 1, LENS[1], LENS[2]))
        size = jnp.where(kind == EXPERTS, info[PAD_LEN], size)
        over = (source + size > HALO + tok) if end else (source < HALO)
        for which in range(EXPERTS):
            slot = SLOTS[which]
            fits = (kind == which) if which < 2 else (kind >= 2)

            @pl.when(over & (count > 0) & fits)
            def _(slot=slot):
                def rows():
                    into = lax.broadcasted_iota(jnp.int32, (slot, HALO), 0)
                    cols = lax.broadcasted_iota(jnp.int32, (slot, HALO), 1)
                    shift = source - HALO - tok if end else source
                    chosen = ((cols == into + shift) & (into < size)).astype(F32).astype(BF16)
                    return nn(chosen, (right if end else left)[...])

                visit(end, slot, pl.ds(target, slot), rows)

    for number, visit in enumerate(visits):
        if number == arrived[0]:
            arrived[1]()
        for end in range(2):
            for_slots(end, visit)


def forward_kernel(
    tok, info, left, right, x_in, d_in, gain, shift, qkv_weight, query_bias, value_bias,
    attn_weight, attn_bias, gains, shifts,
    x_out, d_out, h_out, qkv_out, att_out, mid_out, h2_out,
    x_v, qkv_v, att_v, w_qkv, w_attn, d_v, h_v, mid_v, h2_v, product_v,
    load_sems, patch_sems, h_sems, qkv_sems, att_sems, mid_sems, h2_sems,
):
    width = x_v.shape[1]
    blocks = (info[G_END] + BLK - 1) // BLK
    load_x = pltpu.make_async_copy(x_in, x_v, load_sems.at[0])
    load_qkv = pltpu.make_async_copy(qkv_weight, w_qkv, load_sems.at[1])
    load_attn = pltpu.make_async_copy(attn_weight, w_attn, load_sems.at[2])
    load_x.start()
    load_qkv.start()

    def each(low, high, visit):
        def body(index, carry):
            visit(index)
            return carry

        lax.fori_loop(low, high, body, 0)

    def d_copy(end, slot, at, inward):
        near, far = d_v.at[end, pl.ds(0, slot), :], d_out.at[at, :]
        source, target = (far, near) if inward else (near, far)
        return pltpu.make_async_copy(source, target, patch_sems.at[end, 0])

    def x_copy(end, at):
        return pltpu.make_async_copy(x_v.at[at, :], x_out.at[at, :], patch_sems.at[end, 1])

    def fetch(end, slot, at, rows):
        d_copy(end, slot, at, True).start()

    def add(end, slot, at, rows):
        added = rows()
        x_v[at, :] = (x_v[at, :].astype(F32) + added[:, :width]).astype(BF16)
        x_copy(end, at).start()
        d_copy(end, slot, at, True).wait()
        here = pl.ds(0, slot)
        d_v[end, here, :] = (d_v[end, here, :].astype(F32) + added[:, width:]).astype(BF16)
        d_copy(end, slot, at, False).start()

    patch_ends(tok, info, left, right, (1, load_x.wait), (fetch, add))
    load_attn.start()
    load_qkv.wait()

    def h_copy(index):
        at = pl.ds(pl.multiple_of(index * BLK, BLK), BLK)
        return pltpu.make_async_copy(h_v.at[index % 2], h_out.at[at, :], h_sems.at[index % 2])

    def qkv_copy(index):
        at = pl.ds(pl.multiple_of(index * BLK, BLK), BLK)
        return pltpu.make_async_copy(qkv_v.at[at, :], qkv_out.at[at, :], qkv_sems.at[index])

    sub = BLK // 4

    def norm_part(index, turn):
        at = pl.ds(pl.multiple_of(index * BLK + turn * sub, sub), sub)
        normed, _ = normalize(x_v[at, :].astype(F32))
        hidden = (normed * gain[...] + shift[...]).astype(BF16)
        h_v[index % 2, pl.ds(turn * sub, sub), :] = hidden

    def multiply_part(index, hidden, part):
        at = pl.ds(pl.multiple_of(index * BLK, BLK), BLK)
        cols = pl.ds(part * width, width)
        value = nn(hidden, w_qkv[:, cols])
        if part == 0:
            value = (value + query_bias[...]) * (HD ** (-0.5))
        if part == 2:
            value = value + value_bias[...]
        qkv_v[at, cols] = value.astype(BF16)

    def project(index):
        @pl.when(index >= 2)
        def _():
            h_copy(index - 2).wait()

        @pl.when(index == 0)
        def _():
            for turn in range(4):
                norm_part(index, turn)

        @pl.when((index > 0) & (index < blocks))
        def _():
            hidden = h_v[(index + 1) % 2]
            for turn in range(4):
                norm_part(index, turn)
                if turn < 3:
                    multiply_part(index - 1, hidden, turn)

        @pl.when((index > 0) & (index == blocks))
        def _():
            hidden = h_v[(index + 1) % 2]
            for part in range(3):
                multiply_part(index - 1, hidden, part)

        @pl.when(index < blocks)
        def _():
            h_copy(index).start()

        @pl.when(index > 0)
        def _():
            qkv_copy(index - 1).start()

    each(0, jnp.where(blocks > 0, blocks + 1, 0), project)

    att_v[...] = jnp.zeros_like(att_v)

    masks = head_masks(HEADS)
    wide = HEADS * HD

    def visit(start, slot, bias):
        at = pl.ds(start, slot)
        for group in range(width // wide):
            cols = [pl.ds(part * width + group * wide, wide) for part in range(3)]
            q, k, v = [qkv_v[at, one] for one in cols]
            scores = nt(stacked(k, masks), q)
            probs = []
            for head in range(HEADS):
                prob = softmax_cols(scores[head * slot : (head + 1) * slot], bias)
                probs.append(prob.astype(BF16))
            att_v[at, cols[0]] = tn(jnp.concatenate(probs), stacked(v, masks)).astype(BF16)

    for_items(info, visit)
    load_attn.wait()

    def block_copies(index):
        at = pl.ds(pl.multiple_of(index * BLK, BLK), BLK)
        slot = index % 2
        return (
            pltpu.make_async_copy(mid_v.at[slot], mid_out.at[at, :], mid_sems.at[slot]),
            pltpu.make_async_copy(h2_v.at[slot], h2_out.at[at, :], h2_sems.at[slot]),
        )

    def att_copy(index):
        at = pl.ds(pl.multiple_of(index * BLK, BLK), BLK)
        return pltpu.make_async_copy(att_v.at[at, :], att_out.at[at, :], att_sems.at[index])

    each(0, blocks, lambda index: att_copy(index).start())

    def add_part(index, turn):
        slot = index % 2
        rows = pl.ds(turn * ROW, ROW)
        row = index * BLK + turn * ROW
        at = pl.ds(pl.multiple_of(row, ROW), ROW)
        value = x_v[at, :].astype(F32) + (product_v[slot, rows, :] + attn_bias[...])
        mid_v[slot, rows, :] = value
        normed, _ = normalize(value)
        which = pl.ds(jnp.minimum(group_of(info, row), EXPERTS - 1), 1)
        h2_v[slot, rows, :] = (normed * gains[which, :] + shifts[which, :]).astype(BF16)

    def middle(index):
        @pl.when(index >= 3)
        def _():
            for copy in block_copies(index - 3):
                copy.wait()

        whole = pl.ds(pl.multiple_of(index * BLK, BLK), BLK)
        turns = BLK // ROW

        @pl.when(index == 0)
        def _():
            product_v[0] = nn(att_v[whole, :], w_attn[...])

        @pl.when((index > 0) & (index < blocks))
        def _():
            value = nn(att_v[whole, :], w_attn[...])
            for turn in range(turns):
                add_part(index - 1, turn)
            product_v[index % 2] = value

        @pl.when((index > 0) & (index == blocks))
        def _():
            for turn in range(turns):
                add_part(index - 1, turn)

        @pl.when(index > 0)
        def _():
            for copy in block_copies(index - 1):
                copy.start()

    each(0, jnp.where(blocks > 0, blocks + 1, 0), middle)

    def wait_rows(end, slot, at, rows):
        x_copy(end, at).wait()
        d_copy(end, slot, at, False).wait()

    patch_ends(tok, info, left, right, (-1, None), (wait_rows,))
    each(0, blocks, lambda index: qkv_copy(index).wait())
    each(0, blocks, lambda index: att_copy(index).wait())
    for back in (2, 1):

        @pl.when(blocks >= back)
        def _(back=back):
            for copy in block_copies(blocks - back):
                copy.wait()

    @pl.when(blocks >= 1)
    def _():
        h_copy(blocks - 1).wait()


def forward_rows(
    info, left, right, x, d, gain, shift, qkv_weight, query_bias, value_bias, attn_weight,
    attn_bias, gains, shifts, tok,
):
    rows, width = x.shape
    vmem = pl.BlockSpec(memory_space=pltpu.VMEM)
    any_spec = pl.BlockSpec(memory_space=pl.ANY)
    low = lambda cols: jax.ShapeDtypeStruct((rows, cols), BF16)
    blocks = rows // BLK
    return pl.pallas_call(
        partial(forward_kernel, tok),
        out_shape=[
            low(width),
            low(width),
            low(width),
            low(3 * width),
            low(width),
            jax.ShapeDtypeStruct((rows, width), F32),
            low(width),
        ],
        in_specs=[SMEM_SPEC, vmem, vmem, any_spec, any_spec, vmem, vmem, any_spec, vmem, vmem]
        + [any_spec, vmem, vmem, vmem],
        out_specs=[any_spec] * 7,
        scratch_shapes=[
            pltpu.VMEM((rows, width), BF16),
            pltpu.VMEM((rows, 3 * width), BF16),
            pltpu.VMEM((rows, width), BF16),
            pltpu.VMEM(qkv_weight.shape, BF16),
            pltpu.VMEM(attn_weight.shape, BF16),
            pltpu.VMEM((2, SLOTS[2], width), BF16),
            pltpu.VMEM((2, BLK, width), BF16),
            pltpu.VMEM((2, BLK, width), F32),
            pltpu.VMEM((2, BLK, width), BF16),
            pltpu.VMEM((2, BLK, width), F32),
            pltpu.SemaphoreType.DMA((3,)),
            pltpu.SemaphoreType.DMA((2, 2)),
            pltpu.SemaphoreType.DMA((2,)),
            pltpu.SemaphoreType.DMA((blocks,)),
            pltpu.SemaphoreType.DMA((blocks,)),
            pltpu.SemaphoreType.DMA((2,)),
            pltpu.SemaphoreType.DMA((2,)),
        ],
        input_output_aliases={3: 0, 4: 1},
        compiler_params=pltpu.CompilerParams(vmem_limit_bytes=VMEM),
        cost_estimate=cost(45),
        name="forward_rows",
    )(
        info, left, right, x, d, gain, shift, qkv_weight, query_bias, value_bias, attn_weight,
        attn_bias, gains, shifts,
    )


def unsort_kernel(info, rows, own_rows, left, right, win):
    tok = own_rows.shape[0]
    win[...] = jnp.zeros_like(win)

    def place(index, carry):
        source = info[TABLE + 3 * index]
        target = pl.multiple_of(info[TABLE + 3 * index + 1], 16)
        kind = info[TABLE + 3 * index + 2]
        begin = pl.multiple_of((source // 16) * 16, 16)
        shift = source - begin
        for which in range(EXPERTS):
            slot = SLOTS[which]
            fits = (kind == which) if which < 2 else (kind >= 2)
            size = LENS[which] if which < 2 else jnp.where(kind == 2, LENS[2], info[PAD_LEN])

            @pl.when(fits)
            def _(slot=slot, size=size):
                into = lax.broadcasted_iota(jnp.int32, (slot + 16, slot), 0)
                cols = lax.broadcasted_iota(jnp.int32, (slot + 16, slot), 1)
                chosen = ((into == cols + shift) & (cols < size)).astype(F32).astype(BF16)
                value = rows[pl.ds(target, slot), :]
                to = pl.ds(begin, slot + 16)
                high = value.astype(BF16)
                if rows.dtype == BF16:
                    win[to, :] += nn(chosen, high)
                else:
                    rest = (value - high.astype(F32)).astype(BF16)
                    win[to, :] += nn(chosen, high) + nn(chosen, rest)

        return carry

    lax.fori_loop(0, info[OWN_N], place, 0)
    for part, begin in ((left, 0), (own_rows, HALO), (right, HALO + tok)):
        part[...] = win[pl.ds(begin, part.shape[0]), :].astype(part.dtype)


def unsort_rows(info, rows, tok):
    width = rows.shape[1]
    vmem = pl.BlockSpec(memory_space=pltpu.VMEM)
    return pl.pallas_call(
        unsort_kernel,
        out_shape=[
            jax.ShapeDtypeStruct((tok, width), rows.dtype),
            jax.ShapeDtypeStruct((HALO, width), BF16),
            jax.ShapeDtypeStruct((HALO, width), BF16),
        ],
        in_specs=[SMEM_SPEC, vmem],
        out_specs=[vmem] * 3,
        scratch_shapes=[pltpu.VMEM((tok + HALO + 288, width), F32)],
        compiler_params=pltpu.CompilerParams(vmem_limit_bytes=VMEM),
        cost_estimate=cost(0.1),
        name="unsort_rows",
    )(info, rows)


def full(shape):
    return pl.BlockSpec(shape, lambda *_: (0,) * len(shape))


def held(shape):
    return pl.BlockSpec(shape, lambda *_: (0,) * len(shape), pipeline_mode=pl.Buffered(1))


HEADS, BACK_HEADS = 2, 4


def softmax_cols(scores, bias):
    masked = scores + bias
    expo = jnp.exp(masked - jnp.max(masked, axis=0, keepdims=True))
    return expo * (1.0 / jnp.sum(expo, axis=0, keepdims=True))


def for_items(info, visit):
    def cut(slot, size):
        return jnp.where(lax.broadcasted_iota(jnp.int32, (slot, 1), 0) < size, 0.0, NEG)

    def image(index, carry):
        slot = SLOTS[0]
        visit(pl.multiple_of(index * slot, 16), slot, cut(slot, LENS[0]))
        return carry

    def text(index, carry):
        slot = TXT_PAIR
        rows = lax.broadcasted_iota(jnp.int32, (slot, slot), 0) // TXT_LEN
        cols = lax.broadcasted_iota(jnp.int32, (slot, slot), 1) // TXT_LEN
        start = pl.multiple_of(info[G_TXT] + index * slot, ROW)
        visit(start, slot, jnp.where(rows == cols, 0.0, NEG))
        return carry

    def both(index, carry):
        slot = SLOTS[2]
        real = index < info[N_BOTH]
        start = jnp.where(real, info[G_BOTH] + index * slot, info[G_PAD])
        size = jnp.where(real, LENS[2], info[PAD_LEN])
        visit(pl.multiple_of(start, 16), slot, cut(slot, size))
        return carry

    lax.fori_loop(0, info[N_IMG], image, 0)
    lax.fori_loop(0, (info[N_TXT] + 1) // 2, text, 0)
    lax.fori_loop(0, info[N_BOTH] + info[N_PAD], both, 0)


def head_masks(heads):
    lanes = lax.broadcasted_iota(jnp.int32, (1, heads * HD), 1) // HD
    return [lanes == head for head in range(heads)]


def stacked(value, masks):
    return jnp.concatenate([jnp.where(mask, value, 0) for mask in masks], axis=0)


def own_columns(value, masks):
    rows = value.shape[0] // len(masks)
    result = value[:rows]
    for head in range(1, len(masks)):
        result = jnp.where(masks[head], value[head * rows : (head + 1) * rows], result)
    return result


def attend_back_kernel(info, query, key, value, grad, dq_out, dk_out, dv_out):
    for out in (dq_out, dk_out, dv_out):
        out[...] = jnp.zeros_like(out)
    masks = head_masks(BACK_HEADS)
    wide = BACK_HEADS * HD

    def visit(start, slot, bias):
        at = pl.ds(start, slot)
        for group in range(query.shape[1] // wide):
            cols = pl.ds(group * wide, wide)
            q, k, v, g = query[at, cols], key[at, cols], value[at, cols], grad[at, cols]
            keys = stacked(k, masks)
            scores = nt(keys, q)
            grad_probs = nt(stacked(v, masks), g)
            probs, grad_scores = [], []
            for head in range(BACK_HEADS):
                mine = slice(head * slot, (head + 1) * slot)
                prob = softmax_cols(scores[mine], bias)
                product = prob * grad_probs[mine]
                inner = jnp.sum(product, axis=0, keepdims=True)
                probs.append(prob.astype(BF16))
                grad_scores.append((product - prob * inner).astype(BF16))
            probs, grad_scores = jnp.concatenate(probs), jnp.concatenate(grad_scores)
            dq = tn(grad_scores, keys).astype(BF16)
            dq_out[at, cols] = (dq.astype(F32) * HD ** (-0.5)).astype(BF16)
            dk_out[at, cols] = own_columns(nn(grad_scores, q), masks).astype(BF16)
            dv_out[at, cols] = own_columns(nn(probs, g), masks).astype(BF16)

    for_items(info, visit)


def attend_back(info, qkv, grad):
    rows = qkv.shape[0]
    width = qkv.shape[1] // 3
    spec = pl.BlockSpec((rows, width), lambda p: (0, 0))
    return pl.pallas_call(
        attend_back_kernel,
        grid=(1,),
        out_shape=[jax.ShapeDtypeStruct((rows, width), BF16)] * 3,
        in_specs=[
            SMEM_SPEC,
            spec,
            pl.BlockSpec((rows, width), lambda p: (0, 1)),
            pl.BlockSpec((rows, width), lambda p: (0, 2)),
            spec,
        ],
        out_specs=[spec] * 3,
        compiler_params=pltpu.CompilerParams(vmem_limit_bytes=VMEM),
        cost_estimate=cost(30),
        name="attend_back",
    )(info, qkv, qkv, qkv, grad)


def group_of(info, row):
    return (
        (row >= info[G_TXT]).astype(jnp.int32)
        + (row >= info[G_BOTH]).astype(jnp.int32)
        + (row >= info[G_PAD]).astype(jnp.int32)
    )


def gelu_parts(up):
    size = jnp.abs(up) * (0.5**0.5)
    expo = jnp.exp(-size * size)
    t = 1.0 / (1.0 + 0.3275911 * size)
    poly = 1.061405429 * t - 1.453152027
    poly = poly * t + 1.421413741
    poly = poly * t - 0.284496736
    poly = poly * t + 0.254829592
    tail = 0.5 * (poly * t) * expo
    cdf = jnp.where(up >= 0, 1.0 - tail, tail)
    return (up * cdf, cdf + up * (expo * 0.3989422804014327))


KROWS = 512
COLS = 1


def hidden_kernel(part, chunk, *refs):
    info, h_hbm, g_hbm, up_hbm, b_up, down_hbm = refs[:6]
    refs = refs[6:]
    weight_outs, refs = (refs[:2], refs[2:]) if chunk else (refs[:1], refs[1:])
    bias_out, act_hbm, dup_hbm, left, right, w_up, w_down, acc, stage = refs[:9]
    row_sems, weight_sems, hidden_sems, stage_sems = refs[9:]
    tile = w_up.shape[2]
    cols_at = pl.ds(part * tile, tile)
    bias_out[...] = jnp.zeros_like(bias_out)

    def rows_copies(index):
        at = pl.ds(pl.multiple_of(index * ROW, ROW), ROW)
        return [
            pltpu.make_async_copy(source.at[at, :], left.at[which, at, :], row_sems.at[which, index])
            for which, source in enumerate((h_hbm, g_hbm))
        ]

    def weight_copies(expert):
        return [
            pltpu.make_async_copy(
                up_hbm.at[expert, :, cols_at], w_up.at[expert], weight_sems.at[0, expert]
            ),
            pltpu.make_async_copy(
                down_hbm.at[expert, cols_at, :], w_down.at[expert], weight_sems.at[1, expert]
            ),
        ]

    def hidden_copies(index):
        at = pl.ds(pl.multiple_of(index * ROW, ROW), ROW)
        return [
            pltpu.make_async_copy(right.at[which, at, :], target.at[at, :], hidden_sems.at[which, index])
            for which, target in enumerate((dup_hbm, act_hbm))
        ]

    def stage_copies(slot, expert):
        return [
            pltpu.make_async_copy(
                stage.at[slot, which], out.at[slot, expert], stage_sems.at[slot, which]
            )
            for which, out in enumerate(weight_outs)
        ]

    def each(low, high, visit):
        def body(index, carry):
            visit(index)
            return carry

        lax.fori_loop(low, high, body, 0)

    def start_all(copies):
        for copy in copies:
            copy.start()

    def wait_all(copies):
        for copy in copies:
            copy.wait()

    def prefetch(expert):
        start_all(weight_copies(expert))
        low, high = info[G_IMG + expert] // ROW, info[G_IMG + expert + 1] // ROW
        each(low, high, lambda index: start_all(rows_copies(index)))

    each(0, EXPERTS, prefetch)

    def rows_of(expert, row, size):
        for place in range(size // ROW):
            wait_all(rows_copies(row // ROW + place))
        at = pl.ds(pl.multiple_of(row, ROW), size)
        hidden, grad = left[0, at, :], left[1, at, :]
        wide = tile // COLS
        for turn in range(COLS):
            cols = pl.ds(turn * wide, wide)
            bias = b_up[pl.ds(expert, 1), pl.ds(part * tile + turn * wide, wide)]
            up = nn(hidden, w_up[expert, :, cols]) + bias
            grad_act = nt(grad, w_down[expert, cols, :])
            active, slope = gelu_parts(up)
            grad_up = (slope * grad_act).astype(BF16)
            right[0, at, cols] = grad_up
            right[1, at, cols] = active.astype(BF16)
            bias_out[expert, :, cols] += jnp.sum(grad_up.astype(F32), axis=0, keepdims=True)
        for place in range(size // ROW):
            start_all(hidden_copies(row // ROW + place))

    def put(slot, value):
        if not chunk:
            stage[slot, 0] = value.astype(BF16)
            return
        for pair in range(value.shape[0] // (2 * chunk)):
            for core in range(2):
                first = (2 * pair + core) * chunk
                which = (info[CORE] + core) % 2
                stage[slot, which, pair] = value[first : first + chunk].astype(BF16)

    def one_expert(expert):
        wait_all(weight_copies(expert))
        start = info[G_IMG + expert]
        count = info[G_IMG + expert + 1] - start
        blocks = count // BLK
        each(0, blocks, lambda index: rows_of(expert, start + index * BLK, BLK))

        @pl.when(count % BLK > 0)
        def _():
            rows_of(expert, start + blocks * BLK, ROW)

        def one_side(slot):
            @pl.when(expert > 0)
            def _():
                wait_all(stage_copies(slot, expert - 1))

            def product(local, size):
                at = pl.ds(pl.multiple_of(start + local, ROW), size)
                return tn(left[slot, at, :], right[slot, at, :])

            before = (count - 1) // KROWS

            @pl.when(count == 0)
            def _():
                stage[slot] = jnp.zeros(stage.shape[1:], BF16)

            @pl.when(count > KROWS)
            def _():
                acc[...] = product(0, KROWS)

                def more(index):
                    acc[...] += product(index * KROWS, KROWS)

                each(1, before, more)

            for rest in range(ROW, KROWS + ROW, ROW):
                at_end = (count > 0) & (count - before * KROWS == rest)

                @pl.when(at_end & (before == 0))
                def _(rest=rest):
                    put(slot, product(0, rest))

                @pl.when(at_end & (before > 0))
                def _(rest=rest):
                    put(slot, acc[...] + product(before * KROWS, rest))

            start_all(stage_copies(slot, expert))

        each(0, 2, one_side)

    each(0, EXPERTS, one_expert)
    for slot in range(2):
        wait_all(stage_copies(slot, EXPERTS - 1))
    each(0, info[G_PAD] // ROW, lambda index: wait_all(hidden_copies(index)))


def run_hidden(part, parts, info, h, g, w_up, b_up, w_down, chunk):
    rows, width = h.shape
    tile = w_up.shape[2] // parts
    any_spec = pl.BlockSpec(memory_space=pl.ANY)
    vmem = pl.BlockSpec(memory_space=pltpu.VMEM)
    block = (width // (2 * chunk), chunk, tile) if chunk else (width, tile)
    sides = 2 if chunk else 1
    return pl.pallas_call(
        partial(hidden_kernel, part, chunk),
        out_shape=[jax.ShapeDtypeStruct((2, EXPERTS) + block, BF16)] * sides
        + [
            jax.ShapeDtypeStruct((EXPERTS, 1, tile), F32),
            jax.ShapeDtypeStruct((rows, tile), BF16),
            jax.ShapeDtypeStruct((rows, tile), BF16),
        ],
        in_specs=[SMEM_SPEC, any_spec, any_spec, any_spec, vmem, any_spec],
        out_specs=[any_spec] * sides + [vmem, any_spec, any_spec],
        scratch_shapes=[
            pltpu.VMEM((2, rows, width), BF16),
            pltpu.VMEM((2, rows, tile), BF16),
            pltpu.VMEM((EXPERTS, width, tile), BF16),
            pltpu.VMEM((EXPERTS, tile, width), BF16),
            pltpu.VMEM((width, tile), F32),
            pltpu.VMEM((2, sides) + block, BF16),
            pltpu.SemaphoreType.DMA((2, rows // ROW)),
            pltpu.SemaphoreType.DMA((2, EXPERTS)),
            pltpu.SemaphoreType.DMA((2, rows // ROW)),
            pltpu.SemaphoreType.DMA((2, sides)),
        ],
        compiler_params=pltpu.CompilerParams(vmem_limit_bytes=VMEM),
        cost_estimate=cost(18),
        name="hidden",
    )(info, h, g, w_up, b_up, w_down)


SUMS = 16


def finish_kernel(parts, *refs):
    info = refs[0]
    hbm = refs[1 : 3 + 2 * parts]
    up_hbm, down_hbm, gains, downs, w_attn = refs[3 + 2 * parts : 8 + 2 * parts]
    refs = refs[8 + 2 * parts :]
    sums_out, outs_hbm = refs[0], refs[1:5]
    rows_in, acts, dups = refs[5:7], refs[7 : 7 + parts], refs[7 + parts : 7 + 2 * parts]
    refs = refs[7 + 2 * parts :]
    held_out, (w_up, w_down, lower_s, hidden_s) = refs[:4], refs[4:8]
    row_sems, act_sems, out_sems, weight_sems = refs[8:]
    width = lower_s.shape[2]

    groups = range(EXPERTS + 1)
    counts = [info[G_IMG + group + 1] - info[G_IMG + group] for group in groups]
    firsts = [jnp.int32(0)]
    for group in groups:
        firsts.append(firsts[-1] + (counts[group] + BLK - 1) // BLK)
    total = firsts[-1]

    def block_of(index):
        group = sum([(index >= firsts[k]).astype(jnp.int32) for k in groups[1:]])
        first, start, count = firsts[0], info[G_IMG], counts[0]
        for k in groups[1:]:
            first = jnp.where(group == k, firsts[k], first)
            start = jnp.where(group == k, info[G_IMG + k], start)
            count = jnp.where(group == k, counts[k], count)
        local = (index - first) * BLK
        return group, start + local, count - local, index == first

    def halves(index, visit):
        group, row, left, _ = block_of(index)
        for half in range(BLK // ROW):

            @pl.when(half * ROW < left)
            def _(half=half):
                visit(half, pl.ds(pl.multiple_of(row + half * ROW, ROW), ROW), group < EXPERTS)

    def in_copies(index, half, at):
        here = pl.ds(half * ROW, ROW)
        rows = [
            pltpu.make_async_copy(
                source.at[at, :], target.at[index % 4, here, :], row_sems.at[index % 4, half, which]
            )
            for which, (source, target) in enumerate(zip(hbm[:2], rows_in))
        ]
        hidden = [
            pltpu.make_async_copy(
                source.at[at, :], target.at[index % 3, here, :], act_sems.at[index % 3, half, which]
            )
            for which, (source, target) in enumerate(zip(hbm[2:], acts + dups))
        ]
        return rows, hidden

    def fetch(index, action):
        def visit(half, at, real):
            rows, hidden = in_copies(index, half, at)
            for copy in rows:
                action(copy)

            @pl.when(real)
            def _():
                for copy in hidden:
                    action(copy)

        halves(index, visit)

    def send(index, action):
        def visit(half, at, real):
            here = pl.ds(half * ROW, ROW)
            for which, (source, target) in enumerate(zip(held_out, outs_hbm)):
                action(
                    pltpu.make_async_copy(
                        source.at[index % 2, here, :],
                        target.at[at, :],
                        out_sems.at[index % 2, half, which],
                    )
                )

        halves(index, visit)

    def start(copy):
        copy.start()

    def wait(copy):
        copy.wait()

    def weights(group, action):
        for which, (source, target) in enumerate(((up_hbm, w_up), (down_hbm, w_down))):
            action(
                pltpu.make_async_copy(
                    source.at[group], target.at[group], weight_sems.at[group, which]
                )
            )

    sums_out[...] = jnp.zeros_like(sums_out)

    @pl.when(total > 0)
    def _():
        fetch(0, start)

    weights(0, start)

    @pl.when(total > 1)
    def _():
        fetch(1, start)

    for expert in range(1, EXPERTS):
        weights(expert, start)

    tile = acts[0].shape[2]

    def block(index, waited):
        current, _, _, _ = block_of(index)
        mine = jnp.minimum(current, EXPERTS - 1)

        @pl.when(index + 2 < total)
        def _():
            fetch(index + 2, start)

        for expert in range(EXPERTS):

            @pl.when((waited <= expert) & (expert <= mine))
            def _(expert=expert):
                weights(expert, wait)

        @pl.when(index < total)
        def _():
            fetch(index, wait)

        @pl.when(index >= 3)
        def _():
            send(index - 3, wait)

        slot, old = index % 2, (index + 1) % 2
        behind = jnp.maximum(index - 1, 0)
        group, _, left, _ = block_of(behind)
        left = jnp.where(index > 0, left, 0)
        real = group < EXPERTS
        which = pl.ds(jnp.minimum(group, EXPERTS - 1), 1)
        mixed, dx, proj_out, datt = held_out
        sub = BLK // 4

        def row_part(turn):
            at = pl.ds(turn * sub, sub)
            valid = turn * sub + lax.broadcasted_iota(jnp.int32, (sub, 1), 0) < left
            middle = jnp.where(valid, rows_in[0][behind % 4, at, :], 0.0)
            grad = jnp.where(valid, rows_in[1][behind % 4, at, :].astype(F32), 0.0)
            lower = jnp.where(real, lower_s[old, at, :] + downs[which, :], 0.0)
            grad_hidden = jnp.where(valid & real, hidden_s[old, at, :], 0.0)
            mixed[old, at, :] = (middle + lower).astype(BF16)
            normed, inverse = normalize(middle)
            grad_middle = grad + norm_back(grad_hidden * gains[which, :], normed, inverse)
            dx[old, at, :] = grad_middle
            proj = grad_middle.astype(BF16)
            proj_out[old, at, :] = proj
            dsel = jnp.where(real, grad, 0.0)
            values = (proj.astype(F32), grad_hidden * normed, grad_hidden, dsel)
            return [jnp.sum(value, axis=0, keepdims=True) for value in values]

        taken = index % 3

        def compute(multiply):
            lower_new = jnp.zeros((BLK, width), F32)
            hidden_new = jnp.zeros((BLK, width), F32)
            sums, turn = [0.0] * 4, 0
            for part in range(parts):
                cols = pl.ds(part * tile, tile)
                if multiply:
                    lower_new += nn(acts[part][taken], w_down[mine, cols, :])
                if turn < 4:
                    sums = [x + y for x, y in zip(sums, row_part(turn))]
                    turn += 1
                if multiply:
                    hidden_new += nt(dups[part][taken], w_up[mine, :, cols])
                if turn < 4:
                    sums = [x + y for x, y in zip(sums, row_part(turn))]
                    turn += 1
            while turn < 4:
                sums = [x + y for x, y in zip(sums, row_part(turn))]
                turn += 1
            if multiply:
                lower_s[slot] = lower_new
                hidden_s[slot] = hidden_new
            datt[old] = nt(proj_out[old], w_attn[...]).astype(BF16)
            sums_out[pl.ds(0, 1), :] += sums[0]
            for place, value in enumerate(sums[1:]):
                at = pl.ds(1 + place * EXPERTS + jnp.minimum(group, EXPERTS - 1), 1)
                sums_out[at, :] += value

        multiplied = (index < total) & (current < EXPERTS)

        @pl.when(multiplied)
        def _():
            compute(True)

        @pl.when(jnp.logical_not(multiplied))
        def _():
            compute(False)

        @pl.when(index > 0)
        def _():
            send(index - 1, start)

        return jnp.maximum(waited, mine + 1)

    waited = lax.fori_loop(0, jnp.where(total > 0, total + 1, 0), block, jnp.int32(0))
    for expert in range(EXPERTS):

        @pl.when(waited <= expert)
        def _(expert=expert):
            weights(expert, wait)

    for back in (2, 1):

        @pl.when(total >= back)
        def _(back=back):
            send(total - back, wait)


def finish_experts(info, mid, g, acts, dups, w_up, w_down, gains, downs, w_attn):
    rows, width = mid.shape
    parts = len(acts)
    tile = acts[0].shape[1]
    any_spec = pl.BlockSpec(memory_space=pl.ANY)
    vmem = pl.BlockSpec(memory_space=pltpu.VMEM)
    kinds = (BF16, F32, BF16, BF16)
    return pl.pallas_call(
        partial(finish_kernel, parts),
        out_shape=[jax.ShapeDtypeStruct((SUMS, width), F32)]
        + [jax.ShapeDtypeStruct((rows, width), kind) for kind in kinds],
        in_specs=[SMEM_SPEC] + [any_spec] * (4 + 2 * parts) + [vmem] * 3,
        out_specs=[vmem] + [any_spec] * 4,
        scratch_shapes=[pltpu.VMEM((4, BLK, width), F32), pltpu.VMEM((4, BLK, width), BF16)]
        + [pltpu.VMEM((3, BLK, tile), BF16)] * (2 * parts)
        + [pltpu.VMEM((2, BLK, width), kind) for kind in kinds]
        + [pltpu.VMEM(w_up.shape, BF16), pltpu.VMEM(w_down.shape, BF16)]
        + [pltpu.VMEM((2, BLK, width), F32)] * 2
        + [
            pltpu.SemaphoreType.DMA((4, BLK // ROW, 2)),
            pltpu.SemaphoreType.DMA((3, BLK // ROW, 2 * parts)),
            pltpu.SemaphoreType.DMA((2, BLK // ROW, 4)),
            pltpu.SemaphoreType.DMA((EXPERTS, 2)),
        ],
        compiler_params=pltpu.CompilerParams(vmem_limit_bytes=VMEM),
        cost_estimate=cost(30),
        name="finish_experts",
    )(info, mid, g, *acts, *dups, w_up, w_down, gains, downs, w_attn)


def weights_kernel(dp, seq, info, dq, dk, dv, proj, h, att, send_out, keep_out, acc, attn_acc):
    index = pl.program_id(0)

    @pl.when(index == 0)
    def _():
        acc[...] = jnp.zeros_like(acc)
        attn_acc[...] = jnp.zeros_like(attn_acc)

    @pl.when(index * BLK < info[G_END])
    def _():
        row = index * BLK + lax.broadcasted_iota(jnp.int32, (BLK, 1), 0)
        real = row < info[G_END]
        hidden = h[...]
        width = hidden.shape[1]
        for part, grad in enumerate((dq, dk, dv)):
            acc[pl.ds(part * width, width), :] += tn(grad[...], hidden)
        attn_acc[...] += tn(
            jnp.where(real, proj[...], jnp.zeros_like(proj)),
            jnp.where(real, att[...], jnp.zeros_like(att)),
        )

    @pl.when(index == pl.num_programs(0) - 1)
    def _():
        width = attn_acc.shape[0]
        own = width // (dp * seq)
        half = width // 2
        for out, core in ((keep_out, info[CORE]), (send_out, 1 - info[CORE])):
            for pair in range(dp // 2):
                for place in range(seq):
                    device = (2 * pair + core) * seq + place
                    first = pl.ds(pl.multiple_of(device * 3 * own, 8), 3 * own)
                    second = pl.ds(pl.multiple_of(device * own, 8), own)
                    value = jnp.concatenate([acc[first, :], attn_acc[second, :]], axis=0)
                    value = value.astype(BF16)
                    at = pl.ds(place * 4 * own, 4 * own)
                    for lane in range(2):
                        out[lane, 0, pair, at, :] = value[:, lane * half : (lane + 1) * half]


def weights_kernel_plain(info, dq, dk, dv, proj, h, att, qkv_out, attn_out, acc, attn_acc):
    index = pl.program_id(0)

    @pl.when(index == 0)
    def _():
        acc[...] = jnp.zeros_like(acc)
        attn_acc[...] = jnp.zeros_like(attn_acc)

    @pl.when(index * BLK < info[G_END])
    def _():
        row = index * BLK + lax.broadcasted_iota(jnp.int32, (BLK, 1), 0)
        real = row < info[G_END]
        hidden = h[...]
        width = hidden.shape[1]
        for part, grad in enumerate((dq, dk, dv)):
            acc[pl.ds(part * width, width), :] += tn(grad[...], hidden)
        attn_acc[...] += tn(
            jnp.where(real, proj[...], jnp.zeros_like(proj)),
            jnp.where(real, att[...], jnp.zeros_like(att)),
        )

    @pl.when(index == pl.num_programs(0) - 1)
    def _():
        qkv_out[...] = acc[...].astype(BF16)
        attn_out[...] = attn_acc[...].astype(BF16)


def projection_grads(info, dq, dk, dv, proj, h, att, dp, seq):
    rows, width = h.shape
    spec = pl.BlockSpec((BLK, width), lambda i: (i, 0))
    own = width // (dp * seq)
    direct = own % 8 == 0
    if direct:
        shapes = [(2, 1, dp // 2, seq * 4 * own, width // 2)] * 2
        body = partial(weights_kernel, dp, seq)
    else:
        shapes = [(3 * width, width), (width, width)]
        body = weights_kernel_plain
    results = pl.pallas_call(
        body,
        grid=(rows // BLK,),
        out_shape=[jax.ShapeDtypeStruct(shape, BF16) for shape in shapes],
        in_specs=[SMEM_SPEC] + [spec] * 6,
        out_specs=[full(shape) for shape in shapes],
        scratch_shapes=[pltpu.VMEM((3 * width, width), F32), pltpu.VMEM((width, width), F32)],
        compiler_params=pltpu.CompilerParams(vmem_limit_bytes=VMEM),
        cost_estimate=cost(15),
        name="projection_grads",
    )(info, dq, dk, dv, proj, h, att)
    if direct:
        return results[1], results[0]
    d_qkv = results[0].reshape(dp * seq, -1, width)
    d_attn = results[1].reshape(dp * seq, -1, width)
    d_all = jnp.concatenate([d_qkv, d_attn], axis=1).reshape(1, -1, width)
    half = width // 2
    return core_split(jnp.stack([d_all[..., :half], d_all[..., half:]]))


VECTORS = 24


def last_kernel(parts, *refs):
    (info, x, dx, dq, dk, dv, gain, weight, row_sums) = refs[:9]
    biases = refs[9 : 9 + parts]
    out, packed = refs[9 + parts :]
    width = x.shape[1]
    step = pl.program_id(0)

    @pl.when(step == 0)
    def _():
        packed[...] = jnp.zeros_like(packed)
        packed[pl.ds(4, 10), pl.ds(0, width)] = row_sums[pl.ds(0, 10), :]
        for part, bias in enumerate(biases):
            tile = bias.shape[2]
            for expert in range(EXPERTS):
                packed[pl.ds(14 + part * EXPERTS + expert, 1), pl.ds(0, tile)] = bias[expert]

    @pl.when(step * BLK < info[G_END])
    def _():
        hidden = nt(dq[...], weight[:, pl.ds(0, width)])
        hidden += nt(dk[...], weight[:, pl.ds(width, width)])
        hidden += nt(dv[...], weight[:, pl.ds(2 * width, width)])
        normed, inverse = normalize(x[...].astype(F32))
        totals = (hidden * normed, hidden, dq[...].astype(F32), dv[...].astype(F32))
        for place, value in enumerate(totals):
            packed[pl.ds(place, 1), pl.ds(0, width)] += jnp.sum(value, axis=0, keepdims=True)
        out[...] = dx[...] + norm_back(hidden * gain[...], normed, inverse)


def last_norm(info, x, dx, dq, dk, dv, gain, weight, row_sums, biases):
    rows, width = x.shape
    spec = pl.BlockSpec((BLK, width), lambda i: (i, 0))
    cols = max(width, biases[0].shape[2])
    packed = (VECTORS, cols)
    return pl.pallas_call(
        partial(last_kernel, len(biases)),
        grid=(rows // BLK,),
        out_shape=[jax.ShapeDtypeStruct((rows, width), F32), jax.ShapeDtypeStruct(packed, F32)],
        in_specs=[SMEM_SPEC, spec, spec, spec, spec, spec, full(gain.shape), held((width, 3 * width))]
        + [full(row_sums.shape)]
        + [full(bias.shape) for bias in biases],
        out_specs=[spec, full(packed)],
        compiler_params=pltpu.CompilerParams(vmem_limit_bytes=VMEM),
        cost_estimate=cost(14),
        name="last_norm",
    )(info, x, dx, dq, dk, dv, gain, weight, row_sums, *biases)


def swap(value, bit):
    ways = lax.axis_size("dp")
    return lax.ppermute(value, "dp", [(i, i ^ (1 << bit)) for i in range(ways)])


def half_of(parts, axis, bit, mine):
    own = (lax.axis_index("dp") >> bit) & 1
    which = own if mine else 1 - own
    return [lax.dynamic_index_in_dim(part, which, axis, keepdims=False) for part in parts]


DEPTH = 4


def combine_kernel(blocks, arrays, shapes, seq, ways, half_bit, *refs):
    place, sources = refs[0], refs[1 : 1 + arrays]
    outs = refs[1 + arrays : 1 + arrays + shapes]
    scratch = refs[1 + arrays + shapes :]
    here = lax.rem(place[0], ways)

    def start(copies):
        for copy in copies:
            copy.start()

    def wait(copies):
        for copy in copies:
            copy.wait()

    if half_bit is not None:
        kept_v, got_v, own_v, sent_v, half_sems = scratch[-5:]
        half_in = [
            pltpu.make_async_copy(source, target, half_sems.at[which])
            for which, (source, target) in enumerate(zip(sources[-2:], (kept_v, got_v)))
        ]
        half_out = [
            pltpu.make_async_copy(source, target, half_sems.at[2 + which])
            for which, (source, target) in enumerate(zip((own_v, sent_v), outs[-2:]))
        ]
    if blocks:
        in_buf, out_buf, own_buf, send_buf, total, in_sems, out_sems = scratch[:7]

    def fetch(index):
        return [
            pltpu.make_async_copy(
                sources[which].at[where(place)],
                in_buf.at[index % DEPTH, part],
                in_sems.at[index % DEPTH, part],
            )
            for part, (which, where) in enumerate(blocks[index][0])
        ]

    def send(index):
        _, kind, targets, at = blocks[index]
        slot = index % 2
        if kind == "add":
            held = [out_buf.at[slot]]
        else:
            held = [own_buf.at[slot]] + [send_buf.at[slot, hop] for hop in range(len(targets) - 1)]
        return [
            pltpu.make_async_copy(source, outs[target].at[at], out_sems.at[slot, which])
            for which, (source, target) in enumerate(zip(held, targets))
        ]

    for index in range(min(DEPTH - 1, len(blocks))):
        start(fetch(index))
    if half_bit is not None:
        start(half_in)
    for index, (parts, kind, _, _) in enumerate(blocks):
        if index + DEPTH - 1 < len(blocks):
            start(fetch(index + DEPTH - 1))
        wait(fetch(index))
        if index >= 2:
            wait(send(index - 2))
        slot, source = index % 2, index % DEPTH
        value = in_buf[source, 0].astype(F32)
        for part in range(1, len(parts)):
            value = value + in_buf[source, part].astype(F32)
        if kind == "add":
            out_buf[slot] = value.astype(BF16)
        else:
            total[...] = value
            rows = total.shape[1] // seq
            for hop in range(ways):
                for turn in range(seq // ways):
                    at = lax.rem(here + hop, ways) + turn * ways
                    block = total[:, pl.ds(pl.multiple_of(at * rows, 8), rows), :]
                    to = pl.ds(turn * rows, rows)
                    if hop == 0:
                        own_buf[slot, :, to, :] = block
                    else:
                        send_buf[slot, hop - 1, :, to, :] = block.astype(BF16)
        start(send(index))
    if half_bit is not None:
        wait(half_in)
        rows = own_v.shape[2]
        mine = (place[0] >> half_bit) & 1
        kept_v[...] += got_v[...].astype(F32)
        own_v[...] = kept_v[:, :, pl.ds(pl.multiple_of(mine * rows, 8), rows), :]
        other = pl.ds(pl.multiple_of((1 - mine) * rows, 8), rows)
        sent_v[...] = kept_v[:, :, other, :].astype(BF16)
        start(half_out)
        wait(half_out)
    for index in range(max(0, len(blocks) - 2), len(blocks)):
        wait(send(index))


class Flight:

    def __init__(self):
        self.cells = []

    def start(self, value):
        cell = [value]
        self.cells.append(cell)
        return cell

    def land(self, *outputs, later=()):
        now = [cell for cell in self.cells if not any(cell is other for other in later)]
        outputs, arrays = lax.optimization_barrier((outputs, [cell[0] for cell in now]))
        for cell, array in zip(now, arrays):
            cell[0] = array
        self.cells = [cell for cell in self.cells if any(cell is other for other in later)]
        return outputs


class Sum:

    def __init__(self, flight, kept, sent):
        self.flight = flight
        self.bits = lax.axis_size("dp").bit_length() - 1
        self.seq = lax.axis_size("seq")
        self.many, self.pairs, self.chunk, self.cols = kept.shape[1:]
        every = list(range(self.bits - 1, 0, -1))
        shape = (2, self.many) + (2,) * len(every) + (self.chunk, self.cols)
        cells = [[kept.reshape(shape)], flight.start(swap(sent, 0).reshape(shape))]
        self.lanes = [[(cell, lane, every, True) for cell in cells] for lane in range(2)]
        self.left = [list(every), list(every)]
        self.ways = self.seq
        self.own = None
        self.seq_left = None

    def more(self):
        return bool(self.left[0])

    def direct(self):
        return (self.chunk // self.seq) % 8 == 0

    def sources(self, lane, other, free, value):
        results = []
        for cell, first, bits, whole in self.lanes[lane]:

            def where(place, first=first, bits=bits, whole=whole):
                chosen = []
                for bit in bits:
                    if bit in free:
                        chosen.append((value >> (len(free) - 1 - free.index(bit))) & 1)
                    elif bit == other:
                        chosen.append(1 - place[1 + bit])
                    else:
                        chosen.append(place[1 + bit])
                if whole:
                    return (first, slice(None)) + tuple(chosen)
                group = 0
                for one in chosen:
                    group = group * 2 + one
                return (first + group,)

            results.append((cell[0], where))
        return results


def advance(place, steps, closing=None, halving=None):
    arrays, blocks, payloads, turns = [], [], {}, []
    model = steps[0] if steps else closing or halving

    def add(parts, kind, targets, at):
        known = []
        for array, where in parts:
            found = [i for i, other in enumerate(arrays) if other is array]
            if not found:
                arrays.append(array)
            known.append((found[0] if found else len(arrays) - 1, where))
        blocks.append((known, kind, targets, at))

    for total in steps:
        for lane in range(2):
            left = total.left[lane]
            bit = min(left) if lane == 0 else max(left)
            left.remove(bit)
            free = list(left)
            count = payloads.get(bit, 0)
            turns.append((total, lane, bit, free, count))
            for value in range(2 ** len(free)):
                add(total.sources(lane, bit, free, value), "add", bit, count)
                count += 1
            payloads[bit] = count
    order = sorted(payloads)
    blocks = [(parts, kind, [order.index(bit)], at) for parts, kind, bit, at in blocks]
    seq, many, chunk, cols = model.seq, model.many, model.chunk, model.cols
    shapes = [jax.ShapeDtypeStruct((payloads[bit], many, chunk, cols), BF16) for bit in order]
    split = closing is not None and closing.direct()
    ways = closing.ways if split else 2
    rows = chunk // ways
    first_end = len(shapes)
    if closing is not None:
        if split:
            shapes.append(jax.ShapeDtypeStruct((2, many, rows, cols), F32))
            shapes += [jax.ShapeDtypeStruct((2, many, rows, cols), BF16)] * (ways - 1)
        else:
            shapes.append(jax.ShapeDtypeStruct((2, many, chunk, cols), BF16))
        targets = list(range(first_end, len(shapes)))
        for lane in range(2):
            add(closing.sources(lane, None, [], 0), "ends" if split else "add", targets, lane)
    scratch = []
    if blocks:
        most = max(len(parts) for parts, _, _, _ in blocks)
        end_rows = rows if split else 8
        scratch += [
            pltpu.VMEM((DEPTH, most, many, chunk, cols), BF16),
            pltpu.VMEM((2, many, chunk, cols), BF16),
            pltpu.VMEM((2, many, end_rows, cols), F32),
            pltpu.VMEM((2, ways - 1, many, end_rows, cols), BF16),
            pltpu.VMEM((many, chunk, cols), F32),
            pltpu.SemaphoreType.DMA((DEPTH, most)),
            pltpu.SemaphoreType.DMA((2, ways)),
        ]
    first_half, seq_bit = len(shapes), None
    if halving is not None:
        seq_bit = halving.seq_left.pop(0)
        arrays += [halving.own, halving.got[0][0]]
        whole = halving.own.shape
        half = whole[:2] + (whole[2] // 2,) + whole[3:]
        shapes += [jax.ShapeDtypeStruct(half, kind) for kind in (F32, BF16)]
        scratch += [pltpu.VMEM(whole, F32), pltpu.VMEM(whole, BF16)]
        scratch += [pltpu.VMEM(half, F32), pltpu.VMEM(half, BF16), pltpu.SemaphoreType.DMA((4,))]
    any_spec = pl.BlockSpec(memory_space=pl.ANY)
    results = pl.pallas_call(
        partial(combine_kernel, blocks, len(arrays), len(shapes), seq, ways, seq_bit),
        in_specs=[SMEM_SPEC] + [any_spec] * len(arrays),
        out_specs=[any_spec] * len(shapes),
        out_shape=shapes,
        scratch_shapes=scratch,
        compiler_params=pltpu.CompilerParams(vmem_limit_bytes=VMEM),
        cost_estimate=cost(4),
        name="combine",
    )(place, *arrays)

    def go(results):
        got = {bit: model.flight.start(swap(value, bit)) for bit, value in zip(order, results)}
        for total, lane, bit, free, first in turns:
            total.lanes[lane].append((got[bit], first, free, False))
        if halving is not None:
            halving.own = results[first_half]
            pairs = [(i, i ^ (1 << seq_bit)) for i in range(seq)]
            sent = lax.ppermute(results[first_half + 1], "seq", pairs)
            halving.got = [halving.flight.start(sent)]
        if closing is None:
            return
        parts = results[first_end:first_half]
        if not split:
            half = parts[0].reshape(2, many, seq, chunk // seq, cols)
            here = lax.axis_index("seq")
            parts = [
                lax.dynamic_index_in_dim(half, (here + hop) % seq, 2, keepdims=False)
                for hop in range(seq)
            ]
        closing.own = parts[0].astype(F32)
        closing.seq_left = []
        if split and ways < seq:
            pairs = [(i, i ^ 1) for i in range(seq)]
            closing.got = [closing.flight.start(lax.ppermute(parts[1], "seq", pairs))]
            closing.seq_left = list(range(1, seq.bit_length() - 1))
            return
        closing.got = []
        for hop, send in enumerate(parts[1:]):
            pairs = [(i, (i + hop + 1) % seq) for i in range(seq)]
            closing.got.append(closing.flight.start(lax.ppermute(send, "seq", pairs)))

    return list(results), go


def finish_sum(total):
    value = total.own
    for got in total.got:
        value = value + got[0].astype(F32)
    return value.reshape(2, total.many, -1, total.cols)


def vector_hops():
    seq = lax.axis_size("seq")
    hops = []
    for bit in range(seq.bit_length() - 1):
        pairs = [(i, i ^ (1 << bit)) for i in range(seq)]
        hops.append(partial(lax.ppermute, axis_name="seq", perm=pairs))
    return hops + [partial(swap, bit=bit) for bit in range(lax.axis_size("dp").bit_length() - 1)]


def exchange(x, d, rows):
    seq = lax.axis_size("seq")
    first = jnp.concatenate([x[:rows], d[:rows]], axis=1)
    last = jnp.concatenate([x[-rows:], d[-rows:]], axis=1)
    from_left = lax.ppermute(last, "seq", [(i, i + 1) for i in range(seq - 1)])
    from_right = lax.ppermute(first, "seq", [(i + 1, i) for i in range(seq - 1)])
    return (from_left, from_right)


def core_split(value):
    pairs = lax.axis_size("dp") // 2
    two, many, depth, cols = value.shape
    shaped = value.reshape(two, many, pairs, 2, depth // (2 * pairs), cols)
    kept = half_of([shaped], 3, 0, True)[0]
    sent = half_of([shaped], 3, 0, False)[0]
    return (kept, sent)


PARTS = 3


def per_device(
    tokens, item_types, first_gain, first_shift, qkv_weight, query_bias, value_bias, attn_weight,
    attn_bias, second_gain, second_shift, expert_up, up_bias, expert_down, down_bias, cotangent,
):
    tok, width = tokens.shape
    dp, seq = lax.axis_size("dp"), lax.axis_size("seq")
    rows = capacity(tok)
    chunk = width // dp
    chunk = chunk if chunk % 16 == 0 else 0
    bits = [(lax.axis_index("dp") >> bit) & 1 for bit in range(dp.bit_length() - 1)]
    place = jnp.stack([lax.axis_index("seq")] + bits).astype(jnp.int32)
    left, right = exchange(tokens, cotangent, HALO)
    x, g, info = sort_rows(place, item_types, tokens, cotangent, rows, tok * seq)
    x, g, left, right = lax.optimization_barrier((x, g, left, right))
    x, g, h, qkv, att, mid, h2 = forward_rows(
        info, left, right, x, g, first_gain, first_shift, qkv_weight, query_bias, value_bias,
        attn_weight, attn_bias, second_gain, second_shift, tok,
    )

    flight = Flight()

    def window(sums, tied=(), halving=()):
        late = [total for total in list(sums) + list(halving) if total.seq_left]
        steps = [total for total in sums if total.more()]
        closing = [total for total in sums if not total.more() and total.own is None]
        if not (late or steps or closing):
            return (info,) + tuple(tied)
        ready, go = advance(
            place, steps, closing[0] if closing else None, late[0] if late else None
        )
        gate, ready, tied = lax.optimization_barrier((info, ready, tuple(tied)))
        go(ready)
        return (gate,) + tuple(tied)

    sums, up_biases, acts, dups = [], [], [], []
    gate = info
    for part in range(PARTS):
        results = run_hidden(part, PARTS, gate, h2, g, expert_up, up_bias, expert_down, chunk)
        results = flight.land(*results)
        bias, act, dup = results[-3:]
        up_biases.append(bias)
        acts.append(act)
        dups.append(dup)
        if chunk:
            kept, sent = results[:2]
        else:
            kept, sent = core_split(results[0])
        new = Sum(flight, kept, sent)
        new.ways = 2
        (gate,) = window(sums)
        sums.append(new)
    results = finish_experts(
        gate, mid, g, acts, dups, expert_up, expert_down, second_gain, down_bias, attn_weight
    )
    row_sums, mixed, dx, proj, datt = flight.land(*results)
    (gate,) = window(sums)
    results = attend_back(gate, qkv, datt)
    gate, results = lax.optimization_barrier((gate, results))
    m_rows = unsort_rows(gate, mixed, tok)
    dq, dk, dv, m_own, m_left, m_right = flight.land(*results, *m_rows)
    (gate,) = window(sums)
    kept, sent = flight.land(*projection_grads(gate, dq, dk, dv, proj, h, att, dp, seq))
    last = Sum(flight, kept, sent)
    (gate,) = window(sums)

    def send_rows(left, right):
        to_left = lax.ppermute(left, "seq", [(i + 1, i) for i in range(seq - 1)])
        to_right = lax.ppermute(right, "seq", [(i, i + 1) for i in range(seq - 1)])
        return flight.start(to_left), flight.start(to_right)

    def merge(own, got):
        own = own.at[:HALO].add(got[1][0].astype(own.dtype))
        return own.at[tok - HALO :].add(got[0][0].astype(own.dtype))

    gate, m_left, m_right = lax.optimization_barrier((gate, m_left, m_right))
    m_got = send_rows(m_left, m_right)
    results = last_norm(gate, x, dx, dq, dk, dv, first_gain, qkv_weight, row_sums, up_biases)
    grad_x, packed = flight.land(*results)

    hops = vector_hops()

    def hop(packed, moved=None):
        packed = packed if moved is None else packed + moved[0]
        return packed, flight.start(hops.pop(0)(packed))

    packed, moved = hop(packed)
    (gate,) = window([last], halving=sums[-1:])
    while any(total.own is None or total.seq_left for total in sums):
        (gate,) = window(sums)
    gate, moved[0] = lax.optimization_barrier((gate, moved[0]))
    flight.cells = [cell for cell in flight.cells if cell is not moved]
    packed, moved = hop(packed, moved)
    results = flight.land(merge(m_own, m_got), *unsort_rows(gate, grad_x, tok))
    mixed_out, g_own, left, right = results
    expert_sums = [finish_sum(total) for total in sums]
    packed, moved = hop(packed, moved)
    later = []
    while last.own is None:
        _, g_own = window([last], tied=[g_own])
        if not later:
            g_got = send_rows(left, right)
            later = list(g_got)
        if last.own is None:
            expert_sums = flight.land(*expert_sums, later=later)

    packed, moved = hop(packed, moved)
    (grad_out,) = flight.land(merge(g_own, g_got), later=[moved])
    while hops:
        packed, moved = hop(packed, moved)
    packed = packed + moved[0]
    last_sums = finish_sum(last)

    own = width // (dp * seq)
    rank = lax.axis_index("dp") * seq + lax.axis_index("seq")
    vectors = lax.dynamic_slice(packed, (0, rank * own), (14, own))
    tile = up_biases[0].shape[2]
    up_total = packed[14 : 14 + PARTS * EXPERTS, :tile].reshape(PARTS, EXPERTS, tile)
    sum_up = jnp.concatenate([total[0] for total in expert_sums], axis=-1)
    sum_down = jnp.concatenate([total[1] for total in expert_sums], axis=-1).swapaxes(1, 2)
    last_sums = jnp.concatenate([last_sums[0, 0], last_sums[1, 0]], axis=1).T

    return (
        mixed_out,
        grad_out,
        vectors[0],
        vectors[1],
        last_sums[:, : 3 * own],
        vectors[2],
        vectors[3],
        last_sums[:, 3 * own :],
        vectors[4],
        vectors[5:8],
        vectors[8:11],
        sum_up,
        up_total.swapaxes(0, 1).reshape(EXPERTS, -1),
        sum_down,
        vectors[11:14],
    )


def solution(mesh):
    split = P(("dp", "seq"))
    in_specs = (P(("dp", "seq"), None), P("dp", None)) + (P(),) * 13 + (P(("dp", "seq"), None),)
    out_specs = (
        P(("dp", "seq"), None),
        P(("dp", "seq"), None),
        split,
        split,
        P(None, ("dp", "seq")),
        split,
        split,
        P(None, ("dp", "seq")),
        split,
        P(None, ("dp", "seq")),
        P(None, ("dp", "seq")),
        P(None, ("dp", "seq"), None),
        P(),
        P(None, None, ("dp", "seq")),
        P(None, ("dp", "seq")),
    )
    return jax.shard_map(
        per_device, mesh=mesh, in_specs=in_specs, out_specs=out_specs, check_vma=False
    )
```

```python
from functools import partial

import jax
import jax.numpy as jnp
from jax import lax
from jax.experimental import pallas as pl
from jax.experimental.pallas import tpu as pltpu
from jax.sharding import PartitionSpec as P

HD = 64
EXPERTS = 3
IMG_LEN = 197
TXT_LEN = 64
LENS = (IMG_LEN, TXT_LEN, IMG_LEN + TXT_LEN)
SLOTS = (208, 64, 272)
TXT_PAIR = 128
PAD_ROWS = 384
HALO = 144
ROW = 128
BLK = 256

EPS = 1e-05
NEG = -1e30
VMEM = 60 << 20
F32 = jnp.float32
BF16 = jnp.bfloat16

N_IMG, N_TXT, N_BOTH, N_PAD = 0, 1, 2, 3
G_IMG, G_TXT, G_BOTH, G_PAD, G_END = 4, 5, 6, 7, 8
PAD_LEN, OWN_N, CORE = 9, 10, 11
TABLE = 16
INFO = 256


def nn(a, b):
    return lax.dot_general(a, b, (((1,), (0,)), ((), ())), preferred_element_type=F32)


def nt(a, b):
    return lax.dot_general(a, b, (((1,), (1,)), ((), ())), preferred_element_type=F32)


def tn(a, b):
    return lax.dot_general(a, b, (((0,), (0,)), ((), ())), preferred_element_type=F32)


def cost(microseconds):
    return pl.CostEstimate(flops=int(microseconds * 1e10), bytes_accessed=0, transcendentals=0)


SMEM_SPEC = pl.BlockSpec(memory_space=pltpu.SMEM)


def up_to(value, unit):
    return ((value + unit - 1) // unit) * unit


def normalize(v):
    mean = jnp.mean(v, axis=-1, keepdims=True)
    cent = v - mean
    var = jnp.mean(cent * cent, axis=-1, keepdims=True)
    inverse = lax.rsqrt(var + EPS)
    return (cent * inverse, inverse)


def norm_back(grad, normed, inverse):
    inner = jnp.mean(grad * normed, axis=-1, keepdims=True)
    return inverse * (grad - jnp.mean(grad, axis=-1, keepdims=True) - normed * inner)


def capacity(tok):
    rows = tok + LENS[2] - 1
    best = 0
    for images in range(rows // LENS[0] + 1):
        for both in range((rows - images * LENS[0]) // LENS[2] + 1):
            left = rows - images * LENS[0] - both * LENS[2]
            for pad in (0, 1):
                spare = left - pad * (1 + LENS[2] // 2)
                if spare < 0:
                    continue
                texts = spare // LENS[1]
                for count in range(texts + 1):
                    total = (
                        up_to(images * SLOTS[0], ROW)
                        + up_to(count * SLOTS[1], ROW)
                        + up_to(both * SLOTS[2], ROW)
                        + pad * PAD_ROWS
                    )
                    best = max(best, total)
    return up_to(best, BLK)


def gather_rows(info, wins, outs):
    for out in outs:
        out[...] = jnp.zeros_like(out)

    def place(index, carry):
        source = info[TABLE + 3 * index]
        target = pl.multiple_of(info[TABLE + 3 * index + 1], 16)
        kind = info[TABLE + 3 * index + 2]
        begin = pl.multiple_of((source // 16) * 16, 16)
        shift = source - begin
        for which in range(EXPERTS):
            slot = SLOTS[which]
            fits = (kind == which) if which < 2 else (kind >= 2)
            size = LENS[which] if which < 2 else jnp.where(kind == 2, LENS[2], info[PAD_LEN])

            @pl.when(fits)
            def _(slot=slot, size=size):
                rows = lax.broadcasted_iota(jnp.int32, (slot, slot + 16), 0)
                cols = lax.broadcasted_iota(jnp.int32, (slot, slot + 16), 1)
                chosen = ((cols == rows + shift) & (rows < size)).astype(F32).astype(BF16)
                for win, out in zip(wins, outs):
                    value = nn(chosen, win[pl.ds(begin, slot + 16), :])
                    out[pl.ds(target, slot), :] = value.astype(BF16)

        return carry

    lax.fori_loop(0, info[OWN_N], place, 0)


def sort_kernel(tok, group, place_ref, types, x_own, d_own, x_out, d_out, info, x_win, d_win):
    items = types.shape[1]
    low = place_ref[0] * tok
    info[CORE] = place_ref[1]
    width = x_own.shape[1]
    for win, own_rows in ((x_win, x_own), (d_win, d_own)):
        rest = win.shape[0] - (HALO + tok)
        win[pl.ds(0, HALO), :] = jnp.zeros((HALO, width), BF16)
        win[pl.ds(HALO, tok), :] = own_rows[...]
        win[pl.ds(HALO + tok, rest), :] = jnp.zeros((rest, width), BF16)

    def length(kind):
        return jnp.where(
            kind == 0, LENS[0], jnp.where(kind == 1, LENS[1], jnp.where(kind == 2, LENS[2], 0))
        )

    def owned(start, size):
        middle = (start + start + size) // 2
        return (middle >= low) & (middle < low + tok) & (size > 0)

    def count(index, carry):
        start, images, texts, boths = carry
        kind = types[0, index]
        size = length(kind)
        mine = owned(start, size)
        return (
            start + size,
            images + jnp.where(mine & (kind == 0), 1, 0),
            texts + jnp.where(mine & (kind == 1), 1, 0),
            boths + jnp.where(mine & (kind == 2), 1, 0),
        )

    zero = jnp.int32(0)
    total, images, texts, boths = lax.fori_loop(0, items, count, (zero, zero, zero, zero))
    pad_len = group - total
    pad = owned(total, pad_len)
    g_txt = up_to(images * SLOTS[0], ROW)
    g_both = g_txt + up_to(texts * SLOTS[1], ROW)
    g_pad = g_both + up_to(boths * SLOTS[2], ROW)
    info[N_IMG] = images
    info[N_TXT] = texts
    info[N_BOTH] = boths
    info[N_PAD] = jnp.where(pad, 1, 0)
    info[G_IMG] = zero
    info[G_TXT] = g_txt
    info[G_BOTH] = g_both
    info[G_PAD] = g_pad
    info[G_END] = g_pad + jnp.where(pad, PAD_ROWS, 0)
    info[PAD_LEN] = pad_len

    def note(own, source, target, kind):
        info[TABLE + 3 * own] = source
        info[TABLE + 3 * own + 1] = target
        info[TABLE + 3 * own + 2] = kind

    def place(index, carry):
        start, images, texts, boths, own = carry
        kind = types[0, index]
        size = length(kind)
        mine = owned(start, size)

        @pl.when(mine)
        def _():
            target = jnp.where(
                kind == 0,
                images * SLOTS[0],
                jnp.where(kind == 1, g_txt + texts * SLOTS[1], g_both + boths * SLOTS[2]),
            )
            note(own, start - low + HALO, target, kind)

        return (
            start + size,
            images + jnp.where(mine & (kind == 0), 1, 0),
            texts + jnp.where(mine & (kind == 1), 1, 0),
            boths + jnp.where(mine & (kind == 2), 1, 0),
            own + jnp.where(mine, 1, 0),
        )

    own = lax.fori_loop(0, items, place, (zero, zero, zero, zero, zero))[-1]

    @pl.when(pad)
    def _():
        note(own, total - low + HALO, g_pad, jnp.int32(EXPERTS))

    info[OWN_N] = own + jnp.where(pad, 1, 0)
    gather_rows(info, (x_win, d_win), (x_out, d_out))


def sort_rows(place, types, x, d, rows, group):
    tok, width = x.shape
    vmem = pl.BlockSpec(memory_space=pltpu.VMEM)
    return pl.pallas_call(
        partial(sort_kernel, tok, group),
        out_shape=[
            jax.ShapeDtypeStruct((rows, width), BF16),
            jax.ShapeDtypeStruct((rows, width), BF16),
            jax.ShapeDtypeStruct((INFO,), jnp.int32),
        ],
        in_specs=[SMEM_SPEC, SMEM_SPEC] + [vmem] * 2,
        out_specs=[vmem, vmem, SMEM_SPEC],
        scratch_shapes=[pltpu.VMEM((tok + HALO + 288, width), BF16)] * 2,
        compiler_params=pltpu.CompilerParams(vmem_limit_bytes=VMEM),
        cost_estimate=cost(11),
        name="sort_rows",
    )(place, types, x, d)


def patch_ends(tok, info, left, right, arrived, visits):
    count = info[OWN_N]

    def for_slots(end, visit):
        index = jnp.maximum(count - 1, 0) if end else 0
        source = info[TABLE + 3 * index]
        target = pl.multiple_of(info[TABLE + 3 * index + 1], 16)
        kind = info[TABLE + 3 * index + 2]
        size = jnp.where(kind == 0, LENS[0], jnp.where(kind == 1, LENS[1], LENS[2]))
        size = jnp.where(kind == EXPERTS, info[PAD_LEN], size)
        over = (source + size > HALO + tok) if end else (source < HALO)
        for which in range(EXPERTS):
            slot = SLOTS[which]
            fits = (kind == which) if which < 2 else (kind >= 2)

            @pl.when(over & (count > 0) & fits)
            def _(slot=slot):
                def rows():
                    into = lax.broadcasted_iota(jnp.int32, (slot, HALO), 0)
                    cols = lax.broadcasted_iota(jnp.int32, (slot, HALO), 1)
                    shift = source - HALO - tok if end else source
                    chosen = ((cols == into + shift) & (into < size)).astype(F32).astype(BF16)
                    return nn(chosen, (right if end else left)[...])

                visit(end, slot, pl.ds(target, slot), rows)

    for number, visit in enumerate(visits):
        if number == arrived[0]:
            arrived[1]()
        for end in range(2):
            for_slots(end, visit)


def forward_kernel(
    tok, info, left, right, x_in, d_in, gain, shift, qkv_weight, query_bias, value_bias,
    attn_weight, attn_bias, gains, shifts,
    x_out, d_out, h_out, qkv_out, att_out, mid_out, h2_out,
    x_v, qkv_v, att_v, w_qkv, w_attn, d_v, h_v, mid_v, h2_v, product_v,
    load_sems, patch_sems, h_sems, qkv_sems, att_sems, mid_sems, h2_sems,
):
    width = x_v.shape[1]
    blocks = (info[G_END] + BLK - 1) // BLK
    load_x = pltpu.make_async_copy(x_in, x_v, load_sems.at[0])
    load_qkv = pltpu.make_async_copy(qkv_weight, w_qkv, load_sems.at[1])
    load_attn = pltpu.make_async_copy(attn_weight, w_attn, load_sems.at[2])
    load_x.start()
    load_qkv.start()

    def each(low, high, visit):
        def body(index, carry):
            visit(index)
            return carry

        lax.fori_loop(low, high, body, 0)

    def d_copy(end, slot, at, inward):
        near, far = d_v.at[end, pl.ds(0, slot), :], d_out.at[at, :]
        source, target = (far, near) if inward else (near, far)
        return pltpu.make_async_copy(source, target, patch_sems.at[end, 0])

    def x_copy(end, at):
        return pltpu.make_async_copy(x_v.at[at, :], x_out.at[at, :], patch_sems.at[end, 1])

    def fetch(end, slot, at, rows):
        d_copy(end, slot, at, True).start()

    def add(end, slot, at, rows):
        added = rows()
        x_v[at, :] = (x_v[at, :].astype(F32) + added[:, :width]).astype(BF16)
        x_copy(end, at).start()
        d_copy(end, slot, at, True).wait()
        here = pl.ds(0, slot)
        d_v[end, here, :] = (d_v[end, here, :].astype(F32) + added[:, width:]).astype(BF16)
        d_copy(end, slot, at, False).start()

    patch_ends(tok, info, left, right, (1, load_x.wait), (fetch, add))
    load_attn.start()
    load_qkv.wait()

    def h_copy(index):
        at = pl.ds(pl.multiple_of(index * BLK, BLK), BLK)
        return pltpu.make_async_copy(h_v.at[index % 2], h_out.at[at, :], h_sems.at[index % 2])

    def qkv_copy(index):
        at = pl.ds(pl.multiple_of(index * BLK, BLK), BLK)
        return pltpu.make_async_copy(qkv_v.at[at, :], qkv_out.at[at, :], qkv_sems.at[index])

    sub = BLK // 4

    def norm_part(index, turn):
        at = pl.ds(pl.multiple_of(index * BLK + turn * sub, sub), sub)
        normed, _ = normalize(x_v[at, :].astype(F32))
        hidden = (normed * gain[...] + shift[...]).astype(BF16)
        h_v[index % 2, pl.ds(turn * sub, sub), :] = hidden

    def multiply_part(index, hidden, part):
        at = pl.ds(pl.multiple_of(index * BLK, BLK), BLK)
        cols = pl.ds(part * width, width)
        value = nn(hidden, w_qkv[:, cols])
        if part == 0:
            value = (value + query_bias[...]) * (HD ** (-0.5))
        if part == 2:
            value = value + value_bias[...]
        qkv_v[at, cols] = value.astype(BF16)

    def project(index):
        @pl.when(index >= 2)
        def _():
            h_copy(index - 2).wait()

        @pl.when(index == 0)
        def _():
            for turn in range(4):
                norm_part(index, turn)

        @pl.when((index > 0) & (index < blocks))
        def _():
            hidden = h_v[(index + 1) % 2]
            for turn in range(4):
                norm_part(index, turn)
                if turn < 3:
                    multiply_part(index - 1, hidden, turn)

        @pl.when((index > 0) & (index == blocks))
        def _():
            hidden = h_v[(index + 1) % 2]
            for part in range(3):
                multiply_part(index - 1, hidden, part)

        @pl.when(index < blocks)
        def _():
            h_copy(index).start()

        @pl.when(index > 0)
        def _():
            qkv_copy(index - 1).start()

    each(0, jnp.where(blocks > 0, blocks + 1, 0), project)

    att_v[...] = jnp.zeros_like(att_v)

    masks = head_masks(HEADS)
    wide = HEADS * HD

    def visit(start, slot, bias):
        at = pl.ds(start, slot)
        for group in range(width // wide):
            cols = [pl.ds(part * width + group * wide, wide) for part in range(3)]
            q, k, v = [qkv_v[at, one] for one in cols]
            scores = nt(stacked(k, masks), q)
            probs = []
            for head in range(HEADS):
                prob = softmax_cols(scores[head * slot : (head + 1) * slot], bias)
                probs.append(prob.astype(BF16))
            att_v[at, cols[0]] = tn(jnp.concatenate(probs), stacked(v, masks)).astype(BF16)

    for_items(info, visit)
    load_attn.wait()

    def block_copies(index):
        at = pl.ds(pl.multiple_of(index * BLK, BLK), BLK)
        slot = index % 2
        return (
            pltpu.make_async_copy(mid_v.at[slot], mid_out.at[at, :], mid_sems.at[slot]),
            pltpu.make_async_copy(h2_v.at[slot], h2_out.at[at, :], h2_sems.at[slot]),
        )

    def att_copy(index):
        at = pl.ds(pl.multiple_of(index * BLK, BLK), BLK)
        return pltpu.make_async_copy(att_v.at[at, :], att_out.at[at, :], att_sems.at[index])

    each(0, blocks, lambda index: att_copy(index).start())

    def add_part(index, turn):
        slot = index % 2
        rows = pl.ds(turn * ROW, ROW)
        row = index * BLK + turn * ROW
        at = pl.ds(pl.multiple_of(row, ROW), ROW)
        value = x_v[at, :].astype(F32) + (product_v[slot, rows, :] + attn_bias[...])
        mid_v[slot, rows, :] = value
        normed, _ = normalize(value)
        which = pl.ds(jnp.minimum(group_of(info, row), EXPERTS - 1), 1)
        h2_v[slot, rows, :] = (normed * gains[which, :] + shifts[which, :]).astype(BF16)

    def middle(index):
        @pl.when(index >= 3)
        def _():
            for copy in block_copies(index - 3):
                copy.wait()

        whole = pl.ds(pl.multiple_of(index * BLK, BLK), BLK)
        turns = BLK // ROW

        @pl.when(index == 0)
        def _():
            product_v[0] = nn(att_v[whole, :], w_attn[...])

        @pl.when((index > 0) & (index < blocks))
        def _():
            value = nn(att_v[whole, :], w_attn[...])
            for turn in range(turns):
                add_part(index - 1, turn)
            product_v[index % 2] = value

        @pl.when((index > 0) & (index == blocks))
        def _():
            for turn in range(turns):
                add_part(index - 1, turn)

        @pl.when(index > 0)
        def _():
            for copy in block_copies(index - 1):
                copy.start()

    each(0, jnp.where(blocks > 0, blocks + 1, 0), middle)

    def wait_rows(end, slot, at, rows):
        x_copy(end, at).wait()
        d_copy(end, slot, at, False).wait()

    patch_ends(tok, info, left, right, (-1, None), (wait_rows,))
    each(0, blocks, lambda index: qkv_copy(index).wait())
    each(0, blocks, lambda index: att_copy(index).wait())
    for back in (2, 1):

        @pl.when(blocks >= back)
        def _(back=back):
            for copy in block_copies(blocks - back):
                copy.wait()

    @pl.when(blocks >= 1)
    def _():
        h_copy(blocks - 1).wait()


def forward_rows(
    info, left, right, x, d, gain, shift, qkv_weight, query_bias, value_bias, attn_weight,
    attn_bias, gains, shifts, tok,
):
    rows, width = x.shape
    vmem = pl.BlockSpec(memory_space=pltpu.VMEM)
    any_spec = pl.BlockSpec(memory_space=pl.ANY)
    low = lambda cols: jax.ShapeDtypeStruct((rows, cols), BF16)
    blocks = rows // BLK
    return pl.pallas_call(
        partial(forward_kernel, tok),
        out_shape=[
            low(width),
            low(width),
            low(width),
            low(3 * width),
            low(width),
            jax.ShapeDtypeStruct((rows, width), F32),
            low(width),
        ],
        in_specs=[SMEM_SPEC, vmem, vmem, any_spec, any_spec, vmem, vmem, any_spec, vmem, vmem]
        + [any_spec, vmem, vmem, vmem],
        out_specs=[any_spec] * 7,
        scratch_shapes=[
            pltpu.VMEM((rows, width), BF16),
            pltpu.VMEM((rows, 3 * width), BF16),
            pltpu.VMEM((rows, width), BF16),
            pltpu.VMEM(qkv_weight.shape, BF16),
            pltpu.VMEM(attn_weight.shape, BF16),
            pltpu.VMEM((2, SLOTS[2], width), BF16),
            pltpu.VMEM((2, BLK, width), BF16),
            pltpu.VMEM((2, BLK, width), F32),
            pltpu.VMEM((2, BLK, width), BF16),
            pltpu.VMEM((2, BLK, width), F32),
            pltpu.SemaphoreType.DMA((3,)),
            pltpu.SemaphoreType.DMA((2, 2)),
            pltpu.SemaphoreType.DMA((2,)),
            pltpu.SemaphoreType.DMA((blocks,)),
            pltpu.SemaphoreType.DMA((blocks,)),
            pltpu.SemaphoreType.DMA((2,)),
            pltpu.SemaphoreType.DMA((2,)),
        ],
        input_output_aliases={3: 0, 4: 1},
        compiler_params=pltpu.CompilerParams(vmem_limit_bytes=VMEM),
        cost_estimate=cost(45),
        name="forward_rows",
    )(
        info, left, right, x, d, gain, shift, qkv_weight, query_bias, value_bias, attn_weight,
        attn_bias, gains, shifts,
    )


def unsort_kernel(info, rows, own_rows, left, right, win):
    tok = own_rows.shape[0]
    win[...] = jnp.zeros_like(win)

    def place(index, carry):
        source = info[TABLE + 3 * index]
        target = pl.multiple_of(info[TABLE + 3 * index + 1], 16)
        kind = info[TABLE + 3 * index + 2]
        begin = pl.multiple_of((source // 16) * 16, 16)
        shift = source - begin
        for which in range(EXPERTS):
            slot = SLOTS[which]
            fits = (kind == which) if which < 2 else (kind >= 2)
            size = LENS[which] if which < 2 else jnp.where(kind == 2, LENS[2], info[PAD_LEN])

            @pl.when(fits)
            def _(slot=slot, size=size):
                into = lax.broadcasted_iota(jnp.int32, (slot + 16, slot), 0)
                cols = lax.broadcasted_iota(jnp.int32, (slot + 16, slot), 1)
                chosen = ((into == cols + shift) & (cols < size)).astype(F32).astype(BF16)
                value = rows[pl.ds(target, slot), :]
                to = pl.ds(begin, slot + 16)
                high = value.astype(BF16)
                if rows.dtype == BF16:
                    win[to, :] += nn(chosen, high)
                else:
                    rest = (value - high.astype(F32)).astype(BF16)
                    win[to, :] += nn(chosen, high) + nn(chosen, rest)

        return carry

    lax.fori_loop(0, info[OWN_N], place, 0)
    for part, begin in ((left, 0), (own_rows, HALO), (right, HALO + tok)):
        part[...] = win[pl.ds(begin, part.shape[0]), :].astype(part.dtype)


def unsort_rows(info, rows, tok):
    width = rows.shape[1]
    vmem = pl.BlockSpec(memory_space=pltpu.VMEM)
    return pl.pallas_call(
        unsort_kernel,
        out_shape=[
            jax.ShapeDtypeStruct((tok, width), rows.dtype),
            jax.ShapeDtypeStruct((HALO, width), BF16),
            jax.ShapeDtypeStruct((HALO, width), BF16),
        ],
        in_specs=[SMEM_SPEC, vmem],
        out_specs=[vmem] * 3,
        scratch_shapes=[pltpu.VMEM((tok + HALO + 288, width), F32)],
        compiler_params=pltpu.CompilerParams(vmem_limit_bytes=VMEM),
        cost_estimate=cost(0.1),
        name="unsort_rows",
    )(info, rows)


def full(shape):
    return pl.BlockSpec(shape, lambda *_: (0,) * len(shape))


def held(shape):
    return pl.BlockSpec(shape, lambda *_: (0,) * len(shape), pipeline_mode=pl.Buffered(1))


HEADS, BACK_HEADS = 2, 4


def softmax_cols(scores, bias):
    masked = scores + bias
    expo = jnp.exp(masked - jnp.max(masked, axis=0, keepdims=True))
    return expo * (1.0 / jnp.sum(expo, axis=0, keepdims=True))


def for_items(info, visit):
    def cut(slot, size):
        return jnp.where(lax.broadcasted_iota(jnp.int32, (slot, 1), 0) < size, 0.0, NEG)

    def image(index, carry):
        slot = SLOTS[0]
        visit(pl.multiple_of(index * slot, 16), slot, cut(slot, LENS[0]))
        return carry

    def text(index, carry):
        slot = TXT_PAIR
        rows = lax.broadcasted_iota(jnp.int32, (slot, slot), 0) // TXT_LEN
        cols = lax.broadcasted_iota(jnp.int32, (slot, slot), 1) // TXT_LEN
        start = pl.multiple_of(info[G_TXT] + index * slot, ROW)
        visit(start, slot, jnp.where(rows == cols, 0.0, NEG))
        return carry

    def both(index, carry):
        slot = SLOTS[2]
        real = index < info[N_BOTH]
        start = jnp.where(real, info[G_BOTH] + index * slot, info[G_PAD])
        size = jnp.where(real, LENS[2], info[PAD_LEN])
        visit(pl.multiple_of(start, 16), slot, cut(slot, size))
        return carry

    lax.fori_loop(0, info[N_IMG], image, 0)
    lax.fori_loop(0, (info[N_TXT] + 1) // 2, text, 0)
    lax.fori_loop(0, info[N_BOTH] + info[N_PAD], both, 0)


def head_masks(heads):
    lanes = lax.broadcasted_iota(jnp.int32, (1, heads * HD), 1) // HD
    return [lanes == head for head in range(heads)]


def stacked(value, masks):
    return jnp.concatenate([jnp.where(mask, value, 0) for mask in masks], axis=0)


def own_columns(value, masks):
    rows = value.shape[0] // len(masks)
    result = value[:rows]
    for head in range(1, len(masks)):
        result = jnp.where(masks[head], value[head * rows : (head + 1) * rows], result)
    return result


def attend_back_kernel(info, query, key, value, grad, dq_out, dk_out, dv_out):
    for out in (dq_out, dk_out, dv_out):
        out[...] = jnp.zeros_like(out)
    masks = head_masks(BACK_HEADS)
    wide = BACK_HEADS * HD

    def visit(start, slot, bias):
        at = pl.ds(start, slot)
        for group in range(query.shape[1] // wide):
            cols = pl.ds(group * wide, wide)
            q, k, v, g = query[at, cols], key[at, cols], value[at, cols], grad[at, cols]
            keys = stacked(k, masks)
            scores = nt(keys, q)
            grad_probs = nt(stacked(v, masks), g)
            probs, grad_scores = [], []
            for head in range(BACK_HEADS):
                mine = slice(head * slot, (head + 1) * slot)
                prob = softmax_cols(scores[mine], bias)
                product = prob * grad_probs[mine]
                inner = jnp.sum(product, axis=0, keepdims=True)
                probs.append(prob.astype(BF16))
                grad_scores.append((product - prob * inner).astype(BF16))
            probs, grad_scores = jnp.concatenate(probs), jnp.concatenate(grad_scores)
            dq = tn(grad_scores, keys).astype(BF16)
            dq_out[at, cols] = (dq.astype(F32) * HD ** (-0.5)).astype(BF16)
            dk_out[at, cols] = own_columns(nn(grad_scores, q), masks).astype(BF16)
            dv_out[at, cols] = own_columns(nn(probs, g), masks).astype(BF16)

    for_items(info, visit)


def attend_back(info, qkv, grad):
    rows = qkv.shape[0]
    width = qkv.shape[1] // 3
    spec = pl.BlockSpec((rows, width), lambda p: (0, 0))
    return pl.pallas_call(
        attend_back_kernel,
        grid=(1,),
        out_shape=[jax.ShapeDtypeStruct((rows, width), BF16)] * 3,
        in_specs=[
            SMEM_SPEC,
            spec,
            pl.BlockSpec((rows, width), lambda p: (0, 1)),
            pl.BlockSpec((rows, width), lambda p: (0, 2)),
            spec,
        ],
        out_specs=[spec] * 3,
        compiler_params=pltpu.CompilerParams(vmem_limit_bytes=VMEM),
        cost_estimate=cost(30),
        name="attend_back",
    )(info, qkv, qkv, qkv, grad)


def group_of(info, row):
    return (
        (row >= info[G_TXT]).astype(jnp.int32)
        + (row >= info[G_BOTH]).astype(jnp.int32)
        + (row >= info[G_PAD]).astype(jnp.int32)
    )


def gelu_parts(up):
    size = jnp.abs(up) * (0.5**0.5)
    expo = jnp.exp(-size * size)
    t = 1.0 / (1.0 + 0.3275911 * size)
    poly = 1.061405429 * t - 1.453152027
    poly = poly * t + 1.421413741
    poly = poly * t - 0.284496736
    poly = poly * t + 0.254829592
    tail = 0.5 * (poly * t) * expo
    cdf = jnp.where(up >= 0, 1.0 - tail, tail)
    return (up * cdf, cdf + up * (expo * 0.3989422804014327))


KROWS = 512
COLS = 1


def hidden_kernel(part, chunk, *refs):
    info, h_hbm, g_hbm, up_hbm, b_up, down_hbm = refs[:6]
    refs = refs[6:]
    weight_outs, refs = (refs[:2], refs[2:]) if chunk else (refs[:1], refs[1:])
    bias_out, act_hbm, dup_hbm, left, right, w_up, w_down, acc, stage = refs[:9]
    row_sems, weight_sems, hidden_sems, stage_sems = refs[9:]
    tile = w_up.shape[2]
    cols_at = pl.ds(part * tile, tile)
    bias_out[...] = jnp.zeros_like(bias_out)

    def rows_copies(index):
        at = pl.ds(pl.multiple_of(index * ROW, ROW), ROW)
        return [
            pltpu.make_async_copy(source.at[at, :], left.at[which, at, :], row_sems.at[which, index])
            for which, source in enumerate((h_hbm, g_hbm))
        ]

    def weight_copies(expert):
        return [
            pltpu.make_async_copy(
                up_hbm.at[expert, :, cols_at], w_up.at[expert], weight_sems.at[0, expert]
            ),
            pltpu.make_async_copy(
                down_hbm.at[expert, cols_at, :], w_down.at[expert], weight_sems.at[1, expert]
            ),
        ]

    def hidden_copies(index):
        at = pl.ds(pl.multiple_of(index * ROW, ROW), ROW)
        return [
            pltpu.make_async_copy(right.at[which, at, :], target.at[at, :], hidden_sems.at[which, index])
            for which, target in enumerate((dup_hbm, act_hbm))
        ]

    def stage_copies(slot, expert):
        return [
            pltpu.make_async_copy(
                stage.at[slot, which], out.at[slot, expert], stage_sems.at[slot, which]
            )
            for which, out in enumerate(weight_outs)
        ]

    def each(low, high, visit):
        def body(index, carry):
            visit(index)
            return carry

        lax.fori_loop(low, high, body, 0)

    def start_all(copies):
        for copy in copies:
            copy.start()

    def wait_all(copies):
        for copy in copies:
            copy.wait()

    def prefetch(expert):
        start_all(weight_copies(expert))
        low, high = info[G_IMG + expert] // ROW, info[G_IMG + expert + 1] // ROW
        each(low, high, lambda index: start_all(rows_copies(index)))

    each(0, EXPERTS, prefetch)

    def rows_of(expert, row, size):
        for place in range(size // ROW):
            wait_all(rows_copies(row // ROW + place))
        at = pl.ds(pl.multiple_of(row, ROW), size)
        hidden, grad = left[0, at, :], left[1, at, :]
        wide = tile // COLS
        for turn in range(COLS):
            cols = pl.ds(turn * wide, wide)
            bias = b_up[pl.ds(expert, 1), pl.ds(part * tile + turn * wide, wide)]
            up = nn(hidden, w_up[expert, :, cols]) + bias
            grad_act = nt(grad, w_down[expert, cols, :])
            active, slope = gelu_parts(up)
            grad_up = (slope * grad_act).astype(BF16)
            right[0, at, cols] = grad_up
            right[1, at, cols] = active.astype(BF16)
            bias_out[expert, :, cols] += jnp.sum(grad_up.astype(F32), axis=0, keepdims=True)
        for place in range(size // ROW):
            start_all(hidden_copies(row // ROW + place))

    def put(slot, value):
        if not chunk:
            stage[slot, 0] = value.astype(BF16)
            return
        for pair in range(value.shape[0] // (2 * chunk)):
            for core in range(2):
                first = (2 * pair + core) * chunk
                which = (info[CORE] + core) % 2
                stage[slot, which, pair] = value[first : first + chunk].astype(BF16)

    def one_expert(expert):
        wait_all(weight_copies(expert))
        start = info[G_IMG + expert]
        count = info[G_IMG + expert + 1] - start
        blocks = count // BLK
        each(0, blocks, lambda index: rows_of(expert, start + index * BLK, BLK))

        @pl.when(count % BLK > 0)
        def _():
            rows_of(expert, start + blocks * BLK, ROW)

        def one_side(slot):
            @pl.when(expert > 0)
            def _():
                wait_all(stage_copies(slot, expert - 1))

            def product(local, size):
                at = pl.ds(pl.multiple_of(start + local, ROW), size)
                return tn(left[slot, at, :], right[slot, at, :])

            before = (count - 1) // KROWS

            @pl.when(count == 0)
            def _():
                stage[slot] = jnp.zeros(stage.shape[1:], BF16)

            @pl.when(count > KROWS)
            def _():
                acc[...] = product(0, KROWS)

                def more(index):
                    acc[...] += product(index * KROWS, KROWS)

                each(1, before, more)

            for rest in range(ROW, KROWS + ROW, ROW):
                at_end = (count > 0) & (count - before * KROWS == rest)

                @pl.when(at_end & (before == 0))
                def _(rest=rest):
                    put(slot, product(0, rest))

                @pl.when(at_end & (before > 0))
                def _(rest=rest):
                    put(slot, acc[...] + product(before * KROWS, rest))

            start_all(stage_copies(slot, expert))

        each(0, 2, one_side)

    each(0, EXPERTS, one_expert)
    for slot in range(2):
        wait_all(stage_copies(slot, EXPERTS - 1))
    each(0, info[G_PAD] // ROW, lambda index: wait_all(hidden_copies(index)))


def run_hidden(part, parts, info, h, g, w_up, b_up, w_down, chunk):
    rows, width = h.shape
    tile = w_up.shape[2] // parts
    any_spec = pl.BlockSpec(memory_space=pl.ANY)
    vmem = pl.BlockSpec(memory_space=pltpu.VMEM)
    block = (width // (2 * chunk), chunk, tile) if chunk else (width, tile)
    sides = 2 if chunk else 1
    return pl.pallas_call(
        partial(hidden_kernel, part, chunk),
        out_shape=[jax.ShapeDtypeStruct((2, EXPERTS) + block, BF16)] * sides
        + [
            jax.ShapeDtypeStruct((EXPERTS, 1, tile), F32),
            jax.ShapeDtypeStruct((rows, tile), BF16),
            jax.ShapeDtypeStruct((rows, tile), BF16),
        ],
        in_specs=[SMEM_SPEC, any_spec, any_spec, any_spec, vmem, any_spec],
        out_specs=[any_spec] * sides + [vmem, any_spec, any_spec],
        scratch_shapes=[
            pltpu.VMEM((2, rows, width), BF16),
            pltpu.VMEM((2, rows, tile), BF16),
            pltpu.VMEM((EXPERTS, width, tile), BF16),
            pltpu.VMEM((EXPERTS, tile, width), BF16),
            pltpu.VMEM((width, tile), F32),
            pltpu.VMEM((2, sides) + block, BF16),
            pltpu.SemaphoreType.DMA((2, rows // ROW)),
            pltpu.SemaphoreType.DMA((2, EXPERTS)),
            pltpu.SemaphoreType.DMA((2, rows // ROW)),
            pltpu.SemaphoreType.DMA((2, sides)),
        ],
        compiler_params=pltpu.CompilerParams(vmem_limit_bytes=VMEM),
        cost_estimate=cost(18),
        name="hidden",
    )(info, h, g, w_up, b_up, w_down)


SUMS = 16


def finish_kernel(parts, *refs):
    info = refs[0]
    hbm = refs[1 : 3 + 2 * parts]
    up_hbm, down_hbm, gains, downs, w_attn = refs[3 + 2 * parts : 8 + 2 * parts]
    refs = refs[8 + 2 * parts :]
    sums_out, outs_hbm = refs[0], refs[1:5]
    rows_in, acts, dups = refs[5:7], refs[7 : 7 + parts], refs[7 + parts : 7 + 2 * parts]
    refs = refs[7 + 2 * parts :]
    held_out, (w_up, w_down, lower_s, hidden_s) = refs[:4], refs[4:8]
    row_sems, act_sems, out_sems, weight_sems = refs[8:]
    width = lower_s.shape[2]

    groups = range(EXPERTS + 1)
    counts = [info[G_IMG + group + 1] - info[G_IMG + group] for group in groups]
    firsts = [jnp.int32(0)]
    for group in groups:
        firsts.append(firsts[-1] + (counts[group] + BLK - 1) // BLK)
    total = firsts[-1]

    def block_of(index):
        group = sum([(index >= firsts[k]).astype(jnp.int32) for k in groups[1:]])
        first, start, count = firsts[0], info[G_IMG], counts[0]
        for k in groups[1:]:
            first = jnp.where(group == k, firsts[k], first)
            start = jnp.where(group == k, info[G_IMG + k], start)
            count = jnp.where(group == k, counts[k], count)
        local = (index - first) * BLK
        return group, start + local, count - local, index == first

    def halves(index, visit):
        group, row, left, _ = block_of(index)
        for half in range(BLK // ROW):

            @pl.when(half * ROW < left)
            def _(half=half):
                visit(half, pl.ds(pl.multiple_of(row + half * ROW, ROW), ROW), group < EXPERTS)

    def in_copies(index, half, at):
        here = pl.ds(half * ROW, ROW)
        rows = [
            pltpu.make_async_copy(
                source.at[at, :], target.at[index % 4, here, :], row_sems.at[index % 4, half, which]
            )
            for which, (source, target) in enumerate(zip(hbm[:2], rows_in))
        ]
        hidden = [
            pltpu.make_async_copy(
                source.at[at, :], target.at[index % 3, here, :], act_sems.at[index % 3, half, which]
            )
            for which, (source, target) in enumerate(zip(hbm[2:], acts + dups))
        ]
        return rows, hidden

    def fetch(index, action):
        def visit(half, at, real):
            rows, hidden = in_copies(index, half, at)
            for copy in rows:
                action(copy)

            @pl.when(real)
            def _():
                for copy in hidden:
                    action(copy)

        halves(index, visit)

    def send(index, action):
        def visit(half, at, real):
            here = pl.ds(half * ROW, ROW)
            for which, (source, target) in enumerate(zip(held_out, outs_hbm)):
                action(
                    pltpu.make_async_copy(
                        source.at[index % 2, here, :],
                        target.at[at, :],
                        out_sems.at[index % 2, half, which],
                    )
                )

        halves(index, visit)

    def start(copy):
        copy.start()

    def wait(copy):
        copy.wait()

    def weights(group, action):
        for which, (source, target) in enumerate(((up_hbm, w_up), (down_hbm, w_down))):
            action(
                pltpu.make_async_copy(
                    source.at[group], target.at[group], weight_sems.at[group, which]
                )
            )

    sums_out[...] = jnp.zeros_like(sums_out)

    @pl.when(total > 0)
    def _():
        fetch(0, start)

    weights(0, start)

    @pl.when(total > 1)
    def _():
        fetch(1, start)

    for expert in range(1, EXPERTS):
        weights(expert, start)

    tile = acts[0].shape[2]

    def block(index, waited):
        current, _, _, _ = block_of(index)
        mine = jnp.minimum(current, EXPERTS - 1)

        @pl.when(index + 2 < total)
        def _():
            fetch(index + 2, start)

        for expert in range(EXPERTS):

            @pl.when((waited <= expert) & (expert <= mine))
            def _(expert=expert):
                weights(expert, wait)

        @pl.when(index < total)
        def _():
            fetch(index, wait)

        @pl.when(index >= 3)
        def _():
            send(index - 3, wait)

        slot, old = index % 2, (index + 1) % 2
        behind = jnp.maximum(index - 1, 0)
        group, _, left, _ = block_of(behind)
        left = jnp.where(index > 0, left, 0)
        real = group < EXPERTS
        which = pl.ds(jnp.minimum(group, EXPERTS - 1), 1)
        mixed, dx, proj_out, datt = held_out
        sub = BLK // 4

        def row_part(turn):
            at = pl.ds(turn * sub, sub)
            valid = turn * sub + lax.broadcasted_iota(jnp.int32, (sub, 1), 0) < left
            middle = jnp.where(valid, rows_in[0][behind % 4, at, :], 0.0)
            grad = jnp.where(valid, rows_in[1][behind % 4, at, :].astype(F32), 0.0)
            lower = jnp.where(real, lower_s[old, at, :] + downs[which, :], 0.0)
            grad_hidden = jnp.where(valid & real, hidden_s[old, at, :], 0.0)
            mixed[old, at, :] = (middle + lower).astype(BF16)
            normed, inverse = normalize(middle)
            grad_middle = grad + norm_back(grad_hidden * gains[which, :], normed, inverse)
            dx[old, at, :] = grad_middle
            proj = grad_middle.astype(BF16)
            proj_out[old, at, :] = proj
            dsel = jnp.where(real, grad, 0.0)
            values = (proj.astype(F32), grad_hidden * normed, grad_hidden, dsel)
            return [jnp.sum(value, axis=0, keepdims=True) for value in values]

        taken = index % 3

        def compute(multiply):
            lower_new = jnp.zeros((BLK, width), F32)
            hidden_new = jnp.zeros((BLK, width), F32)
            sums, turn = [0.0] * 4, 0
            for part in range(parts):
                cols = pl.ds(part * tile, tile)
                if multiply:
                    lower_new += nn(acts[part][taken], w_down[mine, cols, :])
                if turn < 4:
                    sums = [x + y for x, y in zip(sums, row_part(turn))]
                    turn += 1
                if multiply:
                    hidden_new += nt(dups[part][taken], w_up[mine, :, cols])
                if turn < 4:
                    sums = [x + y for x, y in zip(sums, row_part(turn))]
                    turn += 1
            while turn < 4:
                sums = [x + y for x, y in zip(sums, row_part(turn))]
                turn += 1
            if multiply:
                lower_s[slot] = lower_new
                hidden_s[slot] = hidden_new
            datt[old] = nt(proj_out[old], w_attn[...]).astype(BF16)
            sums_out[pl.ds(0, 1), :] += sums[0]
            for place, value in enumerate(sums[1:]):
                at = pl.ds(1 + place * EXPERTS + jnp.minimum(group, EXPERTS - 1), 1)
                sums_out[at, :] += value

        multiplied = (index < total) & (current < EXPERTS)

        @pl.when(multiplied)
        def _():
            compute(True)

        @pl.when(jnp.logical_not(multiplied))
        def _():
            compute(False)

        @pl.when(index > 0)
        def _():
            send(index - 1, start)

        return jnp.maximum(waited, mine + 1)

    waited = lax.fori_loop(0, jnp.where(total > 0, total + 1, 0), block, jnp.int32(0))
    for expert in range(EXPERTS):

        @pl.when(waited <= expert)
        def _(expert=expert):
            weights(expert, wait)

    for back in (2, 1):

        @pl.when(total >= back)
        def _(back=back):
            send(total - back, wait)


def finish_experts(info, mid, g, acts, dups, w_up, w_down, gains, downs, w_attn):
    rows, width = mid.shape
    parts = len(acts)
    tile = acts[0].shape[1]
    any_spec = pl.BlockSpec(memory_space=pl.ANY)
    vmem = pl.BlockSpec(memory_space=pltpu.VMEM)
    kinds = (BF16, F32, BF16, BF16)
    return pl.pallas_call(
        partial(finish_kernel, parts),
        out_shape=[jax.ShapeDtypeStruct((SUMS, width), F32)]
        + [jax.ShapeDtypeStruct((rows, width), kind) for kind in kinds],
        in_specs=[SMEM_SPEC] + [any_spec] * (4 + 2 * parts) + [vmem] * 3,
        out_specs=[vmem] + [any_spec] * 4,
        scratch_shapes=[pltpu.VMEM((4, BLK, width), F32), pltpu.VMEM((4, BLK, width), BF16)]
        + [pltpu.VMEM((3, BLK, tile), BF16)] * (2 * parts)
        + [pltpu.VMEM((2, BLK, width), kind) for kind in kinds]
        + [pltpu.VMEM(w_up.shape, BF16), pltpu.VMEM(w_down.shape, BF16)]
        + [pltpu.VMEM((2, BLK, width), F32)] * 2
        + [
            pltpu.SemaphoreType.DMA((4, BLK // ROW, 2)),
            pltpu.SemaphoreType.DMA((3, BLK // ROW, 2 * parts)),
            pltpu.SemaphoreType.DMA((2, BLK // ROW, 4)),
            pltpu.SemaphoreType.DMA((EXPERTS, 2)),
        ],
        compiler_params=pltpu.CompilerParams(vmem_limit_bytes=VMEM),
        cost_estimate=cost(30),
        name="finish_experts",
    )(info, mid, g, *acts, *dups, w_up, w_down, gains, downs, w_attn)


def weights_kernel(dp, seq, info, dq, dk, dv, proj, h, att, send_out, keep_out, acc, attn_acc):
    index = pl.program_id(0)

    @pl.when(index == 0)
    def _():
        acc[...] = jnp.zeros_like(acc)
        attn_acc[...] = jnp.zeros_like(attn_acc)

    @pl.when(index * BLK < info[G_END])
    def _():
        row = index * BLK + lax.broadcasted_iota(jnp.int32, (BLK, 1), 0)
        real = row < info[G_END]
        hidden = h[...]
        width = hidden.shape[1]
        for part, grad in enumerate((dq, dk, dv)):
            acc[pl.ds(part * width, width), :] += tn(grad[...], hidden)
        attn_acc[...] += tn(
            jnp.where(real, proj[...], jnp.zeros_like(proj)),
            jnp.where(real, att[...], jnp.zeros_like(att)),
        )

    @pl.when(index == pl.num_programs(0) - 1)
    def _():
        width = attn_acc.shape[0]
        own = width // (dp * seq)
        half = width // 2
        for out, core in ((keep_out, info[CORE]), (send_out, 1 - info[CORE])):
            for pair in range(dp // 2):
                for place in range(seq):
                    device = (2 * pair + core) * seq + place
                    first = pl.ds(pl.multiple_of(device * 3 * own, 8), 3 * own)
                    second = pl.ds(pl.multiple_of(device * own, 8), own)
                    value = jnp.concatenate([acc[first, :], attn_acc[second, :]], axis=0)
                    value = value.astype(BF16)
                    at = pl.ds(place * 4 * own, 4 * own)
                    for lane in range(2):
                        out[lane, 0, pair, at, :] = value[:, lane * half : (lane + 1) * half]


def weights_kernel_plain(info, dq, dk, dv, proj, h, att, qkv_out, attn_out, acc, attn_acc):
    index = pl.program_id(0)

    @pl.when(index == 0)
    def _():
        acc[...] = jnp.zeros_like(acc)
        attn_acc[...] = jnp.zeros_like(attn_acc)

    @pl.when(index * BLK < info[G_END])
    def _():
        row = index * BLK + lax.broadcasted_iota(jnp.int32, (BLK, 1), 0)
        real = row < info[G_END]
        hidden = h[...]
        width = hidden.shape[1]
        for part, grad in enumerate((dq, dk, dv)):
            acc[pl.ds(part * width, width), :] += tn(grad[...], hidden)
        attn_acc[...] += tn(
            jnp.where(real, proj[...], jnp.zeros_like(proj)),
            jnp.where(real, att[...], jnp.zeros_like(att)),
        )

    @pl.when(index == pl.num_programs(0) - 1)
    def _():
        qkv_out[...] = acc[...].astype(BF16)
        attn_out[...] = attn_acc[...].astype(BF16)


def projection_grads(info, dq, dk, dv, proj, h, att, dp, seq):
    rows, width = h.shape
    spec = pl.BlockSpec((BLK, width), lambda i: (i, 0))
    own = width // (dp * seq)
    direct = own % 8 == 0
    if direct:
        shapes = [(2, 1, dp // 2, seq * 4 * own, width // 2)] * 2
        body = partial(weights_kernel, dp, seq)
    else:
        shapes = [(3 * width, width), (width, width)]
        body = weights_kernel_plain
    results = pl.pallas_call(
        body,
        grid=(rows // BLK,),
        out_shape=[jax.ShapeDtypeStruct(shape, BF16) for shape in shapes],
        in_specs=[SMEM_SPEC] + [spec] * 6,
        out_specs=[full(shape) for shape in shapes],
        scratch_shapes=[pltpu.VMEM((3 * width, width), F32), pltpu.VMEM((width, width), F32)],
        compiler_params=pltpu.CompilerParams(vmem_limit_bytes=VMEM),
        cost_estimate=cost(15),
        name="projection_grads",
    )(info, dq, dk, dv, proj, h, att)
    if direct:
        return results[1], results[0]
    d_qkv = results[0].reshape(dp * seq, -1, width)
    d_attn = results[1].reshape(dp * seq, -1, width)
    d_all = jnp.concatenate([d_qkv, d_attn], axis=1).reshape(1, -1, width)
    half = width // 2
    return core_split(jnp.stack([d_all[..., :half], d_all[..., half:]]))


VECTORS = 24


def last_kernel(parts, *refs):
    (info, x, dx, dq, dk, dv, gain, weight, row_sums) = refs[:9]
    biases = refs[9 : 9 + parts]
    out, packed = refs[9 + parts :]
    width = x.shape[1]
    step = pl.program_id(0)

    @pl.when(step == 0)
    def _():
        packed[...] = jnp.zeros_like(packed)
        packed[pl.ds(4, 10), pl.ds(0, width)] = row_sums[pl.ds(0, 10), :]
        for part, bias in enumerate(biases):
            tile = bias.shape[2]
            for expert in range(EXPERTS):
                packed[pl.ds(14 + part * EXPERTS + expert, 1), pl.ds(0, tile)] = bias[expert]

    @pl.when(step * BLK < info[G_END])
    def _():
        hidden = nt(dq[...], weight[:, pl.ds(0, width)])
        hidden += nt(dk[...], weight[:, pl.ds(width, width)])
        hidden += nt(dv[...], weight[:, pl.ds(2 * width, width)])
        normed, inverse = normalize(x[...].astype(F32))
        totals = (hidden * normed, hidden, dq[...].astype(F32), dv[...].astype(F32))
        for place, value in enumerate(totals):
            packed[pl.ds(place, 1), pl.ds(0, width)] += jnp.sum(value, axis=0, keepdims=True)
        out[...] = dx[...] + norm_back(hidden * gain[...], normed, inverse)


def last_norm(info, x, dx, dq, dk, dv, gain, weight, row_sums, biases):
    rows, width = x.shape
    spec = pl.BlockSpec((BLK, width), lambda i: (i, 0))
    cols = max(width, biases[0].shape[2])
    packed = (VECTORS, cols)
    return pl.pallas_call(
        partial(last_kernel, len(biases)),
        grid=(rows // BLK,),
        out_shape=[jax.ShapeDtypeStruct((rows, width), F32), jax.ShapeDtypeStruct(packed, F32)],
        in_specs=[SMEM_SPEC, spec, spec, spec, spec, spec, full(gain.shape), held((width, 3 * width))]
        + [full(row_sums.shape)]
        + [full(bias.shape) for bias in biases],
        out_specs=[spec, full(packed)],
        compiler_params=pltpu.CompilerParams(vmem_limit_bytes=VMEM),
        cost_estimate=cost(14),
        name="last_norm",
    )(info, x, dx, dq, dk, dv, gain, weight, row_sums, *biases)


def swap(value, bit):
    ways = lax.axis_size("dp")
    return lax.ppermute(value, "dp", [(i, i ^ (1 << bit)) for i in range(ways)])


def half_of(parts, axis, bit, mine):
    own = (lax.axis_index("dp") >> bit) & 1
    which = own if mine else 1 - own
    return [lax.dynamic_index_in_dim(part, which, axis, keepdims=False) for part in parts]


DEPTH = 4


def combine_kernel(blocks, arrays, shapes, seq, ways, half_bit, *refs):
    place, sources = refs[0], refs[1 : 1 + arrays]
    outs = refs[1 + arrays : 1 + arrays + shapes]
    scratch = refs[1 + arrays + shapes :]
    here = lax.rem(place[0], ways)

    def start(copies):
        for copy in copies:
            copy.start()

    def wait(copies):
        for copy in copies:
            copy.wait()

    if half_bit is not None:
        kept_v, got_v, own_v, sent_v, half_sems = scratch[-5:]
        half_in = [
            pltpu.make_async_copy(source, target, half_sems.at[which])
            for which, (source, target) in enumerate(zip(sources[-2:], (kept_v, got_v)))
        ]
        half_out = [
            pltpu.make_async_copy(source, target, half_sems.at[2 + which])
            for which, (source, target) in enumerate(zip((own_v, sent_v), outs[-2:]))
        ]
    if blocks:
        in_buf, out_buf, own_buf, send_buf, total, in_sems, out_sems = scratch[:7]

    def fetch(index):
        return [
            pltpu.make_async_copy(
                sources[which].at[where(place)],
                in_buf.at[index % DEPTH, part],
                in_sems.at[index % DEPTH, part],
            )
            for part, (which, where) in enumerate(blocks[index][0])
        ]

    def send(index):
        _, kind, targets, at = blocks[index]
        slot = index % 2
        if kind == "add":
            held = [out_buf.at[slot]]
        else:
            held = [own_buf.at[slot]] + [send_buf.at[slot, hop] for hop in range(len(targets) - 1)]
        return [
            pltpu.make_async_copy(source, outs[target].at[at], out_sems.at[slot, which])
            for which, (source, target) in enumerate(zip(held, targets))
        ]

    for index in range(min(DEPTH - 1, len(blocks))):
        start(fetch(index))
    if half_bit is not None:
        start(half_in)
    for index, (parts, kind, _, _) in enumerate(blocks):
        if index + DEPTH - 1 < len(blocks):
            start(fetch(index + DEPTH - 1))
        wait(fetch(index))
        if index >= 2:
            wait(send(index - 2))
        slot, source = index % 2, index % DEPTH
        value = in_buf[source, 0].astype(F32)
        for part in range(1, len(parts)):
            value = value + in_buf[source, part].astype(F32)
        if kind == "add":
            out_buf[slot] = value.astype(BF16)
        else:
            total[...] = value
            rows = total.shape[1] // seq
            for hop in range(ways):
                for turn in range(seq // ways):
                    at = lax.rem(here + hop, ways) + turn * ways
                    block = total[:, pl.ds(pl.multiple_of(at * rows, 8), rows), :]
                    to = pl.ds(turn * rows, rows)
                    if hop == 0:
                        own_buf[slot, :, to, :] = block
                    else:
                        send_buf[slot, hop - 1, :, to, :] = block.astype(BF16)
        start(send(index))
    if half_bit is not None:
        wait(half_in)
        rows = own_v.shape[2]
        mine = (place[0] >> half_bit) & 1
        kept_v[...] += got_v[...].astype(F32)
        own_v[...] = kept_v[:, :, pl.ds(pl.multiple_of(mine * rows, 8), rows), :]
        other = pl.ds(pl.multiple_of((1 - mine) * rows, 8), rows)
        sent_v[...] = kept_v[:, :, other, :].astype(BF16)
        start(half_out)
        wait(half_out)
    for index in range(max(0, len(blocks) - 2), len(blocks)):
        wait(send(index))


class Flight:

    def __init__(self):
        self.cells = []

    def start(self, value):
        cell = [value]
        self.cells.append(cell)
        return cell

    def land(self, *outputs, later=()):
        now = [cell for cell in self.cells if not any(cell is other for other in later)]
        outputs, arrays = lax.optimization_barrier((outputs, [cell[0] for cell in now]))
        for cell, array in zip(now, arrays):
            cell[0] = array
        self.cells = [cell for cell in self.cells if any(cell is other for other in later)]
        return outputs


class Sum:

    def __init__(self, flight, kept, sent):
        self.flight = flight
        self.bits = lax.axis_size("dp").bit_length() - 1
        self.seq = lax.axis_size("seq")
        self.many, self.pairs, self.chunk, self.cols = kept.shape[1:]
        every = list(range(self.bits - 1, 0, -1))
        shape = (2, self.many) + (2,) * len(every) + (self.chunk, self.cols)
        cells = [[kept.reshape(shape)], flight.start(swap(sent, 0).reshape(shape))]
        self.lanes = [[(cell, lane, every, True) for cell in cells] for lane in range(2)]
        self.left = [list(every), list(every)]
        self.ways = self.seq
        self.own = None
        self.seq_left = None

    def more(self):
        return bool(self.left[0])

    def direct(self):
        return (self.chunk // self.seq) % 8 == 0

    def sources(self, lane, other, free, value):
        results = []
        for cell, first, bits, whole in self.lanes[lane]:

            def where(place, first=first, bits=bits, whole=whole):
                chosen = []
                for bit in bits:
                    if bit in free:
                        chosen.append((value >> (len(free) - 1 - free.index(bit))) & 1)
                    elif bit == other:
                        chosen.append(1 - place[1 + bit])
                    else:
                        chosen.append(place[1 + bit])
                if whole:
                    return (first, slice(None)) + tuple(chosen)
                group = 0
                for one in chosen:
                    group = group * 2 + one
                return (first + group,)

            results.append((cell[0], where))
        return results


def advance(place, steps, closing=None, halving=None):
    arrays, blocks, payloads, turns = [], [], {}, []
    model = steps[0] if steps else closing or halving

    def add(parts, kind, targets, at):
        known = []
        for array, where in parts:
            found = [i for i, other in enumerate(arrays) if other is array]
            if not found:
                arrays.append(array)
            known.append((found[0] if found else len(arrays) - 1, where))
        blocks.append((known, kind, targets, at))

    for total in steps:
        for lane in range(2):
            left = total.left[lane]
            bit = min(left) if lane == 0 else max(left)
            left.remove(bit)
            free = list(left)
            count = payloads.get(bit, 0)
            turns.append((total, lane, bit, free, count))
            for value in range(2 ** len(free)):
                add(total.sources(lane, bit, free, value), "add", bit, count)
                count += 1
            payloads[bit] = count
    order = sorted(payloads)
    blocks = [(parts, kind, [order.index(bit)], at) for parts, kind, bit, at in blocks]
    seq, many, chunk, cols = model.seq, model.many, model.chunk, model.cols
    shapes = [jax.ShapeDtypeStruct((payloads[bit], many, chunk, cols), BF16) for bit in order]
    split = closing is not None and closing.direct()
    ways = closing.ways if split else 2
    rows = chunk // ways
    first_end = len(shapes)
    if closing is not None:
        if split:
            shapes.append(jax.ShapeDtypeStruct((2, many, rows, cols), F32))
            shapes += [jax.ShapeDtypeStruct((2, many, rows, cols), BF16)] * (ways - 1)
        else:
            shapes.append(jax.ShapeDtypeStruct((2, many, chunk, cols), BF16))
        targets = list(range(first_end, len(shapes)))
        for lane in range(2):
            add(closing.sources(lane, None, [], 0), "ends" if split else "add", targets, lane)
    scratch = []
    if blocks:
        most = max(len(parts) for parts, _, _, _ in blocks)
        end_rows = rows if split else 8
        scratch += [
            pltpu.VMEM((DEPTH, most, many, chunk, cols), BF16),
            pltpu.VMEM((2, many, chunk, cols), BF16),
            pltpu.VMEM((2, many, end_rows, cols), F32),
            pltpu.VMEM((2, ways - 1, many, end_rows, cols), BF16),
            pltpu.VMEM((many, chunk, cols), F32),
            pltpu.SemaphoreType.DMA((DEPTH, most)),
            pltpu.SemaphoreType.DMA((2, ways)),
        ]
    first_half, seq_bit = len(shapes), None
    if halving is not None:
        seq_bit = halving.seq_left.pop(0)
        arrays += [halving.own, halving.got[0][0]]
        whole = halving.own.shape
        half = whole[:2] + (whole[2] // 2,) + whole[3:]
        shapes += [jax.ShapeDtypeStruct(half, kind) for kind in (F32, BF16)]
        scratch += [pltpu.VMEM(whole, F32), pltpu.VMEM(whole, BF16)]
        scratch += [pltpu.VMEM(half, F32), pltpu.VMEM(half, BF16), pltpu.SemaphoreType.DMA((4,))]
    any_spec = pl.BlockSpec(memory_space=pl.ANY)
    results = pl.pallas_call(
        partial(combine_kernel, blocks, len(arrays), len(shapes), seq, ways, seq_bit),
        in_specs=[SMEM_SPEC] + [any_spec] * len(arrays),
        out_specs=[any_spec] * len(shapes),
        out_shape=shapes,
        scratch_shapes=scratch,
        compiler_params=pltpu.CompilerParams(vmem_limit_bytes=VMEM),
        cost_estimate=cost(4),
        name="combine",
    )(place, *arrays)

    def go(results):
        got = {bit: model.flight.start(swap(value, bit)) for bit, value in zip(order, results)}
        for total, lane, bit, free, first in turns:
            total.lanes[lane].append((got[bit], first, free, False))
        if halving is not None:
            halving.own = results[first_half]
            pairs = [(i, i ^ (1 << seq_bit)) for i in range(seq)]
            sent = lax.ppermute(results[first_half + 1], "seq", pairs)
            halving.got = [halving.flight.start(sent)]
        if closing is None:
            return
        parts = results[first_end:first_half]
        if not split:
            half = parts[0].reshape(2, many, seq, chunk // seq, cols)
            here = lax.axis_index("seq")
            parts = [
                lax.dynamic_index_in_dim(half, (here + hop) % seq, 2, keepdims=False)
                for hop in range(seq)
            ]
        closing.own = parts[0].astype(F32)
        closing.seq_left = []
        if split and ways < seq:
            pairs = [(i, i ^ 1) for i in range(seq)]
            closing.got = [closing.flight.start(lax.ppermute(parts[1], "seq", pairs))]
            closing.seq_left = list(range(1, seq.bit_length() - 1))
            return
        closing.got = []
        for hop, send in enumerate(parts[1:]):
            pairs = [(i, (i + hop + 1) % seq) for i in range(seq)]
            closing.got.append(closing.flight.start(lax.ppermute(send, "seq", pairs)))

    return list(results), go


def finish_sum(total):
    value = total.own
    for got in total.got:
        value = value + got[0].astype(F32)
    return value.reshape(2, total.many, -1, total.cols)


def vector_hops():
    seq = lax.axis_size("seq")
    hops = []
    for bit in range(seq.bit_length() - 1):
        pairs = [(i, i ^ (1 << bit)) for i in range(seq)]
        hops.append(partial(lax.ppermute, axis_name="seq", perm=pairs))
    return hops + [partial(swap, bit=bit) for bit in range(lax.axis_size("dp").bit_length() - 1)]


def exchange(x, d, rows):
    seq = lax.axis_size("seq")
    first = jnp.concatenate([x[:rows], d[:rows]], axis=1)
    last = jnp.concatenate([x[-rows:], d[-rows:]], axis=1)
    from_left = lax.ppermute(last, "seq", [(i, i + 1) for i in range(seq - 1)])
    from_right = lax.ppermute(first, "seq", [(i + 1, i) for i in range(seq - 1)])
    return (from_left, from_right)


def core_split(value):
    pairs = lax.axis_size("dp") // 2
    two, many, depth, cols = value.shape
    shaped = value.reshape(two, many, pairs, 2, depth // (2 * pairs), cols)
    kept = half_of([shaped], 3, 0, True)[0]
    sent = half_of([shaped], 3, 0, False)[0]
    return (kept, sent)


PARTS = 3


def per_device(
    tokens, item_types, first_gain, first_shift, qkv_weight, query_bias, value_bias, attn_weight,
    attn_bias, second_gain, second_shift, expert_up, up_bias, expert_down, down_bias, cotangent,
):
    tok, width = tokens.shape
    dp, seq = lax.axis_size("dp"), lax.axis_size("seq")
    rows = capacity(tok)
    chunk = width // dp
    chunk = chunk if chunk % 16 == 0 else 0
    bits = [(lax.axis_index("dp") >> bit) & 1 for bit in range(dp.bit_length() - 1)]
    place = jnp.stack([lax.axis_index("seq")] + bits).astype(jnp.int32)
    left, right = exchange(tokens, cotangent, HALO)
    x, g, info = sort_rows(place, item_types, tokens, cotangent, rows, tok * seq)
    x, g, left, right = lax.optimization_barrier((x, g, left, right))
    x, g, h, qkv, att, mid, h2 = forward_rows(
        info, left, right, x, g, first_gain, first_shift, qkv_weight, query_bias, value_bias,
        attn_weight, attn_bias, second_gain, second_shift, tok,
    )

    flight = Flight()

    def window(sums, tied=(), halving=()):
        late = [total for total in list(sums) + list(halving) if total.seq_left]
        steps = [total for total in sums if total.more()]
        closing = [total for total in sums if not total.more() and total.own is None]
        if not (late or steps or closing):
            return (info,) + tuple(tied)
        ready, go = advance(
            place, steps, closing[0] if closing else None, late[0] if late else None
        )
        gate, ready, tied = lax.optimization_barrier((info, ready, tuple(tied)))
        go(ready)
        return (gate,) + tuple(tied)

    sums, up_biases, acts, dups = [], [], [], []
    gate = info
    for part in range(PARTS):
        results = run_hidden(part, PARTS, gate, h2, g, expert_up, up_bias, expert_down, chunk)
        results = flight.land(*results)
        bias, act, dup = results[-3:]
        up_biases.append(bias)
        acts.append(act)
        dups.append(dup)
        if chunk:
            kept, sent = results[:2]
        else:
            kept, sent = core_split(results[0])
        new = Sum(flight, kept, sent)
        new.ways = 2
        (gate,) = window(sums)
        sums.append(new)
    results = finish_experts(
        gate, mid, g, acts, dups, expert_up, expert_down, second_gain, down_bias, attn_weight
    )
    row_sums, mixed, dx, proj, datt = flight.land(*results)
    (gate,) = window(sums)
    results = attend_back(gate, qkv, datt)
    gate, results = lax.optimization_barrier((gate, results))
    m_rows = unsort_rows(gate, mixed, tok)
    dq, dk, dv, m_own, m_left, m_right = flight.land(*results, *m_rows)
    (gate,) = window(sums)
    kept, sent = flight.land(*projection_grads(gate, dq, dk, dv, proj, h, att, dp, seq))
    last = Sum(flight, kept, sent)
    (gate,) = window(sums)

    def send_rows(left, right):
        to_left = lax.ppermute(left, "seq", [(i + 1, i) for i in range(seq - 1)])
        to_right = lax.ppermute(right, "seq", [(i, i + 1) for i in range(seq - 1)])
        return flight.start(to_left), flight.start(to_right)

    def merge(own, got, at):
        cols = slice(at, at + width)
        own = own.at[:HALO].add(got[1][0][:, cols].astype(own.dtype))
        return own.at[tok - HALO :].add(got[0][0][:, cols].astype(own.dtype))

    results = last_norm(gate, x, dx, dq, dk, dv, first_gain, qkv_weight, row_sums, up_biases)
    grad_x, packed = flight.land(*results)

    hops = vector_hops()

    def hop(packed, moved=None):
        packed = packed if moved is None else packed + moved[0]
        return packed, flight.start(hops.pop(0)(packed))

    packed, moved = hop(packed)
    (gate,) = window([last], halving=sums[-1:])
    while any(total.own is None or total.seq_left for total in sums):
        (gate,) = window(sums)
    gate, moved[0] = lax.optimization_barrier((gate, moved[0]))
    flight.cells = [cell for cell in flight.cells if cell is not moved]
    packed, moved = hop(packed, moved)
    g_own, left, right = flight.land(*unsort_rows(gate, grad_x, tok))
    left = jnp.concatenate([left, m_left], axis=1)
    right = jnp.concatenate([right, m_right], axis=1)
    expert_sums = [finish_sum(total) for total in sums]
    packed, moved = hop(packed, moved)
    later = []
    while last.own is None:
        _, g_own, m_own = window([last], tied=[g_own, m_own])
        if not later:
            g_got = send_rows(left, right)
            later = list(g_got)
        if last.own is None:
            expert_sums = flight.land(*expert_sums, later=later)

    packed, moved = hop(packed, moved)
    merged = (merge(g_own, g_got, 0), merge(m_own, g_got, width))
    grad_out, mixed_out = flight.land(*merged, later=[moved])
    while hops:
        packed, moved = hop(packed, moved)
    packed = packed + moved[0]
    last_sums = finish_sum(last)

    own = width // (dp * seq)
    rank = lax.axis_index("dp") * seq + lax.axis_index("seq")
    vectors = lax.dynamic_slice(packed, (0, rank * own), (14, own))
    tile = up_biases[0].shape[2]
    up_total = packed[14 : 14 + PARTS * EXPERTS, :tile].reshape(PARTS, EXPERTS, tile)
    sum_up = jnp.concatenate([total[0] for total in expert_sums], axis=-1)
    sum_down = jnp.concatenate([total[1] for total in expert_sums], axis=-1).swapaxes(1, 2)
    last_sums = jnp.concatenate([last_sums[0, 0], last_sums[1, 0]], axis=1).T

    return (
        mixed_out,
        grad_out,
        vectors[0],
        vectors[1],
        last_sums[:, : 3 * own],
        vectors[2],
        vectors[3],
        last_sums[:, 3 * own :],
        vectors[4],
        vectors[5:8],
        vectors[8:11],
        sum_up,
        up_total.swapaxes(0, 1).reshape(EXPERTS, -1),
        sum_down,
        vectors[11:14],
    )


def solution(mesh):
    split = P(("dp", "seq"))
    in_specs = (P(("dp", "seq"), None), P("dp", None)) + (P(),) * 13 + (P(("dp", "seq"), None),)
    out_specs = (
        P(("dp", "seq"), None),
        P(("dp", "seq"), None),
        split,
        split,
        P(None, ("dp", "seq")),
        split,
        split,
        P(None, ("dp", "seq")),
        split,
        P(None, ("dp", "seq")),
        P(None, ("dp", "seq")),
        P(None, ("dp", "seq"), None),
        P(),
        P(None, None, ("dp", "seq")),
        P(None, ("dp", "seq")),
    )
    return jax.shard_map(
        per_device, mesh=mesh, in_specs=in_specs, out_specs=out_specs, check_vma=False
    )
```
